32 devices in a mesh: group: 2 (over core), dp: 16 (over z, y, x).
Axes of the slice: x: 2, y: 2, z: 4, core: 2. Of those that a mesh axis runs over, the one named last changes fastest.
Arguments:
- tokens: bfloat16 [2, 16384, 768], P('group', 'dp'), may hold values from -6 to 6
- cotangent: bfloat16 [2, 16384, 768], P('group', 'dp'), may hold values from -6 to 6
- grid_h: int32 [2, 64], P('group', 'dp'), may hold values from 0 to 22, as said below
- grid_w: int32 [2, 64], P('group', 'dp'), may hold values from 0 to 22, as said below
- owner_block: int32 [16], replicated, may hold values from 0 to 15, as said below
- master: float32 [9216, 768], P('dp')
- first_mom: float32 [9216, 768], P('dp'), may hold values from -0.00056339084 to 0.00056339084
- second_mom: float32 [9216, 768], P('dp'), may hold values from 1.4107079e-07 to 5.6428314e-07
- vectors: float32 [14, 768], replicated
- vec_first: float32 [14, 768], replicated, may hold values from -0.0022535634 to 0.0022535634
- vec_second: float32 [14, 768], replicated, may hold values from 2.2571326e-06 to 9.02853e-06
Outputs:
- block_out: bfloat16 [2, 16384, 768], P('group', 'dp')
- input_grad: float32 [2, 16384, 768], P('group', 'dp')
- mat_grad: float32 [9216, 768], P('dp')
- mat_second: float32 [9216, 768], P('dp')
- mat_weight: float32 [9216, 768], P('dp')
- vec_grad: float32 [14, 768], replicated
- vec_second_new: float32 [14, 768], replicated
- vec_weight: float32 [14, 768], replicated
- grad_norm: float32 [], replicated
The draws below stay inside these ranges and needn't reach their ends.
Inputs may be any that keep to these rules, and one draw needn't show every extreme that they name: `grid_h`: A device's image slots are used from the first on, unused ones (height 0) after them; a device of the first group uses 4 // 2 to 4 slots with sides from 12 to 16; of the second group 4 // 4 to 4 // 2 (at least one) with sides from 16 to 22; heights and widths are drawn independently. `grid_w`: zero exactly where grid_h is zero; otherwise as grid_h. `owner_block`: A permutation of 0 to 16 - 1.
All inputs are finite; a program needn't handle non-finite values.
Results may differ from the reference program's by a relative error of at most 0.02.
Values may be sent and summed in bfloat16 or wider, within the bound.
No kernel may reach another device: no remote copies, remote signals or barrier semaphores. Data moves between devices by JAX's collectives and lax.ppermute only.
A program may use at most 320 MiB of HBM per device.

```python
import math
from functools import partial
import jax
import jax.numpy as jnp
from jax import lax

D = 768
HEADS = 12
HEAD_DIM = 64
STACK = 9216
VEC_ROWS = 14
TOK_DEV = 1024
SIDE0 = 16
SIDE1 = 22
IMG_DEV = 4
STEP = 7
TOKENS = 16384
N_DP = 16


def grid_sizes(key):
    base = jax.random.fold_in(key, 11)
    subkeys = jax.random.split(base, 4)
    lo_first = max(1, IMG_DEV // 2)
    hi_second = max(1, IMG_DEV // 2)
    lo_second = max(1, IMG_DEV // 4)
    counts = jnp.stack([jax.random.randint(subkeys[0], (N_DP,), lo_first, IMG_DEV + 1), jax.random.randint(subkeys[1], (N_DP,), lo_second, hi_second + 1)])
    bottoms = jnp.array([SIDE0 * 3 // 4, SIDE1 * 3 // 4], jnp.int32)[:, None, None]
    widths_range = jnp.array([SIDE0 - SIDE0 * 3 // 4 + 1, SIDE1 - SIDE1 * 3 // 4 + 1], jnp.int32)[:, None, None]
    heights = bottoms + jax.random.randint(subkeys[2], (2, N_DP, IMG_DEV), 0, 1 << 20) % widths_range
    widths = bottoms + jax.random.randint(subkeys[3], (2, N_DP, IMG_DEV), 0, 1 << 20) % widths_range
    active = jnp.arange(IMG_DEV)[None, None, :] < counts[:, :, None]
    return (jnp.where(active, heights, 0).reshape(2, N_DP * IMG_DEV).astype(jnp.int32), jnp.where(active, widths, 0).reshape(2, N_DP * IMG_DEV).astype(jnp.int32))


def draw_grid_h(key, part):
    return grid_sizes(key)[0]


def draw_grid_w(key, part):
    return grid_sizes(key)[1]


def owner_order(key):
    return jax.random.permutation(jax.random.fold_in(key, 23), N_DP).astype(jnp.int32)


def draw_owner_block(key, part):
    return owner_order(key)


def draw_master(key, part):
    order = owner_order(key)
    inner = jax.random.fold_in(key, 29)
    base = jax.random.normal(inner, (12 * D, D), jnp.float32)
    row_scale = jnp.concatenate([jnp.full((3 * D,), D ** (-0.5), jnp.float32), jnp.full((D,), 4.0 * D ** (-0.5), jnp.float32), jnp.full((4 * D,), D ** (-0.5), jnp.float32), jnp.full((4 * D,), (4 * D) ** (-0.5), jnp.float32)])
    logical = base * row_scale[:, None]
    return logical.reshape(N_DP, 12 * D // N_DP, D)[order].reshape(12 * D, D)


def draw_vectors(key, part):
    subkeys = jax.random.split(jax.random.fold_in(key, 31), 4)
    gains = jnp.exp(0.15 * jax.random.normal(subkeys[0], (2, D), jnp.float32))
    shifts = 0.3 * jax.random.normal(subkeys[1], (11, D), jnp.float32)
    magnitude = jnp.exp(jax.random.uniform(subkeys[2], (D // 2,), jnp.float32, math.log(0.05), 0.0))
    phase = jax.random.uniform(subkeys[3], (D // 2,), jnp.float32, -math.pi, math.pi)
    freqs = jnp.concatenate([magnitude * jnp.cos(phase), magnitude * jnp.sin(phase)])
    return jnp.concatenate([gains[0:1], shifts[0:1], gains[1:2], shifts[1:2], shifts[2:11], freqs[None]], axis=0)


def block_scale(own_key, extent, pieces, least, top_value):
    def one(axis_at, shards_of):
        steps = jax.random.uniform(jax.random.fold_in(jax.random.fold_in(own_key, 6), axis_at), (shards_of,), jnp.float32, least / len(pieces), top_value / len(pieces))
        return jnp.repeat(jnp.exp(steps), extent[axis_at] // shards_of).reshape((-1,) + (1,) * (len(extent) - axis_at - 1))

    level = one(*pieces[0])
    for cut in pieces[1:]:
        level = level * one(*cut)
    return level


def gaussian(stream_key, shape, scale, reach, shards=(), kind=jnp.bfloat16):
    level = block_scale(stream_key, shape, shards, -0.22, 0.18) if shards else 1.0
    drawn = jax.random.normal(stream_key, shape, jnp.float32) * scale * level
    return jnp.minimum(jnp.maximum(drawn, -reach), reach).astype(kind)


def setup_inputs(seed: int = 0) -> dict:
    seeds = jax.random.split(jax.random.key(seed), 12)
    return {
        "tokens": gaussian(seeds[0], (2, TOKENS, D), 1.0, 6.0, ((0, 2), (1, 16))),
        "cotangent": gaussian(seeds[1], (2, TOKENS, D), 1.0, 6.0, ((0, 2), (1, 16))),
        "grid_h": draw_grid_h(jax.random.fold_in(seeds[11], 71), 0),
        "grid_w": draw_grid_w(jax.random.fold_in(seeds[11], 71), 0),
        "owner_block": draw_owner_block(jax.random.fold_in(seeds[11], 71), 0),
        "master": draw_master(jax.random.fold_in(seeds[11], 71), 0),
        "first_mom": jnp.clip(jax.random.uniform(seeds[6], (STACK, D), jnp.float32, -0.00056339084, 0.00056339084) * block_scale(seeds[6], (STACK, D), ((0, 16),), -0.4, 0.0), -0.00056339084, 0.00056339084),
        "second_mom": jnp.clip(jnp.exp(math.log(5.642831411023508e-07) - 1.3862944 * jax.random.uniform(seeds[7], (STACK, D), jnp.float32) ** block_scale(seeds[7], (STACK, D), ((0, 16),), -0.2, 0.2)), 1.410707852755877e-07, 5.642831411023508e-07),
        "vectors": draw_vectors(jax.random.fold_in(seeds[11], 71), 0),
        "vec_first": jnp.clip(jax.random.uniform(seeds[9], (VEC_ROWS, D), jnp.float32, -0.0022535634, 0.0022535634), -0.0022535634, 0.0022535634),
        "vec_second": jnp.clip(jnp.exp(jax.random.uniform(seeds[10], (VEC_ROWS, D), jnp.float32, math.log(2.257132564409403e-06), math.log(9.028530257637613e-06))), 2.257132564409403e-06, 9.028530257637613e-06),
    }


@jax.custom_vjp
def low(v):
    return lax.optimization_barrier(v.astype(jnp.bfloat16)).astype(jnp.float32)

@jax.custom_vjp
def low_back(v):
    return v

def low_keep(v):
    return (low(v), None)

def low_pass(kept, grad):
    return (grad,)

def back_keep(v):
    return (v, None)

def back_low(kept, grad):
    return (low(grad),)
low.defvjp(low_keep, low_pass)
low_back.defvjp(back_keep, back_low)

def place_tokens(heights, widths, count):
    sizes = heights * widths
    ends = jnp.cumsum(sizes).astype(jnp.int32)
    starts = ends - sizes
    places = jnp.arange(count, dtype=jnp.int32)
    segment = lax.optimization_barrier(jnp.sum((places[:, None] >= ends[None, :]).astype(jnp.int32), axis=1))
    slots = jnp.arange(heights.shape[0], dtype=jnp.int32)
    picks = (segment[:, None] == slots[None, :]).astype(jnp.int32)
    begin = lax.optimization_barrier(jnp.sum(picks * starts[None, :], axis=1))
    across = jnp.maximum(lax.optimization_barrier(jnp.sum(picks * widths[None, :], axis=1)), 1)
    offset = places - begin
    live = places < ends[-1]
    return (segment, offset // across, offset % across, live)

def layer_norm(value, gain, shift):
    centre = value - lax.optimization_barrier(jnp.mean(value, axis=-1, keepdims=True))
    spread = lax.optimization_barrier(jnp.mean(centre * centre, axis=-1, keepdims=True))
    return centre * lax.rsqrt(spread + 1e-06) * gain + shift

def rotate(queries, keys_in, freqs, rows_pos, cols_pos):
    heads = queries.shape[1]
    half = queries.shape[2] // 2
    width = freqs.shape[0]
    freq_x = freqs[:width // 2].reshape(heads, half)
    freq_y = freqs[width // 2:].reshape(heads, half)
    angle = rows_pos.astype(jnp.float32)[:, None, None] * freq_x[None] + cols_pos.astype(jnp.float32)[:, None, None] * freq_y[None]
    cosine = jnp.cos(angle)
    sine = jnp.sin(angle)

    def turn(part):
        first = part[..., :half]
        second = part[..., half:]
        return jnp.concatenate([first * cosine - second * sine, first * sine + second * cosine], axis=-1)
    return (turn(queries), turn(keys_in))

def dot_last(left, right):
    return lax.dot_general(left, right, (((1,), (1,)), ((), ())), precision=lax.Precision.HIGHEST, preferred_element_type=jnp.float32)

def forward_one(inputs, mat, vec, segment, rows_pos, cols_pos):
    width = inputs.shape[1]
    count = inputs.shape[0]
    scale = HEAD_DIM ** (-0.5)
    normed_first = low(layer_norm(inputs, vec[0], vec[1]))
    qkv_full = low_back(dot_last(normed_first, mat[:3 * width]) + vec[4:7].reshape(3 * width))
    queries = qkv_full[:, :width].reshape(count, HEADS, HEAD_DIM)
    keys_pre = qkv_full[:, width:2 * width].reshape(count, HEADS, HEAD_DIM)
    values = low(qkv_full[:, 2 * width:].reshape(count, HEADS, HEAD_DIM))
    query_rot, key_rot = rotate(queries, keys_pre, vec[13], rows_pos, cols_pos)
    query_rot = low(query_rot)
    key_rot = low(key_rot)
    scores = low_back(jnp.einsum('qhd,khd->hqk', query_rot, key_rot, precision=lax.Precision.HIGHEST) * scale)
    same = segment[:, None] == segment[None, :]
    probs = low(jax.nn.softmax(jnp.where(same[None], scores, -1000000000.0), axis=-1))
    mixed = jnp.einsum('hqk,khd->qhd', probs, values, precision=lax.Precision.HIGHEST).reshape(count, width)
    attn_out = low_back(low(mixed))
    branch_one = low_back(dot_last(attn_out, mat[3 * width:4 * width]) + vec[7])
    middle = inputs + branch_one
    normed_second = low(layer_norm(middle, vec[2], vec[3]))
    up_pre = low_back(dot_last(normed_second, mat[4 * width:8 * width]) + vec[8:12].reshape(4 * width))
    hidden = low(jax.nn.gelu(up_pre, approximate=False))
    branch_two = low_back(jnp.dot(hidden, mat[8 * width:], precision=lax.Precision.HIGHEST, preferred_element_type=jnp.float32) + vec[12])
    return middle + branch_two

def adam(weight, first, second, grad, rate, decay):
    first_new = 0.5 * first + 0.5 * grad
    second_new = 0.5 * second + 0.5 * grad * grad
    correct = 1.0 - 0.5 ** STEP
    direction = first_new / correct / (jnp.sqrt(second_new / correct) + 1e-08)
    return (second_new, weight - rate * (direction + decay * weight))

def reference(tokens, cotangent, grid_h, grid_w, owner_block, master, first_mom, second_mom, vectors, vec_first, vec_second):
    width = HEADS * HEAD_DIM
    buffers = 2 * N_DP
    block_rows = 12 * width // N_DP
    placer = partial(place_tokens, count=TOK_DEV)
    segment, rows_pos, cols_pos, live = jax.vmap(placer)(grid_h.reshape(buffers, IMG_DEV), grid_w.reshape(buffers, IMG_DEV))
    inverse = jnp.argsort(owner_block).astype(jnp.int32)
    logical = master.reshape(N_DP, block_rows, width)[inverse].reshape(12 * width, width)
    inputs = tokens.astype(jnp.float32).reshape(buffers, TOK_DEV, width)
    grad_out = cotangent.astype(jnp.float32).reshape(buffers, TOK_DEV, width) * live[..., None].astype(jnp.float32)

    def whole(inputs_all, mat, vec):

        def one(items):
            return jax.checkpoint(forward_one)(items[0], mat, vec, items[1], items[2], items[3])
        return lax.map(one, (inputs_all, segment, rows_pos, cols_pos))
    outputs, pull = jax.vjp(whole, inputs, logical, vectors)
    input_grad, grad_mat, grad_vec = pull(grad_out)
    owner_grad = grad_mat.reshape(N_DP, block_rows, width)[owner_block].reshape(12 * width, width)
    grad_norm = jnp.sqrt(jnp.sum(owner_grad * owner_grad) + jnp.sum(grad_vec * grad_vec))
    clip = jnp.minimum(1.0, 1.0 / (grad_norm + 1e-06))
    mat_grad = owner_grad * clip
    vec_grad = grad_vec * clip
    mat_second, mat_weight = adam(master, first_mom, second_mom, mat_grad, 0.02, 0.05)
    vec_second_new, vec_weight = adam(vectors, vec_first, vec_second, vec_grad, 0.2, 0.0)
    block_out = outputs.astype(jnp.bfloat16).reshape(2, N_DP * TOK_DEV, width)
    return (block_out, input_grad.reshape(2, N_DP * TOK_DEV, width), mat_grad, mat_second, mat_weight, vec_grad, vec_second_new, vec_weight, grad_norm)
```

```python
import functools
import jax
import jax.numpy as jnp
from jax import lax
from jax.experimental import pallas as pl
from jax.experimental.pallas import tpu as pltpu

F32 = jnp.float32
BF16 = jnp.bfloat16
LAST = (((1,), (1,)), ((), ()))
FIRST = (((0,), (0,)), ((), ()))
PLAIN = (((1,), (0,)), ((), ()))
MASKED = -1e9


def mm(left, right, dims):
    return lax.dot_general(left, right, dims, preferred_element_type=F32)


def norm_parts(value):
    centre = value - jnp.mean(value, axis=-1, keepdims=True)
    spread = jnp.mean(centre * centre, axis=-1, keepdims=True)
    inverse = lax.rsqrt(spread + 1e-6)
    return centre * inverse, inverse


def norm_back(unit, inverse, grad, gain):
    scaled = grad * gain
    first = jnp.mean(scaled, axis=-1, keepdims=True)
    second = jnp.mean(scaled * unit, axis=-1, keepdims=True)
    return inverse * (scaled - first - unit * second)


def swap_halves(value):
    lane = lax.broadcasted_iota(jnp.int32, value.shape, 1)
    return jnp.where(
        lane % 64 < 32, pltpu.roll(value, 96, 1), pltpu.roll(value, 32, 1)
    )


def split3(value):
    one = value.astype(BF16).astype(F32)
    rest = value - one
    two = rest.astype(BF16).astype(F32)
    return one, two, rest - two


def attend_kernel(x_ref, g_ref, b_ref, wq_ref, wk_ref, wv_ref, bq_ref, bk_ref, bv_ref,
                  cos_ref, sin_ref, qm_ref, km_ref,
                  n1_ref, q_ref, k_ref, v_ref, attn_ref, stat_ref, n1_s):
    count = x_ref.shape[0]

    @pl.when(pl.program_id(0) == 0)
    def _():
        unit, _ = norm_parts(x_ref[...].astype(F32))
        n1 = (unit * g_ref[...] + b_ref[...]).astype(BF16)
        n1_s[...] = n1
        n1_ref[...] = n1

    w = jnp.concatenate([wq_ref[...], wk_ref[...], wv_ref[...]], axis=0)
    qkv = mm(n1_s[...], w, LAST)
    q = qkv[:, :128] + bq_ref[...]
    k = qkv[:, 128:256] + bk_ref[...]
    v = (qkv[:, 256:] + bv_ref[...]).astype(BF16)
    c = cos_ref[...]
    s = sin_ref[...]
    qr = ((q * c + swap_halves(q) * s).astype(BF16).astype(F32) * 0.125).astype(BF16)
    kr = (k * c + swap_halves(k) * s).astype(BF16)
    q_ref[...] = qr
    k_ref[...] = kr
    v_ref[...] = v
    lane = lax.broadcasted_iota(jnp.int32, (1, 128), 1)
    k_aug = jnp.concatenate([kr, km_ref[...]], axis=1)
    v_aug = jnp.concatenate([v, jnp.ones((count, 128), BF16)], axis=1)
    zero = jnp.zeros((), BF16)
    tile = 256
    for i in range(count // tile):
        rows = pl.ds(i * tile, tile)
        out = None
        stats = []
        for h in (0, 1):
            mine = (lane // 64) == h
            qa = jnp.concatenate(
                [jnp.where(mine, qr[i * tile:(i + 1) * tile], zero), qm_ref[rows, :]], axis=1)
            scores = mm(qa, k_aug, LAST)
            top = jnp.max(scores, axis=-1, keepdims=True)
            e = jnp.exp(scores - top).astype(BF16)
            o = mm(e, v_aug, PLAIN)
            total = o[:, 128:]
            o = o[:, :128] / total
            out = o if out is None else jnp.where(lane < 64, out, o)
            stats.append(top + jnp.log(total[:, :1]))
        attn_ref[rows, :] = out.astype(BF16)
        stat_ref[rows, :] = jnp.where(lane < 64, stats[0], stats[1])


def attend(x, gain, shift, wqkv, bqkv, cos, sin, qm, km):
    count, width = x.shape
    pairs = width // 128
    whole = lambda p: (0, 0)
    col = lambda p: (0, p)
    specs = [
        pl.BlockSpec((count, width), whole),
        pl.BlockSpec((1, width), whole),
        pl.BlockSpec((1, width), whole),
        pl.BlockSpec((128, width), lambda p: (p, 0)),
        pl.BlockSpec((128, width), lambda p: (p + pairs, 0)),
        pl.BlockSpec((128, width), lambda p: (p + 2 * pairs, 0)),
        pl.BlockSpec((1, 128), col),
        pl.BlockSpec((1, 128), lambda p: (0, p + pairs)),
        pl.BlockSpec((1, 128), lambda p: (0, p + 2 * pairs)),
        pl.BlockSpec((count, 128), col),
        pl.BlockSpec((count, 128), col),
        pl.BlockSpec((count, 128), whole),
        pl.BlockSpec((count, 128), whole),
    ]
    outs = [pl.BlockSpec((count, width), whole)] + [pl.BlockSpec((count, 128), col)] * 5
    shape = lambda d: jax.ShapeDtypeStruct((count, width), d)
    return pl.pallas_call(
        attend_kernel,
        grid=(pairs,),
        in_specs=specs,
        out_specs=outs,
        out_shape=[shape(BF16)] * 5 + [shape(F32)],
        scratch_shapes=[pltpu.VMEM((count, width), BF16)],
        compiler_params=pltpu.CompilerParams(vmem_limit_bytes=56 * 2**20),
        name="attend",
    )(x, gain, shift, wqkv, wqkv, wqkv, bqkv, bqkv, bqkv, cos, sin, qm, km)


HALF_ERFC = (
    0.09317889578353007, 0.09147806194869737, 0.10061136147272338, 0.023612303617162326,
    0.20424612730309272, -0.1755704972361086, 0.23011593265708702, -0.06767218931083122,
)


def gelu_both(x):
    e = jnp.exp(x * x * -0.5)
    d = jnp.abs(x) * (0.33 * 0.7071067811865476) + 1.0
    t = pl.reciprocal(d, approx=True)
    t = t * (2.0 - d * t)
    poly = jnp.full_like(t, HALF_ERFC[-1])
    for c in HALF_ERFC[-2::-1]:
        poly = poly * t + c
    tail = poly * t * e
    cdf = jnp.where(x >= 0, 1.0 - tail, tail)
    return x * cdf, cdf + x * e * 0.3989422804014327


def mlp_kernel(n2_ref, dz_ref, w1_ref, w2_ref, b1_ref, out_ref, dn_ref, g1_ref, g2_ref, gb_ref):
    @pl.when(pl.program_id(0) == 0)
    def _():
        out_ref[...] = jnp.zeros_like(out_ref)
        dn_ref[...] = jnp.zeros_like(dn_ref)

    n2 = n2_ref[...]
    dz = dz_ref[...]
    w1 = w1_ref[...]
    w2 = w2_ref[...]
    pre = mm(n2, w1, LAST) + b1_ref[...]
    act, slope = gelu_both(pre)
    hidden = act.astype(BF16)
    out_ref[...] += mm(hidden, w2, PLAIN)
    g2_ref[...] = mm(hidden, dz, FIRST).astype(BF16)
    dpre = (mm(dz, w2, LAST) * slope).astype(BF16)
    gb_ref[...] = jnp.sum(dpre.astype(F32), axis=0, keepdims=True)
    g1_ref[...] = mm(dpre, n2, FIRST).astype(BF16)
    dn_ref[...] += mm(dpre, w1, PLAIN)


def mlp(n2, dz, w1, w2, b1, tile=256):
    count, width = n2.shape
    units = w1.shape[0]
    whole = lambda t: (0, 0)
    row = lambda t: (t, 0)
    return pl.pallas_call(
        mlp_kernel,
        grid=(units // tile,),
        in_specs=[
            pl.BlockSpec((count, width), whole),
            pl.BlockSpec((count, width), whole),
            pl.BlockSpec((tile, width), row),
            pl.BlockSpec((tile, width), row),
            pl.BlockSpec((1, tile), lambda t: (0, t)),
        ],
        out_specs=[
            pl.BlockSpec((count, width), whole),
            pl.BlockSpec((count, width), whole),
            pl.BlockSpec((tile, width), row),
            pl.BlockSpec((tile, width), row),
            pl.BlockSpec((1, tile), lambda t: (0, t)),
        ],
        out_shape=[
            jax.ShapeDtypeStruct((count, width), F32),
            jax.ShapeDtypeStruct((count, width), F32),
            jax.ShapeDtypeStruct((units, width), BF16),
            jax.ShapeDtypeStruct((units, width), BF16),
            jax.ShapeDtypeStruct((1, units), F32),
        ],
        compiler_params=pltpu.CompilerParams(vmem_limit_bytes=56 * 2**20),
        name="mlp",
    )(n2, dz, w1, w2, b1)


def back_kernel(q_ref, k_ref, v_ref, da_ref, at_ref, stat_ref, cos_ref, sin_ref, qm_ref, km_ref,
                pos_ref, n1_ref, wq_ref, wk_ref, wv_ref,
                gq_ref, gk_ref, gv_ref, gb_ref, gf_ref, dn_ref):
    count = q_ref.shape[0]

    @pl.when(pl.program_id(0) == 0)
    def _():
        dn_ref[...] = jnp.zeros_like(dn_ref)

    lane = lax.broadcasted_iota(jnp.int32, (1, 128), 1)
    zero = jnp.zeros((), BF16)
    q = q_ref[...]
    k = k_ref[...]
    v = v_ref[...]
    da = da_ref[...]
    prod = da.astype(F32) * at_ref[...].astype(F32)
    qm = qm_ref[...]
    k_aug = jnp.concatenate([k, km_ref[...]], axis=1)
    v_aug = jnp.concatenate([v, jnp.broadcast_to((lane < 2).astype(BF16), (count, 128))], axis=1)
    tile = 256
    dq = dk = dv = None
    for h in (0, 1):
        mine = (lane // 64) == h
        qh = jnp.where(mine, q, zero)
        kh = jnp.where(mine, k, zero)
        dah = jnp.where(mine, da, zero)
        delta = jnp.sum(jnp.where(mine, prod, 0.0), axis=-1, keepdims=True)
        d1, d2, _ = split3(delta)
        l1, l2, l3 = split3(stat_ref[:, 64 * h:64 * h + 1])
        q_aug = jnp.concatenate(
            [qh, jnp.where(lane == 8, -l1, jnp.where(lane == 9, -l2, jnp.where(lane == 10, -l3, qm.astype(F32)))).astype(BF16)], axis=1)
        da_aug = jnp.concatenate(
            [dah, jnp.where(lane == 0, -d1, jnp.where(lane == 1, -d2, 0.0)).astype(BF16)], axis=1)
        dks, dvs, dqh = [], [], None
        for i in range(count // tile):
            sl = slice(i * tile, (i + 1) * tile)
            p = jnp.exp(mm(k_aug[sl], q_aug, LAST))
            pl_low = p.astype(BF16)
            dp = mm(v_aug[sl], da_aug, LAST)
            ds = (p * dp).astype(BF16)
            dvs.append(mm(pl_low, dah, PLAIN))
            dks.append(mm(ds, qh, PLAIN))
            part = mm(ds, kh[sl], FIRST)
            dqh = part if dqh is None else dqh + part
        dkh = jnp.concatenate(dks, axis=0)
        dvh = jnp.concatenate(dvs, axis=0)
        dq = dqh if dq is None else dq + dqh
        dk = dkh if dk is None else dk + dkh
        dv = dvh if dv is None else dv + dvh
    dq = dq * 0.125
    c = cos_ref[...]
    s = sin_ref[...]
    turned = dq * swap_halves(q.astype(F32) * 8.0) + dk * swap_halves(k.astype(F32))
    turned = jnp.where(lane % 64 < 32, -turned, turned)
    gf_ref[...] = jnp.concatenate(
        [jnp.sum(turned * pos_ref[:, 0:1], axis=0, keepdims=True),
         jnp.sum(turned * pos_ref[:, 1:2], axis=0, keepdims=True)] + [jnp.zeros((6, 128), F32)], axis=0)
    dqp = (dq * c - swap_halves(dq) * s).astype(BF16)
    dkp = (dk * c - swap_halves(dk) * s).astype(BF16)
    dvp = dv.astype(BF16)
    row = lambda a: jnp.sum(a.astype(F32), axis=0, keepdims=True)
    gb_ref[...] = jnp.concatenate([row(dqp), row(dkp), row(dvp), jnp.zeros((5, 128), F32)], axis=0)
    d = jnp.concatenate([dqp, dkp, dvp], axis=1)
    w = jnp.concatenate([wq_ref[...], wk_ref[...], wv_ref[...]], axis=0)
    dn_ref[...] += mm(d, w, PLAIN)
    g = mm(d, n1_ref[...], FIRST).astype(BF16)
    gq_ref[...] = g[:128]
    gk_ref[...] = g[128:256]
    gv_ref[...] = g[256:]


def attend_back(q, k, v, da, attn, stat, cos, sin, qm, km, pos, n1, wqkv):
    count, width = q.shape
    pairs = width // 128
    whole = lambda p: (0, 0)
    col = lambda p: (0, p)
    tall = pl.BlockSpec((count, 128), col)
    fixed = pl.BlockSpec((count, 128), whole)
    w = [pl.BlockSpec((128, width), lambda p, j=j: (p + j * pairs, 0)) for j in range(3)]
    grad = pl.BlockSpec((128, width), lambda p: (p, 0))
    small = pl.BlockSpec((8, 128), col)
    return pl.pallas_call(
        back_kernel,
        grid=(pairs,),
        in_specs=[tall] * 8 + [fixed] * 2 + [pl.BlockSpec((count, 2), whole), pl.BlockSpec((count, width), whole)] + w,
        out_specs=[grad] * 3 + [small] * 2 + [pl.BlockSpec((count, width), whole)],
        out_shape=[jax.ShapeDtypeStruct((width, width), BF16)] * 3
        + [jax.ShapeDtypeStruct((8, width), F32)] * 2
        + [jax.ShapeDtypeStruct((count, width), F32)],
        compiler_params=pltpu.CompilerParams(vmem_limit_bytes=56 * 2**20),
        name="attend_back",
    )(q, k, v, da, attn, stat, cos, sin, qm, km, pos, n1, wqkv, wqkv, wqkv)


from jax.sharding import PartitionSpec as P

HEADS = 12
STEP = 7


def place_tokens(heights, widths, count):
    sizes = heights * widths
    ends = jnp.cumsum(sizes)
    starts = ends - sizes
    places = jnp.arange(count, dtype=jnp.int32)
    segment = jnp.sum((places[:, None] >= ends[None, :]).astype(jnp.int32), axis=1)
    slots = jnp.arange(heights.shape[0], dtype=jnp.int32)
    picks = (segment[:, None] == slots[None, :]).astype(jnp.int32)
    begin = jnp.sum(picks * starts[None, :], axis=1)
    across = jnp.maximum(jnp.sum(picks * widths[None, :], axis=1), 1)
    offset = places - begin
    live = places < ends[-1]
    return (segment, offset // across, offset % across, live)


def layer_norm(value, gain, shift):
    centre = value - jnp.mean(value, axis=-1, keepdims=True)
    spread = jnp.mean(centre * centre, axis=-1, keepdims=True)
    return centre * lax.rsqrt(spread + 1e-06) * gain + shift


def adam(weight, first, second, grad, rate, decay):
    first_new = 0.5 * first + 0.5 * grad
    second_new = 0.5 * second + 0.5 * grad * grad
    correct = 1.0 - 0.5**STEP
    direction = first_new / correct / (jnp.sqrt(second_new / correct) + 1e-08)
    return (second_new, weight - rate * (direction + decay * weight))


def pairwise(bits, total):
    return [(i, i ^ bits) for i in range(total)]


def sum_everywhere(value, devices):
    if devices & (devices - 1):
        return lax.psum(value, "dp")
    step = 1
    while step < devices:
        value = value + lax.ppermute(value, "dp", pairwise(step, devices))
        step *= 2
    return value


def gather_weights(master, owner_block, devices):
    block_rows, width = master.shape
    low = master.astype(BF16)
    inverse = jnp.argsort(owner_block)
    if block_rows % 32:
        gathered = lax.all_gather(low, "dp", axis=0, tiled=True)
        return gathered.reshape(devices, block_rows, width)[inverse].reshape(-1, width)
    half = block_rows // 2
    core = lax.axis_index("group")
    mine = lax.all_gather(
        lax.dynamic_slice_in_dim(low, core * half, half, 0), "dp", axis=0, tiled=False
    )
    other = lax.ppermute(mine, "group", [(0, 1), (1, 0)])
    both = jnp.concatenate([mine, other], axis=0)
    first = inverse + devices * core
    second = inverse + devices * (1 - core)
    order = jnp.stack([first, second], axis=1).reshape(-1)
    return both[order].reshape(-1, width)


def reduce_grads(local_mat, owner_block, devices):
    rows, width = local_mat.shape
    block_rows = rows // devices
    if block_rows % 32 or devices != 16:
        term = local_mat.reshape(devices, block_rows, width)[owner_block].reshape(rows, width)
        share = lax.psum_scatter(term.astype(F32), "dp", scatter_dimension=0, tiled=True)
        return lax.psum(share.astype(BF16), "group").astype(F32)
    half = block_rows // 2
    core = lax.axis_index("group")
    me = lax.axis_index("dp")
    deep = me // 4
    flip = jnp.arange(2)

    def order(side):
        first = jnp.where(side == 0, 1, 2)
        second = 3 - first
        low_bits = (
            (me % 4)
            ^ (first * (1 - flip))[:, None, None]
            ^ (second * (1 - flip))[None, :, None]
        )
        dest = low_bits + 4 * jnp.arange(4)[None, None, :]
        return owner_block[dest.reshape(-1)] * 2 + side

    units = local_mat.reshape(2 * devices, half, width)
    give = units[order(1 - core)]
    keep = units[order(core)]
    got = lax.ppermute(give, "group", [(0, 1), (1, 0)])

    def add(one, two):
        return one.astype(F32) + two.astype(F32)

    def cross(bit0, bit1):
        total = 2 * devices
        perm = [(i, i ^ (bit0 if i < devices else bit1)) for i in range(total)]
        return lambda value: lax.ppermute(value, ("group", "dp"), perm)

    send = add(keep[:8], got[:8]).astype(BF16)
    hold = add(keep[8:], got[8:])
    came = cross(1, 2)(send)
    send = add(hold[:4], came[:4]).astype(BF16)
    hold = add(hold[4:], came[4:])
    came = cross(2, 1)(send)
    hold = add(hold, came)
    low = hold.astype(BF16)
    total = lax.dynamic_index_in_dim(hold, deep, 0, keepdims=False)
    for step in (1, 2, 3):
        part = lax.dynamic_index_in_dim(low, (deep + step) % 4, 0, keepdims=False)
        perm = [(i, (i + 4 * step) % 16) for i in range(16)]
        total = total + lax.ppermute(part, "dp", perm).astype(F32)
    other = lax.ppermute(total.astype(BF16), "group", [(0, 1), (1, 0)]).astype(F32)
    total = total.astype(BF16).astype(F32)
    top = jnp.where(core == 0, total, other)
    bottom = jnp.where(core == 0, other, total)
    return jnp.concatenate([top, bottom], axis=0)


def local(
    tokens,
    cotangent,
    grid_h,
    grid_w,
    owner_block,
    master,
    first_mom,
    second_mom,
    vectors,
    vec_first,
    vec_second,
):
    devices = lax.axis_size("dp")
    count = tokens.shape[1]
    width = tokens.shape[2]
    heads = HEADS
    head_dim = width // heads
    half = head_dim // 2
    segment, rows_pos, cols_pos, live = place_tokens(grid_h[0], grid_w[0], count)
    weights = gather_weights(master, owner_block, devices)
    w_qkv = weights[: 3 * width]
    w_proj = weights[3 * width : 4 * width]
    w_up = weights[4 * width : 8 * width]
    w_down = weights[8 * width :]

    freqs = vectors[13]

    def spread(part):
        return jnp.broadcast_to(part.reshape(heads, 1, half), (heads, 2, half)).reshape(1, width)

    angle = rows_pos.astype(F32)[:, None] * spread(freqs[: width // 2]) + cols_pos.astype(F32)[
        :, None
    ] * spread(freqs[width // 2 :])
    lower = (jnp.arange(width) % head_dim < half)[None]
    cosine = jnp.cos(angle)
    sine = jnp.sin(angle)
    sine = jnp.where(lower, -sine, sine)
    ids = jnp.arange(128)[None]
    match = segment[:, None] == ids
    key_mask = jnp.where(match | ((ids >= 8) & (ids < 11)), 1.0, 0.0).astype(BF16)
    query_mask = jnp.where((ids < 8) & ~match, MASKED, 0.0).astype(BF16)
    places = jnp.stack([rows_pos, cols_pos], axis=1).astype(F32)

    first_in, query, key, value, attn_out, stat = attend(
        tokens[0], vectors[0:1], vectors[1:2], w_qkv, vectors[4:7].reshape(1, 3 * width),
        cosine, sine, query_mask, key_mask,
    )
    inputs = tokens[0].astype(F32)
    middle = inputs + mm(attn_out, w_proj, LAST) + vectors[7]
    normed_second, norm_two_back = jax.vjp(layer_norm, middle, vectors[2], vectors[3])
    second_in = normed_second.astype(BF16)
    grad_two = jnp.where(live[:, None], cotangent[0], jnp.zeros((), BF16))
    grad_out = grad_two.astype(F32)
    branch_two, grad_second_in, grad_up, grad_down, bias_up = mlp(
        second_in, grad_two, w_up, w_down, vectors[8:12].reshape(1, 4 * width)
    )
    block_out = (middle + branch_two + vectors[12]).astype(BF16)
    bias_down = jnp.sum(grad_out, axis=0)
    grad_mid_norm, gain_two, shift_two = norm_two_back(grad_second_in)
    grad_middle = grad_out + grad_mid_norm
    grad_one = grad_middle.astype(BF16)
    grad_proj = mm(grad_one, attn_out, FIRST).astype(BF16)
    bias_proj = jnp.sum(grad_one.astype(F32), axis=0)
    grad_attn = mm(grad_one, w_proj, PLAIN).astype(BF16)
    grad_q, grad_k, grad_v, grad_bias, grad_freq, grad_first_in = attend_back(
        query, key, value, grad_attn, attn_out, stat, cosine, sine, query_mask, key_mask,
        places, first_in, w_qkv,
    )
    unused, norm_one_back = jax.vjp(layer_norm, inputs, vectors[0], vectors[1])
    grad_in_norm, gain_one, shift_one = norm_one_back(grad_first_in)
    input_grad = grad_middle + grad_in_norm
    grad_freqs = grad_freq[:2].reshape(2, heads, 2, half).sum(2).reshape(1, width)
    local_vec = jnp.concatenate(
        [
            gain_one[None],
            shift_one[None],
            gain_two[None],
            shift_two[None],
            grad_bias[:3],
            bias_proj[None],
            bias_up.reshape(4, width),
            bias_down[None],
            grad_freqs,
        ],
        axis=0,
    )
    local_mat = jnp.concatenate([grad_q, grad_k, grad_v, grad_proj, grad_up, grad_down], axis=0)
    share = reduce_grads(local_mat, owner_block, devices)
    vec_total = sum_everywhere(lax.psum(local_vec, "group") if devices & (devices - 1) else
                               local_vec + lax.ppermute(local_vec, "group", [(0, 1), (1, 0)]), devices)
    square = sum_everywhere(jnp.sum(share * share).reshape(1, 1), devices)[0, 0]
    grad_norm = jnp.sqrt(square + jnp.sum(vec_total * vec_total))
    clip = jnp.minimum(1.0, 1.0 / (grad_norm + 1e-06))
    mat_grad = share * clip
    vec_grad = vec_total * clip
    mat_second, mat_weight = adam(master, first_mom, second_mom, mat_grad, 0.02, 0.05)
    vec_second_new, vec_weight = adam(vectors, vec_first, vec_second, vec_grad, 0.2, 0.0)
    return (
        block_out[None],
        input_grad[None],
        mat_grad,
        mat_second,
        mat_weight,
        vec_grad,
        vec_second_new,
        vec_weight,
        grad_norm,
    )


def solution(mesh):
    return jax.shard_map(
        local,
        mesh=mesh,
        in_specs=(
            P("group", "dp", None),
            P("group", "dp", None),
            P("group", "dp"),
            P("group", "dp"),
            P(),
            P("dp", None),
            P("dp", None),
            P("dp", None),
            P(),
            P(),
            P(),
        ),
        out_specs=(
            P("group", "dp", None),
            P("group", "dp", None),
            P("dp", None),
            P("dp", None),
            P("dp", None),
            P(),
            P(),
            P(),
            P(),
        ),
        check_vma=False,
    )
```

```python
import functools
import jax
import jax.numpy as jnp
from jax import lax
from jax.experimental import pallas as pl
from jax.experimental.pallas import tpu as pltpu

F32 = jnp.float32
BF16 = jnp.bfloat16
LAST = (((1,), (1,)), ((), ()))
FIRST = (((0,), (0,)), ((), ()))
PLAIN = (((1,), (0,)), ((), ()))
MASKED = -1e9


def mm(left, right, dims):
    return lax.dot_general(left, right, dims, preferred_element_type=F32)


def norm_parts(value):
    centre = value - jnp.mean(value, axis=-1, keepdims=True)
    spread = jnp.mean(centre * centre, axis=-1, keepdims=True)
    inverse = lax.rsqrt(spread + 1e-6)
    return centre * inverse, inverse


def norm_back(unit, inverse, grad, gain):
    scaled = grad * gain
    first = jnp.mean(scaled, axis=-1, keepdims=True)
    second = jnp.mean(scaled * unit, axis=-1, keepdims=True)
    return inverse * (scaled - first - unit * second)


def swap_halves(value):
    lane = lax.broadcasted_iota(jnp.int32, value.shape, 1)
    return jnp.where(
        lane % 64 < 32, pltpu.roll(value, 96, 1), pltpu.roll(value, 32, 1)
    )


def split3(value):
    one = value.astype(BF16).astype(F32)
    rest = value - one
    two = rest.astype(BF16).astype(F32)
    return one, two, rest - two


LARGE = 208
SMALL = 80


def place_pieces(core, slot_ref, mine, other, block, side, dst, sem):
    for which, (first, second, small) in enumerate((mine, other)):
        @pl.when((core == side) if which == 0 else (core != side))
        def _():
            large_slot = slot_ref[2 * which, block]
            small_slot = slot_ref[2 * which + 1, block]

            @pl.when(large_slot < 8)
            def _():
                pltpu.make_async_copy(first.at[large_slot], dst(0, LARGE), sem).start()

            @pl.when(large_slot >= 8)
            def _():
                pltpu.make_async_copy(second.at[large_slot - 8], dst(0, LARGE), sem).start()

            pltpu.make_async_copy(small.at[small_slot], dst(LARGE, SMALL), sem).start()


def attend_kernel(blocks, core_ref, slot_ref, x_ref, g_ref, b_ref, bq_ref, bk_ref, bv_ref,
                  cos_ref, sin_ref, qm_ref, km_ref, *rest):
    if blocks:
        mine, other = rest[0:3], rest[3:6]
        n1_ref, q_ref, k_ref, v_ref, attn_ref, stat_ref, w_ref, n1_s, w_s, near, far = rest[6:]
    else:
        w_ref, n1_ref, q_ref, k_ref, v_ref, attn_ref, stat_ref, n1_s, w_s, near = rest
    count, width = x_ref.shape
    step = pl.program_id(0)

    @pl.when(step == 0)
    def _():
        if blocks:
            core = core_ref[0]
            rows = w_ref.shape[0] // blocks

            def start(block, target, sem):
                for side in (0, 1):
                    def dst(offset, size):
                        base = block * rows + side * (rows // 2) + offset
                        return target.at[pl.ds(pl.multiple_of(base, 16), size)]
                    place_pieces(core, slot_ref, mine, other, block, side, dst, sem)

            def near_block(block, carry):
                start(block, w_s, near)
                return carry

            def far_block(block, carry):
                start(block, w_ref, far)
                return carry

            lax.fori_loop(0, w_s.shape[0] // rows, near_block, 0)
            lax.fori_loop(0, blocks, far_block, 0)
        else:
            pltpu.make_async_copy(w_ref.at[pl.ds(0, 3 * width)], w_s, near).start()
        unit, _ = norm_parts(x_ref[...].astype(F32))
        n1 = (unit * g_ref[...] + b_ref[...]).astype(BF16)
        n1_s[...] = n1
        n1_ref[...] = n1
        pltpu.make_async_copy(w_s, w_s, near).wait()

    def third(j):
        return w_s[pl.ds(pl.multiple_of(j * width + step * 128, 128), 128), :]

    w = jnp.concatenate([third(0), third(1), third(2)], axis=0)
    qkv = mm(n1_s[...], w, LAST)
    q = qkv[:, :128] + bq_ref[...]
    k = qkv[:, 128:256] + bk_ref[...]
    v = (qkv[:, 256:] + bv_ref[...]).astype(BF16)
    c = cos_ref[...]
    s = sin_ref[...]
    qr = ((q * c + swap_halves(q) * s).astype(BF16).astype(F32) * 0.125).astype(BF16)
    kr = (k * c + swap_halves(k) * s).astype(BF16)
    q_ref[...] = qr
    k_ref[...] = kr
    v_ref[...] = v
    lane = lax.broadcasted_iota(jnp.int32, (1, 128), 1)
    k_aug = jnp.concatenate([kr, km_ref[...]], axis=1)
    v_aug = jnp.concatenate([v, jnp.ones((count, 128), BF16)], axis=1)
    zero = jnp.zeros((), BF16)
    tile = 256
    for i in range(count // tile):
        rows = pl.ds(i * tile, tile)
        out = None
        stats = []
        for h in (0, 1):
            mine_lanes = (lane // 64) == h
            qa = jnp.concatenate(
                [jnp.where(mine_lanes, qr[i * tile:(i + 1) * tile], zero), qm_ref[rows, :]], axis=1)
            scores = mm(qa, k_aug, LAST)
            top = jnp.max(scores, axis=-1, keepdims=True)
            e = jnp.exp(scores - top).astype(BF16)
            o = mm(e, v_aug, PLAIN)
            total = o[:, 128:]
            o = o[:, :128] / total
            out = o if out is None else jnp.where(lane < 64, out, o)
            stats.append(top + jnp.log(total[:, :1]))
        attn_ref[rows, :] = out.astype(BF16)
        stat_ref[rows, :] = jnp.where(lane < 64, stats[0], stats[1])

    if blocks:
        @pl.when(step == pl.num_programs(0) - 1)
        def _():
            pltpu.make_async_copy(w_ref, w_ref, far).wait()


def attend(core, slots, x, gain, shift, bqkv, cos, sin, qm, km, weights, stack):
    count, width = x.shape
    pairs = width // 128
    pieces = isinstance(weights, tuple)
    blocks = slots.shape[1] if pieces else 0
    whole = lambda p: (0, 0)
    col = lambda p: (0, p)
    smem = pl.BlockSpec(memory_space=pltpu.SMEM)
    hbm = pl.BlockSpec(memory_space=pl.ANY)
    given = weights if pieces else (weights,)
    specs = [smem, smem] + [
        pl.BlockSpec((count, width), whole),
        pl.BlockSpec((1, width), whole),
        pl.BlockSpec((1, width), whole),
        pl.BlockSpec((1, 128), col),
        pl.BlockSpec((1, 128), lambda p: (0, p + pairs)),
        pl.BlockSpec((1, 128), lambda p: (0, p + 2 * pairs)),
        pl.BlockSpec((count, 128), col),
        pl.BlockSpec((count, 128), col),
        pl.BlockSpec((count, 128), whole),
        pl.BlockSpec((count, 128), whole),
    ] + [hbm] * len(given)
    outs = [pl.BlockSpec((count, width), whole)] + [pl.BlockSpec((count, 128), col)] * 5
    shape = lambda d: jax.ShapeDtypeStruct((count, width), d)
    shapes = [shape(BF16)] * 5 + [shape(F32)]
    scratch = [pltpu.VMEM((count, width), BF16), pltpu.VMEM((3 * width, width), BF16), pltpu.SemaphoreType.DMA]
    if pieces:
        outs.append(hbm)
        shapes.append(jax.ShapeDtypeStruct((stack, width), BF16))
        scratch.append(pltpu.SemaphoreType.DMA)
    return pl.pallas_call(
        functools.partial(attend_kernel, blocks),
        grid=(pairs,),
        in_specs=specs,
        out_specs=outs,
        out_shape=shapes,
        scratch_shapes=scratch,
        compiler_params=pltpu.CompilerParams(vmem_limit_bytes=56 * 2**20),
        cost_estimate=pl.CostEstimate(flops=30 * 10**9, bytes_accessed=40 * 10**6, transcendentals=0),
        name="attend",
    )(core, slots, x, gain, shift, bqkv, bqkv, bqkv, cos, sin, qm, km, *given)


HALF_ERFC = (
    0.09317889578353007, 0.09147806194869737, 0.10061136147272338, 0.023612303617162326,
    0.20424612730309272, -0.1755704972361086, 0.23011593265708702, -0.06767218931083122,
)


def gelu_both(x):
    e = jnp.exp(x * x * -0.5)
    d = jnp.abs(x) * (0.33 * 0.7071067811865476) + 1.0
    t = pl.reciprocal(d, approx=True)
    t = t * (2.0 - d * t)
    poly = jnp.full_like(t, HALF_ERFC[-1])
    for c in HALF_ERFC[-2::-1]:
        poly = poly * t + c
    tail = poly * t * e
    cdf = jnp.where(x >= 0, 1.0 - tail, tail)
    return x * cdf, cdf + x * e * 0.3989422804014327


def send_rows(core, block_rows, stage, row, base, keep_ref, give_ref, sem):
    if not block_rows:
        rows = stage.shape[0]
        pltpu.make_async_copy(
            stage, keep_ref.at[pl.ds(pl.multiple_of(row - base, 64), rows)], sem
        ).start()
        return

    def one(index, carry):
        at = row + 64 * index
        block = lax.div(at, block_rows)
        inner = pl.ds(pl.multiple_of(at - block * block_rows, 64), 64)
        slot = lax.div(block, 2) - base // 2
        source = stage.at[pl.ds(pl.multiple_of(64 * index, 64), 64)]
        own = lax.rem(block, 2) == core

        @pl.when(own)
        def _():
            pltpu.make_async_copy(source, keep_ref.at[slot, inner], sem).start()

        @pl.when(jnp.logical_not(own))
        def _():
            pltpu.make_async_copy(source, give_ref.at[slot, inner], sem).start()

        return carry

    lax.fori_loop(0, stage.shape[0] // 64, one, 0)


def mlp_kernel(block_rows, base, core_ref, x_ref, at_ref, cot_ref, live_ref, vec_ref, wo_ref, w1_ref, w2_ref, b1_ref,
               out_ref, dm_ref, da_ref, sums_ref, gb_ref, keep_ref, give_ref,
               middle_s, n2_s, dz_s, acc_s, stage_s, proj_s, sems):
    step = pl.program_id(0)
    last = pl.num_programs(0) - 1
    count, width = x_ref.shape
    core = core_ref[0]
    tile = w1_ref.shape[0]

    @pl.when(step == 0)
    def _():
        middle = x_ref[...].astype(F32) + mm(at_ref[...], wo_ref[...], LAST) + vec_ref[7:8, :]
        middle_s[...] = middle
        unit, _ = norm_parts(middle)
        n2_s[...] = (unit * vec_ref[2:3, :] + vec_ref[3:4, :]).astype(BF16)
        dz_s[...] = jnp.where(live_ref[...] > 0.5, cot_ref[...].astype(F32), 0.0).astype(BF16)
        acc_s[...] = jnp.zeros_like(acc_s)
        dm_ref[...] = jnp.zeros_like(dm_ref)

    slot = lax.rem(step, 2)

    @pl.when(step >= 2)
    def _():
        pltpu.make_async_copy(stage_s.at[slot], stage_s.at[slot], sems.at[slot]).wait()

    n2 = n2_s[...]
    dz = dz_s[...]
    w1 = w1_ref[...]
    w2 = w2_ref[...]
    pre = mm(n2, w1, LAST) + b1_ref[...]
    act, slope = gelu_both(pre)
    hidden = act.astype(BF16)
    acc_s[...] += mm(hidden, w2, PLAIN)
    stage_s[slot, 1] = mm(hidden, dz, FIRST).astype(BF16)
    dpre = (mm(dz, w2, LAST) * slope).astype(BF16)
    gb_ref[...] = jnp.sum(dpre.astype(F32), axis=0, keepdims=True)
    stage_s[slot, 0] = mm(dpre, n2, FIRST).astype(BF16)
    dm_ref[...] += mm(dpre, w1, PLAIN)
    for j in (0, 1):
        send_rows(core, block_rows, stage_s.at[slot, j], (4 + 4 * j) * width + step * tile,
                  base, keep_ref, give_ref, sems.at[slot])

    @pl.when(step == last)
    def _():
        middle = middle_s[...]
        out_ref[...] = (middle + acc_s[...] + vec_ref[12:13, :]).astype(BF16)
        unit, inverse = norm_parts(middle)
        dn = dm_ref[...]
        dy = dz_s[...].astype(F32)
        dm = dy + norm_back(unit, inverse, dn, vec_ref[2:3, :])
        dm_ref[...] = dm
        low = dm.astype(BF16)
        row = lambda a: jnp.sum(a, axis=0, keepdims=True)
        sums_ref[...] = jnp.concatenate(
            [row(dn * unit), row(dn), row(low.astype(F32)), row(dy), jnp.zeros((4, width), F32)], axis=0)
        proj_s[...] = mm(low, at_ref[...], FIRST).astype(BF16)
        send_rows(core, block_rows, proj_s, 3 * width, base, keep_ref, give_ref, sems.at[2])
        da_ref[...] = mm(low, wo_ref[...], PLAIN).astype(BF16)
        pltpu.make_async_copy(stage_s.at[slot], stage_s.at[slot], sems.at[slot]).wait()
        pltpu.make_async_copy(stage_s.at[1 - slot], stage_s.at[1 - slot], sems.at[1 - slot]).wait()
        pltpu.make_async_copy(proj_s, proj_s, sems.at[2]).wait()


def grad_shapes(block_rows, rows, width):
    if block_rows:
        half = jax.ShapeDtypeStruct((rows // block_rows // 2, block_rows, width), BF16)
        return [half, half]
    return [jax.ShapeDtypeStruct((rows, width), BF16), jax.ShapeDtypeStruct((16, width), BF16)]


def mlp(core, x, attn, cot, live, vectors, weights, b1, block_rows, tile=256):
    count, width = x.shape
    units = 4 * width
    stack = weights.shape[0]
    base = 3 * width // block_rows if block_rows else 3 * width
    whole = lambda t: (0, 0)
    big = pl.BlockSpec((count, width), whole)
    hbm = pl.BlockSpec(memory_space=pl.ANY)
    return pl.pallas_call(
        functools.partial(mlp_kernel, block_rows, base),
        grid=(units // tile,),
        in_specs=[pl.BlockSpec(memory_space=pltpu.SMEM), big, big, big, pl.BlockSpec((count, 1), whole),
                  pl.BlockSpec(vectors.shape, whole),
                  pl.BlockSpec((width, width), lambda t: (3, 0)),
                  pl.BlockSpec((tile, width), lambda t: (4 * width // tile + t, 0)),
                  pl.BlockSpec((tile, width), lambda t: (8 * width // tile + t, 0)),
                  pl.BlockSpec((1, tile), lambda t: (0, t))],
        out_specs=[big, big, big, pl.BlockSpec((8, width), whole), pl.BlockSpec((1, tile), lambda t: (0, t)), hbm, hbm],
        out_shape=[
            jax.ShapeDtypeStruct((count, width), BF16),
            jax.ShapeDtypeStruct((count, width), F32),
            jax.ShapeDtypeStruct((count, width), BF16),
            jax.ShapeDtypeStruct((8, width), F32),
            jax.ShapeDtypeStruct((1, units), F32),
        ] + grad_shapes(block_rows, stack - 3 * width, width),
        scratch_shapes=[
            pltpu.VMEM((count, width), F32),
            pltpu.VMEM((count, width), BF16),
            pltpu.VMEM((count, width), BF16),
            pltpu.VMEM((count, width), F32),
            pltpu.VMEM((2, 2, tile, width), BF16),
            pltpu.VMEM((width, width), BF16),
            pltpu.SemaphoreType.DMA((3,)),
        ],
        compiler_params=pltpu.CompilerParams(vmem_limit_bytes=60 * 2**20),
        cost_estimate=pl.CostEstimate(flops=60 * 10**9, bytes_accessed=50 * 10**6, transcendentals=0),
        name="mlp",
    )(core, x, attn, cot, live, vectors, weights, weights, weights, b1)


def back_kernel(block_rows, start, first, final, core_ref, q_ref, k_ref, v_ref, da_ref, at_ref, stat_ref, cos_ref, sin_ref,
                qm_ref, km_ref, pos_ref, n1_ref, wq_ref, wk_ref, wv_ref, *rest):
    if not first:
        before_ref, rest = rest[0], rest[3:]
    if final:
        x_ref, dm_ref, vec_ref = rest[:3]
        rest = rest[3:]
        gb_ref, gf_ref, ig_ref, ln_ref, keep_ref, give_ref, dn_ref, stage_s, sems = rest
    else:
        gb_ref, gf_ref, dn_ref, keep_ref, give_ref, stage_s, sems = rest
    count = q_ref.shape[0]
    width = n1_ref.shape[1]
    step = pl.program_id(0)
    core = core_ref[0]

    @pl.when(step == 0)
    def _():
        dn_ref[...] = jnp.zeros_like(dn_ref) if first else before_ref[...]

    lane = lax.broadcasted_iota(jnp.int32, (1, 128), 1)
    zero = jnp.zeros((), BF16)
    q = q_ref[...]
    k = k_ref[...]
    v = v_ref[...]
    da = da_ref[...]
    prod = da.astype(F32) * at_ref[...].astype(F32)
    qm = qm_ref[...].astype(F32)
    k_aug = jnp.concatenate([k, km_ref[...]], axis=1)
    v_aug = jnp.concatenate([v, jnp.broadcast_to((lane < 2).astype(BF16), (count, 128))], axis=1)
    tile = 256
    dq = dk = dv = None
    for h in (0, 1):
        mine = (lane // 64) == h
        qh = jnp.where(mine, q, zero)
        kh = jnp.where(mine, k, zero)
        dah = jnp.where(mine, da, zero)
        delta = jnp.sum(jnp.where(mine, prod, 0.0), axis=-1, keepdims=True)
        d1, d2, _ = split3(delta)
        l1, l2, l3 = split3(stat_ref[:, 64 * h:64 * h + 1])
        extra = jnp.where(lane == 8, -l1, jnp.where(lane == 9, -l2, jnp.where(lane == 10, -l3, qm)))
        q_aug = jnp.concatenate([qh, extra.astype(BF16)], axis=1)
        da_aug = jnp.concatenate(
            [dah, jnp.where(lane == 0, -d1, jnp.where(lane == 1, -d2, 0.0)).astype(BF16)], axis=1)
        dks, dvs, dqh = [], [], None
        for i in range(count // tile):
            sl = slice(i * tile, (i + 1) * tile)
            p = jnp.exp(mm(k_aug[sl], q_aug, LAST))
            dp = mm(v_aug[sl], da_aug, LAST)
            ds = (p * dp).astype(BF16)
            dvs.append(mm(p.astype(BF16), dah, PLAIN))
            dks.append(mm(ds, qh, PLAIN))
            part = mm(ds, kh[sl], FIRST)
            dqh = part if dqh is None else dqh + part
        dkh = jnp.concatenate(dks, axis=0)
        dvh = jnp.concatenate(dvs, axis=0)
        dq = dqh if dq is None else dq + dqh
        dk = dkh if dk is None else dk + dkh
        dv = dvh if dv is None else dv + dvh
    dq = dq * 0.125
    c = cos_ref[...]
    s = sin_ref[...]
    turned = dq * swap_halves(q.astype(F32) * 8.0) + dk * swap_halves(k.astype(F32))
    turned = jnp.where(lane % 64 < 32, -turned, turned)
    row = lambda a: jnp.sum(a, axis=0, keepdims=True)
    gf_ref[...] = jnp.concatenate(
        [row(turned * pos_ref[:, 0:1]), row(turned * pos_ref[:, 1:2]), jnp.zeros((6, 128), F32)], axis=0)
    dqp = (dq * c - swap_halves(dq) * s).astype(BF16)
    dkp = (dk * c - swap_halves(dk) * s).astype(BF16)
    dvp = dv.astype(BF16)
    gb_ref[...] = jnp.concatenate(
        [row(dqp.astype(F32)), row(dkp.astype(F32)), row(dvp.astype(F32)), jnp.zeros((5, 128), F32)], axis=0)
    d = jnp.concatenate([dqp, dkp, dvp], axis=1)
    w = jnp.concatenate([wq_ref[...], wk_ref[...], wv_ref[...]], axis=0)
    dn_ref[...] += mm(d, w, PLAIN)
    slot = lax.rem(step, 2)

    @pl.when(step >= 2)
    def _():
        pltpu.make_async_copy(stage_s.at[slot], stage_s.at[slot], sems.at[slot]).wait()

    stage_s[slot] = mm(d, n1_ref[...], FIRST).astype(BF16)
    for j in range(3):
        send_rows(core, block_rows, stage_s.at[slot, pl.ds(128 * j, 128)], j * width + (start + step) * 128,
                  0, keep_ref, give_ref, sems.at[slot])

    @pl.when(step == pl.num_programs(0) - 1)
    def _():
        pltpu.make_async_copy(stage_s.at[slot], stage_s.at[slot], sems.at[slot]).wait()
        pltpu.make_async_copy(stage_s.at[1 - slot], stage_s.at[1 - slot], sems.at[1 - slot]).wait()
        if final:
            unit, inverse = norm_parts(x_ref[...].astype(F32))
            dn = dn_ref[...]
            ig_ref[...] = dm_ref[...] + norm_back(unit, inverse, dn, vec_ref[0:1, :])
            ln_ref[...] = jnp.concatenate([row(dn * unit), row(dn), jnp.zeros((6, width), F32)], axis=0)


def attend_back(core, start, stop, before, final, q, k, v, da, attn, stat, cos, sin, qm, km, pos, n1, weights, block_rows):
    count, width = q.shape
    pairs = width // 128
    whole = lambda p: (0, 0)
    col = lambda p: (0, p + start)
    big = pl.BlockSpec((count, width), whole)
    tall = pl.BlockSpec((count, 128), col)
    fixed = pl.BlockSpec((count, 128), whole)
    hbm = pl.BlockSpec(memory_space=pl.ANY)
    w = [pl.BlockSpec((128, width), lambda p, j=j: (p + start + j * pairs, 0)) for j in range(3)]
    small = pl.BlockSpec((8, 128), lambda p: (0, p))
    in_specs = ([pl.BlockSpec(memory_space=pltpu.SMEM)] + [tall] * 8 + [fixed] * 2
                + [pl.BlockSpec((count, 2), whole), big] + w)
    operands = [core, q, k, v, da, attn, stat, cos, sin, qm, km, pos, n1, weights, weights, weights]
    out_specs = [small] * 2
    out_shape = [jax.ShapeDtypeStruct((8, 128 * (stop - start)), F32)] * 2
    dn_shape = jax.ShapeDtypeStruct((count, width), F32)
    scratch = [pltpu.VMEM((2, 384, width), BF16), pltpu.SemaphoreType.DMA((2,))]
    aliases = {}
    if before is not None:
        aliases = {len(operands) + 1: 4 if final else 3, len(operands) + 2: 5 if final else 4}
        in_specs += [big, hbm, hbm]
        operands += list(before)
    if final is not None:
        in_specs += [big, big, pl.BlockSpec(final[2].shape, whole)]
        operands += list(final)
        out_specs += [big, pl.BlockSpec((8, width), whole), hbm, hbm]
        out_shape += [dn_shape, jax.ShapeDtypeStruct((8, width), F32)] + grad_shapes(block_rows, 3 * width, width)
        scratch = [pltpu.VMEM((count, width), F32)] + scratch
    else:
        out_specs += [big, hbm, hbm]
        out_shape += [dn_shape] + grad_shapes(block_rows, 3 * width, width)
    return pl.pallas_call(
        functools.partial(back_kernel, block_rows, start, before is None, final is not None),
        grid=(stop - start,),
        in_specs=in_specs,
        out_specs=out_specs,
        out_shape=out_shape,
        scratch_shapes=scratch,
        input_output_aliases=aliases,
        compiler_params=pltpu.CompilerParams(vmem_limit_bytes=60 * 2**20),
        cost_estimate=pl.CostEstimate(flops=10 * 10**9 * (stop - start), bytes_accessed=30 * 10**6, transcendentals=0),
        name="attend_back",
    )(*operands)


def fold_kernel(pos_ref, *refs):
    keep, got, send_ref, hold_ref = refs[:4], refs[4:8], refs[8], refs[9]
    for k in range(4):
        out = (send_ref, hold_ref)[k // 2]
        out[k % 2, 0] = (keep[k][0].astype(F32) + got[k][0].astype(F32)).astype(BF16)


def fold(pos, keep, got):
    count, rows, width = keep.shape
    quarter = [pl.BlockSpec((1, rows // 2, width // 2), lambda i, pos, k=k: (i, pos[k, 0], pos[k, 1])) for k in range(4)]
    out = pl.BlockSpec((2, 1, rows // 2, width // 2), lambda i, pos: (0, i, 0, 0))
    shape = jax.ShapeDtypeStruct((2, count, rows // 2, width // 2), BF16)
    return pl.pallas_call(
        fold_kernel,
        grid_spec=pltpu.PrefetchScalarGridSpec(
            num_scalar_prefetch=1, grid=(count,), in_specs=quarter * 2, out_specs=[out, out]),
        out_shape=[shape, shape],
        name="fold",
    )(pos, *([keep] * 4), *([got] * 4))


def adam_kernel(scal_ref, a_ref, b_ref, w_ref, m_ref, v_ref, g_out, v_out, w_out):
    clip = scal_ref[0]
    own = scal_ref[1] > 0.5
    grad = jnp.where(own, a_ref[:, 0, 0].astype(F32), b_ref[:, 0, 0].astype(F32))
    grad = grad[:, :w_ref.shape[0] // grad.shape[0]].reshape(w_ref.shape) * clip
    second, weight = adam(w_ref[...], m_ref[...], v_ref[...], grad, 0.02, 0.05)
    g_out[...] = grad
    v_out[...] = second
    w_out[...] = weight


def adam_rows(scal, mine, other, weight, first, second):
    rows, width = weight.shape
    deep, tall, wide, piece, cols = mine.shape
    part = pl.BlockSpec((deep, 1, 1, piece, cols), lambda y, x: (0, y, x, 0, 0))
    flat = pl.BlockSpec((rows // tall, width // wide), lambda y, x: (y, x))
    shape = jax.ShapeDtypeStruct((rows, width), F32)
    return pl.pallas_call(
        adam_kernel,
        grid=(tall, wide),
        in_specs=[pl.BlockSpec(memory_space=pltpu.SMEM), part, part, flat, flat, flat],
        out_specs=[flat] * 3,
        out_shape=[shape] * 3,
        name="adam",
    )(scal, mine, other, weight, first, second)


from jax.sharding import PartitionSpec as P

HEADS = 12
STEP = 7


def place_tokens(heights, widths, count):
    sizes = heights * widths
    ends = jnp.cumsum(sizes)
    starts = ends - sizes
    places = jnp.arange(count, dtype=jnp.int32)
    segment = jnp.sum((places[:, None] >= ends[None, :]).astype(jnp.int32), axis=1)
    slots = jnp.arange(heights.shape[0], dtype=jnp.int32)
    picks = (segment[:, None] == slots[None, :]).astype(jnp.int32)
    begin = jnp.sum(picks * starts[None, :], axis=1)
    across = jnp.maximum(jnp.sum(picks * widths[None, :], axis=1), 1)
    offset = places - begin
    live = places < ends[-1]
    return (segment, offset // across, offset % across, live)


def adam(weight, first, second, grad, rate, decay):
    first_new = 0.5 * first + 0.5 * grad
    second_new = 0.5 * second + 0.5 * grad * grad
    correct = 1.0 - 0.5**STEP
    direction = first_new / correct / (jnp.sqrt(second_new / correct) + 1e-08)
    return (second_new, weight - rate * (direction + decay * weight))


def pairwise(bits, total):
    return [(i, i ^ bits) for i in range(total)]


def sum_everywhere(value, devices):
    if devices & (devices - 1):
        return lax.psum(value, "dp")
    step = 1
    while step < devices:
        value = value + lax.ppermute(value, "dp", pairwise(step, devices))
        step *= 2
    return value


CORES = ("group", "dp")
SWAP = [(0, 1), (1, 0)]


def cross(value, bit0, bit1, devices):
    perm = [(i, i ^ (bit0 if i < devices else bit1)) for i in range(2 * devices)]
    return lax.ppermute(value, CORES, perm)


def along_z(values, devices):
    return [
        lax.ppermute(v, "dp", [(i, (i + 4 * (s + 1)) % devices) for i in range(devices)])
        for s, v in enumerate(values)
    ]


def gather_pieces(master, inverse, core, me, devices, tables):
    block_rows, width = master.shape
    half = block_rows // 2
    mine = lax.dynamic_slice_in_dim(master, core * half, half, 0).astype(BF16)
    large = mine[:LARGE]
    small = mine[LARGE:]
    up = along_z([large] * 3, devices)
    small = jnp.stack([small, cross(small, 1, 2, devices)])
    small = jnp.concatenate([small, cross(small, 2, 1, devices)])
    large = jnp.stack([large] + up)
    large, small, tables = lax.optimization_barrier((large, small, tables))
    first = jnp.concatenate([large, cross(large, 1, 2, devices)])
    small = jnp.concatenate([small] + along_z([small] * 3, devices))
    second = cross(first, 2, 1, devices)
    other = [lax.ppermute(a, "group", SWAP) for a in (first, second, small)]
    deep = lax.rem(me // 4 - inverse // 4 + 4, 4)
    apart = me ^ inverse
    one = jnp.where(core == 0, apart & 1, (apart >> 1) & 1)
    two = jnp.where(core == 0, (apart >> 1) & 1, apart & 1)
    slots = jnp.stack([
        8 * two + 4 * one + deep,
        4 * deep + 2 * two + one,
        8 * one + 4 * two + deep,
        4 * deep + 2 * one + two,
    ]).astype(jnp.int32)
    return (first, second, small, *other), slots, tables


def reduce_blocks(keep, give, core, me, devices):
    count, rows, width = keep.shape
    x, y, z = me & 1, (me >> 1) & 1, me // 4
    one = jnp.where(core == 0, x, y)
    two = jnp.where(core == 0, y, x)
    pairs = [(1 - one, 1 - two), (1 - one, two), (one, 1 - two), (one, two)]
    pos = jnp.stack([
        jnp.stack([jnp.where(core == 0, b, a), jnp.where(core == 0, a, b)]) for a, b in pairs
    ]).astype(jnp.int32)
    got = lax.ppermute(give, "group", SWAP)
    send, hold = fold(pos, keep, got)
    came = cross(send, 1, 2, devices)

    def add(a, b):
        return a.astype(F32) + b.astype(F32)

    again = cross(add(hold[0], came[0]).astype(BF16), 2, 1, devices)
    total = add(add(hold[1], came[1]), again).reshape(count, 4, rows // 8, width // 2)
    low = total.astype(BF16)
    pick = lambda a, at: lax.dynamic_index_in_dim(a, at, 1, keepdims=False)
    parts = along_z([pick(low, lax.rem(z + s, 4)) for s in (1, 2, 3)], devices)
    total = pick(total, z)
    for part in parts:
        total = add(total, part)
    return total


def share_blocks(total, owner_block, core, devices):
    blocks, rows, cols = total.shape
    square = jnp.sum(total * total)
    lane = jnp.arange(cols)
    one, two, three = split3(square)
    extra = jnp.where(lane == 0, one, jnp.where(lane == 1, two, jnp.where(lane == 2, three, 0.0)))
    extra = jnp.broadcast_to(extra.astype(BF16), (devices, 8, cols))
    load = jnp.concatenate([total.astype(BF16)[owner_block // 2], extra], axis=1)
    mine = lax.all_to_all(load, "dp", 0, 0, tiled=True)
    other = lax.ppermute(mine, "group", SWAP)

    def squares(a):
        return jnp.sum(a[:, rows, :3].astype(F32))

    shape = (4, 2, 2, rows + 8, cols)
    return mine.reshape(shape), other.reshape(shape), squares(mine) + squares(other)


def reduce_plain(local_mat, owner_block, devices):
    rows, width = local_mat.shape
    block_rows = rows // devices
    term = local_mat.reshape(devices, block_rows, width)[owner_block].reshape(rows, width)
    share = lax.psum_scatter(term.astype(F32), "dp", scatter_dimension=0, tiled=True)
    return lax.psum(share.astype(BF16), "group").astype(F32)


def local(
    tokens,
    cotangent,
    grid_h,
    grid_w,
    owner_block,
    master,
    first_mom,
    second_mom,
    vectors,
    vec_first,
    vec_second,
):
    devices = lax.axis_size("dp")
    core = lax.axis_index("group")
    me = lax.axis_index("dp")
    count = tokens.shape[1]
    width = tokens.shape[2]
    heads = HEADS
    head_dim = width // heads
    half = head_dim // 2
    block_rows = master.shape[0]
    stack = devices * block_rows
    quick = devices == 16 and block_rows == 2 * (LARGE + SMALL) and width % 256 == 0
    inverse = jnp.argsort(owner_block)
    segment, rows_pos, cols_pos, live = place_tokens(grid_h[0], grid_w[0], count)
    freqs = vectors[13]

    def spread(part):
        return jnp.broadcast_to(part.reshape(heads, 1, half), (heads, 2, half)).reshape(1, width)

    angle = rows_pos.astype(F32)[:, None] * spread(freqs[: width // 2]) + cols_pos.astype(F32)[
        :, None
    ] * spread(freqs[width // 2 :])
    lower = (jnp.arange(width) % head_dim < half)[None]
    cosine = jnp.cos(angle)
    sine = jnp.sin(angle)
    sine = jnp.where(lower, -sine, sine)
    ids = jnp.arange(128)[None]
    match = segment[:, None] == ids
    key_mask = jnp.where(match | ((ids >= 8) & (ids < 11)), 1.0, 0.0).astype(BF16)
    query_mask = jnp.where((ids < 8) & ~match, MASKED, 0.0).astype(BF16)
    places = jnp.stack([rows_pos, cols_pos], axis=1).astype(F32)
    alive = live[:, None].astype(F32)
    tables = (cosine, sine, key_mask, query_mask, places, alive)
    if quick:
        weights, slots, tables = gather_pieces(master, inverse, core, me, devices, tables)
    else:
        low = lax.all_gather(master.astype(BF16), "dp", axis=0, tiled=True)
        weights = low.reshape(devices, block_rows, width)[inverse].reshape(stack, width)
        slots = jnp.zeros((4, devices), jnp.int32)
    cosine, sine, key_mask, query_mask, places, alive = tables
    here = core.reshape(1).astype(jnp.int32)
    x = tokens[0]
    first_in, query, key, value, attn, stat, *placed = attend(
        here, slots, x, vectors[0:1], vectors[1:2], vectors[4:7].reshape(1, 3 * width),
        cosine, sine, query_mask, key_mask, weights, stack,
    )
    if quick:
        weights = placed[0]
    whole_rows = block_rows if quick else 0
    block_out, grad_middle, grad_attn, sums, bias_up, keep_mlp, give_mlp = mlp(
        here, x, attn, cotangent[0], alive, vectors, weights, vectors[8:12].reshape(1, 4 * width), whole_rows
    )
    if quick:
        late = reduce_blocks(keep_mlp, give_mlp, core, me, devices)
    pairs = width // 128
    fixed = (query, key, value, grad_attn, attn, stat, cosine, sine, query_mask, key_mask, places, first_in, weights)
    cut = pairs // 2
    gb1, gf1, *before = attend_back(here, 0, cut, None, None, *fixed, whole_rows)
    gb2, gf2, input_grad, norm_sums, keep_qkv, give_qkv = attend_back(
        here, cut, pairs, before, (x, grad_middle, vectors), *fixed, whole_rows
    )
    grad_bias = jnp.concatenate([gb1, gb2], axis=1)
    grad_freq = jnp.concatenate([gf1, gf2], axis=1)
    grad_freqs = grad_freq[:2].reshape(2, heads, 2, half).sum(2).reshape(1, width)
    local_vec = jnp.concatenate(
        [norm_sums[:2], sums[:2], grad_bias[:3], sums[2:3], bias_up.reshape(4, width), sums[3:4], grad_freqs],
        axis=0,
    )
    if quick:
        early = reduce_blocks(keep_qkv, give_qkv, core, me, devices)
        vec_total = sum_everywhere(local_vec + lax.ppermute(local_vec, "group", SWAP), devices)
        total = jnp.concatenate([early, late])
        mine, other, square = share_blocks(total, owner_block, core, devices)
    else:
        vec_total = lax.psum(local_vec, CORES)
        share = reduce_plain(jnp.concatenate([keep_qkv, keep_mlp]), owner_block, devices)
        square = lax.psum(jnp.sum(share * share), "dp")
    grad_norm = jnp.sqrt(square + jnp.sum(vec_total * vec_total))
    clip = jnp.minimum(1.0, 1.0 / (grad_norm + 1e-06))
    vec_grad = vec_total * clip
    vec_second_new, vec_weight = adam(vectors, vec_first, vec_second, vec_grad, 0.2, 0.0)
    if quick:
        own = (owner_block[me] % 2 == core).astype(F32)
        mat_grad, mat_second, mat_weight = adam_rows(
            jnp.stack([clip, own]), mine, other, master, first_mom, second_mom
        )
    else:
        mat_grad = share * clip
        mat_second, mat_weight = adam(master, first_mom, second_mom, mat_grad, 0.02, 0.05)
    return (
        block_out[None],
        input_grad[None],
        mat_grad,
        mat_second,
        mat_weight,
        vec_grad,
        vec_second_new,
        vec_weight,
        grad_norm,
    )


def solution(mesh):
    return jax.shard_map(
        local,
        mesh=mesh,
        in_specs=(
            P("group", "dp", None),
            P("group", "dp", None),
            P("group", "dp"),
            P("group", "dp"),
            P(),
            P("dp", None),
            P("dp", None),
            P("dp", None),
            P(),
            P(),
            P(),
        ),
        out_specs=(
            P("group", "dp", None),
            P("group", "dp", None),
            P("dp", None),
            P("dp", None),
            P("dp", None),
            P(),
            P(),
            P(),
            P(),
        ),
        check_vma=False,
    )
```

```python
import functools
import jax
import jax.numpy as jnp
from jax import lax
from jax.experimental import pallas as pl
from jax.experimental.pallas import tpu as pltpu

F32 = jnp.float32
BF16 = jnp.bfloat16
LAST = (((1,), (1,)), ((), ()))
FIRST = (((0,), (0,)), ((), ()))
PLAIN = (((1,), (0,)), ((), ()))
MASKED = -1e9
SHORT = pl.CostEstimate(flops=1000, bytes_accessed=1000, transcendentals=0)


def mm(left, right, dims):
    return lax.dot_general(left, right, dims, preferred_element_type=F32)


def norm_parts(value):
    centre = value - jnp.mean(value, axis=-1, keepdims=True)
    spread = jnp.mean(centre * centre, axis=-1, keepdims=True)
    inverse = lax.rsqrt(spread + 1e-6)
    return centre * inverse, inverse


def norm_back(unit, inverse, grad, gain):
    scaled = grad * gain
    first = jnp.mean(scaled, axis=-1, keepdims=True)
    second = jnp.mean(scaled * unit, axis=-1, keepdims=True)
    return inverse * (scaled - first - unit * second)


def swap_halves(value):
    lane = lax.broadcasted_iota(jnp.int32, value.shape, 1)
    return jnp.where(
        lane % 64 < 32, pltpu.roll(value, 96, 1), pltpu.roll(value, 32, 1)
    )


def split3(value):
    one = value.astype(BF16).astype(F32)
    rest = value - one
    two = rest.astype(BF16).astype(F32)
    return one, two, rest - two


LARGE = 208
SMALL = 80


def place_pieces(core, slot_ref, mine, other, block, side, dst, sem):
    for which, (first, second, small) in enumerate((mine, other)):
        @pl.when((core == side) if which == 0 else (core != side))
        def _():
            large_slot = slot_ref[2 * which, block]
            small_slot = slot_ref[2 * which + 1, block]

            @pl.when(large_slot < 8)
            def _():
                pltpu.make_async_copy(first.at[large_slot], dst(0, LARGE), sem).start()

            @pl.when(large_slot >= 8)
            def _():
                pltpu.make_async_copy(second.at[large_slot - 8], dst(0, LARGE), sem).start()

            pltpu.make_async_copy(small.at[small_slot], dst(LARGE, SMALL), sem).start()


def attend_kernel(blocks, core_ref, slot_ref, x_ref, g_ref, b_ref, bq_ref, bk_ref, bv_ref,
                  cos_ref, sin_ref, qm_ref, km_ref, *rest):
    if blocks:
        mine, other = rest[0:3], rest[3:6]
        n1_ref, q_ref, k_ref, v_ref, attn_ref, stat_ref, w_ref, n1_s, w_s, near, far, back = rest[6:]
    else:
        w_ref, n1_ref, q_ref, k_ref, v_ref, attn_ref, stat_ref, n1_s, w_s, near = rest
    count, width = x_ref.shape
    step = pl.program_id(0)

    @pl.when(step == 0)
    def _():
        if blocks:
            core = core_ref[0]
            rows = w_ref.shape[0] // blocks

            def start(block, sem):
                for side in (0, 1):
                    def dst(offset, size):
                        base = block * rows + side * (rows // 2) + offset
                        return w_s.at[pl.ds(pl.multiple_of(base, 16), size)]
                    place_pieces(core, slot_ref, mine, other, block, side, dst, sem)

            def near_block(block, carry):
                start(block, near)
                return carry

            def far_block(block, carry):
                start(block, far)
                return carry

            lax.fori_loop(0, 3 * width // rows, near_block, 0)
            lax.fori_loop(3 * width // rows, blocks, far_block, 0)
        else:
            pltpu.make_async_copy(w_ref.at[pl.ds(0, 3 * width)], w_s, near).start()
        unit, _ = norm_parts(x_ref[...].astype(F32))
        n1 = (unit * g_ref[...] + b_ref[...]).astype(BF16)
        n1_s[...] = n1
        n1_ref[...] = n1
        head = w_s.at[pl.ds(0, 3 * width)]
        pltpu.make_async_copy(head, head, near).wait()

    if blocks:
        @pl.when(step == 1)
        def _():
            tail = w_s.at[pl.ds(3 * width, w_s.shape[0] - 3 * width)]
            pltpu.make_async_copy(tail, tail, far).wait()
            pltpu.make_async_copy(w_s, w_ref, back).start()

    def third(j):
        return w_s[pl.ds(pl.multiple_of(j * width + step * 128, 128), 128), :]

    w = jnp.concatenate([third(0), third(1), third(2)], axis=0)
    qkv = mm(n1_s[...], w, LAST)
    q = qkv[:, :128] + bq_ref[...]
    k = qkv[:, 128:256] + bk_ref[...]
    v = (qkv[:, 256:] + bv_ref[...]).astype(BF16)
    c = cos_ref[...]
    s = sin_ref[...]
    qr = ((q * c + swap_halves(q) * s).astype(BF16).astype(F32) * 0.125).astype(BF16)
    kr = (k * c + swap_halves(k) * s).astype(BF16)
    q_ref[...] = qr
    k_ref[...] = kr
    v_ref[...] = v
    lane = lax.broadcasted_iota(jnp.int32, (1, 128), 1)
    k_aug = jnp.concatenate([kr, km_ref[...]], axis=1)
    v_aug = jnp.concatenate([v, jnp.ones((count, 128), BF16)], axis=1)
    zero = jnp.zeros((), BF16)
    tile = 256
    for i in range(count // tile):
        rows = pl.ds(i * tile, tile)
        out = None
        stats = []
        for h in (0, 1):
            mine_lanes = (lane // 64) == h
            qa = jnp.concatenate(
                [jnp.where(mine_lanes, qr[i * tile:(i + 1) * tile], zero), qm_ref[rows, :]], axis=1)
            scores = mm(qa, k_aug, LAST)
            top = jnp.max(scores, axis=-1, keepdims=True)
            e = jnp.exp(scores - top).astype(BF16)
            o = mm(e, v_aug, PLAIN)
            total = o[:, 128:]
            o = o[:, :128] / total
            out = o if out is None else jnp.where(lane < 64, out, o)
            stats.append(top + jnp.log(total[:, :1]))
        attn_ref[rows, :] = out.astype(BF16)
        stat_ref[rows, :] = jnp.where(lane < 64, stats[0], stats[1])

    if blocks:
        @pl.when(step == pl.num_programs(0) - 1)
        def _():
            pltpu.make_async_copy(w_s, w_ref, back).wait()


def attend(core, slots, x, gain, shift, bqkv, cos, sin, qm, km, weights, stack):
    count, width = x.shape
    pairs = width // 128
    pieces = isinstance(weights, tuple)
    blocks = slots.shape[1] if pieces else 0
    whole = lambda p: (0, 0)
    col = lambda p: (0, p)
    smem = pl.BlockSpec(memory_space=pltpu.SMEM)
    hbm = pl.BlockSpec(memory_space=pl.ANY)
    given = weights if pieces else (weights,)
    specs = [smem, smem] + [
        pl.BlockSpec((count, width), whole),
        pl.BlockSpec((1, width), whole),
        pl.BlockSpec((1, width), whole),
        pl.BlockSpec((1, 128), col),
        pl.BlockSpec((1, 128), lambda p: (0, p + pairs)),
        pl.BlockSpec((1, 128), lambda p: (0, p + 2 * pairs)),
        pl.BlockSpec((count, 128), col),
        pl.BlockSpec((count, 128), col),
        pl.BlockSpec((count, 128), whole),
        pl.BlockSpec((count, 128), whole),
    ] + [hbm] * len(given)
    outs = [pl.BlockSpec((count, width), whole)] + [pl.BlockSpec((count, 128), col)] * 5
    shape = lambda d: jax.ShapeDtypeStruct((count, width), d)
    shapes = [shape(BF16)] * 5 + [shape(F32)]
    scratch = [pltpu.VMEM((count, width), BF16), pltpu.VMEM((stack if pieces else 3 * width, width), BF16), pltpu.SemaphoreType.DMA]
    if pieces:
        outs.append(hbm)
        shapes.append(jax.ShapeDtypeStruct((stack, width), BF16))
        scratch += [pltpu.SemaphoreType.DMA] * 2
    return pl.pallas_call(
        functools.partial(attend_kernel, blocks),
        grid=(pairs,),
        in_specs=specs,
        out_specs=outs,
        out_shape=shapes,
        scratch_shapes=scratch,
        compiler_params=pltpu.CompilerParams(vmem_limit_bytes=56 * 2**20),
        cost_estimate=SHORT,
        name="attend",
    )(core, slots, x, gain, shift, bqkv, bqkv, bqkv, cos, sin, qm, km, *given)


HALF_ERFC = (
    0.09317889578353007, 0.09147806194869737, 0.10061136147272338, 0.023612303617162326,
    0.20424612730309272, -0.1755704972361086, 0.23011593265708702, -0.06767218931083122,
)


def gelu_both(x):
    e = jnp.exp(x * x * -0.5)
    d = jnp.abs(x) * (0.33 * 0.7071067811865476) + 1.0
    t = pl.reciprocal(d, approx=True)
    t = t * (2.0 - d * t)
    poly = jnp.full_like(t, HALF_ERFC[-1])
    for c in HALF_ERFC[-2::-1]:
        poly = poly * t + c
    tail = poly * t * e
    cdf = jnp.where(x >= 0, 1.0 - tail, tail)
    return x * cdf, cdf + x * e * 0.3989422804014327


def send_rows(core, block_rows, stage, row, base, keep_ref, give_ref, sem):
    if not block_rows:
        rows = stage.shape[0]
        pltpu.make_async_copy(
            stage, keep_ref.at[pl.ds(pl.multiple_of(row - base, 64), rows)], sem
        ).start()
        return

    def one(index, carry):
        at = row + 64 * index
        block = lax.div(at, block_rows)
        inner = pl.ds(pl.multiple_of(at - block * block_rows, 64), 64)
        slot = lax.div(block, 2) - base // 2
        source = stage.at[pl.ds(pl.multiple_of(64 * index, 64), 64)]
        own = lax.rem(block, 2) == core

        @pl.when(own)
        def _():
            pltpu.make_async_copy(source, keep_ref.at[slot, inner], sem).start()

        @pl.when(jnp.logical_not(own))
        def _():
            pltpu.make_async_copy(source, give_ref.at[slot, inner], sem).start()

        return carry

    lax.fori_loop(0, stage.shape[0] // 64, one, 0)


def mlp_kernel(block_rows, base, core_ref, x_ref, at_ref, cot_ref, live_ref, vec_ref, wo_ref, w1_ref, w2_ref, b1_ref,
               out_ref, dm_ref, da_ref, sums_ref, gb_ref, keep_ref, give_ref,
               middle_s, n2_s, dz_s, acc_s, stage_s, proj_s, sems):
    step = pl.program_id(0)
    last = pl.num_programs(0) - 1
    count, width = x_ref.shape
    core = core_ref[0]
    tile = w1_ref.shape[0]

    @pl.when(step == 0)
    def _():
        middle = x_ref[...].astype(F32) + mm(at_ref[...], wo_ref[...], LAST) + vec_ref[7:8, :]
        middle_s[...] = middle
        unit, _ = norm_parts(middle)
        n2_s[...] = (unit * vec_ref[2:3, :] + vec_ref[3:4, :]).astype(BF16)
        dz_s[...] = jnp.where(live_ref[...] > 0.5, cot_ref[...].astype(F32), 0.0).astype(BF16)
        acc_s[...] = jnp.zeros_like(acc_s)
        dm_ref[...] = jnp.zeros_like(dm_ref)

    slot = lax.rem(step, 2)

    @pl.when(step >= 2)
    def _():
        pltpu.make_async_copy(stage_s.at[slot], stage_s.at[slot], sems.at[slot]).wait()

    n2 = n2_s[...]
    dz = dz_s[...]
    w1 = w1_ref[...]
    w2 = w2_ref[...]
    pre = mm(n2, w1, LAST) + b1_ref[...]
    act, slope = gelu_both(pre)
    hidden = act.astype(BF16)
    acc_s[...] += mm(hidden, w2, PLAIN)
    stage_s[slot, 1] = mm(hidden, dz, FIRST).astype(BF16)
    dpre = (mm(dz, w2, LAST) * slope).astype(BF16)
    gb_ref[...] = jnp.sum(dpre.astype(F32), axis=0, keepdims=True)
    stage_s[slot, 0] = mm(dpre, n2, FIRST).astype(BF16)
    dm_ref[...] += mm(dpre, w1, PLAIN)
    for j in (0, 1):
        send_rows(core, block_rows, stage_s.at[slot, j], (4 + 4 * j) * width + step * tile,
                  base, keep_ref, give_ref, sems.at[slot])

    @pl.when(step == last)
    def _():
        middle = middle_s[...]
        out_ref[...] = (middle + acc_s[...] + vec_ref[12:13, :]).astype(BF16)
        unit, inverse = norm_parts(middle)
        dn = dm_ref[...]
        dy = dz_s[...].astype(F32)
        dm = dy + norm_back(unit, inverse, dn, vec_ref[2:3, :])
        dm_ref[...] = dm
        low = dm.astype(BF16)
        row = lambda a: jnp.sum(a, axis=0, keepdims=True)
        sums_ref[...] = jnp.concatenate(
            [row(dn * unit), row(dn), row(low.astype(F32)), row(dy), jnp.zeros((4, width), F32)], axis=0)
        proj_s[...] = mm(low, at_ref[...], FIRST).astype(BF16)
        send_rows(core, block_rows, proj_s, 3 * width, base, keep_ref, give_ref, sems.at[2])
        da_ref[...] = mm(low, wo_ref[...], PLAIN).astype(BF16)
        pltpu.make_async_copy(stage_s.at[slot], stage_s.at[slot], sems.at[slot]).wait()
        pltpu.make_async_copy(stage_s.at[1 - slot], stage_s.at[1 - slot], sems.at[1 - slot]).wait()
        pltpu.make_async_copy(proj_s, proj_s, sems.at[2]).wait()


def grad_shapes(block_rows, rows, width):
    if block_rows:
        half = jax.ShapeDtypeStruct((rows // block_rows // 2, block_rows, width), BF16)
        return [half, half]
    return [jax.ShapeDtypeStruct((rows, width), BF16), jax.ShapeDtypeStruct((16, width), BF16)]


def mlp(core, x, attn, cot, live, vectors, weights, b1, block_rows, tile=256):
    count, width = x.shape
    units = 4 * width
    stack = weights.shape[0]
    base = 3 * width // block_rows if block_rows else 3 * width
    whole = lambda t: (0, 0)
    big = pl.BlockSpec((count, width), whole)
    hbm = pl.BlockSpec(memory_space=pl.ANY)
    return pl.pallas_call(
        functools.partial(mlp_kernel, block_rows, base),
        grid=(units // tile,),
        in_specs=[pl.BlockSpec(memory_space=pltpu.SMEM), big, big, big, pl.BlockSpec((count, 1), whole),
                  pl.BlockSpec(vectors.shape, whole),
                  pl.BlockSpec((width, width), lambda t: (3, 0)),
                  pl.BlockSpec((tile, width), lambda t: (4 * width // tile + t, 0)),
                  pl.BlockSpec((tile, width), lambda t: (8 * width // tile + t, 0)),
                  pl.BlockSpec((1, tile), lambda t: (0, t))],
        out_specs=[big, big, big, pl.BlockSpec((8, width), whole), pl.BlockSpec((1, tile), lambda t: (0, t)), hbm, hbm],
        out_shape=[
            jax.ShapeDtypeStruct((count, width), BF16),
            jax.ShapeDtypeStruct((count, width), F32),
            jax.ShapeDtypeStruct((count, width), BF16),
            jax.ShapeDtypeStruct((8, width), F32),
            jax.ShapeDtypeStruct((1, units), F32),
        ] + grad_shapes(block_rows, stack - 3 * width, width),
        scratch_shapes=[
            pltpu.VMEM((count, width), F32),
            pltpu.VMEM((count, width), BF16),
            pltpu.VMEM((count, width), BF16),
            pltpu.VMEM((count, width), F32),
            pltpu.VMEM((2, 2, tile, width), BF16),
            pltpu.VMEM((width, width), BF16),
            pltpu.SemaphoreType.DMA((3,)),
        ],
        compiler_params=pltpu.CompilerParams(vmem_limit_bytes=60 * 2**20),
        cost_estimate=SHORT,
        name="mlp",
    )(core, x, attn, cot, live, vectors, weights, weights, weights, b1)


def back_kernel(first, q_ref, k_ref, v_ref, da_ref, at_ref, stat_ref, cos_ref, sin_ref,
                qm_ref, km_ref, pos_ref, *rest):
    dq_ref, dk_ref, dv_ref, gb_ref, gf_ref = rest if first else rest[5:]
    count = q_ref.shape[0]
    lane = lax.broadcasted_iota(jnp.int32, (1, 128), 1)
    zero = jnp.zeros((), BF16)
    q = q_ref[...]
    k = k_ref[...]
    v = v_ref[...]
    da = da_ref[...]
    prod = da.astype(F32) * at_ref[...].astype(F32)
    qm = qm_ref[...].astype(F32)
    k_aug = jnp.concatenate([k, km_ref[...]], axis=1)
    v_aug = jnp.concatenate([v, jnp.broadcast_to((lane < 2).astype(BF16), (count, 128))], axis=1)
    tile = 256
    dq = dk = dv = None
    for h in (0, 1):
        mine = (lane // 64) == h
        qh = jnp.where(mine, q, zero)
        kh = jnp.where(mine, k, zero)
        dah = jnp.where(mine, da, zero)
        delta = jnp.sum(jnp.where(mine, prod, 0.0), axis=-1, keepdims=True)
        d1, d2, _ = split3(delta)
        l1, l2, l3 = split3(stat_ref[:, 64 * h:64 * h + 1])
        extra = jnp.where(lane == 8, -l1, jnp.where(lane == 9, -l2, jnp.where(lane == 10, -l3, qm)))
        q_aug = jnp.concatenate([qh, extra.astype(BF16)], axis=1)
        da_aug = jnp.concatenate(
            [dah, jnp.where(lane == 0, -d1, jnp.where(lane == 1, -d2, 0.0)).astype(BF16)], axis=1)
        dks, dvs, dqh = [], [], None
        for i in range(count // tile):
            sl = slice(i * tile, (i + 1) * tile)
            p = jnp.exp(mm(k_aug[sl], q_aug, LAST))
            dp = mm(v_aug[sl], da_aug, LAST)
            ds = (p * dp).astype(BF16)
            dvs.append(mm(p.astype(BF16), dah, PLAIN))
            dks.append(mm(ds, qh, PLAIN))
            part = mm(ds, kh[sl], FIRST)
            dqh = part if dqh is None else dqh + part
        dkh = jnp.concatenate(dks, axis=0)
        dvh = jnp.concatenate(dvs, axis=0)
        dq = dqh if dq is None else dq + dqh
        dk = dkh if dk is None else dk + dkh
        dv = dvh if dv is None else dv + dvh
    dq = dq * 0.125
    c = cos_ref[...]
    s = sin_ref[...]
    turned = dq * swap_halves(q.astype(F32) * 8.0) + dk * swap_halves(k.astype(F32))
    turned = jnp.where(lane % 64 < 32, -turned, turned)
    row = lambda a: jnp.sum(a, axis=0, keepdims=True)
    gf_ref[...] = jnp.concatenate(
        [row(turned * pos_ref[:, 0:1]), row(turned * pos_ref[:, 1:2]), jnp.zeros((6, 128), F32)], axis=0)
    dqp = (dq * c - swap_halves(dq) * s).astype(BF16)
    dkp = (dk * c - swap_halves(dk) * s).astype(BF16)
    dvp = dv.astype(BF16)
    gb_ref[...] = jnp.concatenate(
        [row(dqp.astype(F32)), row(dkp.astype(F32)), row(dvp.astype(F32)), jnp.zeros((5, 128), F32)], axis=0)
    dq_ref[...] = dqp
    dk_ref[...] = dkp
    dv_ref[...] = dvp


def attend_back(start, stop, before, q, k, v, da, attn, stat, cos, sin, qm, km, pos):
    count, width = q.shape
    whole = lambda p: (0, 0)
    col = lambda p: (0, p + start)
    tall = pl.BlockSpec((count, 128), col)
    fixed = pl.BlockSpec((count, 128), whole)
    small = pl.BlockSpec((8, 128), col)
    in_specs = [tall] * 8 + [fixed] * 2 + [pl.BlockSpec((count, 2), whole)]
    operands = [q, k, v, da, attn, stat, cos, sin, qm, km, pos]
    aliases = {}
    if before is not None:
        aliases = {len(operands) + i: i for i in range(5)}
        in_specs += [pl.BlockSpec(memory_space=pl.ANY)] * 5
        operands += list(before)
    return pl.pallas_call(
        functools.partial(back_kernel, before is None),
        grid=(stop - start,),
        in_specs=in_specs,
        out_specs=[tall] * 3 + [small] * 2,
        out_shape=[jax.ShapeDtypeStruct((count, width), BF16)] * 3 + [jax.ShapeDtypeStruct((8, width), F32)] * 2,
        input_output_aliases=aliases,
        compiler_params=pltpu.CompilerParams(vmem_limit_bytes=56 * 2**20),
        cost_estimate=SHORT,
        name="attend_back",
    )(*operands)


def qkv_grad_kernel(block_rows, core_ref, dq_ref, dk_ref, dv_ref, n1_ref, keep_ref, give_ref, stage_s, sem):
    width = n1_ref.shape[1]
    cols = dq_ref.shape[1]
    step = pl.program_id(0)
    n1 = n1_ref[...]
    for j, ref in enumerate((dq_ref, dk_ref, dv_ref)):
        stage_s[step, j] = mm(ref[...], n1, FIRST).astype(BF16)
        send_rows(core_ref[0], block_rows, stage_s.at[step, j], j * width + step * cols, 0, keep_ref, give_ref, sem)

    @pl.when(step == pl.num_programs(0) - 1)
    def _():
        pltpu.make_async_copy(stage_s, stage_s, sem).wait()


def qkv_grad(core, dq, dk, dv, n1, block_rows):
    count, width = n1.shape
    cols = width // 2
    tall = pl.BlockSpec((count, cols), lambda p: (0, p))
    hbm = pl.BlockSpec(memory_space=pl.ANY)
    return pl.pallas_call(
        functools.partial(qkv_grad_kernel, block_rows),
        grid=(2,),
        in_specs=[pl.BlockSpec(memory_space=pltpu.SMEM)] + [tall] * 3 + [pl.BlockSpec((count, width), lambda p: (0, 0))],
        out_specs=[hbm, hbm],
        out_shape=grad_shapes(block_rows, 3 * width, width),
        scratch_shapes=[pltpu.VMEM((2, 3, cols, width), BF16), pltpu.SemaphoreType.DMA],
        compiler_params=pltpu.CompilerParams(vmem_limit_bytes=56 * 2**20),
        cost_estimate=SHORT,
        name="qkv_grad",
    )(core, dq, dk, dv, n1)


def input_kernel(dq_ref, dk_ref, dv_ref, w_ref, x_ref, dm_ref, vec_ref, ig_ref, ln_ref):
    d = jnp.concatenate([dq_ref[...], dk_ref[...], dv_ref[...]], axis=1)
    dn = mm(d, w_ref[...], PLAIN)
    unit, inverse = norm_parts(x_ref[...].astype(F32))
    ig_ref[...] = dm_ref[...] + norm_back(unit, inverse, dn, vec_ref[0:1, :])
    row = lambda a: jnp.sum(a, axis=0, keepdims=True)
    sums = jnp.concatenate([row(dn * unit), row(dn), jnp.zeros((6, dn.shape[1]), F32)], axis=0)

    @pl.when(pl.program_id(0) == 0)
    def _():
        ln_ref[...] = sums

    @pl.when(pl.program_id(0) > 0)
    def _():
        ln_ref[...] += sums


def input_back(dq, dk, dv, weights, x, dm, vectors):
    count, width = x.shape
    tile = 256
    part = pl.BlockSpec((tile, width), lambda i: (i, 0))
    whole = lambda i: (0, 0)
    return pl.pallas_call(
        input_kernel,
        grid=(count // tile,),
        in_specs=[part] * 3 + [pl.BlockSpec((3 * width, width), whole), part, part, pl.BlockSpec(vectors.shape, whole)],
        out_specs=[part, pl.BlockSpec((8, width), whole)],
        out_shape=[jax.ShapeDtypeStruct((count, width), F32), jax.ShapeDtypeStruct((8, width), F32)],
        compiler_params=pltpu.CompilerParams(vmem_limit_bytes=56 * 2**20),
        cost_estimate=SHORT,
        name="input_back",
    )(dq, dk, dv, weights, x, dm, vectors)


def fold_kernel(count, pos_ref, *refs):
    out_ref = refs[-1]
    ways = out_ref.shape[0]
    for k in range(ways):
        total = refs[k][0].astype(F32) + refs[ways + k][0].astype(F32)
        for more in refs[2 * ways:-1]:
            total = total + more[0, 0].astype(F32)
        out_ref[k, 0] = total.astype(BF16)


def fold(pos, keep, got, ways, more=()):
    count, rows, width = keep.shape
    quarter = [pl.BlockSpec((1, rows // 2, width // 2), lambda i, pos, k=k: (i, pos[k, 0], pos[k, 1])) for k in ways]
    extra = [pl.BlockSpec((1, 1, rows // 2, width // 2), lambda i, pos, at=at: (at, i, 0, 0)) for _, at in more]
    out = pl.BlockSpec((len(ways), 1, rows // 2, width // 2), lambda i, pos: (0, i, 0, 0))
    shape = jax.ShapeDtypeStruct((len(ways), count, rows // 2, width // 2), BF16)
    return pl.pallas_call(
        functools.partial(fold_kernel, len(more)),
        grid_spec=pltpu.PrefetchScalarGridSpec(
            num_scalar_prefetch=1, grid=(count,), in_specs=quarter * 2 + extra, out_specs=out),
        out_shape=shape,
        cost_estimate=SHORT,
        name="fold",
    )(pos, *([keep] * len(ways)), *([got] * len(ways)), *[a for a, _ in more])


def adam_kernel(scal_ref, a_ref, b_ref, w_ref, m_ref, v_ref, g_out, v_out, w_out):
    clip = scal_ref[0]
    own = scal_ref[1] > 0.5
    grad = jnp.where(own, a_ref[:, 0, 0].astype(F32), b_ref[:, 0, 0].astype(F32))
    grad = grad[:, :w_ref.shape[0] // grad.shape[0]].reshape(w_ref.shape) * clip
    second, weight = adam(w_ref[...], m_ref[...], v_ref[...], grad, 0.02, 0.05)
    g_out[...] = grad
    v_out[...] = second
    w_out[...] = weight


def adam_rows(scal, mine, other, weight, first, second):
    rows, width = weight.shape
    deep, tall, wide, piece, cols = mine.shape
    part = pl.BlockSpec((deep, 1, 1, piece, cols), lambda y, x: (0, y, x, 0, 0))
    flat = pl.BlockSpec((rows // tall, width // wide), lambda y, x: (y, x))
    shape = jax.ShapeDtypeStruct((rows, width), F32)
    return pl.pallas_call(
        adam_kernel,
        grid=(tall, wide),
        in_specs=[pl.BlockSpec(memory_space=pltpu.SMEM), part, part, flat, flat, flat],
        out_specs=[flat] * 3,
        out_shape=[shape] * 3,
        name="adam",
    )(scal, mine, other, weight, first, second)


from jax.sharding import PartitionSpec as P

HEADS = 12
STEP = 7


def place_tokens(heights, widths, count):
    sizes = heights * widths
    ends = jnp.cumsum(sizes)
    starts = ends - sizes
    places = jnp.arange(count, dtype=jnp.int32)
    segment = jnp.sum((places[:, None] >= ends[None, :]).astype(jnp.int32), axis=1)
    slots = jnp.arange(heights.shape[0], dtype=jnp.int32)
    picks = (segment[:, None] == slots[None, :]).astype(jnp.int32)
    begin = jnp.sum(picks * starts[None, :], axis=1)
    across = jnp.maximum(jnp.sum(picks * widths[None, :], axis=1), 1)
    offset = places - begin
    live = places < ends[-1]
    return (segment, offset // across, offset % across, live)


def adam(weight, first, second, grad, rate, decay):
    first_new = 0.5 * first + 0.5 * grad
    second_new = 0.5 * second + 0.5 * grad * grad
    correct = 1.0 - 0.5**STEP
    direction = first_new / correct / (jnp.sqrt(second_new / correct) + 1e-08)
    return (second_new, weight - rate * (direction + decay * weight))


def pairwise(bits, total):
    return [(i, i ^ bits) for i in range(total)]


def sum_everywhere(value, devices):
    if devices & (devices - 1):
        return lax.psum(value, "dp")
    step = 1
    while step < devices:
        value = value + lax.ppermute(value, "dp", pairwise(step, devices))
        step *= 2
    return value


CORES = ("group", "dp")
SWAP = [(0, 1), (1, 0)]


def cross(value, bit0, bit1, devices):
    perm = [(i, i ^ (bit0 if i < devices else bit1)) for i in range(2 * devices)]
    return lax.ppermute(value, CORES, perm)


def along_z(values, devices):
    return [
        lax.ppermute(v, "dp", [(i, (i + 4 * (s + 1)) % devices) for i in range(devices)])
        for s, v in enumerate(values)
    ]


def gather_pieces(master, inverse, core, me, devices, tables):
    block_rows, width = master.shape
    half = block_rows // 2
    mine = lax.dynamic_slice_in_dim(master, core * half, half, 0).astype(BF16)
    large = mine[:LARGE]
    small = mine[LARGE:]
    up = along_z([large] * 3, devices)
    small = jnp.stack([small, cross(small, 1, 2, devices)])
    small = jnp.concatenate([small, cross(small, 2, 1, devices)])
    large = jnp.stack([large] + up)
    large, small, tables = lax.optimization_barrier((large, small, tables))
    first = jnp.concatenate([large, cross(large, 1, 2, devices)])
    small = jnp.concatenate([small] + along_z([small] * 3, devices))
    second = cross(first, 2, 1, devices)
    other = [lax.ppermute(a, "group", SWAP) for a in (first, second, small)]
    deep = lax.rem(me // 4 - inverse // 4 + 4, 4)
    apart = me ^ inverse
    one = jnp.where(core == 0, apart & 1, (apart >> 1) & 1)
    two = jnp.where(core == 0, (apart >> 1) & 1, apart & 1)
    slots = jnp.stack([
        8 * two + 4 * one + deep,
        4 * deep + 2 * two + one,
        8 * one + 4 * two + deep,
        4 * deep + 2 * one + two,
    ]).astype(jnp.int32)
    return (first, second, small, *other), slots, tables


def quarters(core, me):
    x, y = me & 1, (me >> 1) & 1
    one = jnp.where(core == 0, x, y)
    two = jnp.where(core == 0, y, x)
    pairs = [(1 - one, 1 - two), (1 - one, two), (one, 1 - two), (one, two)]
    return jnp.stack([
        jnp.stack([jnp.where(core == 0, b, a), jnp.where(core == 0, a, b)]) for a, b in pairs
    ]).astype(jnp.int32)


def sum_z(low, me, devices):
    count, rows, cols = low.shape
    z = me // 4
    low = low.reshape(count, 4, rows // 4, cols)
    pick = lambda at: lax.dynamic_index_in_dim(low, at, 1, keepdims=False)
    return (pick(z), *along_z([pick(lax.rem(z + s, 4)) for s in (1, 2, 3)], devices))


def total_of(parts):
    total = parts[0].astype(F32)
    for part in parts[1:]:
        total = total + part.astype(F32)
    return total


def share_blocks(total, owner_block, core, devices):
    blocks, rows, cols = total.shape
    square = jnp.sum(total * total)
    lane = jnp.arange(cols)
    one, two, three = split3(square)
    extra = jnp.where(lane == 0, one, jnp.where(lane == 1, two, jnp.where(lane == 2, three, 0.0)))
    extra = jnp.broadcast_to(extra.astype(BF16), (devices, 8, cols))
    load = jnp.concatenate([total.astype(BF16)[owner_block // 2], extra], axis=1)
    mine = lax.all_to_all(load, "dp", 0, 0, tiled=True)
    other = lax.ppermute(mine, "group", SWAP)

    def squares(a):
        return jnp.sum(a[:, rows, :3].astype(F32))

    shape = (4, 2, 2, rows + 8, cols)
    return mine.reshape(shape), other.reshape(shape), squares(mine) + squares(other)


def reduce_plain(local_mat, owner_block, devices):
    rows, width = local_mat.shape
    block_rows = rows // devices
    term = local_mat.reshape(devices, block_rows, width)[owner_block].reshape(rows, width)
    share = lax.psum_scatter(term.astype(F32), "dp", scatter_dimension=0, tiled=True)
    return lax.psum(share.astype(BF16), "group").astype(F32)


def local(
    tokens,
    cotangent,
    grid_h,
    grid_w,
    owner_block,
    master,
    first_mom,
    second_mom,
    vectors,
    vec_first,
    vec_second,
):
    devices = lax.axis_size("dp")
    core = lax.axis_index("group")
    me = lax.axis_index("dp")
    count = tokens.shape[1]
    width = tokens.shape[2]
    heads = HEADS
    head_dim = width // heads
    half = head_dim // 2
    block_rows = master.shape[0]
    stack = devices * block_rows
    quick = devices == 16 and block_rows == 2 * (LARGE + SMALL) and width % 256 == 0
    inverse = jnp.argsort(owner_block)
    segment, rows_pos, cols_pos, live = place_tokens(grid_h[0], grid_w[0], count)
    freqs = vectors[13]

    def spread(part):
        return jnp.broadcast_to(part.reshape(heads, 1, half), (heads, 2, half)).reshape(1, width)

    angle = rows_pos.astype(F32)[:, None] * spread(freqs[: width // 2]) + cols_pos.astype(F32)[
        :, None
    ] * spread(freqs[width // 2 :])
    lower = (jnp.arange(width) % head_dim < half)[None]
    cosine = jnp.cos(angle)
    sine = jnp.sin(angle)
    sine = jnp.where(lower, -sine, sine)
    ids = jnp.arange(128)[None]
    match = segment[:, None] == ids
    key_mask = jnp.where(match | ((ids >= 8) & (ids < 11)), 1.0, 0.0).astype(BF16)
    query_mask = jnp.where((ids < 8) & ~match, MASKED, 0.0).astype(BF16)
    places = jnp.stack([rows_pos, cols_pos], axis=1).astype(F32)
    alive = live[:, None].astype(F32)
    tables = (cosine, sine, key_mask, query_mask, places, alive)
    if quick:
        weights, slots, tables = gather_pieces(master, inverse, core, me, devices, tables)
    else:
        low = lax.all_gather(master.astype(BF16), "dp", axis=0, tiled=True)
        weights = low.reshape(devices, block_rows, width)[inverse].reshape(stack, width)
        slots = jnp.zeros((4, devices), jnp.int32)
    cosine, sine, key_mask, query_mask, places, alive = tables
    here = core.reshape(1).astype(jnp.int32)
    x = tokens[0]
    first_in, query, key, value, attn, stat, *placed = attend(
        here, slots, x, vectors[0:1], vectors[1:2], vectors[4:7].reshape(1, 3 * width),
        cosine, sine, query_mask, key_mask, weights, stack,
    )
    if quick:
        weights = placed[0]
    whole_rows = block_rows if quick else 0
    block_out, grad_middle, grad_attn, sums, bias_up, keep_mlp, give_mlp = mlp(
        here, x, attn, cotangent[0], alive, vectors, weights, vectors[8:12].reshape(1, 4 * width), whole_rows
    )
    pairs = width // 128
    tie = lax.optimization_barrier
    if quick:
        pos = quarters(core, me)
        got = lax.ppermute(give_mlp, "group", SWAP)
    back = None
    cuts = (0, 1, pairs - 2, pairs)
    for start, stop in zip(cuts[:-1], cuts[1:]):
        back = attend_back(
            start, stop, back, query, key, value, grad_attn, attn, stat, cosine, sine, query_mask, key_mask, places
        )
        if quick and start == 0:
            send, back = tie((fold(pos, keep_mlp, got, (0, 1)), back))
            came = cross(send, 1, 2, devices)
        if quick and start == 1:
            send, back = tie((fold(pos, keep_mlp, got, (2,), ((came, 0),)), back))
            again = cross(send, 2, 1, devices)
    grad_q, grad_k, grad_v, grad_bias, grad_freq = back
    if quick:
        low, grad_q = tie((fold(pos, keep_mlp, got, (3,), ((came, 1), (again, 0)))[0], grad_q))
        late = sum_z(low, me, devices)
    keep_qkv, give_qkv = qkv_grad(here, grad_q, grad_k, grad_v, first_in, whole_rows)
    grad_v, give_qkv = tie((grad_v, give_qkv))
    input_grad, norm_sums = input_back(grad_q, grad_k, grad_v, weights, x, grad_middle, vectors)
    grad_freqs = grad_freq[:2].reshape(2, heads, 2, half).sum(2).reshape(1, width)
    local_vec = jnp.concatenate(
        [norm_sums[:2], sums[:2], grad_bias[:3], sums[2:3], bias_up.reshape(4, width), sums[3:4], grad_freqs],
        axis=0,
    )
    if quick:
        got_qkv = lax.ppermute(give_qkv, "group", SWAP)
        got_qkv, norm_sums = tie((got_qkv, norm_sums))
        came = cross(fold(pos, keep_qkv, got_qkv, (0, 1)), 1, 2, devices)
        came, late = tie((came, late))
        again = cross(fold(pos, keep_qkv, got_qkv, (2,), ((came, 0),)), 2, 1, devices)
        early = sum_z(fold(pos, keep_qkv, got_qkv, (3,), ((came, 1), (again, 0)))[0], me, devices)
        early, late = total_of(early), total_of(late)
        vec_total = sum_everywhere(local_vec + lax.ppermute(local_vec, "group", SWAP), devices)
        total, vec_total = lax.optimization_barrier((jnp.concatenate([early, late]), vec_total))
        mine, other, square = share_blocks(total, owner_block, core, devices)
    else:
        vec_total = lax.psum(local_vec, CORES)
        share = reduce_plain(jnp.concatenate([keep_qkv, keep_mlp]), owner_block, devices)
        square = lax.psum(jnp.sum(share * share), "dp")
    grad_norm = jnp.sqrt(square + jnp.sum(vec_total * vec_total))
    clip = jnp.minimum(1.0, 1.0 / (grad_norm + 1e-06))
    vec_grad = vec_total * clip
    vec_second_new, vec_weight = adam(vectors, vec_first, vec_second, vec_grad, 0.2, 0.0)
    if quick:
        own = (owner_block[me] % 2 == core).astype(F32)
        mat_grad, mat_second, mat_weight = adam_rows(
            jnp.stack([clip, own]), mine, other, master, first_mom, second_mom
        )
    else:
        mat_grad = share * clip
        mat_second, mat_weight = adam(master, first_mom, second_mom, mat_grad, 0.02, 0.05)
    return (
        block_out[None],
        input_grad[None],
        mat_grad,
        mat_second,
        mat_weight,
        vec_grad,
        vec_second_new,
        vec_weight,
        grad_norm,
    )


def solution(mesh):
    return jax.shard_map(
        local,
        mesh=mesh,
        in_specs=(
            P("group", "dp", None),
            P("group", "dp", None),
            P("group", "dp"),
            P("group", "dp"),
            P(),
            P("dp", None),
            P("dp", None),
            P("dp", None),
            P(),
            P(),
            P(),
        ),
        out_specs=(
            P("group", "dp", None),
            P("group", "dp", None),
            P("dp", None),
            P("dp", None),
            P("dp", None),
            P(),
            P(),
            P(),
            P(),
        ),
        check_vma=False,
    )
```

```python
import functools
import jax
import jax.numpy as jnp
from jax import lax
from jax.experimental import pallas as pl
from jax.experimental.pallas import tpu as pltpu

F32 = jnp.float32
BF16 = jnp.bfloat16
LAST = (((1,), (1,)), ((), ()))
FIRST = (((0,), (0,)), ((), ()))
PLAIN = (((1,), (0,)), ((), ()))
MASKED = -1e9
SHORT = pl.CostEstimate(flops=1000, bytes_accessed=1000, transcendentals=0)


def mm(left, right, dims):
    return lax.dot_general(left, right, dims, preferred_element_type=F32)


def norm_parts(value):
    centre = value - jnp.mean(value, axis=-1, keepdims=True)
    spread = jnp.mean(centre * centre, axis=-1, keepdims=True)
    inverse = lax.rsqrt(spread + 1e-6)
    return centre * inverse, inverse


def norm_back(unit, inverse, grad, gain):
    scaled = grad * gain
    first = jnp.mean(scaled, axis=-1, keepdims=True)
    second = jnp.mean(scaled * unit, axis=-1, keepdims=True)
    return inverse * (scaled - first - unit * second)


def swap_halves(value):
    lane = lax.broadcasted_iota(jnp.int32, value.shape, 1)
    return jnp.where(
        lane % 64 < 32, pltpu.roll(value, 96, 1), pltpu.roll(value, 32, 1)
    )


def split3(value):
    one = value.astype(BF16).astype(F32)
    rest = value - one
    two = rest.astype(BF16).astype(F32)
    return one, two, rest - two


LARGE = 208
SMALL = 80


def place_pieces(core, slot_ref, mine, other, block, side, dst, sem):
    for which, (first, second, small) in enumerate((mine, other)):
        @pl.when((core == side) if which == 0 else (core != side))
        def _():
            large_slot = slot_ref[2 * which, block]
            small_slot = slot_ref[2 * which + 1, block]

            @pl.when(large_slot < 8)
            def _():
                pltpu.make_async_copy(first.at[large_slot], dst(0, LARGE), sem).start()

            @pl.when(large_slot >= 8)
            def _():
                pltpu.make_async_copy(second.at[large_slot - 8], dst(0, LARGE), sem).start()

            pltpu.make_async_copy(small.at[small_slot], dst(LARGE, SMALL), sem).start()


def attend_kernel(blocks, core_ref, slot_ref, x_ref, g_ref, b_ref, bq_ref, bk_ref, bv_ref,
                  cos_ref, sin_ref, qm_ref, km_ref, *rest):
    if blocks:
        mine, other = rest[0:3], rest[3:6]
        n1_ref, q_ref, k_ref, v_ref, attn_ref, stat_ref, w_ref, n1_s, w_s, near, far, back = rest[6:]
    else:
        w_ref, n1_ref, q_ref, k_ref, v_ref, attn_ref, stat_ref, n1_s, w_s, near = rest
    count, width = x_ref.shape
    step = pl.program_id(0)

    @pl.when(step == 0)
    def _():
        if blocks:
            core = core_ref[0]
            rows = w_ref.shape[0] // blocks

            def start(block, sem):
                for side in (0, 1):
                    def dst(offset, size):
                        base = block * rows + side * (rows // 2) + offset
                        return w_s.at[pl.ds(pl.multiple_of(base, 16), size)]
                    place_pieces(core, slot_ref, mine, other, block, side, dst, sem)

            def near_block(block, carry):
                start(block, near)
                return carry

            def far_block(block, carry):
                start(block, far)
                return carry

            lax.fori_loop(0, 3 * width // rows, near_block, 0)
            lax.fori_loop(3 * width // rows, blocks, far_block, 0)
        else:
            pltpu.make_async_copy(w_ref.at[pl.ds(0, 3 * width)], w_s, near).start()
        unit, _ = norm_parts(x_ref[...].astype(F32))
        n1 = (unit * g_ref[...] + b_ref[...]).astype(BF16)
        n1_s[...] = n1
        n1_ref[...] = n1
        head = w_s.at[pl.ds(0, 3 * width)]
        pltpu.make_async_copy(head, head, near).wait()

    if blocks:
        @pl.when(step == 1)
        def _():
            tail = w_s.at[pl.ds(3 * width, w_s.shape[0] - 3 * width)]
            pltpu.make_async_copy(tail, tail, far).wait()
            pltpu.make_async_copy(w_s, w_ref, back).start()

    def third(j):
        return w_s[pl.ds(pl.multiple_of(j * width + step * 128, 128), 128), :]

    w = jnp.concatenate([third(0), third(1), third(2)], axis=0)
    qkv = mm(n1_s[...], w, LAST)
    q = qkv[:, :128] + bq_ref[...]
    k = qkv[:, 128:256] + bk_ref[...]
    v = (qkv[:, 256:] + bv_ref[...]).astype(BF16)
    c = cos_ref[...]
    s = sin_ref[...]
    qr = ((q * c + swap_halves(q) * s).astype(BF16).astype(F32) * 0.125).astype(BF16)
    kr = (k * c + swap_halves(k) * s).astype(BF16)
    q_ref[...] = qr
    k_ref[...] = kr
    v_ref[...] = v
    lane = lax.broadcasted_iota(jnp.int32, (1, 128), 1)
    k_aug = jnp.concatenate([kr, km_ref[...]], axis=1)
    v_aug = jnp.concatenate([v, jnp.ones((count, 128), BF16)], axis=1)
    zero = jnp.zeros((), BF16)
    tile = 256
    for i in range(count // tile):
        rows = pl.ds(i * tile, tile)
        out = None
        stats = []
        for h in (0, 1):
            mine_lanes = (lane // 64) == h
            qa = jnp.concatenate(
                [jnp.where(mine_lanes, qr[i * tile:(i + 1) * tile], zero), qm_ref[rows, :]], axis=1)
            scores = mm(qa, k_aug, LAST)
            top = jnp.max(scores, axis=-1, keepdims=True)
            e = jnp.exp(scores - top).astype(BF16)
            o = mm(e, v_aug, PLAIN)
            total = o[:, 128:]
            o = o[:, :128] / total
            out = o if out is None else jnp.where(lane < 64, out, o)
            stats.append(top + jnp.log(total[:, :1]))
        attn_ref[rows, :] = out.astype(BF16)
        stat_ref[rows, :] = jnp.where(lane < 64, stats[0], stats[1])

    if blocks:
        @pl.when(step == pl.num_programs(0) - 1)
        def _():
            pltpu.make_async_copy(w_s, w_ref, back).wait()


def attend(core, slots, x, gain, shift, bqkv, cos, sin, qm, km, weights, stack):
    count, width = x.shape
    pairs = width // 128
    pieces = isinstance(weights, tuple)
    blocks = slots.shape[1] if pieces else 0
    whole = lambda p: (0, 0)
    col = lambda p: (0, p)
    smem = pl.BlockSpec(memory_space=pltpu.SMEM)
    hbm = pl.BlockSpec(memory_space=pl.ANY)
    given = weights if pieces else (weights,)
    specs = [smem, smem] + [
        pl.BlockSpec((count, width), whole),
        pl.BlockSpec((1, width), whole),
        pl.BlockSpec((1, width), whole),
        pl.BlockSpec((1, 128), col),
        pl.BlockSpec((1, 128), lambda p: (0, p + pairs)),
        pl.BlockSpec((1, 128), lambda p: (0, p + 2 * pairs)),
        pl.BlockSpec((count, 128), col),
        pl.BlockSpec((count, 128), col),
        pl.BlockSpec((count, 128), whole),
        pl.BlockSpec((count, 128), whole),
    ] + [hbm] * len(given)
    outs = [pl.BlockSpec((count, width), whole)] + [pl.BlockSpec((count, 128), col)] * 5
    shape = lambda d: jax.ShapeDtypeStruct((count, width), d)
    shapes = [shape(BF16)] * 5 + [shape(F32)]
    scratch = [pltpu.VMEM((count, width), BF16), pltpu.VMEM((stack if pieces else 3 * width, width), BF16), pltpu.SemaphoreType.DMA]
    if pieces:
        outs.append(hbm)
        shapes.append(jax.ShapeDtypeStruct((stack, width), BF16))
        scratch += [pltpu.SemaphoreType.DMA] * 2
    return pl.pallas_call(
        functools.partial(attend_kernel, blocks),
        grid=(pairs,),
        in_specs=specs,
        out_specs=outs,
        out_shape=shapes,
        scratch_shapes=scratch,
        compiler_params=pltpu.CompilerParams(vmem_limit_bytes=56 * 2**20),
        cost_estimate=SHORT,
        name="attend",
    )(core, slots, x, gain, shift, bqkv, bqkv, bqkv, cos, sin, qm, km, *given)


def gelu_both(x):
    cdf = 0.5 + 0.5 * lax.erf(x * 0.7071067811865476)
    return x * cdf, cdf + x * jnp.exp(x * x * -0.5) * 0.3989422804014327


def send_rows(core, block_rows, stage, row, base, keep_ref, give_ref, sem):
    if not block_rows:
        rows = stage.shape[0]
        pltpu.make_async_copy(
            stage, keep_ref.at[pl.ds(pl.multiple_of(row - base, 64), rows)], sem
        ).start()
        return

    def one(index, carry):
        at = row + 64 * index
        block = lax.div(at, block_rows)
        inner = pl.ds(pl.multiple_of(at - block * block_rows, 64), 64)
        slot = lax.div(block, 2) - base // 2
        source = stage.at[pl.ds(pl.multiple_of(64 * index, 64), 64)]
        own = lax.rem(block, 2) == core

        @pl.when(own)
        def _():
            pltpu.make_async_copy(source, keep_ref.at[slot, inner], sem).start()

        @pl.when(jnp.logical_not(own))
        def _():
            pltpu.make_async_copy(source, give_ref.at[slot, inner], sem).start()

        return carry

    lax.fori_loop(0, stage.shape[0] // 64, one, 0)


def mlp_kernel(block_rows, base, core_ref, x_ref, at_ref, cot_ref, live_ref, vec_ref, wo_ref, w1_ref, w2_ref, b1_ref,
               out_ref, dm_ref, da_ref, sums_ref, gb_ref, keep_ref, give_ref,
               middle_s, n2_s, dz_s, acc_s, stage_s, proj_s, sems):
    step = pl.program_id(0)
    last = pl.num_programs(0) - 1
    count, width = x_ref.shape
    core = core_ref[0]
    tile = w1_ref.shape[0]

    @pl.when(step == 0)
    def _():
        middle = x_ref[...].astype(F32) + mm(at_ref[...], wo_ref[...], LAST) + vec_ref[7:8, :]
        middle_s[...] = middle
        unit, _ = norm_parts(middle)
        n2_s[...] = (unit * vec_ref[2:3, :] + vec_ref[3:4, :]).astype(BF16)
        dz_s[...] = jnp.where(live_ref[...] > 0.5, cot_ref[...].astype(F32), 0.0).astype(BF16)
        acc_s[...] = jnp.zeros_like(acc_s)
        dm_ref[...] = jnp.zeros_like(dm_ref)

    slot = lax.rem(step, 2)

    @pl.when(step >= 2)
    def _():
        pltpu.make_async_copy(stage_s.at[slot], stage_s.at[slot], sems.at[slot]).wait()

    n2 = n2_s[...]
    dz = dz_s[...]
    w1 = w1_ref[...]
    w2 = w2_ref[...]
    pre = mm(w1, n2, LAST) + b1_ref[...].reshape(tile, 1)
    back = mm(w2, dz, LAST)
    act, slope = gelu_both(pre)
    hidden = act.astype(BF16)
    stage_s[slot, 1] = mm(hidden, dz, PLAIN).astype(BF16)
    dpre = (back * slope).astype(BF16)
    gb_ref[...] = jnp.sum(dpre.astype(F32), axis=1, keepdims=True).reshape(1, tile)
    stage_s[slot, 0] = mm(dpre, n2, PLAIN).astype(BF16)
    acc_s[...] += mm(hidden, w2, FIRST)
    dm_ref[...] += mm(dpre, w1, FIRST)
    for j in (0, 1):
        send_rows(core, block_rows, stage_s.at[slot, j], (4 + 4 * j) * width + step * tile,
                  base, keep_ref, give_ref, sems.at[slot])

    @pl.when(step == last)
    def _():
        middle = middle_s[...]
        out_ref[...] = (middle + acc_s[...] + vec_ref[12:13, :]).astype(BF16)
        unit, inverse = norm_parts(middle)
        dn = dm_ref[...]
        dy = dz_s[...].astype(F32)
        dm = dy + norm_back(unit, inverse, dn, vec_ref[2:3, :])
        dm_ref[...] = dm
        low = dm.astype(BF16)
        row = lambda a: jnp.sum(a, axis=0, keepdims=True)
        sums_ref[...] = jnp.concatenate(
            [row(dn * unit), row(dn), row(low.astype(F32)), row(dy), jnp.zeros((4, width), F32)], axis=0)
        proj_s[...] = mm(low, at_ref[...], FIRST).astype(BF16)
        send_rows(core, block_rows, proj_s, 3 * width, base, keep_ref, give_ref, sems.at[2])
        da_ref[...] = mm(low, wo_ref[...], PLAIN).astype(BF16)
        pltpu.make_async_copy(stage_s.at[slot], stage_s.at[slot], sems.at[slot]).wait()
        pltpu.make_async_copy(stage_s.at[1 - slot], stage_s.at[1 - slot], sems.at[1 - slot]).wait()
        pltpu.make_async_copy(proj_s, proj_s, sems.at[2]).wait()


def grad_shapes(block_rows, rows, width):
    if block_rows:
        half = jax.ShapeDtypeStruct((rows // block_rows // 2, block_rows, width), BF16)
        return [half, half]
    return [jax.ShapeDtypeStruct((rows, width), BF16), jax.ShapeDtypeStruct((16, width), BF16)]


def mlp(core, x, attn, cot, live, vectors, weights, b1, block_rows, tile=512):
    count, width = x.shape
    units = 4 * width
    stack = weights.shape[0]
    base = 3 * width // block_rows if block_rows else 3 * width
    whole = lambda t: (0, 0)
    big = pl.BlockSpec((count, width), whole)
    hbm = pl.BlockSpec(memory_space=pl.ANY)
    return pl.pallas_call(
        functools.partial(mlp_kernel, block_rows, base),
        grid=(units // tile,),
        in_specs=[pl.BlockSpec(memory_space=pltpu.SMEM), big, big, big, pl.BlockSpec((count, 1), whole),
                  pl.BlockSpec(vectors.shape, whole),
                  pl.BlockSpec((width, width), lambda t: (3, 0)),
                  pl.BlockSpec((tile, width), lambda t: (4 * width // tile + t, 0)),
                  pl.BlockSpec((tile, width), lambda t: (8 * width // tile + t, 0)),
                  pl.BlockSpec((1, tile), lambda t: (0, t))],
        out_specs=[big, big, big, pl.BlockSpec((8, width), whole), pl.BlockSpec((1, tile), lambda t: (0, t)), hbm, hbm],
        out_shape=[
            jax.ShapeDtypeStruct((count, width), BF16),
            jax.ShapeDtypeStruct((count, width), F32),
            jax.ShapeDtypeStruct((count, width), BF16),
            jax.ShapeDtypeStruct((8, width), F32),
            jax.ShapeDtypeStruct((1, units), F32),
        ] + grad_shapes(block_rows, stack - 3 * width, width),
        scratch_shapes=[
            pltpu.VMEM((count, width), F32),
            pltpu.VMEM((count, width), BF16),
            pltpu.VMEM((count, width), BF16),
            pltpu.VMEM((count, width), F32),
            pltpu.VMEM((2, 2, tile, width), BF16),
            pltpu.VMEM((width, width), BF16),
            pltpu.SemaphoreType.DMA((3,)),
        ],
        compiler_params=pltpu.CompilerParams(vmem_limit_bytes=60 * 2**20),
        cost_estimate=SHORT,
        name="mlp",
    )(core, x, attn, cot, live, vectors, weights, weights, weights, b1)


def back_kernel(first, q_ref, k_ref, v_ref, da_ref, at_ref, stat_ref, cos_ref, sin_ref,
                qm_ref, km_ref, pos_ref, *rest):
    dq_ref, dk_ref, dv_ref, gb_ref, gf_ref = rest if first else rest[5:]
    count = q_ref.shape[0]
    lane = lax.broadcasted_iota(jnp.int32, (1, 128), 1)
    zero = jnp.zeros((), BF16)
    q = q_ref[...]
    k = k_ref[...]
    v = v_ref[...]
    da = da_ref[...]
    prod = da.astype(F32) * at_ref[...].astype(F32)
    qm = qm_ref[...].astype(F32)
    k_aug = jnp.concatenate([k, km_ref[...]], axis=1)
    v_aug = jnp.concatenate([v, jnp.broadcast_to((lane < 2).astype(BF16), (count, 128))], axis=1)
    tile = 256
    dq = dk = dv = None
    for h in (0, 1):
        mine = (lane // 64) == h
        qh = jnp.where(mine, q, zero)
        kh = jnp.where(mine, k, zero)
        dah = jnp.where(mine, da, zero)
        delta = jnp.sum(jnp.where(mine, prod, 0.0), axis=-1, keepdims=True)
        d1, d2, _ = split3(delta)
        l1, l2, l3 = split3(stat_ref[:, 64 * h:64 * h + 1])
        extra = jnp.where(lane == 8, -l1, jnp.where(lane == 9, -l2, jnp.where(lane == 10, -l3, qm)))
        q_aug = jnp.concatenate([qh, extra.astype(BF16)], axis=1)
        da_aug = jnp.concatenate(
            [dah, jnp.where(lane == 0, -d1, jnp.where(lane == 1, -d2, 0.0)).astype(BF16)], axis=1)
        dks, dvs, dqh = [], [], None
        for i in range(count // tile):
            sl = slice(i * tile, (i + 1) * tile)
            p = jnp.exp(mm(k_aug[sl], q_aug, LAST))
            dp = mm(v_aug[sl], da_aug, LAST)
            ds = (p * dp).astype(BF16)
            dvs.append(mm(p.astype(BF16), dah, PLAIN))
            dks.append(mm(ds, qh, PLAIN))
            part = mm(ds, kh[sl], FIRST)
            dqh = part if dqh is None else dqh + part
        dkh = jnp.concatenate(dks, axis=0)
        dvh = jnp.concatenate(dvs, axis=0)
        dq = dqh if dq is None else dq + dqh
        dk = dkh if dk is None else dk + dkh
        dv = dvh if dv is None else dv + dvh
    dq = dq * 0.125
    c = cos_ref[...]
    s = sin_ref[...]
    turned = dq * swap_halves(q.astype(F32) * 8.0) + dk * swap_halves(k.astype(F32))
    turned = jnp.where(lane % 64 < 32, -turned, turned)
    row = lambda a: jnp.sum(a, axis=0, keepdims=True)
    gf_ref[...] = jnp.concatenate(
        [row(turned * pos_ref[:, 0:1]), row(turned * pos_ref[:, 1:2]), jnp.zeros((6, 128), F32)], axis=0)
    dqp = (dq * c - swap_halves(dq) * s).astype(BF16)
    dkp = (dk * c - swap_halves(dk) * s).astype(BF16)
    dvp = dv.astype(BF16)
    gb_ref[...] = jnp.concatenate(
        [row(dqp.astype(F32)), row(dkp.astype(F32)), row(dvp.astype(F32)), jnp.zeros((5, 128), F32)], axis=0)
    dq_ref[...] = dqp
    dk_ref[...] = dkp
    dv_ref[...] = dvp


def attend_back(start, stop, before, q, k, v, da, attn, stat, cos, sin, qm, km, pos):
    count, width = q.shape
    whole = lambda p: (0, 0)
    col = lambda p: (0, p + start)
    tall = pl.BlockSpec((count, 128), col)
    fixed = pl.BlockSpec((count, 128), whole)
    small = pl.BlockSpec((8, 128), col)
    in_specs = [tall] * 8 + [fixed] * 2 + [pl.BlockSpec((count, 2), whole)]
    operands = [q, k, v, da, attn, stat, cos, sin, qm, km, pos]
    aliases = {}
    if before is not None:
        aliases = {len(operands) + i: i for i in range(5)}
        in_specs += [pl.BlockSpec(memory_space=pl.ANY)] * 5
        operands += list(before)
    return pl.pallas_call(
        functools.partial(back_kernel, before is None),
        grid=(stop - start,),
        in_specs=in_specs,
        out_specs=[tall] * 3 + [small] * 2,
        out_shape=[jax.ShapeDtypeStruct((count, width), BF16)] * 3 + [jax.ShapeDtypeStruct((8, width), F32)] * 2,
        input_output_aliases=aliases,
        compiler_params=pltpu.CompilerParams(vmem_limit_bytes=56 * 2**20),
        cost_estimate=SHORT,
        name="attend_back",
    )(*operands)


def qkv_grad_kernel(block_rows, core_ref, dq_ref, dk_ref, dv_ref, n1_ref, keep_ref, give_ref, stage_s, sem):
    width = n1_ref.shape[1]
    cols = dq_ref.shape[1]
    step = pl.program_id(0)
    n1 = n1_ref[...]
    for j, ref in enumerate((dq_ref, dk_ref, dv_ref)):
        stage_s[step, j] = mm(ref[...], n1, FIRST).astype(BF16)
        send_rows(core_ref[0], block_rows, stage_s.at[step, j], j * width + step * cols, 0, keep_ref, give_ref, sem)

    @pl.when(step == pl.num_programs(0) - 1)
    def _():
        pltpu.make_async_copy(stage_s, stage_s, sem).wait()


def qkv_grad(core, dq, dk, dv, n1, block_rows):
    count, width = n1.shape
    cols = width // 2
    tall = pl.BlockSpec((count, cols), lambda p: (0, p))
    hbm = pl.BlockSpec(memory_space=pl.ANY)
    return pl.pallas_call(
        functools.partial(qkv_grad_kernel, block_rows),
        grid=(2,),
        in_specs=[pl.BlockSpec(memory_space=pltpu.SMEM)] + [tall] * 3 + [pl.BlockSpec((count, width), lambda p: (0, 0))],
        out_specs=[hbm, hbm],
        out_shape=grad_shapes(block_rows, 3 * width, width),
        scratch_shapes=[pltpu.VMEM((2, 3, cols, width), BF16), pltpu.SemaphoreType.DMA],
        compiler_params=pltpu.CompilerParams(vmem_limit_bytes=56 * 2**20),
        cost_estimate=SHORT,
        name="qkv_grad",
    )(core, dq, dk, dv, n1)


def input_kernel(dq_ref, dk_ref, dv_ref, w_ref, x_ref, dm_ref, vec_ref, ig_ref, ln_ref):
    d = jnp.concatenate([dq_ref[...], dk_ref[...], dv_ref[...]], axis=1)
    dn = mm(d, w_ref[...], PLAIN)
    unit, inverse = norm_parts(x_ref[...].astype(F32))
    ig_ref[...] = dm_ref[...] + norm_back(unit, inverse, dn, vec_ref[0:1, :])
    row = lambda a: jnp.sum(a, axis=0, keepdims=True)
    sums = jnp.concatenate([row(dn * unit), row(dn), jnp.zeros((6, dn.shape[1]), F32)], axis=0)

    @pl.when(pl.program_id(0) == 0)
    def _():
        ln_ref[...] = sums

    @pl.when(pl.program_id(0) > 0)
    def _():
        ln_ref[...] += sums


def input_back(dq, dk, dv, weights, x, dm, vectors):
    count, width = x.shape
    tile = 256
    part = pl.BlockSpec((tile, width), lambda i: (i, 0))
    whole = lambda i: (0, 0)
    return pl.pallas_call(
        input_kernel,
        grid=(count // tile,),
        in_specs=[part] * 3 + [pl.BlockSpec((3 * width, width), whole), part, part, pl.BlockSpec(vectors.shape, whole)],
        out_specs=[part, pl.BlockSpec((8, width), whole)],
        out_shape=[jax.ShapeDtypeStruct((count, width), F32), jax.ShapeDtypeStruct((8, width), F32)],
        compiler_params=pltpu.CompilerParams(vmem_limit_bytes=56 * 2**20),
        cost_estimate=SHORT,
        name="input_back",
    )(dq, dk, dv, weights, x, dm, vectors)


def fold_kernel(count, pos_ref, *refs):
    out_ref = refs[-1]
    ways = out_ref.shape[0]
    for k in range(ways):
        total = refs[k][...].astype(F32) + refs[ways + k][...].astype(F32)
        for more in refs[2 * ways:-1]:
            total = total + more[0].astype(F32)
        out_ref[k] = total.astype(BF16)


def fold(pos, keep, got, ways, more=()):
    count, rows, width = keep.shape
    some = count // 2
    quarter = [pl.BlockSpec((some, rows // 2, width // 2), lambda i, pos, k=k: (i, pos[k, 0], pos[k, 1])) for k in ways]
    extra = [pl.BlockSpec((1, some, rows // 2, width // 2), lambda i, pos, at=at: (at, i, 0, 0)) for _, at in more]
    out = pl.BlockSpec((len(ways), some, rows // 2, width // 2), lambda i, pos: (0, i, 0, 0))
    shape = jax.ShapeDtypeStruct((len(ways), count, rows // 2, width // 2), BF16)
    return pl.pallas_call(
        functools.partial(fold_kernel, len(more)),
        grid_spec=pltpu.PrefetchScalarGridSpec(
            num_scalar_prefetch=1, grid=(count // some,), in_specs=quarter * 2 + extra, out_specs=out),
        compiler_params=pltpu.CompilerParams(vmem_limit_bytes=40 * 2**20),
        out_shape=shape,
        cost_estimate=SHORT,
        name="fold",
    )(pos, *([keep] * len(ways)), *([got] * len(ways)), *[a for a, _ in more])


def adam_kernel(scal_ref, a_ref, b_ref, w_ref, m_ref, v_ref, g_out, v_out, w_out):
    clip = scal_ref[0]
    own = scal_ref[1] > 0.5
    grad = jnp.where(own, a_ref[:, 0, 0].astype(F32), b_ref[:, 0, 0].astype(F32))
    grad = grad[:, :w_ref.shape[0] // grad.shape[0]].reshape(w_ref.shape) * clip
    second, weight = adam(w_ref[...], m_ref[...], v_ref[...], grad, 0.02, 0.05)
    g_out[...] = grad
    v_out[...] = second
    w_out[...] = weight


def adam_rows(scal, mine, other, weight, first, second):
    rows, width = weight.shape
    deep, tall, wide, piece, cols = mine.shape
    part = pl.BlockSpec((deep, 1, 1, piece, cols), lambda y, x: (0, y, x, 0, 0))
    flat = pl.BlockSpec((rows // tall, width // wide), lambda y, x: (y, x))
    shape = jax.ShapeDtypeStruct((rows, width), F32)
    return pl.pallas_call(
        adam_kernel,
        grid=(tall, wide),
        in_specs=[pl.BlockSpec(memory_space=pltpu.SMEM), part, part, flat, flat, flat],
        out_specs=[flat] * 3,
        out_shape=[shape] * 3,
        name="adam",
    )(scal, mine, other, weight, first, second)


from jax.sharding import PartitionSpec as P

HEADS = 12
STEP = 7


def place_tokens(heights, widths, count):
    sizes = heights * widths
    ends = jnp.cumsum(sizes)
    starts = ends - sizes
    places = jnp.arange(count, dtype=jnp.int32)
    segment = jnp.sum((places[:, None] >= ends[None, :]).astype(jnp.int32), axis=1)
    slots = jnp.arange(heights.shape[0], dtype=jnp.int32)
    picks = (segment[:, None] == slots[None, :]).astype(jnp.int32)
    begin = jnp.sum(picks * starts[None, :], axis=1)
    across = jnp.maximum(jnp.sum(picks * widths[None, :], axis=1), 1)
    offset = places - begin
    live = places < ends[-1]
    return (segment, offset // across, offset % across, live)


def adam(weight, first, second, grad, rate, decay):
    first_new = 0.5 * first + 0.5 * grad
    second_new = 0.5 * second + 0.5 * grad * grad
    correct = 1.0 - 0.5**STEP
    direction = first_new / correct / (jnp.sqrt(second_new / correct) + 1e-08)
    return (second_new, weight - rate * (direction + decay * weight))


def pairwise(bits, total):
    return [(i, i ^ bits) for i in range(total)]


def sum_part(value, devices, step, stop):
    while step < stop:
        value = value + lax.ppermute(value, "dp", pairwise(step, devices))
        step *= 2
    return value


CORES = ("group", "dp")
SWAP = [(0, 1), (1, 0)]


def cross(value, bit0, bit1, devices):
    perm = [(i, i ^ (bit0 if i < devices else bit1)) for i in range(2 * devices)]
    return lax.ppermute(value, CORES, perm)


def along_z(values, devices):
    return [
        lax.ppermute(v, "dp", [(i, (i + 4 * (s + 1)) % devices) for i in range(devices)])
        for s, v in enumerate(values)
    ]


def gather_pieces(master, inverse, core, me, devices, tables):
    block_rows, width = master.shape
    half = block_rows // 2
    mine = lax.dynamic_slice_in_dim(master, core * half, half, 0).astype(BF16)
    large = mine[:LARGE]
    small = mine[LARGE:]
    up = along_z([large] * 3, devices)
    small = jnp.stack([small, cross(small, 1, 2, devices)])
    small = jnp.concatenate([small, cross(small, 2, 1, devices)])
    large = jnp.stack([large] + up)
    large, small, tables = lax.optimization_barrier((large, small, tables))
    first = jnp.concatenate([large, cross(large, 1, 2, devices)])
    small = jnp.concatenate([small] + along_z([small] * 3, devices))
    second = cross(first, 2, 1, devices)
    other = [lax.ppermute(a, "group", SWAP) for a in (first, second, small)]
    deep = lax.rem(me // 4 - inverse // 4 + 4, 4)
    apart = me ^ inverse
    one = jnp.where(core == 0, apart & 1, (apart >> 1) & 1)
    two = jnp.where(core == 0, (apart >> 1) & 1, apart & 1)
    slots = jnp.stack([
        8 * two + 4 * one + deep,
        4 * deep + 2 * two + one,
        8 * one + 4 * two + deep,
        4 * deep + 2 * one + two,
    ]).astype(jnp.int32)
    return (first, second, small, *other), slots, tables


def quarters(core, me):
    x, y = me & 1, (me >> 1) & 1
    one = jnp.where(core == 0, x, y)
    two = jnp.where(core == 0, y, x)
    pairs = [(1 - one, 1 - two), (1 - one, two), (one, 1 - two), (one, two)]
    return jnp.stack([
        jnp.stack([jnp.where(core == 0, b, a), jnp.where(core == 0, a, b)]) for a, b in pairs
    ]).astype(jnp.int32)


def sum_z(low, me, devices):
    count, rows, cols = low.shape
    z = me // 4
    low = low.reshape(count, 4, rows // 4, cols)
    pick = lambda at: lax.dynamic_index_in_dim(low, at, 1, keepdims=False)
    return (pick(z), *along_z([pick(lax.rem(z + s, 4)) for s in (1, 2, 3)], devices))


def total_of(parts):
    total = parts[0].astype(F32)
    for part in parts[1:]:
        total = total + part.astype(F32)
    return total


def share_blocks(total, owner_block, core, devices):
    blocks, rows, cols = total.shape
    square = jnp.sum(total * total)
    lane = jnp.arange(cols)
    one, two, three = split3(square)
    extra = jnp.where(lane == 0, one, jnp.where(lane == 1, two, jnp.where(lane == 2, three, 0.0)))
    extra = jnp.broadcast_to(extra.astype(BF16), (devices, 8, cols))
    load = jnp.concatenate([total.astype(BF16)[owner_block // 2], extra], axis=1)
    mine = lax.all_to_all(load, "dp", 0, 0, tiled=True)
    other = lax.ppermute(mine, "group", SWAP)

    def squares(a):
        return jnp.sum(a[:, rows, :3].astype(F32))

    shape = (4, 2, 2, rows + 8, cols)
    return mine.reshape(shape), other.reshape(shape), squares(mine) + squares(other)


def reduce_plain(local_mat, owner_block, devices):
    rows, width = local_mat.shape
    block_rows = rows // devices
    term = local_mat.reshape(devices, block_rows, width)[owner_block].reshape(rows, width)
    share = lax.psum_scatter(term.astype(F32), "dp", scatter_dimension=0, tiled=True)
    return lax.psum(share.astype(BF16), "group").astype(F32)


def local(
    tokens,
    cotangent,
    grid_h,
    grid_w,
    owner_block,
    master,
    first_mom,
    second_mom,
    vectors,
    vec_first,
    vec_second,
):
    devices = lax.axis_size("dp")
    core = lax.axis_index("group")
    me = lax.axis_index("dp")
    count = tokens.shape[1]
    width = tokens.shape[2]
    heads = HEADS
    head_dim = width // heads
    half = head_dim // 2
    block_rows = master.shape[0]
    stack = devices * block_rows
    quick = devices == 16 and block_rows == 2 * (LARGE + SMALL) and width % 256 == 0
    inverse = jnp.argsort(owner_block)
    segment, rows_pos, cols_pos, live = place_tokens(grid_h[0], grid_w[0], count)
    freqs = vectors[13]

    def spread(part):
        return jnp.broadcast_to(part.reshape(heads, 1, half), (heads, 2, half)).reshape(1, width)

    angle = rows_pos.astype(F32)[:, None] * spread(freqs[: width // 2]) + cols_pos.astype(F32)[
        :, None
    ] * spread(freqs[width // 2 :])
    lower = (jnp.arange(width) % head_dim < half)[None]
    cosine = jnp.cos(angle)
    sine = jnp.sin(angle)
    sine = jnp.where(lower, -sine, sine)
    ids = jnp.arange(128)[None]
    match = segment[:, None] == ids
    key_mask = jnp.where(match | ((ids >= 8) & (ids < 11)), 1.0, 0.0).astype(BF16)
    query_mask = jnp.where((ids < 8) & ~match, MASKED, 0.0).astype(BF16)
    places = jnp.stack([rows_pos, cols_pos], axis=1).astype(F32)
    alive = live[:, None].astype(F32)
    tables = (cosine, sine, key_mask, query_mask, places, alive)
    if quick:
        weights, slots, tables = gather_pieces(master, inverse, core, me, devices, tables)
    else:
        low = lax.all_gather(master.astype(BF16), "dp", axis=0, tiled=True)
        weights = low.reshape(devices, block_rows, width)[inverse].reshape(stack, width)
        slots = jnp.zeros((4, devices), jnp.int32)
    cosine, sine, key_mask, query_mask, places, alive = tables
    here = core.reshape(1).astype(jnp.int32)
    x = tokens[0]
    first_in, query, key, value, attn, stat, *placed = attend(
        here, slots, x, vectors[0:1], vectors[1:2], vectors[4:7].reshape(1, 3 * width),
        cosine, sine, query_mask, key_mask, weights, stack,
    )
    if quick:
        weights = placed[0]
    whole_rows = block_rows if quick else 0
    block_out, grad_middle, grad_attn, sums, bias_up, keep_mlp, give_mlp = mlp(
        here, x, attn, cotangent[0], alive, vectors, weights, vectors[8:12].reshape(1, 4 * width), whole_rows
    )
    pairs = width // 128
    tie = lax.optimization_barrier
    if quick:
        pos = quarters(core, me)
        got = lax.ppermute(give_mlp, "group", SWAP)
    back = None
    cuts = (0, 1, pairs - 2, pairs)
    for start, stop in zip(cuts[:-1], cuts[1:]):
        back = attend_back(
            start, stop, back, query, key, value, grad_attn, attn, stat, cosine, sine, query_mask, key_mask, places
        )
        if quick and start == 0:
            send, back = tie((fold(pos, keep_mlp, got, (0, 1)), back))
            came = cross(send, 1, 2, devices)
        if quick and start == 1:
            send, back = tie((fold(pos, keep_mlp, got, (2,), ((came, 0),)), back))
            again = cross(send, 2, 1, devices)
    grad_q, grad_k, grad_v, grad_bias, grad_freq = back
    if quick:
        low, grad_q = tie((fold(pos, keep_mlp, got, (3,), ((came, 1), (again, 0)))[0], grad_q))
        late = sum_z(low, me, devices)
    keep_qkv, give_qkv = qkv_grad(here, grad_q, grad_k, grad_v, first_in, whole_rows)
    grad_v, give_qkv = tie((grad_v, give_qkv))
    input_grad, norm_sums = input_back(grad_q, grad_k, grad_v, weights, x, grad_middle, vectors)
    grad_freqs = grad_freq[:2].reshape(2, heads, 2, half).sum(2).reshape(1, width)
    local_vec = jnp.concatenate(
        [norm_sums[:2], sums[:2], grad_bias[:3], sums[2:3], bias_up.reshape(4, width), sums[3:4], grad_freqs],
        axis=0,
    )
    if quick:
        got_qkv = lax.ppermute(give_qkv, "group", SWAP)
        got_qkv, norm_sums, late = tie((got_qkv, norm_sums, late))
        vec_total = sum_part(local_vec + lax.ppermute(local_vec, "group", SWAP), devices, 1, 4)
        came = cross(fold(pos, keep_qkv, got_qkv, (0, 1)), 1, 2, devices)
        came, vec_total = tie((came, vec_total))
        again = cross(fold(pos, keep_qkv, got_qkv, (2,), ((came, 0),)), 2, 1, devices)
        vec_total = sum_part(vec_total, devices, 4, devices)
        again, vec_total = tie((again, vec_total))
        early = sum_z(fold(pos, keep_qkv, got_qkv, (3,), ((came, 1), (again, 0)))[0], me, devices)
        early, late = total_of(early), total_of(late)
        total = jnp.concatenate([early, late])
        mine, other, square = share_blocks(total, owner_block, core, devices)
    else:
        vec_total = lax.psum(local_vec, CORES)
        share = reduce_plain(jnp.concatenate([keep_qkv, keep_mlp]), owner_block, devices)
        square = lax.psum(jnp.sum(share * share), "dp")
    grad_norm = jnp.sqrt(square + jnp.sum(vec_total * vec_total))
    clip = jnp.minimum(1.0, 1.0 / (grad_norm + 1e-06))
    vec_grad = vec_total * clip
    vec_second_new, vec_weight = adam(vectors, vec_first, vec_second, vec_grad, 0.2, 0.0)
    if quick:
        own = (owner_block[me] % 2 == core).astype(F32)
        mat_grad, mat_second, mat_weight = adam_rows(
            jnp.stack([clip, own]), mine, other, master, first_mom, second_mom
        )
    else:
        mat_grad = share * clip
        mat_second, mat_weight = adam(master, first_mom, second_mom, mat_grad, 0.02, 0.05)
    return (
        block_out[None],
        input_grad[None],
        mat_grad,
        mat_second,
        mat_weight,
        vec_grad,
        vec_second_new,
        vec_weight,
        grad_norm,
    )


def solution(mesh):
    return jax.shard_map(
        local,
        mesh=mesh,
        in_specs=(
            P("group", "dp", None),
            P("group", "dp", None),
            P("group", "dp"),
            P("group", "dp"),
            P(),
            P("dp", None),
            P("dp", None),
            P("dp", None),
            P(),
            P(),
            P(),
        ),
        out_specs=(
            P("group", "dp", None),
            P("group", "dp", None),
            P("dp", None),
            P("dp", None),
            P("dp", None),
            P(),
            P(),
            P(),
            P(),
        ),
        check_vma=False,
    )
```

```python
import functools
import jax
import jax.numpy as jnp
from jax import lax
from jax.experimental import pallas as pl
from jax.experimental.pallas import tpu as pltpu

F32 = jnp.float32
BF16 = jnp.bfloat16
LAST = (((1,), (1,)), ((), ()))
FIRST = (((0,), (0,)), ((), ()))
PLAIN = (((1,), (0,)), ((), ()))
MASKED = -1e9
SHORT = pl.CostEstimate(flops=1000, bytes_accessed=1000, transcendentals=0)


def mm(left, right, dims):
    return lax.dot_general(left, right, dims, preferred_element_type=F32)


def norm_parts(value):
    centre = value - jnp.mean(value, axis=-1, keepdims=True)
    spread = jnp.mean(centre * centre, axis=-1, keepdims=True)
    inverse = lax.rsqrt(spread + 1e-6)
    return centre * inverse, inverse


def norm_back(unit, inverse, grad, gain):
    scaled = grad * gain
    first = jnp.mean(scaled, axis=-1, keepdims=True)
    second = jnp.mean(scaled * unit, axis=-1, keepdims=True)
    return inverse * (scaled - first - unit * second)


def swap_halves(value):
    lane = lax.broadcasted_iota(jnp.int32, value.shape, 1)
    return jnp.where(
        lane % 64 < 32, pltpu.roll(value, 96, 1), pltpu.roll(value, 32, 1)
    )


def split3(value):
    one = value.astype(BF16).astype(F32)
    rest = value - one
    two = rest.astype(BF16).astype(F32)
    return one, two, rest - two


LARGE = 192
SMALL = 96


def place_pieces(core, slot_ref, mine, other, block, side, dst, sem):
    for which, (first, second, small) in enumerate((mine, other)):
        @pl.when((core == side) if which == 0 else (core != side))
        def _():
            large_slot = slot_ref[2 * which, block]
            small_slot = slot_ref[2 * which + 1, block]

            @pl.when(large_slot < 8)
            def _():
                pltpu.make_async_copy(first.at[large_slot], dst(0, LARGE), sem).start()

            @pl.when(large_slot >= 8)
            def _():
                pltpu.make_async_copy(second.at[large_slot - 8], dst(0, LARGE), sem).start()

            pltpu.make_async_copy(small.at[small_slot], dst(LARGE, SMALL), sem).start()


def attend_kernel(blocks, core_ref, slot_ref, x_ref, g_ref, b_ref, bq_ref, bk_ref, bv_ref,
                  cos_ref, sin_ref, qm_ref, km_ref, *rest):
    if blocks:
        mine, other = rest[0:3], rest[3:6]
        n1_ref, q_ref, k_ref, v_ref, attn_ref, stat_ref, w_ref, n1_s, w_s, near, far, back = rest[6:]
    else:
        w_ref, n1_ref, q_ref, k_ref, v_ref, attn_ref, stat_ref, n1_s, w_s, near = rest
    count, width = x_ref.shape
    step = pl.program_id(0)

    @pl.when(step == 0)
    def _():
        if blocks:
            core = core_ref[0]
            rows = w_ref.shape[0] // blocks

            def start(block, sem):
                for side in (0, 1):
                    def dst(offset, size):
                        base = block * rows + side * (rows // 2) + offset
                        return w_s.at[pl.ds(pl.multiple_of(base, 16), size)]
                    place_pieces(core, slot_ref, mine, other, block, side, dst, sem)

            def near_block(block, carry):
                start(block, near)
                return carry

            def far_block(block, carry):
                start(block, far)
                return carry

            lax.fori_loop(0, 3 * width // rows, near_block, 0)
            lax.fori_loop(3 * width // rows, blocks, far_block, 0)
        else:
            pltpu.make_async_copy(w_ref.at[pl.ds(0, 3 * width)], w_s, near).start()
        unit, _ = norm_parts(x_ref[...].astype(F32))
        n1 = (unit * g_ref[...] + b_ref[...]).astype(BF16)
        n1_s[...] = n1
        n1_ref[...] = n1
        head = w_s.at[pl.ds(0, 3 * width)]
        pltpu.make_async_copy(head, head, near).wait()

    if blocks:
        @pl.when(step == 1)
        def _():
            tail = w_s.at[pl.ds(3 * width, w_s.shape[0] - 3 * width)]
            pltpu.make_async_copy(tail, tail, far).wait()
            pltpu.make_async_copy(w_s, w_ref, back).start()

    def third(j):
        return w_s[pl.ds(pl.multiple_of(j * width + step * 128, 128), 128), :]

    w = jnp.concatenate([third(0), third(1), third(2)], axis=0)
    qkv = mm(n1_s[...], w, LAST)
    q = qkv[:, :128] + bq_ref[...]
    k = qkv[:, 128:256] + bk_ref[...]
    v = (qkv[:, 256:] + bv_ref[...]).astype(BF16)
    c = cos_ref[...]
    s = sin_ref[...]
    qr = ((q * c + swap_halves(q) * s).astype(BF16).astype(F32) * 0.125).astype(BF16)
    kr = (k * c + swap_halves(k) * s).astype(BF16)
    q_ref[...] = qr
    k_ref[...] = kr
    v_ref[...] = v
    lane = lax.broadcasted_iota(jnp.int32, (1, 128), 1)
    k_aug = jnp.concatenate([kr, km_ref[...]], axis=1)
    v_aug = jnp.concatenate([v, jnp.ones((count, 128), BF16)], axis=1)
    zero = jnp.zeros((), BF16)
    tile = 256
    for i in range(count // tile):
        rows = pl.ds(i * tile, tile)
        out = None
        stats = []
        for h in (0, 1):
            mine_lanes = (lane // 64) == h
            qa = jnp.concatenate(
                [jnp.where(mine_lanes, qr[i * tile:(i + 1) * tile], zero), qm_ref[rows, :]], axis=1)
            scores = mm(qa, k_aug, LAST)
            top = jnp.max(scores, axis=-1, keepdims=True)
            e = jnp.exp(scores - top).astype(BF16)
            o = mm(e, v_aug, PLAIN)
            total = o[:, 128:]
            o = o[:, :128] / total
            out = o if out is None else jnp.where(lane < 64, out, o)
            stats.append(top + jnp.log(total[:, :1]))
        attn_ref[rows, :] = out.astype(BF16)
        stat_ref[rows, :] = jnp.where(lane < 64, stats[0], stats[1])

    if blocks:
        @pl.when(step == pl.num_programs(0) - 1)
        def _():
            pltpu.make_async_copy(w_s, w_ref, back).wait()


def attend(core, slots, x, gain, shift, bqkv, cos, sin, qm, km, weights, stack):
    count, width = x.shape
    pairs = width // 128
    pieces = isinstance(weights, tuple)
    blocks = slots.shape[1] if pieces else 0
    whole = lambda p: (0, 0)
    col = lambda p: (0, p)
    smem = pl.BlockSpec(memory_space=pltpu.SMEM)
    hbm = pl.BlockSpec(memory_space=pl.ANY)
    given = weights if pieces else (weights,)
    specs = [smem, smem] + [
        pl.BlockSpec((count, width), whole),
        pl.BlockSpec((1, width), whole),
        pl.BlockSpec((1, width), whole),
        pl.BlockSpec((1, 128), col),
        pl.BlockSpec((1, 128), lambda p: (0, p + pairs)),
        pl.BlockSpec((1, 128), lambda p: (0, p + 2 * pairs)),
        pl.BlockSpec((count, 128), col),
        pl.BlockSpec((count, 128), col),
        pl.BlockSpec((count, 128), whole),
        pl.BlockSpec((count, 128), whole),
    ] + [hbm] * len(given)
    outs = [pl.BlockSpec((count, width), whole)] + [pl.BlockSpec((count, 128), col)] * 5
    shape = lambda d: jax.ShapeDtypeStruct((count, width), d)
    shapes = [shape(BF16)] * 5 + [shape(F32)]
    scratch = [pltpu.VMEM((count, width), BF16), pltpu.VMEM((stack if pieces else 3 * width, width), BF16), pltpu.SemaphoreType.DMA]
    if pieces:
        outs.append(hbm)
        shapes.append(jax.ShapeDtypeStruct((stack, width), BF16))
        scratch += [pltpu.SemaphoreType.DMA] * 2
    return pl.pallas_call(
        functools.partial(attend_kernel, blocks),
        grid=(pairs,),
        in_specs=specs,
        out_specs=outs,
        out_shape=shapes,
        scratch_shapes=scratch,
        compiler_params=pltpu.CompilerParams(vmem_limit_bytes=56 * 2**20),
        cost_estimate=SHORT,
        name="attend",
    )(core, slots, x, gain, shift, bqkv, bqkv, bqkv, cos, sin, qm, km, *given)


def gelu_both(x):
    cdf = 0.5 + 0.5 * lax.erf(x * 0.7071067811865476)
    return x * cdf, cdf + x * jnp.exp(x * x * -0.5) * 0.3989422804014327


def send_rows(core, block_rows, stage, row, base, keep_ref, give_ref, sem):
    if not block_rows:
        rows = stage.shape[0]
        pltpu.make_async_copy(
            stage, keep_ref.at[pl.ds(pl.multiple_of(row - base, 64), rows)], sem
        ).start()
        return

    def one(index, carry):
        at = row + 64 * index
        block = lax.div(at, block_rows)
        inner = pl.ds(pl.multiple_of(at - block * block_rows, 64), 64)
        slot = lax.div(block, 2) - base // 2
        source = stage.at[pl.ds(pl.multiple_of(64 * index, 64), 64)]
        own = lax.rem(block, 2) == core

        @pl.when(own)
        def _():
            pltpu.make_async_copy(source, keep_ref.at[slot, inner], sem).start()

        @pl.when(jnp.logical_not(own))
        def _():
            pltpu.make_async_copy(source, give_ref.at[slot, inner], sem).start()

        return carry

    lax.fori_loop(0, stage.shape[0] // 64, one, 0)


def mlp_kernel(block_rows, base, core_ref, x_ref, at_ref, cot_ref, live_ref, vec_ref, wo_ref, w1_ref, w2_ref, b1_ref,
               out_ref, dm_ref, da_ref, sums_ref, gb_ref, keep_ref, give_ref,
               middle_s, n2_s, dz_s, acc_s, stage_s, proj_s, sems):
    step = pl.program_id(0)
    last = pl.num_programs(0) - 1
    count, width = x_ref.shape
    core = core_ref[0]
    tile = w1_ref.shape[0]

    @pl.when(step == 0)
    def _():
        middle = x_ref[...].astype(F32) + mm(at_ref[...], wo_ref[...], LAST) + vec_ref[7:8, :]
        middle_s[...] = middle
        unit, _ = norm_parts(middle)
        n2_s[...] = (unit * vec_ref[2:3, :] + vec_ref[3:4, :]).astype(BF16)
        dz_s[...] = jnp.where(live_ref[...] > 0.5, cot_ref[...].astype(F32), 0.0).astype(BF16)
        acc_s[...] = jnp.zeros_like(acc_s)
        dm_ref[...] = jnp.zeros_like(dm_ref)

    slot = lax.rem(step, 2)

    @pl.when(step >= 2)
    def _():
        pltpu.make_async_copy(stage_s.at[slot], stage_s.at[slot], sems.at[slot]).wait()

    n2 = n2_s[...]
    dz = dz_s[...]
    w1 = w1_ref[...]
    w2 = w2_ref[...]
    pre = mm(w1, n2, LAST) + b1_ref[...].reshape(tile, 1)
    back = mm(w2, dz, LAST)
    act, slope = gelu_both(pre)
    hidden = act.astype(BF16)
    stage_s[slot, 1] = mm(hidden, dz, PLAIN).astype(BF16)
    dpre = (back * slope).astype(BF16)
    gb_ref[...] = jnp.sum(dpre.astype(F32), axis=1, keepdims=True).reshape(1, tile)
    stage_s[slot, 0] = mm(dpre, n2, PLAIN).astype(BF16)
    acc_s[...] += mm(hidden, w2, FIRST)
    dm_ref[...] += mm(dpre, w1, FIRST)
    for j in (0, 1):
        send_rows(core, block_rows, stage_s.at[slot, j], (4 + 4 * j) * width + step * tile,
                  base, keep_ref, give_ref, sems.at[slot])

    @pl.when(step == last)
    def _():
        middle = middle_s[...]
        out_ref[...] = (middle + acc_s[...] + vec_ref[12:13, :]).astype(BF16)
        unit, inverse = norm_parts(middle)
        dn = dm_ref[...]
        dy = dz_s[...].astype(F32)
        dm = dy + norm_back(unit, inverse, dn, vec_ref[2:3, :])
        dm_ref[...] = dm
        low = dm.astype(BF16)
        row = lambda a: jnp.sum(a, axis=0, keepdims=True)
        sums_ref[...] = jnp.concatenate(
            [row(dn * unit), row(dn), row(low.astype(F32)), row(dy), jnp.zeros((4, width), F32)], axis=0)
        proj_s[...] = mm(low, at_ref[...], FIRST).astype(BF16)
        send_rows(core, block_rows, proj_s, 3 * width, base, keep_ref, give_ref, sems.at[2])
        da_ref[...] = mm(low, wo_ref[...], PLAIN).astype(BF16)
        pltpu.make_async_copy(stage_s.at[slot], stage_s.at[slot], sems.at[slot]).wait()
        pltpu.make_async_copy(stage_s.at[1 - slot], stage_s.at[1 - slot], sems.at[1 - slot]).wait()
        pltpu.make_async_copy(proj_s, proj_s, sems.at[2]).wait()


def grad_shapes(block_rows, rows, width):
    if block_rows:
        half = jax.ShapeDtypeStruct((rows // block_rows // 2, block_rows, width), BF16)
        return [half, half]
    return [jax.ShapeDtypeStruct((rows, width), BF16), jax.ShapeDtypeStruct((16, width), BF16)]


def mlp(core, x, attn, cot, live, vectors, weights, b1, block_rows, tile=512):
    count, width = x.shape
    units = 4 * width
    stack = weights.shape[0]
    base = 3 * width // block_rows if block_rows else 3 * width
    whole = lambda t: (0, 0)
    big = pl.BlockSpec((count, width), whole)
    hbm = pl.BlockSpec(memory_space=pl.ANY)
    return pl.pallas_call(
        functools.partial(mlp_kernel, block_rows, base),
        grid=(units // tile,),
        in_specs=[pl.BlockSpec(memory_space=pltpu.SMEM), big, big, big, pl.BlockSpec((count, 1), whole),
                  pl.BlockSpec(vectors.shape, whole),
                  pl.BlockSpec((width, width), lambda t: (3, 0)),
                  pl.BlockSpec((tile, width), lambda t: (4 * width // tile + t, 0)),
                  pl.BlockSpec((tile, width), lambda t: (8 * width // tile + t, 0)),
                  pl.BlockSpec((1, tile), lambda t: (0, t))],
        out_specs=[big, big, big, pl.BlockSpec((8, width), whole), pl.BlockSpec((1, tile), lambda t: (0, t)), hbm, hbm],
        out_shape=[
            jax.ShapeDtypeStruct((count, width), BF16),
            jax.ShapeDtypeStruct((count, width), F32),
            jax.ShapeDtypeStruct((count, width), BF16),
            jax.ShapeDtypeStruct((8, width), F32),
            jax.ShapeDtypeStruct((1, units), F32),
        ] + grad_shapes(block_rows, stack - 3 * width, width),
        scratch_shapes=[
            pltpu.VMEM((count, width), F32),
            pltpu.VMEM((count, width), BF16),
            pltpu.VMEM((count, width), BF16),
            pltpu.VMEM((count, width), F32),
            pltpu.VMEM((2, 2, tile, width), BF16),
            pltpu.VMEM((width, width), BF16),
            pltpu.SemaphoreType.DMA((3,)),
        ],
        compiler_params=pltpu.CompilerParams(vmem_limit_bytes=60 * 2**20),
        cost_estimate=SHORT,
        name="mlp",
    )(core, x, attn, cot, live, vectors, weights, weights, weights, b1)


def back_kernel(first, q_ref, k_ref, v_ref, da_ref, at_ref, stat_ref, cos_ref, sin_ref,
                qm_ref, km_ref, pos_ref, *rest):
    dq_ref, dk_ref, dv_ref, gb_ref, gf_ref = rest if first else rest[5:]
    count = q_ref.shape[0]
    lane = lax.broadcasted_iota(jnp.int32, (1, 128), 1)
    zero = jnp.zeros((), BF16)
    q = q_ref[...]
    k = k_ref[...]
    v = v_ref[...]
    da = da_ref[...]
    prod = da.astype(F32) * at_ref[...].astype(F32)
    qm = qm_ref[...].astype(F32)
    k_aug = jnp.concatenate([k, km_ref[...]], axis=1)
    v_aug = jnp.concatenate([v, jnp.broadcast_to((lane < 2).astype(BF16), (count, 128))], axis=1)
    tile = 256
    dq = dk = dv = None
    for h in (0, 1):
        mine = (lane // 64) == h
        qh = jnp.where(mine, q, zero)
        kh = jnp.where(mine, k, zero)
        dah = jnp.where(mine, da, zero)
        delta = jnp.sum(jnp.where(mine, prod, 0.0), axis=-1, keepdims=True)
        d1, d2, _ = split3(delta)
        l1, l2, l3 = split3(stat_ref[:, 64 * h:64 * h + 1])
        extra = jnp.where(lane == 8, -l1, jnp.where(lane == 9, -l2, jnp.where(lane == 10, -l3, qm)))
        q_aug = jnp.concatenate([qh, extra.astype(BF16)], axis=1)
        da_aug = jnp.concatenate(
            [dah, jnp.where(lane == 0, -d1, jnp.where(lane == 1, -d2, 0.0)).astype(BF16)], axis=1)
        dks, dvs, dqh = [], [], None
        for i in range(count // tile):
            sl = slice(i * tile, (i + 1) * tile)
            p = jnp.exp(mm(k_aug[sl], q_aug, LAST))
            dp = mm(v_aug[sl], da_aug, LAST)
            ds = (p * dp).astype(BF16)
            dvs.append(mm(p.astype(BF16), dah, PLAIN))
            dks.append(mm(ds, qh, PLAIN))
            part = mm(ds, kh[sl], FIRST)
            dqh = part if dqh is None else dqh + part
        dkh = jnp.concatenate(dks, axis=0)
        dvh = jnp.concatenate(dvs, axis=0)
        dq = dqh if dq is None else dq + dqh
        dk = dkh if dk is None else dk + dkh
        dv = dvh if dv is None else dv + dvh
    dq = dq * 0.125
    c = cos_ref[...]
    s = sin_ref[...]
    turned = dq * swap_halves(q.astype(F32) * 8.0) + dk * swap_halves(k.astype(F32))
    turned = jnp.where(lane % 64 < 32, -turned, turned)
    row = lambda a: jnp.sum(a, axis=0, keepdims=True)
    gf_ref[...] = jnp.concatenate(
        [row(turned * pos_ref[:, 0:1]), row(turned * pos_ref[:, 1:2]), jnp.zeros((6, 128), F32)], axis=0)
    dqp = (dq * c - swap_halves(dq) * s).astype(BF16)
    dkp = (dk * c - swap_halves(dk) * s).astype(BF16)
    dvp = dv.astype(BF16)
    gb_ref[...] = jnp.concatenate(
        [row(dqp.astype(F32)), row(dkp.astype(F32)), row(dvp.astype(F32)), jnp.zeros((5, 128), F32)], axis=0)
    dq_ref[...] = dqp
    dk_ref[...] = dkp
    dv_ref[...] = dvp


def attend_back(start, stop, before, q, k, v, da, attn, stat, cos, sin, qm, km, pos):
    count, width = q.shape
    whole = lambda p: (0, 0)
    col = lambda p: (0, p + start)
    tall = pl.BlockSpec((count, 128), col)
    fixed = pl.BlockSpec((count, 128), whole)
    small = pl.BlockSpec((8, 128), col)
    in_specs = [tall] * 8 + [fixed] * 2 + [pl.BlockSpec((count, 2), whole)]
    operands = [q, k, v, da, attn, stat, cos, sin, qm, km, pos]
    aliases = {}
    if before is not None:
        aliases = {len(operands) + i: i for i in range(5)}
        in_specs += [pl.BlockSpec(memory_space=pl.ANY)] * 5
        operands += list(before)
    return pl.pallas_call(
        functools.partial(back_kernel, before is None),
        grid=(stop - start,),
        in_specs=in_specs,
        out_specs=[tall] * 3 + [small] * 2,
        out_shape=[jax.ShapeDtypeStruct((count, width), BF16)] * 3 + [jax.ShapeDtypeStruct((8, width), F32)] * 2,
        input_output_aliases=aliases,
        compiler_params=pltpu.CompilerParams(vmem_limit_bytes=56 * 2**20),
        cost_estimate=SHORT,
        name="attend_back",
    )(*operands)


def qkv_grad_kernel(block_rows, core_ref, dq_ref, dk_ref, dv_ref, n1_ref, keep_ref, give_ref, stage_s, sem):
    width = n1_ref.shape[1]
    cols = dq_ref.shape[1]
    step = pl.program_id(0)
    n1 = n1_ref[...]
    for j, ref in enumerate((dq_ref, dk_ref, dv_ref)):
        stage_s[step, j] = mm(ref[...], n1, FIRST).astype(BF16)
        send_rows(core_ref[0], block_rows, stage_s.at[step, j], j * width + step * cols, 0, keep_ref, give_ref, sem)

    @pl.when(step == pl.num_programs(0) - 1)
    def _():
        pltpu.make_async_copy(stage_s, stage_s, sem).wait()


def qkv_grad(core, dq, dk, dv, n1, block_rows):
    count, width = n1.shape
    cols = width // 2
    tall = pl.BlockSpec((count, cols), lambda p: (0, p))
    hbm = pl.BlockSpec(memory_space=pl.ANY)
    return pl.pallas_call(
        functools.partial(qkv_grad_kernel, block_rows),
        grid=(2,),
        in_specs=[pl.BlockSpec(memory_space=pltpu.SMEM)] + [tall] * 3 + [pl.BlockSpec((count, width), lambda p: (0, 0))],
        out_specs=[hbm, hbm],
        out_shape=grad_shapes(block_rows, 3 * width, width),
        scratch_shapes=[pltpu.VMEM((2, 3, cols, width), BF16), pltpu.SemaphoreType.DMA],
        compiler_params=pltpu.CompilerParams(vmem_limit_bytes=56 * 2**20),
        cost_estimate=SHORT,
        name="qkv_grad",
    )(core, dq, dk, dv, n1)


def input_kernel(dq_ref, dk_ref, dv_ref, w_ref, x_ref, dm_ref, vec_ref, sums_ref, gb_ref, gf_ref, up_ref, ig_ref, out_ref):
    step = pl.program_id(0)
    d = jnp.concatenate([dq_ref[...], dk_ref[...], dv_ref[...]], axis=1)
    dn = mm(d, w_ref[...], PLAIN)
    unit, inverse = norm_parts(x_ref[...].astype(F32))
    ig_ref[...] = dm_ref[...] + norm_back(unit, inverse, dn, vec_ref[0:1, :])
    row = lambda a: jnp.sum(a, axis=0, keepdims=True)
    sums = jnp.concatenate([row(dn * unit), row(dn)], axis=0)

    @pl.when(step == 0)
    def _():
        width = dn.shape[1]
        half = width // 2
        out_ref[0:2] = sums
        out_ref[2:4] = sums_ref[0:2]
        out_ref[4:7] = gb_ref[0:3]
        out_ref[7:8] = sums_ref[2:3]
        for i in range(4):
            out_ref[8 + i:9 + i] = up_ref[:, i * width:(i + 1) * width]
        out_ref[12:13] = sums_ref[3:4]
        lane = lax.broadcasted_iota(jnp.int32, (width, half), 0)
        slot = lax.broadcasted_iota(jnp.int32, (width, half), 1)
        pick = jnp.where((lane // 64 == slot // 32) & (lane % 32 == slot % 32), 1.0, 0.0)
        both = lax.dot_general(gf_ref[...], pick, PLAIN, precision=lax.Precision.HIGHEST, preferred_element_type=F32)
        out_ref[13:14, :half] = both[0:1]
        out_ref[13:14, half:] = both[1:2]

    @pl.when(step > 0)
    def _():
        out_ref[0:2] += sums


def input_back(dq, dk, dv, weights, x, dm, vectors, sums, grad_bias, grad_freq, bias_up):
    count, width = x.shape
    tile = 256
    part = pl.BlockSpec((tile, width), lambda i: (i, 0))
    whole = lambda i: (0, 0)
    fixed = lambda a: pl.BlockSpec(a.shape, whole)
    return pl.pallas_call(
        input_kernel,
        grid=(count // tile,),
        in_specs=[part] * 3 + [pl.BlockSpec((3 * width, width), whole), part, part]
        + [fixed(a) for a in (vectors, sums, grad_bias, grad_freq, bias_up)],
        out_specs=[part, fixed(vectors)],
        out_shape=[jax.ShapeDtypeStruct((count, width), F32), jax.ShapeDtypeStruct(vectors.shape, F32)],
        compiler_params=pltpu.CompilerParams(vmem_limit_bytes=56 * 2**20),
        cost_estimate=SHORT,
        name="input_back",
    )(dq, dk, dv, weights, x, dm, vectors, sums, grad_bias, grad_freq, bias_up)


def fold_kernel(count, pos_ref, *refs):
    out_ref = refs[-1]
    ways = out_ref.shape[0]
    for k in range(ways):
        total = refs[k][...].astype(F32) + refs[ways + k][...].astype(F32)
        for more in refs[2 * ways:-1]:
            total = total + more[0].astype(F32)
        out_ref[k] = total.astype(BF16)


def fold(pos, keep, got, ways, more=()):
    count, rows, width = keep.shape
    some = count // 2
    quarter = [pl.BlockSpec((some, rows // 2, width // 2), lambda i, pos, k=k: (i, pos[k, 0], pos[k, 1])) for k in ways]
    extra = [pl.BlockSpec((1, some, rows // 2, width // 2), lambda i, pos, at=at: (at, i, 0, 0)) for _, at in more]
    out = pl.BlockSpec((len(ways), some, rows // 2, width // 2), lambda i, pos: (0, i, 0, 0))
    shape = jax.ShapeDtypeStruct((len(ways), count, rows // 2, width // 2), BF16)
    return pl.pallas_call(
        functools.partial(fold_kernel, len(more)),
        grid_spec=pltpu.PrefetchScalarGridSpec(
            num_scalar_prefetch=1, grid=(count // some,), in_specs=quarter * 2 + extra, out_specs=out),
        compiler_params=pltpu.CompilerParams(vmem_limit_bytes=40 * 2**20),
        out_shape=shape,
        cost_estimate=SHORT,
        name="fold",
    )(pos, *([keep] * len(ways)), *([got] * len(ways)), *[a for a, _ in more])


def pack_kernel(owner_ref, *refs):
    early, late, out_ref, total_s = refs[:4], refs[4:8], refs[8], refs[9]
    square = None
    start = 0
    for parts in (early, late):
        total = parts[0][...].astype(F32)
        for part in parts[1:]:
            total = total + part[...].astype(F32)
        total_s[start:start + total.shape[0]] = total.astype(BF16)
        start += total.shape[0]
        more = jnp.sum(total * total).reshape(1, 1)
        square = more if square is None else square + more
    rows = total_s.shape[1]
    lane = lax.broadcasted_iota(jnp.int32, (8, out_ref.shape[2]), 1)
    one, two, three = split3(square)
    extra = jnp.where(lane == 0, one, jnp.where(lane == 1, two, jnp.where(lane == 2, three, 0.0))).astype(BF16)
    for p in range(out_ref.shape[0]):
        out_ref[p, :rows] = total_s[lax.div(owner_ref[p], 2)]
        out_ref[p, rows:] = extra


def pack(owner, early, late):
    blocks = early[0].shape[0] + late[0].shape[0]
    rows, cols = early[0].shape[1:]
    vmem = pl.BlockSpec(memory_space=pltpu.VMEM)
    return pl.pallas_call(
        pack_kernel,
        in_specs=[pl.BlockSpec(memory_space=pltpu.SMEM)] + [vmem] * 8,
        out_specs=vmem,
        out_shape=jax.ShapeDtypeStruct((owner.shape[0], rows + 8, cols), BF16),
        scratch_shapes=[pltpu.VMEM((blocks, rows, cols), BF16)],
        compiler_params=pltpu.CompilerParams(vmem_limit_bytes=32 * 2**20),
        cost_estimate=SHORT,
        name="pack",
    )(owner, *early, *late)


def clip_of(square, vec):
    norm = jnp.sqrt(square + jnp.sum(vec * vec).reshape(1, 1))
    return norm, jnp.minimum(1.0, 1.0 / (norm + 1e-06))


def adam_kernel(own_ref, a_ref, b_ref, as_ref, bs_ref, vt_ref, vw_ref, vm_ref, vv_ref, w_ref, m_ref, v_ref,
                g_out, v_out, w_out, vg_out, vv_out, vw_out, norm_out):
    def squares(ref):
        block = ref[...].astype(F32)
        lane = lax.broadcasted_iota(jnp.int32, block.shape, 4)
        row = lax.broadcasted_iota(jnp.int32, block.shape, 3)
        return jnp.sum(jnp.where((lane < 3) & (row == 0), block, 0.0)).reshape(1, 1)

    norm, clip = clip_of(squares(as_ref) + squares(bs_ref), vt_ref[...])
    own = own_ref[0] > 0
    grad = jnp.where(own, a_ref[:, 0, 0].astype(F32), b_ref[:, 0, 0].astype(F32))
    grad = grad[:, :w_ref.shape[0] // grad.shape[0]].reshape(w_ref.shape) * clip
    second, weight = adam(w_ref[...], m_ref[...], v_ref[...], grad, 0.02, 0.05)
    g_out[...] = grad
    v_out[...] = second
    w_out[...] = weight

    @pl.when((pl.program_id(0) == 0) & (pl.program_id(1) == 0))
    def _():
        vec_grad = vt_ref[...] * clip
        second, weight = adam(vw_ref[...], vm_ref[...], vv_ref[...], vec_grad, 0.2, 0.0)
        vg_out[...] = vec_grad
        vv_out[...] = second
        vw_out[...] = weight
        norm_out[...] = jnp.broadcast_to(norm, norm_out.shape)


def adam_rows(own, mine, other, vec_total, vectors, vec_first, vec_second, weight, first, second):
    rows, width = weight.shape
    deep, tall, wide, piece, cols = mine.shape
    part = pl.BlockSpec((deep, 1, 1, piece, cols), lambda y, x: (0, y, x, 0, 0))
    marks = pl.BlockSpec((deep, tall, wide, 8, 128), lambda y, x: (0, 0, 0, piece // 8 - 1, 0))
    flat = pl.BlockSpec((rows // tall, width // wide), lambda y, x: (y, x))
    vec = pl.BlockSpec(vectors.shape, lambda y, x: (0, 0))
    shape = jax.ShapeDtypeStruct((rows, width), F32)
    small = jax.ShapeDtypeStruct(vectors.shape, F32)
    return pl.pallas_call(
        adam_kernel,
        grid=(tall, wide),
        in_specs=[pl.BlockSpec(memory_space=pltpu.SMEM), part, part, marks, marks] + [vec] * 4 + [flat] * 3,
        out_specs=[flat] * 3 + [vec] * 3 + [pl.BlockSpec((8, 128), lambda y, x: (0, 0))],
        out_shape=[shape] * 3 + [small] * 3 + [jax.ShapeDtypeStruct((8, 128), F32)],
        compiler_params=pltpu.CompilerParams(vmem_limit_bytes=40 * 2**20),
        cost_estimate=SHORT,
        name="adam",
    )(own, mine, other, mine, other, vec_total, vectors, vec_first, vec_second, weight, first, second)


from jax.sharding import PartitionSpec as P

HEADS = 12
STEP = 7


def place_tokens(heights, widths, count):
    sizes = heights * widths
    ends = jnp.cumsum(sizes)
    starts = ends - sizes
    places = jnp.arange(count, dtype=jnp.int32)
    segment = jnp.sum((places[:, None] >= ends[None, :]).astype(jnp.int32), axis=1)
    slots = jnp.arange(heights.shape[0], dtype=jnp.int32)
    picks = (segment[:, None] == slots[None, :]).astype(jnp.int32)
    begin = jnp.sum(picks * starts[None, :], axis=1)
    across = jnp.maximum(jnp.sum(picks * widths[None, :], axis=1), 1)
    offset = places - begin
    live = places < ends[-1]
    return (segment, offset // across, offset % across, live)


def adam(weight, first, second, grad, rate, decay):
    first_new = 0.5 * first + 0.5 * grad
    second_new = 0.5 * second + 0.5 * grad * grad
    correct = 1.0 - 0.5**STEP
    direction = first_new / correct / (jnp.sqrt(second_new / correct) + 1e-08)
    return (second_new, weight - rate * (direction + decay * weight))


def pairwise(bits, total):
    return [(i, i ^ bits) for i in range(total)]


def sum_part(value, devices, step, stop):
    while step < stop:
        value = value + lax.ppermute(value, "dp", pairwise(step, devices))
        step *= 2
    return value


CORES = ("group", "dp")
SWAP = [(0, 1), (1, 0)]


def cross(value, bit0, bit1, devices):
    perm = [(i, i ^ (bit0 if i < devices else bit1)) for i in range(2 * devices)]
    return lax.ppermute(value, CORES, perm)


def along_z(values, devices):
    return [
        lax.ppermute(v, "dp", [(i, (i + 4 * (s + 1)) % devices) for i in range(devices)])
        for s, v in enumerate(values)
    ]


def along_line(value, devices, step, up):
    last = devices // 4
    perm = []
    for z in range(last):
        near = z - 1 if up else z + 1
        far = z - step if up else z + step
        if 0 <= far < last:
            perm += [(4 * near + i, 4 * z + i) for i in range(4)]
    return lax.ppermute(value, "dp", perm)


def gather_pieces(master, inverse, core, me, devices, tables):
    tie = lax.optimization_barrier
    block_rows, width = master.shape
    half = block_rows // 2
    mine = lax.dynamic_slice_in_dim(master, core * half, half, 0).astype(BF16)
    large = mine[:LARGE]
    small = mine[LARGE:]
    z = me // 4
    deep = lax.rem(z - inverse // 4 + 4, 4)
    apart = me ^ inverse
    one = jnp.where(core == 0, apart & 1, (apart >> 1) & 1)
    two = jnp.where(core == 0, (apart >> 1) & 1, apart & 1)
    slots = jnp.stack([
        8 * two + 4 * one + deep,
        4 * deep + 2 * two + one,
        8 * one + 4 * two + deep,
        4 * deep + 2 * one + two,
    ]).astype(jnp.int32)
    up = along_z([large] * 3, devices)
    small = jnp.stack([small, cross(small, 1, 2, devices)])
    small = jnp.concatenate([small, cross(small, 2, 1, devices)])
    large = jnp.stack([large] + up)
    large, small, tables, slots = tie((large, small, tables, slots))
    first = cross(large, 1, 2, devices)
    ups = [along_line(small, devices, 1, True)]
    downs = [along_line(small, devices, 1, False)]
    first, ups[0], downs[0] = tie((first, ups[0], downs[0]))
    first = jnp.concatenate([large, first])
    second = cross(first, 2, 1, devices)
    for step in (2, 3):
        ups.append(along_line(ups[-1], devices, step, True))
        downs.append(along_line(downs[-1], devices, step, False))
    small = jnp.concatenate([small] + [jnp.where(z >= s, ups[s - 1], downs[3 - s]) for s in (1, 2, 3)])
    other = [lax.ppermute(a, "group", SWAP) for a in (first, second, small)]
    return (first, second, small, *other), slots, tables


def quarters(core, me):
    x, y = me & 1, (me >> 1) & 1
    one = jnp.where(core == 0, x, y)
    two = jnp.where(core == 0, y, x)
    pairs = [(1 - one, 1 - two), (1 - one, two), (one, 1 - two), (one, two)]
    return jnp.stack([
        jnp.stack([jnp.where(core == 0, b, a), jnp.where(core == 0, a, b)]) for a, b in pairs
    ]).astype(jnp.int32)


def sum_z(low, me, devices):
    count, rows, cols = low.shape
    z = me // 4
    low = low.reshape(count, 4, rows // 4, cols)
    pick = lambda at: lax.dynamic_index_in_dim(low, at, 1, keepdims=False)
    return (pick(z), *along_z([pick(lax.rem(z + s, 4)) for s in (1, 2, 3)], devices))


def reduce_plain(local_mat, owner_block, devices):
    rows, width = local_mat.shape
    block_rows = rows // devices
    term = local_mat.reshape(devices, block_rows, width)[owner_block].reshape(rows, width)
    share = lax.psum_scatter(term.astype(F32), "dp", scatter_dimension=0, tiled=True)
    return lax.psum(share.astype(BF16), "group").astype(F32)


def local(
    tokens,
    cotangent,
    grid_h,
    grid_w,
    owner_block,
    master,
    first_mom,
    second_mom,
    vectors,
    vec_first,
    vec_second,
):
    devices = lax.axis_size("dp")
    core = lax.axis_index("group")
    me = lax.axis_index("dp")
    count = tokens.shape[1]
    width = tokens.shape[2]
    heads = HEADS
    head_dim = width // heads
    half = head_dim // 2
    block_rows = master.shape[0]
    stack = devices * block_rows
    quick = devices == 16 and block_rows == 2 * (LARGE + SMALL) and width % 256 == 0
    inverse = jnp.argsort(owner_block)
    segment, rows_pos, cols_pos, live = place_tokens(grid_h[0], grid_w[0], count)
    freqs = vectors[13]

    def spread(part):
        return jnp.broadcast_to(part.reshape(heads, 1, half), (heads, 2, half)).reshape(1, width)

    angle = rows_pos.astype(F32)[:, None] * spread(freqs[: width // 2]) + cols_pos.astype(F32)[
        :, None
    ] * spread(freqs[width // 2 :])
    lower = (jnp.arange(width) % head_dim < half)[None]
    cosine = jnp.cos(angle)
    sine = jnp.sin(angle)
    sine = jnp.where(lower, -sine, sine)
    ids = jnp.arange(128)[None]
    match = segment[:, None] == ids
    key_mask = jnp.where(match | ((ids >= 8) & (ids < 11)), 1.0, 0.0).astype(BF16)
    query_mask = jnp.where((ids < 8) & ~match, MASKED, 0.0).astype(BF16)
    places = jnp.stack([rows_pos, cols_pos], axis=1).astype(F32)
    alive = live[:, None].astype(F32)
    bias_qkv = vectors[4:7].reshape(1, 3 * width)
    bias_one = vectors[8:12].reshape(1, 4 * width)
    tables = (cosine, sine, key_mask, query_mask, places, alive, bias_qkv, bias_one)
    if quick:
        weights, slots, tables = gather_pieces(master, inverse, core, me, devices, tables)
    else:
        low = lax.all_gather(master.astype(BF16), "dp", axis=0, tiled=True)
        weights = low.reshape(devices, block_rows, width)[inverse].reshape(stack, width)
        slots = jnp.zeros((4, devices), jnp.int32)
    cosine, sine, key_mask, query_mask, places, alive, bias_qkv, bias_one = tables
    here = core.reshape(1).astype(jnp.int32)
    x = tokens[0]
    first_in, query, key, value, attn, stat, *placed = attend(
        here, slots, x, vectors[0:1], vectors[1:2], bias_qkv,
        cosine, sine, query_mask, key_mask, weights, stack,
    )
    if quick:
        weights = placed[0]
    whole_rows = block_rows if quick else 0
    block_out, grad_middle, grad_attn, sums, bias_up, keep_mlp, give_mlp = mlp(
        here, x, attn, cotangent[0], alive, vectors, weights, bias_one, whole_rows
    )
    pairs = width // 128
    tie = lax.optimization_barrier
    if quick:
        pos = quarters(core, me)
        got = lax.ppermute(give_mlp, "group", SWAP)
    back = None
    cuts = (0, 1, pairs - 2, pairs)
    for start, stop in zip(cuts[:-1], cuts[1:]):
        back = attend_back(
            start, stop, back, query, key, value, grad_attn, attn, stat, cosine, sine, query_mask, key_mask, places
        )
        if quick and start == 0:
            send, back = tie((fold(pos, keep_mlp, got, (0, 1)), back))
            came = cross(send, 1, 2, devices)
        if quick and start == 1:
            send, back = tie((fold(pos, keep_mlp, got, (2,), ((came, 0),)), back))
            again = cross(send, 2, 1, devices)
    grad_q, grad_k, grad_v, grad_bias, grad_freq = back
    if quick:
        low, grad_q = tie((fold(pos, keep_mlp, got, (3,), ((came, 1), (again, 0)))[0], grad_q))
        late = sum_z(low, me, devices)
    keep_qkv, give_qkv = qkv_grad(here, grad_q, grad_k, grad_v, first_in, whole_rows)
    grad_v, give_qkv = tie((grad_v, give_qkv))
    input_grad, local_vec = input_back(
        grad_q, grad_k, grad_v, weights, x, grad_middle, vectors, sums, grad_bias, grad_freq, bias_up
    )
    if quick:
        got_qkv = lax.ppermute(give_qkv, "group", SWAP)
        got_qkv, local_vec, late = tie((got_qkv, local_vec, late))
        vec_total = sum_part(local_vec + lax.ppermute(local_vec, "group", SWAP), devices, 1, 4)
        came = cross(fold(pos, keep_qkv, got_qkv, (0, 1)), 1, 2, devices)
        came, vec_total = tie((came, vec_total))
        again = cross(fold(pos, keep_qkv, got_qkv, (2,), ((came, 0),)), 2, 1, devices)
        vec_total = sum_part(vec_total, devices, 4, devices)
        again, vec_total = tie((again, vec_total))
        early = sum_z(fold(pos, keep_qkv, got_qkv, (3,), ((came, 1), (again, 0)))[0], me, devices)
        load = pack(owner_block, early, late)
        mine = lax.all_to_all(load, "dp", 0, 0, tiled=True)
        other = lax.ppermute(mine, "group", SWAP)
        shape = (devices // 4, 2, 2, *load.shape[1:])
        own = (owner_block[me] % 2 == core).astype(jnp.int32).reshape(1)
        mat_grad, mat_second, mat_weight, vec_grad, vec_second_new, vec_weight, norm = adam_rows(
            own, mine.reshape(shape), other.reshape(shape), vec_total, vectors, vec_first, vec_second,
            master, first_mom, second_mom,
        )
        grad_norm = norm[0, 0]
    else:
        vec_total = lax.psum(local_vec, CORES)
        share = reduce_plain(jnp.concatenate([keep_qkv, keep_mlp]), owner_block, devices)
        square = lax.psum(jnp.sum(share * share), "dp")
        grad_norm = jnp.sqrt(square + jnp.sum(vec_total * vec_total))
        clip = jnp.minimum(1.0, 1.0 / (grad_norm + 1e-06))
        mat_grad = share * clip
        mat_second, mat_weight = adam(master, first_mom, second_mom, mat_grad, 0.02, 0.05)
        vec_grad = vec_total * clip
        vec_second_new, vec_weight = adam(vectors, vec_first, vec_second, vec_grad, 0.2, 0.0)
    return (
        block_out[None],
        input_grad[None],
        mat_grad,
        mat_second,
        mat_weight,
        vec_grad,
        vec_second_new,
        vec_weight,
        grad_norm,
    )


def solution(mesh):
    return jax.shard_map(
        local,
        mesh=mesh,
        in_specs=(
            P("group", "dp", None),
            P("group", "dp", None),
            P("group", "dp"),
            P("group", "dp"),
            P(),
            P("dp", None),
            P("dp", None),
            P("dp", None),
            P(),
            P(),
            P(),
        ),
        out_specs=(
            P("group", "dp", None),
            P("group", "dp", None),
            P("dp", None),
            P("dp", None),
            P("dp", None),
            P(),
            P(),
            P(),
            P(),
        ),
        check_vma=False,
    )
```

```python
import functools
import jax
import jax.numpy as jnp
from jax import lax
from jax.experimental import pallas as pl
from jax.experimental.pallas import tpu as pltpu

F32 = jnp.float32
BF16 = jnp.bfloat16
LAST = (((1,), (1,)), ((), ()))
FIRST = (((0,), (0,)), ((), ()))
PLAIN = (((1,), (0,)), ((), ()))
MASKED = -1e9
SHORT = pl.CostEstimate(flops=1000, bytes_accessed=1000, transcendentals=0)


def mm(left, right, dims):
    return lax.dot_general(left, right, dims, preferred_element_type=F32)


def norm_parts(value):
    centre = value - jnp.mean(value, axis=-1, keepdims=True)
    spread = jnp.mean(centre * centre, axis=-1, keepdims=True)
    inverse = lax.rsqrt(spread + 1e-6)
    return centre * inverse, inverse


def norm_back(unit, inverse, grad, gain):
    scaled = grad * gain
    first = jnp.mean(scaled, axis=-1, keepdims=True)
    second = jnp.mean(scaled * unit, axis=-1, keepdims=True)
    return inverse * (scaled - first - unit * second)


def swap_halves(value):
    lane = lax.broadcasted_iota(jnp.int32, value.shape, 1)
    return jnp.where(
        lane % 64 < 32, pltpu.roll(value, 96, 1), pltpu.roll(value, 32, 1)
    )


def split3(value):
    one = value.astype(BF16).astype(F32)
    rest = value - one
    two = rest.astype(BF16).astype(F32)
    return one, two, rest - two


LARGE = 208
SMALL = 80


def place_pieces(core, slot_ref, mine, other, block, side, dst, sem):
    for which, (first, second, small) in enumerate((mine, other)):
        @pl.when((core == side) if which == 0 else (core != side))
        def _():
            large_slot = slot_ref[2 * which, block]
            small_slot = slot_ref[2 * which + 1, block]

            @pl.when(large_slot < 8)
            def _():
                pltpu.make_async_copy(first.at[large_slot], dst(0, LARGE), sem).start()

            @pl.when(large_slot >= 8)
            def _():
                pltpu.make_async_copy(second.at[large_slot - 8], dst(0, LARGE), sem).start()

            pltpu.make_async_copy(small.at[small_slot], dst(LARGE, SMALL), sem).start()


def attend_kernel(blocks, core_ref, slot_ref, x_ref, g_ref, b_ref, bq_ref, bk_ref, bv_ref,
                  cos_ref, sin_ref, qm_ref, km_ref, *rest):
    if blocks:
        mine, other = rest[0:3], rest[3:6]
        n1_ref, q_ref, k_ref, v_ref, attn_ref, stat_ref, w_ref, n1_s, w_s, near, far, back = rest[6:]
    else:
        w_ref, n1_ref, q_ref, k_ref, v_ref, attn_ref, stat_ref, n1_s, w_s, near = rest
    count, width = x_ref.shape
    step = pl.program_id(0)

    @pl.when(step == 0)
    def _():
        if blocks:
            core = core_ref[0]
            rows = w_ref.shape[0] // blocks

            def start(block, sem):
                for side in (0, 1):
                    def dst(offset, size):
                        base = block * rows + side * (rows // 2) + offset
                        return w_s.at[pl.ds(pl.multiple_of(base, 16), size)]
                    place_pieces(core, slot_ref, mine, other, block, side, dst, sem)

            def near_block(block, carry):
                start(block, near)
                return carry

            def far_block(block, carry):
                start(block, far)
                return carry

            lax.fori_loop(0, 3 * width // rows, near_block, 0)
            lax.fori_loop(3 * width // rows, blocks, far_block, 0)
        else:
            pltpu.make_async_copy(w_ref.at[pl.ds(0, 3 * width)], w_s, near).start()
        unit, _ = norm_parts(x_ref[...].astype(F32))
        n1 = (unit * g_ref[...] + b_ref[...]).astype(BF16)
        n1_s[...] = n1
        n1_ref[...] = n1
        head = w_s.at[pl.ds(0, 3 * width)]
        pltpu.make_async_copy(head, head, near).wait()

    if blocks:
        @pl.when(step == 1)
        def _():
            tail = w_s.at[pl.ds(3 * width, w_s.shape[0] - 3 * width)]
            pltpu.make_async_copy(tail, tail, far).wait()
            pltpu.make_async_copy(w_s, w_ref, back).start()

    def third(j):
        return w_s[pl.ds(pl.multiple_of(j * width + step * 128, 128), 128), :]

    w = jnp.concatenate([third(0), third(1), third(2)], axis=0)
    qkv = mm(n1_s[...], w, LAST)
    q = qkv[:, :128] + bq_ref[...]
    k = qkv[:, 128:256] + bk_ref[...]
    v = (qkv[:, 256:] + bv_ref[...]).astype(BF16)
    c = cos_ref[...]
    s = sin_ref[...]
    qr = ((q * c + swap_halves(q) * s).astype(BF16).astype(F32) * 0.125).astype(BF16)
    kr = (k * c + swap_halves(k) * s).astype(BF16)
    q_ref[...] = qr
    k_ref[...] = kr
    v_ref[...] = v
    lane = lax.broadcasted_iota(jnp.int32, (1, 128), 1)
    k_aug = jnp.concatenate([kr, km_ref[...]], axis=1)
    v_aug = jnp.concatenate([v, jnp.ones((count, 128), BF16)], axis=1)
    zero = jnp.zeros((), BF16)
    tile = 256
    for i in range(count // tile):
        rows = pl.ds(i * tile, tile)
        out = None
        stats = []
        for h in (0, 1):
            mine_lanes = (lane // 64) == h
            qa = jnp.concatenate(
                [jnp.where(mine_lanes, qr[i * tile:(i + 1) * tile], zero), qm_ref[rows, :]], axis=1)
            scores = mm(qa, k_aug, LAST)
            top = jnp.max(scores, axis=-1, keepdims=True)
            e = jnp.exp(scores - top).astype(BF16)
            o = mm(e, v_aug, PLAIN)
            total = o[:, 128:]
            o = o[:, :128] / total
            out = o if out is None else jnp.where(lane < 64, out, o)
            stats.append(top + jnp.log(total[:, :1]))
        attn_ref[rows, :] = out.astype(BF16)
        stat_ref[rows, :] = jnp.where(lane < 64, stats[0], stats[1])

    if blocks:
        @pl.when(step == pl.num_programs(0) - 1)
        def _():
            pltpu.make_async_copy(w_s, w_ref, back).wait()


def attend(core, slots, x, gain, shift, bqkv, cos, sin, qm, km, weights, stack):
    count, width = x.shape
    pairs = width // 128
    pieces = isinstance(weights, tuple)
    blocks = slots.shape[1] if pieces else 0
    whole = lambda p: (0, 0)
    col = lambda p: (0, p)
    smem = pl.BlockSpec(memory_space=pltpu.SMEM)
    hbm = pl.BlockSpec(memory_space=pl.ANY)
    given = weights if pieces else (weights,)
    specs = [smem, smem] + [
        pl.BlockSpec((count, width), whole),
        pl.BlockSpec((1, width), whole),
        pl.BlockSpec((1, width), whole),
        pl.BlockSpec((1, 128), col),
        pl.BlockSpec((1, 128), lambda p: (0, p + pairs)),
        pl.BlockSpec((1, 128), lambda p: (0, p + 2 * pairs)),
        pl.BlockSpec((count, 128), col),
        pl.BlockSpec((count, 128), col),
        pl.BlockSpec((count, 128), whole),
        pl.BlockSpec((count, 128), whole),
    ] + [hbm] * len(given)
    outs = [pl.BlockSpec((count, width), whole)] + [pl.BlockSpec((count, 128), col)] * 5
    shape = lambda d: jax.ShapeDtypeStruct((count, width), d)
    shapes = [shape(BF16)] * 5 + [shape(F32)]
    scratch = [pltpu.VMEM((count, width), BF16), pltpu.VMEM((stack if pieces else 3 * width, width), BF16), pltpu.SemaphoreType.DMA]
    if pieces:
        outs.append(hbm)
        shapes.append(jax.ShapeDtypeStruct((stack, width), BF16))
        scratch += [pltpu.SemaphoreType.DMA] * 2
    return pl.pallas_call(
        functools.partial(attend_kernel, blocks),
        grid=(pairs,),
        in_specs=specs,
        out_specs=outs,
        out_shape=shapes,
        scratch_shapes=scratch,
        compiler_params=pltpu.CompilerParams(vmem_limit_bytes=56 * 2**20),
        cost_estimate=SHORT,
        name="attend",
    )(core, slots, x, gain, shift, bqkv, bqkv, bqkv, cos, sin, qm, km, *given)


def gelu_both(x):
    cdf = 0.5 + 0.5 * lax.erf(x * 0.7071067811865476)
    return x * cdf, cdf + x * jnp.exp(x * x * -0.5) * 0.3989422804014327


def send_rows(core, block_rows, stage, row, base, keep_ref, give_ref, sem):
    if not block_rows:
        rows = stage.shape[0]
        pltpu.make_async_copy(
            stage, keep_ref.at[pl.ds(pl.multiple_of(row - base, 64), rows)], sem
        ).start()
        return

    def one(index, carry):
        at = row + 64 * index
        block = lax.div(at, block_rows)
        inner = pl.ds(pl.multiple_of(at - block * block_rows, 64), 64)
        slot = lax.div(block, 2) - base // 2
        source = stage.at[pl.ds(pl.multiple_of(64 * index, 64), 64)]
        own = lax.rem(block, 2) == core

        @pl.when(own)
        def _():
            pltpu.make_async_copy(source, keep_ref.at[slot, inner], sem).start()

        @pl.when(jnp.logical_not(own))
        def _():
            pltpu.make_async_copy(source, give_ref.at[slot, inner], sem).start()

        return carry

    lax.fori_loop(0, stage.shape[0] // 64, one, 0)


def mlp_kernel(block_rows, base, core_ref, x_ref, at_ref, cot_ref, live_ref, vec_ref, wo_ref, w1_ref, w2_ref, b1_ref,
               out_ref, dm_ref, da_ref, sums_ref, gb_ref, keep_ref, give_ref,
               middle_s, n2_s, dz_s, acc_s, stage_s, proj_s, sems):
    step = pl.program_id(0)
    last = pl.num_programs(0) - 1
    count, width = x_ref.shape
    core = core_ref[0]
    tile = w1_ref.shape[0]

    @pl.when(step == 0)
    def _():
        middle = x_ref[...].astype(F32) + mm(at_ref[...], wo_ref[...], LAST) + vec_ref[7:8, :]
        middle_s[...] = middle
        unit, _ = norm_parts(middle)
        n2_s[...] = (unit * vec_ref[2:3, :] + vec_ref[3:4, :]).astype(BF16)
        dz_s[...] = jnp.where(live_ref[...] > 0.5, cot_ref[...].astype(F32), 0.0).astype(BF16)
        acc_s[...] = jnp.zeros_like(acc_s)
        dm_ref[...] = jnp.zeros_like(dm_ref)

    slot = lax.rem(step, 2)

    @pl.when(step >= 2)
    def _():
        pltpu.make_async_copy(stage_s.at[slot], stage_s.at[slot], sems.at[slot]).wait()

    n2 = n2_s[...]
    dz = dz_s[...]
    w1 = w1_ref[...]
    w2 = w2_ref[...]
    pre = mm(w1, n2, LAST) + b1_ref[...].reshape(tile, 1)
    back = mm(w2, dz, LAST)
    act, slope = gelu_both(pre)
    hidden = act.astype(BF16)
    stage_s[slot, 1] = mm(hidden, dz, PLAIN).astype(BF16)
    dpre = (back * slope).astype(BF16)
    gb_ref[...] = jnp.sum(dpre.astype(F32), axis=1, keepdims=True).reshape(1, tile)
    stage_s[slot, 0] = mm(dpre, n2, PLAIN).astype(BF16)
    acc_s[...] += mm(hidden, w2, FIRST)
    dm_ref[...] += mm(dpre, w1, FIRST)
    for j in (0, 1):
        send_rows(core, block_rows, stage_s.at[slot, j], (4 + 4 * j) * width + step * tile,
                  base, keep_ref, give_ref, sems.at[slot])

    @pl.when(step == last)
    def _():
        middle = middle_s[...]
        out_ref[...] = (middle + acc_s[...] + vec_ref[12:13, :]).astype(BF16)
        unit, inverse = norm_parts(middle)
        dn = dm_ref[...]
        dy = dz_s[...].astype(F32)
        dm = dy + norm_back(unit, inverse, dn, vec_ref[2:3, :])
        dm_ref[...] = dm
        low = dm.astype(BF16)
        row = lambda a: jnp.sum(a, axis=0, keepdims=True)
        sums_ref[...] = jnp.concatenate(
            [row(dn * unit), row(dn), row(low.astype(F32)), row(dy), jnp.zeros((4, width), F32)], axis=0)
        proj_s[...] = mm(low, at_ref[...], FIRST).astype(BF16)
        send_rows(core, block_rows, proj_s, 3 * width, base, keep_ref, give_ref, sems.at[2])
        da_ref[...] = mm(low, wo_ref[...], PLAIN).astype(BF16)
        pltpu.make_async_copy(stage_s.at[slot], stage_s.at[slot], sems.at[slot]).wait()
        pltpu.make_async_copy(stage_s.at[1 - slot], stage_s.at[1 - slot], sems.at[1 - slot]).wait()
        pltpu.make_async_copy(proj_s, proj_s, sems.at[2]).wait()


def grad_shapes(block_rows, rows, width):
    if block_rows:
        half = jax.ShapeDtypeStruct((rows // block_rows // 2, block_rows, width), BF16)
        return [half, half]
    return [jax.ShapeDtypeStruct((rows, width), BF16), jax.ShapeDtypeStruct((16, width), BF16)]


def mlp(core, x, attn, cot, live, vectors, weights, b1, block_rows, tile=512):
    count, width = x.shape
    units = 4 * width
    stack = weights.shape[0]
    base = 3 * width // block_rows if block_rows else 3 * width
    whole = lambda t: (0, 0)
    big = pl.BlockSpec((count, width), whole)
    hbm = pl.BlockSpec(memory_space=pl.ANY)
    return pl.pallas_call(
        functools.partial(mlp_kernel, block_rows, base),
        grid=(units // tile,),
        in_specs=[pl.BlockSpec(memory_space=pltpu.SMEM), big, big, big, pl.BlockSpec((count, 1), whole),
                  pl.BlockSpec(vectors.shape, whole),
                  pl.BlockSpec((width, width), lambda t: (3, 0)),
                  pl.BlockSpec((tile, width), lambda t: (4 * width // tile + t, 0)),
                  pl.BlockSpec((tile, width), lambda t: (8 * width // tile + t, 0)),
                  pl.BlockSpec((1, tile), lambda t: (0, t))],
        out_specs=[big, big, big, pl.BlockSpec((8, width), whole), pl.BlockSpec((1, tile), lambda t: (0, t)), hbm, hbm],
        out_shape=[
            jax.ShapeDtypeStruct((count, width), BF16),
            jax.ShapeDtypeStruct((count, width), F32),
            jax.ShapeDtypeStruct((count, width), BF16),
            jax.ShapeDtypeStruct((8, width), F32),
            jax.ShapeDtypeStruct((1, units), F32),
        ] + grad_shapes(block_rows, stack - 3 * width, width),
        scratch_shapes=[
            pltpu.VMEM((count, width), F32),
            pltpu.VMEM((count, width), BF16),
            pltpu.VMEM((count, width), BF16),
            pltpu.VMEM((count, width), F32),
            pltpu.VMEM((2, 2, tile, width), BF16),
            pltpu.VMEM((width, width), BF16),
            pltpu.SemaphoreType.DMA((3,)),
        ],
        compiler_params=pltpu.CompilerParams(vmem_limit_bytes=60 * 2**20),
        cost_estimate=SHORT,
        name="mlp",
    )(core, x, attn, cot, live, vectors, weights, weights, weights, b1)


def back_kernel(first, q_ref, k_ref, v_ref, da_ref, at_ref, stat_ref, cos_ref, sin_ref,
                qm_ref, km_ref, pos_ref, *rest):
    dq_ref, dk_ref, dv_ref, gb_ref, gf_ref = rest if first else rest[5:]
    count = q_ref.shape[0]
    lane = lax.broadcasted_iota(jnp.int32, (1, 128), 1)
    zero = jnp.zeros((), BF16)
    q = q_ref[...]
    k = k_ref[...]
    v = v_ref[...]
    da = da_ref[...]
    prod = da.astype(F32) * at_ref[...].astype(F32)
    qm = qm_ref[...].astype(F32)
    k_aug = jnp.concatenate([k, km_ref[...]], axis=1)
    v_aug = jnp.concatenate([v, jnp.broadcast_to((lane < 2).astype(BF16), (count, 128))], axis=1)
    tile = 256
    dq = dk = dv = None
    for h in (0, 1):
        mine = (lane // 64) == h
        qh = jnp.where(mine, q, zero)
        kh = jnp.where(mine, k, zero)
        dah = jnp.where(mine, da, zero)
        delta = jnp.sum(jnp.where(mine, prod, 0.0), axis=-1, keepdims=True)
        d1, d2, _ = split3(delta)
        l1, l2, l3 = split3(stat_ref[:, 64 * h:64 * h + 1])
        extra = jnp.where(lane == 8, -l1, jnp.where(lane == 9, -l2, jnp.where(lane == 10, -l3, qm)))
        q_aug = jnp.concatenate([qh, extra.astype(BF16)], axis=1)
        da_aug = jnp.concatenate(
            [dah, jnp.where(lane == 0, -d1, jnp.where(lane == 1, -d2, 0.0)).astype(BF16)], axis=1)
        dks, dvs, dqh = [], [], None
        for i in range(count // tile):
            sl = slice(i * tile, (i + 1) * tile)
            p = jnp.exp(mm(k_aug[sl], q_aug, LAST))
            dp = mm(v_aug[sl], da_aug, LAST)
            ds = (p * dp).astype(BF16)
            dvs.append(mm(p.astype(BF16), dah, PLAIN))
            dks.append(mm(ds, qh, PLAIN))
            part = mm(ds, kh[sl], FIRST)
            dqh = part if dqh is None else dqh + part
        dkh = jnp.concatenate(dks, axis=0)
        dvh = jnp.concatenate(dvs, axis=0)
        dq = dqh if dq is None else dq + dqh
        dk = dkh if dk is None else dk + dkh
        dv = dvh if dv is None else dv + dvh
    dq = dq * 0.125
    c = cos_ref[...]
    s = sin_ref[...]
    turned = dq * swap_halves(q.astype(F32) * 8.0) + dk * swap_halves(k.astype(F32))
    turned = jnp.where(lane % 64 < 32, -turned, turned)
    row = lambda a: jnp.sum(a, axis=0, keepdims=True)
    gf_ref[...] = jnp.concatenate(
        [row(turned * pos_ref[:, 0:1]), row(turned * pos_ref[:, 1:2]), jnp.zeros((6, 128), F32)], axis=0)
    dqp = (dq * c - swap_halves(dq) * s).astype(BF16)
    dkp = (dk * c - swap_halves(dk) * s).astype(BF16)
    dvp = dv.astype(BF16)
    gb_ref[...] = jnp.concatenate(
        [row(dqp.astype(F32)), row(dkp.astype(F32)), row(dvp.astype(F32)), jnp.zeros((5, 128), F32)], axis=0)
    dq_ref[...] = dqp
    dk_ref[...] = dkp
    dv_ref[...] = dvp


def attend_back(start, stop, before, q, k, v, da, attn, stat, cos, sin, qm, km, pos):
    count, width = q.shape
    whole = lambda p: (0, 0)
    col = lambda p: (0, p + start)
    tall = pl.BlockSpec((count, 128), col)
    fixed = pl.BlockSpec((count, 128), whole)
    small = pl.BlockSpec((8, 128), col)
    in_specs = [tall] * 8 + [fixed] * 2 + [pl.BlockSpec((count, 2), whole)]
    operands = [q, k, v, da, attn, stat, cos, sin, qm, km, pos]
    aliases = {}
    if before is not None:
        aliases = {len(operands) + i: i for i in range(5)}
        in_specs += [pl.BlockSpec(memory_space=pl.ANY)] * 5
        operands += list(before)
    return pl.pallas_call(
        functools.partial(back_kernel, before is None),
        grid=(stop - start,),
        in_specs=in_specs,
        out_specs=[tall] * 3 + [small] * 2,
        out_shape=[jax.ShapeDtypeStruct((count, width), BF16)] * 3 + [jax.ShapeDtypeStruct((8, width), F32)] * 2,
        input_output_aliases=aliases,
        compiler_params=pltpu.CompilerParams(vmem_limit_bytes=56 * 2**20),
        cost_estimate=SHORT,
        name="attend_back",
    )(*operands)


def qkv_grad_kernel(block_rows, core_ref, dq_ref, dk_ref, dv_ref, n1_ref, keep_ref, give_ref, stage_s, sem):
    width = n1_ref.shape[1]
    cols = dq_ref.shape[1]
    step = pl.program_id(0)
    n1 = n1_ref[...]
    for j, ref in enumerate((dq_ref, dk_ref, dv_ref)):
        stage_s[step, j] = mm(ref[...], n1, FIRST).astype(BF16)
        send_rows(core_ref[0], block_rows, stage_s.at[step, j], j * width + step * cols, 0, keep_ref, give_ref, sem)

    @pl.when(step == pl.num_programs(0) - 1)
    def _():
        pltpu.make_async_copy(stage_s, stage_s, sem).wait()


def qkv_grad(core, dq, dk, dv, n1, block_rows):
    count, width = n1.shape
    cols = width // 2
    tall = pl.BlockSpec((count, cols), lambda p: (0, p))
    hbm = pl.BlockSpec(memory_space=pl.ANY)
    return pl.pallas_call(
        functools.partial(qkv_grad_kernel, block_rows),
        grid=(2,),
        in_specs=[pl.BlockSpec(memory_space=pltpu.SMEM)] + [tall] * 3 + [pl.BlockSpec((count, width), lambda p: (0, 0))],
        out_specs=[hbm, hbm],
        out_shape=grad_shapes(block_rows, 3 * width, width),
        scratch_shapes=[pltpu.VMEM((2, 3, cols, width), BF16), pltpu.SemaphoreType.DMA],
        compiler_params=pltpu.CompilerParams(vmem_limit_bytes=56 * 2**20),
        cost_estimate=SHORT,
        name="qkv_grad",
    )(core, dq, dk, dv, n1)


def input_kernel(dq_ref, dk_ref, dv_ref, w_ref, x_ref, dm_ref, vec_ref, sums_ref, gb_ref, gf_ref, up_ref, ig_ref, out_ref):
    step = pl.program_id(0)
    d = jnp.concatenate([dq_ref[...], dk_ref[...], dv_ref[...]], axis=1)
    dn = mm(d, w_ref[...], PLAIN)
    unit, inverse = norm_parts(x_ref[...].astype(F32))
    ig_ref[...] = dm_ref[...] + norm_back(unit, inverse, dn, vec_ref[0:1, :])
    row = lambda a: jnp.sum(a, axis=0, keepdims=True)
    sums = jnp.concatenate([row(dn * unit), row(dn)], axis=0)

    @pl.when(step == 0)
    def _():
        width = dn.shape[1]
        half = width // 2
        out_ref[0:2] = sums
        out_ref[2:4] = sums_ref[0:2]
        out_ref[4:7] = gb_ref[0:3]
        out_ref[7:8] = sums_ref[2:3]
        for i in range(4):
            out_ref[8 + i:9 + i] = up_ref[:, i * width:(i + 1) * width]
        out_ref[12:13] = sums_ref[3:4]
        lane = lax.broadcasted_iota(jnp.int32, (width, half), 0)
        slot = lax.broadcasted_iota(jnp.int32, (width, half), 1)
        pick = jnp.where((lane // 64 == slot // 32) & (lane % 32 == slot % 32), 1.0, 0.0)
        both = lax.dot_general(gf_ref[...], pick, PLAIN, precision=lax.Precision.HIGHEST, preferred_element_type=F32)
        out_ref[13:14, :half] = both[0:1]
        out_ref[13:14, half:] = both[1:2]

    @pl.when(step > 0)
    def _():
        out_ref[0:2] += sums


def input_back(dq, dk, dv, weights, x, dm, vectors, sums, grad_bias, grad_freq, bias_up):
    count, width = x.shape
    tile = 256
    part = pl.BlockSpec((tile, width), lambda i: (i, 0))
    whole = lambda i: (0, 0)
    fixed = lambda a: pl.BlockSpec(a.shape, whole)
    return pl.pallas_call(
        input_kernel,
        grid=(count // tile,),
        in_specs=[part] * 3 + [pl.BlockSpec((3 * width, width), whole), part, part]
        + [fixed(a) for a in (vectors, sums, grad_bias, grad_freq, bias_up)],
        out_specs=[part, fixed(vectors)],
        out_shape=[jax.ShapeDtypeStruct((count, width), F32), jax.ShapeDtypeStruct(vectors.shape, F32)],
        compiler_params=pltpu.CompilerParams(vmem_limit_bytes=56 * 2**20),
        cost_estimate=SHORT,
        name="input_back",
    )(dq, dk, dv, weights, x, dm, vectors, sums, grad_bias, grad_freq, bias_up)


def fold_kernel(count, pos_ref, *refs):
    out_ref = refs[-1]
    ways = out_ref.shape[0]
    for k in range(ways):
        total = refs[k][...].astype(F32) + refs[ways + k][...].astype(F32)
        for more in refs[2 * ways:-1]:
            total = total + more[0].astype(F32)
        out_ref[k] = total.astype(BF16)


def fold(pos, keep, got, ways, more=()):
    count, rows, width = keep.shape
    some = count // 2
    quarter = [pl.BlockSpec((some, rows // 2, width // 2), lambda i, pos, k=k: (i, pos[k, 0], pos[k, 1])) for k in ways]
    extra = [pl.BlockSpec((1, some, rows // 2, width // 2), lambda i, pos, at=at: (at, i, 0, 0)) for _, at in more]
    out = pl.BlockSpec((len(ways), some, rows // 2, width // 2), lambda i, pos: (0, i, 0, 0))
    shape = jax.ShapeDtypeStruct((len(ways), count, rows // 2, width // 2), BF16)
    return pl.pallas_call(
        functools.partial(fold_kernel, len(more)),
        grid_spec=pltpu.PrefetchScalarGridSpec(
            num_scalar_prefetch=1, grid=(count // some,), in_specs=quarter * 2 + extra, out_specs=out),
        compiler_params=pltpu.CompilerParams(vmem_limit_bytes=40 * 2**20),
        out_shape=shape,
        cost_estimate=SHORT,
        name="fold",
    )(pos, *([keep] * len(ways)), *([got] * len(ways)), *[a for a, _ in more])


def pack_kernel(owner_ref, *refs):
    early, late, out_ref, total_s = refs[:4], refs[4:8], refs[8], refs[9]
    square = None
    start = 0
    for parts in (early, late):
        total = parts[0][...].astype(F32)
        for part in parts[1:]:
            total = total + part[...].astype(F32)
        total_s[start:start + total.shape[0]] = total.astype(BF16)
        start += total.shape[0]
        more = jnp.sum(total * total).reshape(1, 1)
        square = more if square is None else square + more
    rows = total_s.shape[1]
    lane = lax.broadcasted_iota(jnp.int32, (8, out_ref.shape[2]), 1)
    one, two, three = split3(square)
    extra = jnp.where(lane == 0, one, jnp.where(lane == 1, two, jnp.where(lane == 2, three, 0.0))).astype(BF16)
    for p in range(out_ref.shape[0]):
        out_ref[p, :rows] = total_s[lax.div(owner_ref[p], 2)]
        out_ref[p, rows:] = extra


def pack(owner, early, late):
    blocks = early[0].shape[0] + late[0].shape[0]
    rows, cols = early[0].shape[1:]
    vmem = pl.BlockSpec(memory_space=pltpu.VMEM)
    return pl.pallas_call(
        pack_kernel,
        in_specs=[pl.BlockSpec(memory_space=pltpu.SMEM)] + [vmem] * 8,
        out_specs=vmem,
        out_shape=jax.ShapeDtypeStruct((owner.shape[0], rows + 8, cols), BF16),
        scratch_shapes=[pltpu.VMEM((blocks, rows, cols), BF16)],
        compiler_params=pltpu.CompilerParams(vmem_limit_bytes=32 * 2**20),
        cost_estimate=SHORT,
        name="pack",
    )(owner, *early, *late)


def clip_of(square, vec):
    norm = jnp.sqrt(square + jnp.sum(vec * vec).reshape(1, 1))
    return norm, jnp.minimum(1.0, 1.0 / (norm + 1e-06))


def adam_kernel(own_ref, a_ref, b_ref, as_ref, bs_ref, vt_ref, vw_ref, vm_ref, vv_ref, w_ref, m_ref, v_ref,
                g_out, v_out, w_out, vg_out, vv_out, vw_out, norm_out):
    def squares(ref):
        block = ref[...].astype(F32)
        lane = lax.broadcasted_iota(jnp.int32, block.shape, 4)
        row = lax.broadcasted_iota(jnp.int32, block.shape, 3)
        return jnp.sum(jnp.where((lane < 3) & (row == 0), block, 0.0)).reshape(1, 1)

    norm, clip = clip_of(squares(as_ref) + squares(bs_ref), vt_ref[...])
    own = own_ref[0] > 0
    grad = jnp.where(own, a_ref[:, 0, 0].astype(F32), b_ref[:, 0, 0].astype(F32))
    grad = grad[:, :w_ref.shape[0] // grad.shape[0]].reshape(w_ref.shape) * clip
    second, weight = adam(w_ref[...], m_ref[...], v_ref[...], grad, 0.02, 0.05)
    g_out[...] = grad
    v_out[...] = second
    w_out[...] = weight

    @pl.when((pl.program_id(0) == 0) & (pl.program_id(1) == 0))
    def _():
        vec_grad = vt_ref[...] * clip
        second, weight = adam(vw_ref[...], vm_ref[...], vv_ref[...], vec_grad, 0.2, 0.0)
        vg_out[...] = vec_grad
        vv_out[...] = second
        vw_out[...] = weight
        norm_out[...] = jnp.broadcast_to(norm, norm_out.shape)


def adam_rows(own, mine, other, vec_total, vectors, vec_first, vec_second, weight, first, second):
    rows, width = weight.shape
    deep, tall, wide, piece, cols = mine.shape
    part = pl.BlockSpec((deep, 1, 1, piece, cols), lambda y, x: (0, y, x, 0, 0))
    marks = pl.BlockSpec((deep, tall, wide, 8, 128), lambda y, x: (0, 0, 0, piece // 8 - 1, 0))
    flat = pl.BlockSpec((rows // tall, width // wide), lambda y, x: (y, x))
    vec = pl.BlockSpec(vectors.shape, lambda y, x: (0, 0))
    shape = jax.ShapeDtypeStruct((rows, width), F32)
    small = jax.ShapeDtypeStruct(vectors.shape, F32)
    return pl.pallas_call(
        adam_kernel,
        grid=(tall, wide),
        in_specs=[pl.BlockSpec(memory_space=pltpu.SMEM), part, part, marks, marks] + [vec] * 4 + [flat] * 3,
        out_specs=[flat] * 3 + [vec] * 3 + [pl.BlockSpec((8, 128), lambda y, x: (0, 0))],
        out_shape=[shape] * 3 + [small] * 3 + [jax.ShapeDtypeStruct((8, 128), F32)],
        compiler_params=pltpu.CompilerParams(vmem_limit_bytes=60 * 2**20),
        cost_estimate=SHORT,
        name="adam",
    )(own, mine, other, mine, other, vec_total, vectors, vec_first, vec_second, weight, first, second)


from jax.sharding import PartitionSpec as P

HEADS = 12
STEP = 7


def place_tokens(heights, widths, count):
    sizes = heights * widths
    ends = jnp.cumsum(sizes)
    starts = ends - sizes
    places = jnp.arange(count, dtype=jnp.int32)
    segment = jnp.sum((places[:, None] >= ends[None, :]).astype(jnp.int32), axis=1)
    slots = jnp.arange(heights.shape[0], dtype=jnp.int32)
    picks = (segment[:, None] == slots[None, :]).astype(jnp.int32)
    begin = jnp.sum(picks * starts[None, :], axis=1)
    across = jnp.maximum(jnp.sum(picks * widths[None, :], axis=1), 1)
    offset = places - begin
    live = places < ends[-1]
    return (segment, offset // across, offset % across, live)


def adam(weight, first, second, grad, rate, decay):
    first_new = 0.5 * first + 0.5 * grad
    second_new = 0.5 * second + 0.5 * grad * grad
    correct = 1.0 - 0.5**STEP
    direction = first_new / correct / (jnp.sqrt(second_new / correct) + 1e-08)
    return (second_new, weight - rate * (direction + decay * weight))


def pairwise(bits, total):
    return [(i, i ^ bits) for i in range(total)]


def sum_part(value, devices, step, stop):
    while step < stop:
        value = value + lax.ppermute(value, "dp", pairwise(step, devices))
        step *= 2
    return value


CORES = ("group", "dp")
SWAP = [(0, 1), (1, 0)]


def cross(value, bit0, bit1, devices):
    perm = [(i, i ^ (bit0 if i < devices else bit1)) for i in range(2 * devices)]
    return lax.ppermute(value, CORES, perm)


def along_z(values, devices):
    return [
        lax.ppermute(v, "dp", [(i, (i + 4 * (s + 1)) % devices) for i in range(devices)])
        for s, v in enumerate(values)
    ]


def along_line(value, devices, step, up):
    last = devices // 4
    perm = []
    for z in range(last):
        near = z - 1 if up else z + 1
        far = z - step if up else z + step
        if 0 <= far < last:
            perm += [(4 * near + i, 4 * z + i) for i in range(4)]
    return lax.ppermute(value, "dp", perm)


def gather_pieces(master, inverse, core, me, devices, tables):
    tie = lax.optimization_barrier
    block_rows, width = master.shape
    half = block_rows // 2
    mine = lax.dynamic_slice_in_dim(master, core * half, half, 0).astype(BF16)
    large = mine[:LARGE]
    small = mine[LARGE:]
    z = me // 4
    deep = lax.rem(z - inverse // 4 + 4, 4)
    apart = me ^ inverse
    one = jnp.where(core == 0, apart & 1, (apart >> 1) & 1)
    two = jnp.where(core == 0, (apart >> 1) & 1, apart & 1)
    slots = jnp.stack([
        8 * two + 4 * one + deep,
        4 * deep + 2 * two + one,
        8 * one + 4 * two + deep,
        4 * deep + 2 * one + two,
    ]).astype(jnp.int32)
    up = along_z([large] * 3, devices)
    small = jnp.stack([small, cross(small, 1, 2, devices)])
    small = jnp.concatenate([small, cross(small, 2, 1, devices)])
    large = jnp.stack([large] + up)
    large, small, tables, slots = tie((large, small, tables, slots))
    first = cross(large, 1, 2, devices)
    ups = [along_line(small, devices, 1, True)]
    downs = [along_line(small, devices, 1, False)]
    first, ups[0], downs[0] = tie((first, ups[0], downs[0]))
    first = jnp.concatenate([large, first])
    second = cross(first, 2, 1, devices)
    for step in (2, 3):
        ups.append(along_line(ups[-1], devices, step, True))
        downs.append(along_line(downs[-1], devices, step, False))
    small = jnp.concatenate([small] + [jnp.where(z >= s, ups[s - 1], downs[3 - s]) for s in (1, 2, 3)])
    other = [lax.ppermute(a, "group", SWAP) for a in (first, second, small)]
    return (first, second, small, *other), slots, tables


def quarters(core, me):
    x, y = me & 1, (me >> 1) & 1
    one = jnp.where(core == 0, x, y)
    two = jnp.where(core == 0, y, x)
    pairs = [(1 - one, 1 - two), (1 - one, two), (one, 1 - two), (one, two)]
    return jnp.stack([
        jnp.stack([jnp.where(core == 0, b, a), jnp.where(core == 0, a, b)]) for a, b in pairs
    ]).astype(jnp.int32)


def sum_z(low, me, devices):
    count, rows, cols = low.shape
    z = me // 4
    low = low.reshape(count, 4, rows // 4, cols)
    pick = lambda at: lax.dynamic_index_in_dim(low, at, 1, keepdims=False)
    return (pick(z), *along_z([pick(lax.rem(z + s, 4)) for s in (1, 2, 3)], devices))


def reduce_plain(local_mat, owner_block, devices):
    rows, width = local_mat.shape
    block_rows = rows // devices
    term = local_mat.reshape(devices, block_rows, width)[owner_block].reshape(rows, width)
    share = lax.psum_scatter(term.astype(F32), "dp", scatter_dimension=0, tiled=True)
    return lax.psum(share.astype(BF16), "group").astype(F32)


def local(
    tokens,
    cotangent,
    grid_h,
    grid_w,
    owner_block,
    master,
    first_mom,
    second_mom,
    vectors,
    vec_first,
    vec_second,
):
    devices = lax.axis_size("dp")
    core = lax.axis_index("group")
    me = lax.axis_index("dp")
    count = tokens.shape[1]
    width = tokens.shape[2]
    heads = HEADS
    head_dim = width // heads
    half = head_dim // 2
    block_rows = master.shape[0]
    stack = devices * block_rows
    quick = devices == 16 and block_rows == 2 * (LARGE + SMALL) and width % 256 == 0
    inverse = jnp.argsort(owner_block)
    segment, rows_pos, cols_pos, live = place_tokens(grid_h[0], grid_w[0], count)
    freqs = vectors[13]

    def spread(part):
        return jnp.broadcast_to(part.reshape(heads, 1, half), (heads, 2, half)).reshape(1, width)

    angle = rows_pos.astype(F32)[:, None] * spread(freqs[: width // 2]) + cols_pos.astype(F32)[
        :, None
    ] * spread(freqs[width // 2 :])
    lower = (jnp.arange(width) % head_dim < half)[None]
    cosine = jnp.cos(angle)
    sine = jnp.sin(angle)
    sine = jnp.where(lower, -sine, sine)
    ids = jnp.arange(128)[None]
    match = segment[:, None] == ids
    key_mask = jnp.where(match | ((ids >= 8) & (ids < 11)), 1.0, 0.0).astype(BF16)
    query_mask = jnp.where((ids < 8) & ~match, MASKED, 0.0).astype(BF16)
    places = jnp.stack([rows_pos, cols_pos], axis=1).astype(F32)
    alive = live[:, None].astype(F32)
    bias_qkv = vectors[4:7].reshape(1, 3 * width)
    bias_one = vectors[8:12].reshape(1, 4 * width)
    tables = (cosine, sine, key_mask, query_mask, places, alive, bias_qkv, bias_one)
    if quick:
        weights, slots, tables = gather_pieces(master, inverse, core, me, devices, tables)
    else:
        low = lax.all_gather(master.astype(BF16), "dp", axis=0, tiled=True)
        weights = low.reshape(devices, block_rows, width)[inverse].reshape(stack, width)
        slots = jnp.zeros((4, devices), jnp.int32)
    cosine, sine, key_mask, query_mask, places, alive, bias_qkv, bias_one = tables
    here = core.reshape(1).astype(jnp.int32)
    x = tokens[0]
    first_in, query, key, value, attn, stat, *placed = attend(
        here, slots, x, vectors[0:1], vectors[1:2], bias_qkv,
        cosine, sine, query_mask, key_mask, weights, stack,
    )
    if quick:
        weights = placed[0]
    whole_rows = block_rows if quick else 0
    block_out, grad_middle, grad_attn, sums, bias_up, keep_mlp, give_mlp = mlp(
        here, x, attn, cotangent[0], alive, vectors, weights, bias_one, whole_rows
    )
    pairs = width // 128
    tie = lax.optimization_barrier
    if quick:
        pos = quarters(core, me)
        got = lax.ppermute(give_mlp, "group", SWAP)
    back = None
    cuts = (0, 1, pairs - 1, pairs)
    for start, stop in zip(cuts[:-1], cuts[1:]):
        back = attend_back(
            start, stop, back, query, key, value, grad_attn, attn, stat, cosine, sine, query_mask, key_mask, places
        )
        if quick and start == 0:
            send, back = tie((fold(pos, keep_mlp, got, (0, 1)), back))
            came = cross(send, 1, 2, devices)
        if quick and start == 1:
            send, back = tie((fold(pos, keep_mlp, got, (2,), ((came, 0),)), back))
            again = cross(send, 2, 1, devices)
    grad_q, grad_k, grad_v, grad_bias, grad_freq = back
    keep_qkv, give_qkv = qkv_grad(here, grad_q, grad_k, grad_v, first_in, whole_rows)
    if quick:
        again, give_qkv = tie((again, give_qkv))
        low, grad_v, give_qkv = tie((fold(pos, keep_mlp, got, (3,), ((came, 1), (again, 0)))[0], grad_v, give_qkv))
        late = sum_z(low, me, devices)
    input_grad, local_vec = input_back(
        grad_q, grad_k, grad_v, weights, x, grad_middle, vectors, sums, grad_bias, grad_freq, bias_up
    )
    if quick:
        got_qkv = lax.ppermute(give_qkv, "group", SWAP)
        got_qkv, local_vec, late = tie((got_qkv, local_vec, late))
        vec_total = sum_part(local_vec + lax.ppermute(local_vec, "group", SWAP), devices, 4, devices)
        came = cross(fold(pos, keep_qkv, got_qkv, (0, 1)), 1, 2, devices)
        came, vec_total = tie((came, vec_total))
        again = cross(fold(pos, keep_qkv, got_qkv, (2,), ((came, 0),)), 2, 1, devices)
        early = sum_z(fold(pos, keep_qkv, got_qkv, (3,), ((came, 1), (again, 0)))[0], me, devices)
        early, vec_total = tie((early, sum_part(vec_total, devices, 1, 4)))
        load = pack(owner_block, early, late)
        mine = lax.all_to_all(load, "dp", 0, 0, tiled=True)
        other = lax.ppermute(mine, "group", SWAP)
        shape = (devices // 4, 2, 2, *load.shape[1:])
        own = (owner_block[me] % 2 == core).astype(jnp.int32).reshape(1)
        mat_grad, mat_second, mat_weight, vec_grad, vec_second_new, vec_weight, norm = adam_rows(
            own, mine.reshape(shape), other.reshape(shape), vec_total, vectors, vec_first, vec_second,
            master, first_mom, second_mom,
        )
        grad_norm = norm[0, 0]
    else:
        vec_total = lax.psum(local_vec, CORES)
        share = reduce_plain(jnp.concatenate([keep_qkv, keep_mlp]), owner_block, devices)
        square = lax.psum(jnp.sum(share * share), "dp")
        grad_norm = jnp.sqrt(square + jnp.sum(vec_total * vec_total))
        clip = jnp.minimum(1.0, 1.0 / (grad_norm + 1e-06))
        mat_grad = share * clip
        mat_second, mat_weight = adam(master, first_mom, second_mom, mat_grad, 0.02, 0.05)
        vec_grad = vec_total * clip
        vec_second_new, vec_weight = adam(vectors, vec_first, vec_second, vec_grad, 0.2, 0.0)
    return (
        block_out[None],
        input_grad[None],
        mat_grad,
        mat_second,
        mat_weight,
        vec_grad,
        vec_second_new,
        vec_weight,
        grad_norm,
    )


def solution(mesh):
    return jax.shard_map(
        local,
        mesh=mesh,
        in_specs=(
            P("group", "dp", None),
            P("group", "dp", None),
            P("group", "dp"),
            P("group", "dp"),
            P(),
            P("dp", None),
            P("dp", None),
            P("dp", None),
            P(),
            P(),
            P(),
        ),
        out_specs=(
            P("group", "dp", None),
            P("group", "dp", None),
            P("dp", None),
            P("dp", None),
            P("dp", None),
            P(),
            P(),
            P(),
            P(),
        ),
        check_vma=False,
    )
```

```python
import functools
import jax
import jax.numpy as jnp
from jax import lax
from jax.experimental import pallas as pl
from jax.experimental.pallas import tpu as pltpu

F32 = jnp.float32
BF16 = jnp.bfloat16
LAST = (((1,), (1,)), ((), ()))
FIRST = (((0,), (0,)), ((), ()))
PLAIN = (((1,), (0,)), ((), ()))
MASKED = -1e9
SHORT = pl.CostEstimate(flops=1000, bytes_accessed=1000, transcendentals=0)


def mm(left, right, dims):
    return lax.dot_general(left, right, dims, preferred_element_type=F32)


def norm_parts(value):
    centre = value - jnp.mean(value, axis=-1, keepdims=True)
    spread = jnp.mean(centre * centre, axis=-1, keepdims=True)
    inverse = lax.rsqrt(spread + 1e-6)
    return centre * inverse, inverse


def norm_back(unit, inverse, grad, gain):
    scaled = grad * gain
    first = jnp.mean(scaled, axis=-1, keepdims=True)
    second = jnp.mean(scaled * unit, axis=-1, keepdims=True)
    return inverse * (scaled - first - unit * second)


def swap_halves(value):
    lane = lax.broadcasted_iota(jnp.int32, value.shape, 1)
    return jnp.where(
        lane % 64 < 32, pltpu.roll(value, 96, 1), pltpu.roll(value, 32, 1)
    )


def split3(value):
    one = value.astype(BF16).astype(F32)
    rest = value - one
    two = rest.astype(BF16).astype(F32)
    return one, two, rest - two


LARGE = 208
SMALL = 80


def place_pieces(core, slot_ref, mine, other, block, side, dst, sem):
    for which, (first, second, small) in enumerate((mine, other)):
        @pl.when((core == side) if which == 0 else (core != side))
        def _():
            large_slot = slot_ref[2 * which, block]
            small_slot = slot_ref[2 * which + 1, block]

            @pl.when(large_slot < 8)
            def _():
                pltpu.make_async_copy(first.at[large_slot], dst(0, LARGE), sem).start()

            @pl.when(large_slot >= 8)
            def _():
                pltpu.make_async_copy(second.at[large_slot - 8], dst(0, LARGE), sem).start()

            pltpu.make_async_copy(small.at[small_slot], dst(LARGE, SMALL), sem).start()


def attend_kernel(blocks, core_ref, slot_ref, x_ref, g_ref, b_ref, bq_ref, bk_ref, bv_ref,
                  cos_ref, sin_ref, qm_ref, km_ref, *rest):
    if blocks:
        mine, other = rest[0:3], rest[3:6]
        n1_ref, q_ref, k_ref, v_ref, attn_ref, stat_ref, w_ref, n1_s, w_s, near, far, back = rest[6:]
    else:
        w_ref, n1_ref, q_ref, k_ref, v_ref, attn_ref, stat_ref, n1_s, w_s, near = rest
    count, width = x_ref.shape
    step = pl.program_id(0)

    @pl.when(step == 0)
    def _():
        if blocks:
            core = core_ref[0]
            rows = w_ref.shape[0] // blocks

            def start(block, sem):
                for side in (0, 1):
                    def dst(offset, size):
                        base = block * rows + side * (rows // 2) + offset
                        return w_s.at[pl.ds(pl.multiple_of(base, 16), size)]
                    place_pieces(core, slot_ref, mine, other, block, side, dst, sem)

            def near_block(block, carry):
                start(block, near)
                return carry

            def far_block(block, carry):
                start(block, far)
                return carry

            lax.fori_loop(0, 3 * width // rows, near_block, 0)
            lax.fori_loop(3 * width // rows, blocks, far_block, 0)
        else:
            pltpu.make_async_copy(w_ref.at[pl.ds(0, 3 * width)], w_s, near).start()
        unit, _ = norm_parts(x_ref[...].astype(F32))
        n1 = (unit * g_ref[...] + b_ref[...]).astype(BF16)
        n1_s[...] = n1
        n1_ref[...] = n1
        head = w_s.at[pl.ds(0, 3 * width)]
        pltpu.make_async_copy(head, head, near).wait()

    if blocks:
        @pl.when(step == 1)
        def _():
            tail = w_s.at[pl.ds(3 * width, w_s.shape[0] - 3 * width)]
            pltpu.make_async_copy(tail, tail, far).wait()
            pltpu.make_async_copy(w_s, w_ref, back).start()

    def third(j):
        return w_s[pl.ds(pl.multiple_of(j * width + step * 128, 128), 128), :]

    w = jnp.concatenate([third(0), third(1), third(2)], axis=0)
    qkv = mm(n1_s[...], w, LAST)
    q = qkv[:, :128] + bq_ref[...]
    k = qkv[:, 128:256] + bk_ref[...]
    v = (qkv[:, 256:] + bv_ref[...]).astype(BF16)
    c = cos_ref[...]
    s = sin_ref[...]
    qr = ((q * c + swap_halves(q) * s).astype(BF16).astype(F32) * 0.125).astype(BF16)
    kr = (k * c + swap_halves(k) * s).astype(BF16)
    q_ref[...] = qr
    k_ref[...] = kr
    v_ref[...] = v
    lane = lax.broadcasted_iota(jnp.int32, (1, 128), 1)
    k_aug = jnp.concatenate([kr, km_ref[...]], axis=1)
    v_aug = jnp.concatenate([v, jnp.ones((count, 128), BF16)], axis=1)
    zero = jnp.zeros((), BF16)
    tile = 256
    for i in range(count // tile):
        rows = pl.ds(i * tile, tile)
        out = None
        stats = []
        for h in (0, 1):
            mine_lanes = (lane // 64) == h
            qa = jnp.concatenate(
                [jnp.where(mine_lanes, qr[i * tile:(i + 1) * tile], zero), qm_ref[rows, :]], axis=1)
            scores = mm(qa, k_aug, LAST)
            top = jnp.max(scores, axis=-1, keepdims=True)
            e = jnp.exp(scores - top).astype(BF16)
            o = mm(e, v_aug, PLAIN)
            total = o[:, 128:]
            o = o[:, :128] / total
            out = o if out is None else jnp.where(lane < 64, out, o)
            stats.append(top + jnp.log(total[:, :1]))
        attn_ref[rows, :] = out.astype(BF16)
        stat_ref[rows, :] = jnp.where(lane < 64, stats[0], stats[1])

    if blocks:
        @pl.when(step == pl.num_programs(0) - 1)
        def _():
            pltpu.make_async_copy(w_s, w_ref, back).wait()


def attend(core, slots, x, gain, shift, bqkv, cos, sin, qm, km, weights, stack):
    count, width = x.shape
    pairs = width // 128
    pieces = isinstance(weights, tuple)
    blocks = slots.shape[1] if pieces else 0
    whole = lambda p: (0, 0)
    col = lambda p: (0, p)
    smem = pl.BlockSpec(memory_space=pltpu.SMEM)
    hbm = pl.BlockSpec(memory_space=pl.ANY)
    given = weights if pieces else (weights,)
    specs = [smem, smem] + [
        pl.BlockSpec((count, width), whole),
        pl.BlockSpec((1, width), whole),
        pl.BlockSpec((1, width), whole),
        pl.BlockSpec((1, 128), col),
        pl.BlockSpec((1, 128), lambda p: (0, p + pairs)),
        pl.BlockSpec((1, 128), lambda p: (0, p + 2 * pairs)),
        pl.BlockSpec((count, 128), col),
        pl.BlockSpec((count, 128), col),
        pl.BlockSpec((count, 128), whole),
        pl.BlockSpec((count, 128), whole),
    ] + [hbm] * len(given)
    outs = [pl.BlockSpec((count, width), whole)] + [pl.BlockSpec((count, 128), col)] * 5
    shape = lambda d: jax.ShapeDtypeStruct((count, width), d)
    shapes = [shape(BF16)] * 5 + [shape(F32)]
    scratch = [pltpu.VMEM((count, width), BF16), pltpu.VMEM((stack if pieces else 3 * width, width), BF16), pltpu.SemaphoreType.DMA]
    if pieces:
        outs.append(hbm)
        shapes.append(jax.ShapeDtypeStruct((stack, width), BF16))
        scratch += [pltpu.SemaphoreType.DMA] * 2
    return pl.pallas_call(
        functools.partial(attend_kernel, blocks),
        grid=(pairs,),
        in_specs=specs,
        out_specs=outs,
        out_shape=shapes,
        scratch_shapes=scratch,
        compiler_params=pltpu.CompilerParams(vmem_limit_bytes=56 * 2**20),
        cost_estimate=SHORT,
        name="attend",
    )(core, slots, x, gain, shift, bqkv, bqkv, bqkv, cos, sin, qm, km, *given)


def gelu_both(x):
    cdf = 0.5 + 0.5 * lax.erf(x * 0.7071067811865476)
    return x * cdf, cdf + x * jnp.exp(x * x * -0.5) * 0.3989422804014327


def send_rows(core, block_rows, stage, row, base, keep_ref, give_ref, sem):
    if not block_rows:
        rows = stage.shape[0]
        pltpu.make_async_copy(
            stage, keep_ref.at[pl.ds(pl.multiple_of(row - base, 64), rows)], sem
        ).start()
        return

    def one(index, carry):
        at = row + 64 * index
        block = lax.div(at, block_rows)
        inner = pl.ds(pl.multiple_of(at - block * block_rows, 64), 64)
        slot = lax.div(block, 2) - base // 2
        source = stage.at[pl.ds(pl.multiple_of(64 * index, 64), 64)]
        own = lax.rem(block, 2) == core

        @pl.when(own)
        def _():
            pltpu.make_async_copy(source, keep_ref.at[slot, inner], sem).start()

        @pl.when(jnp.logical_not(own))
        def _():
            pltpu.make_async_copy(source, give_ref.at[slot, inner], sem).start()

        return carry

    lax.fori_loop(0, stage.shape[0] // 64, one, 0)


def mlp_kernel(block_rows, base, core_ref, x_ref, at_ref, cot_ref, live_ref, vec_ref, wo_ref, w1_ref, w2_ref, b1_ref,
               out_ref, dm_ref, da_ref, sums_ref, gb_ref, keep_ref, give_ref,
               middle_s, n2_s, dz_s, acc_s, stage_s, proj_s, sems):
    step = pl.program_id(0)
    last = pl.num_programs(0) - 1
    count, width = x_ref.shape
    core = core_ref[0]
    tile = w1_ref.shape[0]

    @pl.when(step == 0)
    def _():
        middle = x_ref[...].astype(F32) + mm(at_ref[...], wo_ref[...], LAST) + vec_ref[7:8, :]
        middle_s[...] = middle
        unit, _ = norm_parts(middle)
        n2_s[...] = (unit * vec_ref[2:3, :] + vec_ref[3:4, :]).astype(BF16)
        dz_s[...] = jnp.where(live_ref[...] > 0.5, cot_ref[...].astype(F32), 0.0).astype(BF16)
        acc_s[...] = jnp.zeros_like(acc_s)
        dm_ref[...] = jnp.zeros_like(dm_ref)

    slot = lax.rem(step, 2)

    @pl.when(step >= 2)
    def _():
        pltpu.make_async_copy(stage_s.at[slot], stage_s.at[slot], sems.at[slot]).wait()

    n2 = n2_s[...]
    dz = dz_s[...]
    w1 = w1_ref[...]
    w2 = w2_ref[...]
    pre = mm(w1, n2, LAST) + b1_ref[...].reshape(tile, 1)
    back = mm(w2, dz, LAST)
    act, slope = gelu_both(pre)
    hidden = act.astype(BF16)
    stage_s[slot, 1] = mm(hidden, dz, PLAIN).astype(BF16)
    dpre = (back * slope).astype(BF16)
    gb_ref[...] = jnp.sum(dpre.astype(F32), axis=1, keepdims=True).reshape(1, tile)
    stage_s[slot, 0] = mm(dpre, n2, PLAIN).astype(BF16)
    acc_s[...] += mm(hidden, w2, FIRST)
    dm_ref[...] += mm(dpre, w1, FIRST)
    for j in (0, 1):
        send_rows(core, block_rows, stage_s.at[slot, j], (4 + 4 * j) * width + step * tile,
                  base, keep_ref, give_ref, sems.at[slot])

    @pl.when(step == last)
    def _():
        middle = middle_s[...]
        out_ref[...] = (middle + acc_s[...] + vec_ref[12:13, :]).astype(BF16)
        unit, inverse = norm_parts(middle)
        dn = dm_ref[...]
        dy = dz_s[...].astype(F32)
        dm = dy + norm_back(unit, inverse, dn, vec_ref[2:3, :])
        dm_ref[...] = dm
        low = dm.astype(BF16)
        row = lambda a: jnp.sum(a, axis=0, keepdims=True)
        sums_ref[...] = jnp.concatenate(
            [row(dn * unit), row(dn), row(low.astype(F32)), row(dy), jnp.zeros((4, width), F32)], axis=0)
        proj_s[...] = mm(low, at_ref[...], FIRST).astype(BF16)
        send_rows(core, block_rows, proj_s, 3 * width, base, keep_ref, give_ref, sems.at[2])
        da_ref[...] = mm(low, wo_ref[...], PLAIN).astype(BF16)
        pltpu.make_async_copy(stage_s.at[slot], stage_s.at[slot], sems.at[slot]).wait()
        pltpu.make_async_copy(stage_s.at[1 - slot], stage_s.at[1 - slot], sems.at[1 - slot]).wait()
        pltpu.make_async_copy(proj_s, proj_s, sems.at[2]).wait()


def grad_shapes(block_rows, rows, width):
    if block_rows:
        half = jax.ShapeDtypeStruct((rows // block_rows // 2, block_rows, width), BF16)
        return [half, half]
    return [jax.ShapeDtypeStruct((rows, width), BF16), jax.ShapeDtypeStruct((16, width), BF16)]


def mlp(core, x, attn, cot, live, vectors, weights, b1, block_rows, tile=512):
    count, width = x.shape
    units = 4 * width
    stack = weights.shape[0]
    base = 3 * width // block_rows if block_rows else 3 * width
    whole = lambda t: (0, 0)
    big = pl.BlockSpec((count, width), whole)
    hbm = pl.BlockSpec(memory_space=pl.ANY)
    return pl.pallas_call(
        functools.partial(mlp_kernel, block_rows, base),
        grid=(units // tile,),
        in_specs=[pl.BlockSpec(memory_space=pltpu.SMEM), big, big, big, pl.BlockSpec((count, 1), whole),
                  pl.BlockSpec(vectors.shape, whole),
                  pl.BlockSpec((width, width), lambda t: (3, 0)),
                  pl.BlockSpec((tile, width), lambda t: (4 * width // tile + t, 0)),
                  pl.BlockSpec((tile, width), lambda t: (8 * width // tile + t, 0)),
                  pl.BlockSpec((1, tile), lambda t: (0, t))],
        out_specs=[big, big, big, pl.BlockSpec((8, width), whole), pl.BlockSpec((1, tile), lambda t: (0, t)), hbm, hbm],
        out_shape=[
            jax.ShapeDtypeStruct((count, width), BF16),
            jax.ShapeDtypeStruct((count, width), F32),
            jax.ShapeDtypeStruct((count, width), BF16),
            jax.ShapeDtypeStruct((8, width), F32),
            jax.ShapeDtypeStruct((1, units), F32),
        ] + grad_shapes(block_rows, stack - 3 * width, width),
        scratch_shapes=[
            pltpu.VMEM((count, width), F32),
            pltpu.VMEM((count, width), BF16),
            pltpu.VMEM((count, width), BF16),
            pltpu.VMEM((count, width), F32),
            pltpu.VMEM((2, 2, tile, width), BF16),
            pltpu.VMEM((width, width), BF16),
            pltpu.SemaphoreType.DMA((3,)),
        ],
        compiler_params=pltpu.CompilerParams(vmem_limit_bytes=60 * 2**20),
        cost_estimate=SHORT,
        name="mlp",
    )(core, x, attn, cot, live, vectors, weights, weights, weights, b1)


def back_kernel(first, q_ref, k_ref, v_ref, da_ref, at_ref, stat_ref, cos_ref, sin_ref,
                qm_ref, km_ref, pos_ref, *rest):
    dq_ref, dk_ref, dv_ref, gb_ref, gf_ref = rest if first else rest[5:]
    count = q_ref.shape[0]
    lane = lax.broadcasted_iota(jnp.int32, (1, 128), 1)
    zero = jnp.zeros((), BF16)
    q = q_ref[...]
    k = k_ref[...]
    v = v_ref[...]
    da = da_ref[...]
    prod = da.astype(F32) * at_ref[...].astype(F32)
    qm = qm_ref[...].astype(F32)
    k_aug = jnp.concatenate([k, km_ref[...]], axis=1)
    v_aug = jnp.concatenate([v, jnp.broadcast_to((lane < 2).astype(BF16), (count, 128))], axis=1)
    tile = 256
    dq = dk = dv = None
    for h in (0, 1):
        mine = (lane // 64) == h
        qh = jnp.where(mine, q, zero)
        kh = jnp.where(mine, k, zero)
        dah = jnp.where(mine, da, zero)
        delta = jnp.sum(jnp.where(mine, prod, 0.0), axis=-1, keepdims=True)
        d1, d2, _ = split3(delta)
        l1, l2, l3 = split3(stat_ref[:, 64 * h:64 * h + 1])
        extra = jnp.where(lane == 8, -l1, jnp.where(lane == 9, -l2, jnp.where(lane == 10, -l3, qm)))
        q_aug = jnp.concatenate([qh, extra.astype(BF16)], axis=1)
        da_aug = jnp.concatenate(
            [dah, jnp.where(lane == 0, -d1, jnp.where(lane == 1, -d2, 0.0)).astype(BF16)], axis=1)
        dks, dvs, dqh = [], [], None
        for i in range(count // tile):
            sl = slice(i * tile, (i + 1) * tile)
            p = jnp.exp(mm(k_aug[sl], q_aug, LAST))
            dp = mm(v_aug[sl], da_aug, LAST)
            ds = (p * dp).astype(BF16)
            dvs.append(mm(p.astype(BF16), dah, PLAIN))
            dks.append(mm(ds, qh, PLAIN))
            part = mm(ds, kh[sl], FIRST)
            dqh = part if dqh is None else dqh + part
        dkh = jnp.concatenate(dks, axis=0)
        dvh = jnp.concatenate(dvs, axis=0)
        dq = dqh if dq is None else dq + dqh
        dk = dkh if dk is None else dk + dkh
        dv = dvh if dv is None else dv + dvh
    dq = dq * 0.125
    c = cos_ref[...]
    s = sin_ref[...]
    turned = dq * swap_halves(q.astype(F32) * 8.0) + dk * swap_halves(k.astype(F32))
    turned = jnp.where(lane % 64 < 32, -turned, turned)
    row = lambda a: jnp.sum(a, axis=0, keepdims=True)
    gf_ref[...] = jnp.concatenate(
        [row(turned * pos_ref[:, 0:1]), row(turned * pos_ref[:, 1:2]), jnp.zeros((6, 128), F32)], axis=0)
    dqp = (dq * c - swap_halves(dq) * s).astype(BF16)
    dkp = (dk * c - swap_halves(dk) * s).astype(BF16)
    dvp = dv.astype(BF16)
    gb_ref[...] = jnp.concatenate(
        [row(dqp.astype(F32)), row(dkp.astype(F32)), row(dvp.astype(F32)), jnp.zeros((5, 128), F32)], axis=0)
    dq_ref[...] = dqp
    dk_ref[...] = dkp
    dv_ref[...] = dvp


def attend_back(start, stop, before, q, k, v, da, attn, stat, cos, sin, qm, km, pos):
    count, width = q.shape
    whole = lambda p: (0, 0)
    col = lambda p: (0, p + start)
    tall = pl.BlockSpec((count, 128), col)
    fixed = pl.BlockSpec((count, 128), whole)
    small = pl.BlockSpec((8, 128), col)
    in_specs = [tall] * 8 + [fixed] * 2 + [pl.BlockSpec((count, 2), whole)]
    operands = [q, k, v, da, attn, stat, cos, sin, qm, km, pos]
    aliases = {}
    if before is not None:
        aliases = {len(operands) + i: i for i in range(5)}
        in_specs += [pl.BlockSpec(memory_space=pl.ANY)] * 5
        operands += list(before)
    return pl.pallas_call(
        functools.partial(back_kernel, before is None),
        grid=(stop - start,),
        in_specs=in_specs,
        out_specs=[tall] * 3 + [small] * 2,
        out_shape=[jax.ShapeDtypeStruct((count, width), BF16)] * 3 + [jax.ShapeDtypeStruct((8, width), F32)] * 2,
        input_output_aliases=aliases,
        compiler_params=pltpu.CompilerParams(vmem_limit_bytes=56 * 2**20),
        cost_estimate=SHORT,
        name="attend_back",
    )(*operands)


def qkv_grad_kernel(block_rows, core_ref, dq_ref, dk_ref, dv_ref, n1_ref, keep_ref, give_ref, stage_s, sem):
    width = n1_ref.shape[1]
    cols = dq_ref.shape[1]
    step = pl.program_id(0)
    n1 = n1_ref[...]
    for j, ref in enumerate((dq_ref, dk_ref, dv_ref)):
        stage_s[step, j] = mm(ref[...], n1, FIRST).astype(BF16)
        send_rows(core_ref[0], block_rows, stage_s.at[step, j], j * width + step * cols, 0, keep_ref, give_ref, sem)

    @pl.when(step == pl.num_programs(0) - 1)
    def _():
        pltpu.make_async_copy(stage_s, stage_s, sem).wait()


def qkv_grad(core, dq, dk, dv, n1, block_rows):
    count, width = n1.shape
    cols = width // 2
    tall = pl.BlockSpec((count, cols), lambda p: (0, p))
    hbm = pl.BlockSpec(memory_space=pl.ANY)
    return pl.pallas_call(
        functools.partial(qkv_grad_kernel, block_rows),
        grid=(2,),
        in_specs=[pl.BlockSpec(memory_space=pltpu.SMEM)] + [tall] * 3 + [pl.BlockSpec((count, width), lambda p: (0, 0))],
        out_specs=[hbm, hbm],
        out_shape=grad_shapes(block_rows, 3 * width, width),
        scratch_shapes=[pltpu.VMEM((2, 3, cols, width), BF16), pltpu.SemaphoreType.DMA],
        compiler_params=pltpu.CompilerParams(vmem_limit_bytes=56 * 2**20),
        cost_estimate=SHORT,
        name="qkv_grad",
    )(core, dq, dk, dv, n1)


def input_kernel(dq_ref, dk_ref, dv_ref, w_ref, x_ref, dm_ref, vec_ref, sums_ref, gb_ref, gf_ref, up_ref, ig_ref, out_ref):
    step = pl.program_id(0)
    d = jnp.concatenate([dq_ref[...], dk_ref[...], dv_ref[...]], axis=1)
    dn = mm(d, w_ref[...], PLAIN)
    unit, inverse = norm_parts(x_ref[...].astype(F32))
    ig_ref[...] = dm_ref[...] + norm_back(unit, inverse, dn, vec_ref[0:1, :])
    row = lambda a: jnp.sum(a, axis=0, keepdims=True)
    sums = jnp.concatenate([row(dn * unit), row(dn)], axis=0)

    @pl.when(step == 0)
    def _():
        width = dn.shape[1]
        half = width // 2
        out_ref[0:2] = sums
        out_ref[2:4] = sums_ref[0:2]
        out_ref[4:7] = gb_ref[0:3]
        out_ref[7:8] = sums_ref[2:3]
        for i in range(4):
            out_ref[8 + i:9 + i] = up_ref[:, i * width:(i + 1) * width]
        out_ref[12:13] = sums_ref[3:4]
        lane = lax.broadcasted_iota(jnp.int32, (width, half), 0)
        slot = lax.broadcasted_iota(jnp.int32, (width, half), 1)
        pick = jnp.where((lane // 64 == slot // 32) & (lane % 32 == slot % 32), 1.0, 0.0)
        both = lax.dot_general(gf_ref[...], pick, PLAIN, precision=lax.Precision.HIGHEST, preferred_element_type=F32)
        out_ref[13:14, :half] = both[0:1]
        out_ref[13:14, half:] = both[1:2]

    @pl.when(step > 0)
    def _():
        out_ref[0:2] += sums


def input_back(dq, dk, dv, weights, x, dm, vectors, sums, grad_bias, grad_freq, bias_up):
    count, width = x.shape
    tile = 256
    part = pl.BlockSpec((tile, width), lambda i: (i, 0))
    whole = lambda i: (0, 0)
    fixed = lambda a: pl.BlockSpec(a.shape, whole)
    return pl.pallas_call(
        input_kernel,
        grid=(count // tile,),
        in_specs=[part] * 3 + [pl.BlockSpec((3 * width, width), whole), part, part]
        + [fixed(a) for a in (vectors, sums, grad_bias, grad_freq, bias_up)],
        out_specs=[part, fixed(vectors)],
        out_shape=[jax.ShapeDtypeStruct((count, width), F32), jax.ShapeDtypeStruct(vectors.shape, F32)],
        compiler_params=pltpu.CompilerParams(vmem_limit_bytes=56 * 2**20),
        cost_estimate=SHORT,
        name="input_back",
    )(dq, dk, dv, weights, x, dm, vectors, sums, grad_bias, grad_freq, bias_up)


def fold_kernel(count, pos_ref, *refs):
    out_ref = refs[-1]
    ways = out_ref.shape[0]
    for k in range(ways):
        total = refs[k][...].astype(F32) + refs[ways + k][...].astype(F32)
        for more in refs[2 * ways:-1]:
            total = total + more[0].astype(F32)
        out_ref[k] = total.astype(BF16)


def fold(pos, keep, got, ways, more=()):
    count, rows, width = keep.shape
    some = count // 2
    quarter = [pl.BlockSpec((some, rows // 2, width // 2), lambda i, pos, k=k: (i, pos[k, 0], pos[k, 1])) for k in ways]
    extra = [pl.BlockSpec((1, some, rows // 2, width // 2), lambda i, pos, at=at: (at, i, 0, 0)) for _, at in more]
    out = pl.BlockSpec((len(ways), some, rows // 2, width // 2), lambda i, pos: (0, i, 0, 0))
    shape = jax.ShapeDtypeStruct((len(ways), count, rows // 2, width // 2), BF16)
    return pl.pallas_call(
        functools.partial(fold_kernel, len(more)),
        grid_spec=pltpu.PrefetchScalarGridSpec(
            num_scalar_prefetch=1, grid=(count // some,), in_specs=quarter * 2 + extra, out_specs=out),
        compiler_params=pltpu.CompilerParams(vmem_limit_bytes=40 * 2**20),
        out_shape=shape,
        cost_estimate=SHORT,
        name="fold",
    )(pos, *([keep] * len(ways)), *([got] * len(ways)), *[a for a, _ in more])


def pack_kernel(owner_ref, *refs):
    early, late, out_ref, total_s = refs[:4], refs[4:8], refs[8], refs[9]
    square = None
    start = 0
    for parts in (early, late):
        total = parts[0][...].astype(F32)
        for part in parts[1:]:
            total = total + part[...].astype(F32)
        total_s[start:start + total.shape[0]] = total.astype(BF16)
        start += total.shape[0]
        more = jnp.sum(total * total).reshape(1, 1)
        square = more if square is None else square + more
    rows = total_s.shape[1]
    lane = lax.broadcasted_iota(jnp.int32, (8, out_ref.shape[2]), 1)
    one, two, three = split3(square)
    extra = jnp.where(lane == 0, one, jnp.where(lane == 1, two, jnp.where(lane == 2, three, 0.0))).astype(BF16)
    for p in range(out_ref.shape[0]):
        out_ref[p, :rows] = total_s[lax.div(owner_ref[p], 2)]
        out_ref[p, rows:] = extra


def pack(owner, early, late):
    blocks = early[0].shape[0] + late[0].shape[0]
    rows, cols = early[0].shape[1:]
    vmem = pl.BlockSpec(memory_space=pltpu.VMEM)
    return pl.pallas_call(
        pack_kernel,
        in_specs=[pl.BlockSpec(memory_space=pltpu.SMEM)] + [vmem] * 8,
        out_specs=vmem,
        out_shape=jax.ShapeDtypeStruct((owner.shape[0], rows + 8, cols), BF16),
        scratch_shapes=[pltpu.VMEM((blocks, rows, cols), BF16)],
        compiler_params=pltpu.CompilerParams(vmem_limit_bytes=32 * 2**20),
        cost_estimate=SHORT,
        name="pack",
    )(owner, *early, *late)


def clip_of(square, vec):
    norm = jnp.sqrt(square + jnp.sum(vec * vec).reshape(1, 1))
    return norm, jnp.minimum(1.0, 1.0 / (norm + 1e-06))


def adam_kernel(own_ref, a_ref, b_ref, as_ref, bs_ref, vt_ref, vw_ref, vm_ref, vv_ref, w_ref, m_ref, v_ref,
                g_out, v_out, w_out, vg_out, vv_out, vw_out, norm_out):
    def squares(ref):
        block = ref[...].astype(F32)
        lane = lax.broadcasted_iota(jnp.int32, block.shape, 4)
        row = lax.broadcasted_iota(jnp.int32, block.shape, 3)
        return jnp.sum(jnp.where((lane < 3) & (row == 0), block, 0.0)).reshape(1, 1)

    norm, clip = clip_of(squares(as_ref) + squares(bs_ref), vt_ref[...])
    own = own_ref[0] > 0
    grad = jnp.where(own, a_ref[:, 0, 0].astype(F32), b_ref[:, 0, 0].astype(F32))
    grad = grad[:, :w_ref.shape[0] // grad.shape[0]].reshape(w_ref.shape) * clip
    second, weight = adam(w_ref[...], m_ref[...], v_ref[...], grad, 0.02, 0.05)
    g_out[...] = grad
    v_out[...] = second
    w_out[...] = weight

    @pl.when((pl.program_id(0) == 0) & (pl.program_id(1) == 0))
    def _():
        vec_grad = vt_ref[...] * clip
        second, weight = adam(vw_ref[...], vm_ref[...], vv_ref[...], vec_grad, 0.2, 0.0)
        vg_out[...] = vec_grad
        vv_out[...] = second
        vw_out[...] = weight
        norm_out[...] = norm


def adam_rows(own, mine, other, vec_total, vectors, vec_first, vec_second, weight, first, second):
    rows, width = weight.shape
    deep, tall, wide, piece, cols = mine.shape
    part = pl.BlockSpec((deep, 1, 1, piece, cols), lambda y, x: (0, y, x, 0, 0))
    marks = pl.BlockSpec((deep, tall, wide, 8, 128), lambda y, x: (0, 0, 0, piece // 8 - 1, 0))
    flat = pl.BlockSpec((rows // tall, width // wide), lambda y, x: (y, x))
    vec = pl.BlockSpec(vectors.shape, lambda y, x: (0, 0))
    shape = jax.ShapeDtypeStruct((rows, width), F32)
    small = jax.ShapeDtypeStruct(vectors.shape, F32)
    return pl.pallas_call(
        adam_kernel,
        grid=(tall, wide),
        in_specs=[pl.BlockSpec(memory_space=pltpu.SMEM), part, part, marks, marks] + [vec] * 4 + [flat] * 3,
        out_specs=[flat] * 3 + [vec] * 3 + [pl.BlockSpec((1, 1), lambda y, x: (0, 0))],
        out_shape=[shape] * 3 + [small] * 3 + [jax.ShapeDtypeStruct((1, 1), F32)],
        compiler_params=pltpu.CompilerParams(vmem_limit_bytes=60 * 2**20),
        cost_estimate=SHORT,
        name="adam",
    )(own, mine, other, mine, other, vec_total, vectors, vec_first, vec_second, weight, first, second)


from jax.sharding import PartitionSpec as P

HEADS = 12
STEP = 7


def place_tokens(heights, widths, count):
    sizes = heights * widths
    ends = jnp.cumsum(sizes)
    starts = ends - sizes
    places = jnp.arange(count, dtype=jnp.int32)
    segment = jnp.sum((places[:, None] >= ends[None, :]).astype(jnp.int32), axis=1)
    slots = jnp.arange(heights.shape[0], dtype=jnp.int32)
    picks = (segment[:, None] == slots[None, :]).astype(jnp.int32)
    begin = jnp.sum(picks * starts[None, :], axis=1)
    across = jnp.maximum(jnp.sum(picks * widths[None, :], axis=1), 1)
    offset = places - begin
    live = places < ends[-1]
    return (segment, offset // across, offset % across, live)


def adam(weight, first, second, grad, rate, decay):
    first_new = 0.5 * first + 0.5 * grad
    second_new = 0.5 * second + 0.5 * grad * grad
    correct = 1.0 - 0.5**STEP
    direction = first_new / correct / (jnp.sqrt(second_new / correct) + 1e-08)
    return (second_new, weight - rate * (direction + decay * weight))


def pairwise(bits, total):
    return [(i, i ^ bits) for i in range(total)]


def sum_part(value, devices, step, stop):
    while step < stop:
        value = value + lax.ppermute(value, "dp", pairwise(step, devices))
        step *= 2
    return value


CORES = ("group", "dp")
SWAP = [(0, 1), (1, 0)]


def cross(value, bit0, bit1, devices):
    perm = [(i, i ^ (bit0 if i < devices else bit1)) for i in range(2 * devices)]
    return lax.ppermute(value, CORES, perm)


def along_z(values, devices):
    return [
        lax.ppermute(v, "dp", [(i, (i + 4 * (s + 1)) % devices) for i in range(devices)])
        for s, v in enumerate(values)
    ]


def along_line(value, devices, step, up):
    last = devices // 4
    perm = []
    for z in range(last):
        near = z - 1 if up else z + 1
        far = z - step if up else z + step
        if 0 <= far < last:
            perm += [(4 * near + i, 4 * z + i) for i in range(4)]
    return lax.ppermute(value, "dp", perm)


def gather_pieces(master, inverse, core, me, devices, tables):
    tie = lax.optimization_barrier
    block_rows, width = master.shape
    half = block_rows // 2
    mine = lax.dynamic_slice_in_dim(master, core * half, half, 0).astype(BF16)
    large = mine[:LARGE]
    small = mine[LARGE:]
    z = me // 4
    deep = lax.rem(z - inverse // 4 + 4, 4)
    apart = me ^ inverse
    one = jnp.where(core == 0, apart & 1, (apart >> 1) & 1)
    two = jnp.where(core == 0, (apart >> 1) & 1, apart & 1)
    slots = jnp.stack([
        8 * two + 4 * one + deep,
        4 * deep + 2 * two + one,
        8 * one + 4 * two + deep,
        4 * deep + 2 * one + two,
    ]).astype(jnp.int32)
    up = along_z([large] * 3, devices)
    small = jnp.stack([small, cross(small, 1, 2, devices)])
    small = jnp.concatenate([small, cross(small, 2, 1, devices)])
    large = jnp.stack([large] + up)
    large, small, tables, slots = tie((large, small, tables, slots))
    first = cross(large, 1, 2, devices)
    ups = [along_line(small, devices, 1, True)]
    downs = [along_line(small, devices, 1, False)]
    first, ups[0], downs[0] = tie((first, ups[0], downs[0]))
    first = jnp.concatenate([large, first])
    second = cross(first, 2, 1, devices)
    for step in (2, 3):
        ups.append(along_line(ups[-1], devices, step, True))
        downs.append(along_line(downs[-1], devices, step, False))
    small = jnp.concatenate([small] + [jnp.where(z >= s, ups[s - 1], downs[3 - s]) for s in (1, 2, 3)])
    other = [lax.ppermute(a, "group", SWAP) for a in (first, second, small)]
    return (first, second, small, *other), slots, tables


def quarters(core, me):
    x, y = me & 1, (me >> 1) & 1
    one = jnp.where(core == 0, x, y)
    two = jnp.where(core == 0, y, x)
    pairs = [(1 - one, 1 - two), (1 - one, two), (one, 1 - two), (one, two)]
    return jnp.stack([
        jnp.stack([jnp.where(core == 0, b, a), jnp.where(core == 0, a, b)]) for a, b in pairs
    ]).astype(jnp.int32)


def sum_z(low, me, devices):
    count, rows, cols = low.shape
    z = me // 4
    low = low.reshape(count, 4, rows // 4, cols)
    pick = lambda at: lax.dynamic_index_in_dim(low, at, 1, keepdims=False)
    return (pick(z), *along_z([pick(lax.rem(z + s, 4)) for s in (1, 2, 3)], devices))


def reduce_plain(local_mat, owner_block, devices):
    rows, width = local_mat.shape
    block_rows = rows // devices
    term = local_mat.reshape(devices, block_rows, width)[owner_block].reshape(rows, width)
    share = lax.psum_scatter(term.astype(F32), "dp", scatter_dimension=0, tiled=True)
    return lax.psum(share.astype(BF16), "group").astype(F32)


def local(
    tokens,
    cotangent,
    grid_h,
    grid_w,
    owner_block,
    master,
    first_mom,
    second_mom,
    vectors,
    vec_first,
    vec_second,
):
    devices = lax.axis_size("dp")
    core = lax.axis_index("group")
    me = lax.axis_index("dp")
    count = tokens.shape[1]
    width = tokens.shape[2]
    heads = HEADS
    head_dim = width // heads
    half = head_dim // 2
    block_rows = master.shape[0]
    stack = devices * block_rows
    quick = devices == 16 and block_rows == 2 * (LARGE + SMALL) and width % 256 == 0
    inverse = jnp.argsort(owner_block)
    segment, rows_pos, cols_pos, live = place_tokens(grid_h[0], grid_w[0], count)
    freqs = vectors[13]

    def spread(part):
        return jnp.broadcast_to(part.reshape(heads, 1, half), (heads, 2, half)).reshape(1, width)

    angle = rows_pos.astype(F32)[:, None] * spread(freqs[: width // 2]) + cols_pos.astype(F32)[
        :, None
    ] * spread(freqs[width // 2 :])
    lower = (jnp.arange(width) % head_dim < half)[None]
    cosine = jnp.cos(angle)
    sine = jnp.sin(angle)
    sine = jnp.where(lower, -sine, sine)
    ids = jnp.arange(128)[None]
    match = segment[:, None] == ids
    key_mask = jnp.where(match | ((ids >= 8) & (ids < 11)), 1.0, 0.0).astype(BF16)
    query_mask = jnp.where((ids < 8) & ~match, MASKED, 0.0).astype(BF16)
    places = jnp.stack([rows_pos, cols_pos], axis=1).astype(F32)
    alive = live[:, None].astype(F32)
    bias_qkv = vectors[4:7].reshape(1, 3 * width)
    bias_one = vectors[8:12].reshape(1, 4 * width)
    tables = (cosine, sine, key_mask, query_mask, places, alive, bias_qkv, bias_one)
    if quick:
        weights, slots, tables = gather_pieces(master, inverse, core, me, devices, tables)
    else:
        low = lax.all_gather(master.astype(BF16), "dp", axis=0, tiled=True)
        weights = low.reshape(devices, block_rows, width)[inverse].reshape(stack, width)
        slots = jnp.zeros((4, devices), jnp.int32)
    cosine, sine, key_mask, query_mask, places, alive, bias_qkv, bias_one = tables
    here = core.reshape(1).astype(jnp.int32)
    x = tokens[0]
    first_in, query, key, value, attn, stat, *placed = attend(
        here, slots, x, vectors[0:1], vectors[1:2], bias_qkv,
        cosine, sine, query_mask, key_mask, weights, stack,
    )
    if quick:
        weights = placed[0]
    whole_rows = block_rows if quick else 0
    block_out, grad_middle, grad_attn, sums, bias_up, keep_mlp, give_mlp = mlp(
        here, x, attn, cotangent[0], alive, vectors, weights, bias_one, whole_rows
    )
    pairs = width // 128
    tie = lax.optimization_barrier
    if quick:
        pos = quarters(core, me)
        got = lax.ppermute(give_mlp, "group", SWAP)
    back = None
    cuts = (0, 1, pairs - 1, pairs)
    for start, stop in zip(cuts[:-1], cuts[1:]):
        back = attend_back(
            start, stop, back, query, key, value, grad_attn, attn, stat, cosine, sine, query_mask, key_mask, places
        )
        if quick and start == 0:
            send, back = tie((fold(pos, keep_mlp, got, (0, 1)), back))
            came = cross(send, 1, 2, devices)
        if quick and start == 1:
            send, back = tie((fold(pos, keep_mlp, got, (2,), ((came, 0),)), back))
            again = cross(send, 2, 1, devices)
    grad_q, grad_k, grad_v, grad_bias, grad_freq = back
    keep_qkv, give_qkv = qkv_grad(here, grad_q, grad_k, grad_v, first_in, whole_rows)
    if quick:
        again, give_qkv = tie((again, give_qkv))
        low, grad_v, give_qkv = tie((fold(pos, keep_mlp, got, (3,), ((came, 1), (again, 0)))[0], grad_v, give_qkv))
        late = sum_z(low, me, devices)
    if quick:
        got_qkv = lax.ppermute(give_qkv, "group", SWAP)
        send = fold(pos, keep_qkv, got_qkv, (0, 1))
        third = send.shape[2] // 3
        send = [send[:, :, third * i:third * (i + 1)] for i in range(3)]
        send, grad_v = tie((send, grad_v))
    input_grad, local_vec = input_back(
        grad_q, grad_k, grad_v, weights, x, grad_middle, vectors, sums, grad_bias, grad_freq, bias_up
    )
    if quick:
        send[2], local_vec = tie((send[2], local_vec))
        came = [cross(a, 1, 2, devices) for a in send]
        came, local_vec, late = tie((came, local_vec, late))
        came = jnp.concatenate(came, axis=2)
        again = cross(fold(pos, keep_qkv, got_qkv, (2,), ((came, 0),)), 2, 1, devices)
        vec_total = sum_part(local_vec + lax.ppermute(local_vec, "group", SWAP), devices, 4, devices)
        again, vec_total = tie((again, vec_total))
        early = sum_z(fold(pos, keep_qkv, got_qkv, (3,), ((came, 1), (again, 0)))[0], me, devices)
        early, vec_total = tie((early, sum_part(vec_total, devices, 1, 4)))
        load = pack(owner_block, early, late)
        mine = lax.all_to_all(load, "dp", 0, 0, tiled=True)
        other = lax.ppermute(mine, "group", SWAP)
        shape = (devices // 4, 2, 2, *load.shape[1:])
        own = (owner_block[me] % 2 == core).astype(jnp.int32).reshape(1)
        mat_grad, mat_second, mat_weight, vec_grad, vec_second_new, vec_weight, norm = adam_rows(
            own, mine.reshape(shape), other.reshape(shape), vec_total, vectors, vec_first, vec_second,
            master, first_mom, second_mom,
        )
        grad_norm = norm.reshape(())
    else:
        vec_total = lax.psum(local_vec, CORES)
        share = reduce_plain(jnp.concatenate([keep_qkv, keep_mlp]), owner_block, devices)
        square = lax.psum(jnp.sum(share * share), "dp")
        grad_norm = jnp.sqrt(square + jnp.sum(vec_total * vec_total))
        clip = jnp.minimum(1.0, 1.0 / (grad_norm + 1e-06))
        mat_grad = share * clip
        mat_second, mat_weight = adam(master, first_mom, second_mom, mat_grad, 0.02, 0.05)
        vec_grad = vec_total * clip
        vec_second_new, vec_weight = adam(vectors, vec_first, vec_second, vec_grad, 0.2, 0.0)
    return (
        block_out[None],
        input_grad[None],
        mat_grad,
        mat_second,
        mat_weight,
        vec_grad,
        vec_second_new,
        vec_weight,
        grad_norm,
    )


def solution(mesh):
    return jax.shard_map(
        local,
        mesh=mesh,
        in_specs=(
            P("group", "dp", None),
            P("group", "dp", None),
            P("group", "dp"),
            P("group", "dp"),
            P(),
            P("dp", None),
            P("dp", None),
            P("dp", None),
            P(),
            P(),
            P(),
        ),
        out_specs=(
            P("group", "dp", None),
            P("group", "dp", None),
            P("dp", None),
            P("dp", None),
            P("dp", None),
            P(),
            P(),
            P(),
            P(),
        ),
        check_vma=False,
    )
```

```python
import functools
import jax
import jax.numpy as jnp
from jax import lax
from jax.experimental import pallas as pl
from jax.experimental.pallas import tpu as pltpu

F32 = jnp.float32
BF16 = jnp.bfloat16
LAST = (((1,), (1,)), ((), ()))
FIRST = (((0,), (0,)), ((), ()))
PLAIN = (((1,), (0,)), ((), ()))
MASKED = -1e9
SHORT = pl.CostEstimate(flops=1000, bytes_accessed=1000, transcendentals=0)


def mm(left, right, dims):
    return lax.dot_general(left, right, dims, preferred_element_type=F32)


def norm_parts(value):
    centre = value - jnp.mean(value, axis=-1, keepdims=True)
    spread = jnp.mean(centre * centre, axis=-1, keepdims=True)
    inverse = lax.rsqrt(spread + 1e-6)
    return centre * inverse, inverse


def norm_back(unit, inverse, grad, gain):
    scaled = grad * gain
    first = jnp.mean(scaled, axis=-1, keepdims=True)
    second = jnp.mean(scaled * unit, axis=-1, keepdims=True)
    return inverse * (scaled - first - unit * second)


def swap_halves(value):
    lane = lax.broadcasted_iota(jnp.int32, value.shape, 1)
    return jnp.where(
        lane % 64 < 32, pltpu.roll(value, 96, 1), pltpu.roll(value, 32, 1)
    )


def split3(value):
    one = value.astype(BF16).astype(F32)
    rest = value - one
    two = rest.astype(BF16).astype(F32)
    return one, two, rest - two


LARGE = 208
SMALL = 80


def place_pieces(core, slot_ref, mine, other, block, side, dst, sem):
    for which, (first, second, small) in enumerate((mine, other)):
        @pl.when((core == side) if which == 0 else (core != side))
        def _():
            large_slot = slot_ref[2 * which, block]
            small_slot = slot_ref[2 * which + 1, block]

            @pl.when(large_slot < 8)
            def _():
                pltpu.make_async_copy(first.at[large_slot], dst(0, LARGE), sem).start()

            @pl.when(large_slot >= 8)
            def _():
                pltpu.make_async_copy(second.at[large_slot - 8], dst(0, LARGE), sem).start()

            pltpu.make_async_copy(small.at[small_slot], dst(LARGE, SMALL), sem).start()


def attend_kernel(blocks, core_ref, slot_ref, n1_ref, bq_ref, bk_ref, bv_ref,
                  cos_ref, sin_ref, qm_ref, km_ref, *rest):
    if blocks:
        mine, other = rest[0:3], rest[3:6]
        q_ref, k_ref, v_ref, attn_ref, stat_ref, w_ref, w_s, near, far, back = rest[6:]
    else:
        w_ref, q_ref, k_ref, v_ref, attn_ref, stat_ref, w_s, near = rest
    count, width = n1_ref.shape
    step = pl.program_id(0)

    @pl.when(step == 0)
    def _():
        if blocks:
            core = core_ref[0]
            rows = w_ref.shape[0] // blocks

            def start(block, sem):
                for side in (0, 1):
                    def dst(offset, size):
                        base = block * rows + side * (rows // 2) + offset
                        return w_s.at[pl.ds(pl.multiple_of(base, 16), size)]
                    place_pieces(core, slot_ref, mine, other, block, side, dst, sem)

            def near_block(block, carry):
                start(block, near)
                return carry

            def far_block(block, carry):
                start(block, far)
                return carry

            lax.fori_loop(0, 3 * width // rows, near_block, 0)
            lax.fori_loop(3 * width // rows, blocks, far_block, 0)
        else:
            pltpu.make_async_copy(w_ref.at[pl.ds(0, 3 * width)], w_s, near).start()
        head = w_s.at[pl.ds(0, 3 * width)]
        pltpu.make_async_copy(head, head, near).wait()

    if blocks:
        @pl.when(step == 1)
        def _():
            tail = w_s.at[pl.ds(3 * width, w_s.shape[0] - 3 * width)]
            pltpu.make_async_copy(tail, tail, far).wait()
            pltpu.make_async_copy(w_s, w_ref, back).start()

    def third(j):
        return w_s[pl.ds(pl.multiple_of(j * width + step * 128, 128), 128), :]

    w = jnp.concatenate([third(0), third(1), third(2)], axis=0)
    qkv = mm(n1_ref[...], w, LAST)
    q = qkv[:, :128] + bq_ref[...]
    k = qkv[:, 128:256] + bk_ref[...]
    v = (qkv[:, 256:] + bv_ref[...]).astype(BF16)
    c = cos_ref[...]
    s = sin_ref[...]
    qr = ((q * c + swap_halves(q) * s).astype(BF16).astype(F32) * 0.125).astype(BF16)
    kr = (k * c + swap_halves(k) * s).astype(BF16)
    q_ref[...] = qr
    k_ref[...] = kr
    v_ref[...] = v
    lane = lax.broadcasted_iota(jnp.int32, (1, 128), 1)
    k_aug = jnp.concatenate([kr, km_ref[...]], axis=1)
    v_aug = jnp.concatenate([v, jnp.ones((count, 128), BF16)], axis=1)
    zero = jnp.zeros((), BF16)
    tile = 256
    for i in range(count // tile):
        rows = pl.ds(i * tile, tile)
        out = None
        stats = []
        for h in (0, 1):
            mine_lanes = (lane // 64) == h
            qa = jnp.concatenate(
                [jnp.where(mine_lanes, qr[i * tile:(i + 1) * tile], zero), qm_ref[rows, :]], axis=1)
            scores = mm(qa, k_aug, LAST)
            top = jnp.max(scores, axis=-1, keepdims=True)
            e = jnp.exp(scores - top).astype(BF16)
            o = mm(e, v_aug, PLAIN)
            total = o[:, 128:]
            o = o[:, :128] / total
            out = o if out is None else jnp.where(lane < 64, out, o)
            stats.append(top + jnp.log(total[:, :1]))
        attn_ref[rows, :] = out.astype(BF16)
        stat_ref[rows, :] = jnp.where(lane < 64, stats[0], stats[1])

    if blocks:
        @pl.when(step == pl.num_programs(0) - 1)
        def _():
            pltpu.make_async_copy(w_s, w_ref, back).wait()


def attend(core, slots, n1, bqkv, cos, sin, qm, km, weights, stack):
    count, width = n1.shape
    pairs = width // 128
    pieces = isinstance(weights, tuple)
    blocks = slots.shape[1] if pieces else 0
    whole = lambda p: (0, 0)
    col = lambda p: (0, p)
    smem = pl.BlockSpec(memory_space=pltpu.SMEM)
    hbm = pl.BlockSpec(memory_space=pl.ANY)
    given = weights if pieces else (weights,)
    specs = [smem, smem] + [
        pl.BlockSpec((count, width), whole),
        pl.BlockSpec((1, 128), col),
        pl.BlockSpec((1, 128), lambda p: (0, p + pairs)),
        pl.BlockSpec((1, 128), lambda p: (0, p + 2 * pairs)),
        pl.BlockSpec((count, 128), col),
        pl.BlockSpec((count, 128), col),
        pl.BlockSpec((count, 128), whole),
        pl.BlockSpec((count, 128), whole),
    ] + [hbm] * len(given)
    outs = [pl.BlockSpec((count, 128), col)] * 5
    shape = lambda d: jax.ShapeDtypeStruct((count, width), d)
    shapes = [shape(BF16)] * 4 + [shape(F32)]
    scratch = [pltpu.VMEM((stack if pieces else 3 * width, width), BF16), pltpu.SemaphoreType.DMA]
    if pieces:
        outs.append(hbm)
        shapes.append(jax.ShapeDtypeStruct((stack, width), BF16))
        scratch += [pltpu.SemaphoreType.DMA] * 2
    return pl.pallas_call(
        functools.partial(attend_kernel, blocks),
        grid=(pairs,),
        in_specs=specs,
        out_specs=outs,
        out_shape=shapes,
        scratch_shapes=scratch,
        compiler_params=pltpu.CompilerParams(vmem_limit_bytes=56 * 2**20),
        cost_estimate=SHORT,
        name="attend",
    )(core, slots, n1, bqkv, bqkv, bqkv, cos, sin, qm, km, *given)


def gelu_both(x):
    cdf = 0.5 + 0.5 * lax.erf(x * 0.7071067811865476)
    return x * cdf, cdf + x * jnp.exp(x * x * -0.5) * 0.3989422804014327


def send_rows(core, block_rows, stage, row, base, keep_ref, give_ref, sem):
    if not block_rows:
        rows = stage.shape[0]
        pltpu.make_async_copy(
            stage, keep_ref.at[pl.ds(pl.multiple_of(row - base, 64), rows)], sem
        ).start()
        return

    def one(index, carry):
        at = row + 64 * index
        block = lax.div(at, block_rows)
        inner = pl.ds(pl.multiple_of(at - block * block_rows, 64), 64)
        slot = lax.div(block, 2) - base // 2
        source = stage.at[pl.ds(pl.multiple_of(64 * index, 64), 64)]
        own = lax.rem(block, 2) == core

        @pl.when(own)
        def _():
            pltpu.make_async_copy(source, keep_ref.at[slot, inner], sem).start()

        @pl.when(jnp.logical_not(own))
        def _():
            pltpu.make_async_copy(source, give_ref.at[slot, inner], sem).start()

        return carry

    lax.fori_loop(0, stage.shape[0] // 64, one, 0)


def mlp_kernel(block_rows, base, core_ref, x_ref, at_ref, dz_ref, vec_ref, wo_ref, w1_ref, w2_ref, b1_ref,
               out_ref, dm_ref, da_ref, sums_ref, gb_ref, keep_ref, give_ref,
               middle_s, n2_s, acc_s, stage_s, proj_s, sems):
    step = pl.program_id(0)
    last = pl.num_programs(0) - 1
    count, width = x_ref.shape
    core = core_ref[0]
    tile = w1_ref.shape[0]

    @pl.when(step == 0)
    def _():
        middle = x_ref[...].astype(F32) + mm(at_ref[...], wo_ref[...], LAST) + vec_ref[7:8, :]
        middle_s[...] = middle
        unit, _ = norm_parts(middle)
        n2_s[...] = (unit * vec_ref[2:3, :] + vec_ref[3:4, :]).astype(BF16)
        acc_s[...] = jnp.zeros_like(acc_s)
        dm_ref[...] = jnp.zeros_like(dm_ref)

    slot = lax.rem(step, 2)

    @pl.when(step >= 2)
    def _():
        pltpu.make_async_copy(stage_s.at[slot], stage_s.at[slot], sems.at[slot]).wait()

    n2 = n2_s[...]
    dz = dz_ref[...]
    w1 = w1_ref[...]
    w2 = w2_ref[...]
    pre = mm(w1, n2, LAST) + b1_ref[...].reshape(tile, 1)
    back = mm(w2, dz, LAST)
    act, slope = gelu_both(pre)
    hidden = act.astype(BF16)
    stage_s[slot, 1] = mm(hidden, dz, PLAIN).astype(BF16)
    dpre = (back * slope).astype(BF16)
    gb_ref[...] = jnp.sum(dpre.astype(F32), axis=1, keepdims=True).reshape(1, tile)
    stage_s[slot, 0] = mm(dpre, n2, PLAIN).astype(BF16)
    acc_s[...] += mm(hidden, w2, FIRST)
    dm_ref[...] += mm(dpre, w1, FIRST)
    for j in (0, 1):
        send_rows(core, block_rows, stage_s.at[slot, j], (4 + 4 * j) * width + step * tile,
                  base, keep_ref, give_ref, sems.at[slot])

    @pl.when(step == last)
    def _():
        middle = middle_s[...]
        out_ref[...] = (middle + acc_s[...] + vec_ref[12:13, :]).astype(BF16)
        unit, inverse = norm_parts(middle)
        dn = dm_ref[...]
        dy = dz_ref[...].astype(F32)
        dm = dy + norm_back(unit, inverse, dn, vec_ref[2:3, :])
        dm_ref[...] = dm
        low = dm.astype(BF16)
        row = lambda a: jnp.sum(a, axis=0, keepdims=True)
        sums_ref[...] = jnp.concatenate(
            [row(dn * unit), row(dn), row(low.astype(F32)), row(dy), jnp.zeros((4, width), F32)], axis=0)
        proj_s[...] = mm(low, at_ref[...], FIRST).astype(BF16)
        send_rows(core, block_rows, proj_s, 3 * width, base, keep_ref, give_ref, sems.at[2])
        da_ref[...] = mm(low, wo_ref[...], PLAIN).astype(BF16)
        pltpu.make_async_copy(stage_s.at[slot], stage_s.at[slot], sems.at[slot]).wait()
        pltpu.make_async_copy(stage_s.at[1 - slot], stage_s.at[1 - slot], sems.at[1 - slot]).wait()
        pltpu.make_async_copy(proj_s, proj_s, sems.at[2]).wait()


def grad_shapes(block_rows, rows, width):
    if block_rows:
        half = jax.ShapeDtypeStruct((rows // block_rows // 2, block_rows, width), BF16)
        return [half, half]
    return [jax.ShapeDtypeStruct((rows, width), BF16), jax.ShapeDtypeStruct((16, width), BF16)]


def mlp(core, x, attn, dz, vectors, weights, b1, block_rows, tile=512):
    count, width = x.shape
    units = 4 * width
    stack = weights.shape[0]
    base = 3 * width // block_rows if block_rows else 3 * width
    whole = lambda t: (0, 0)
    big = pl.BlockSpec((count, width), whole)
    hbm = pl.BlockSpec(memory_space=pl.ANY)
    return pl.pallas_call(
        functools.partial(mlp_kernel, block_rows, base),
        grid=(units // tile,),
        in_specs=[pl.BlockSpec(memory_space=pltpu.SMEM), big, big, big, pl.BlockSpec(vectors.shape, whole),
                  pl.BlockSpec((width, width), lambda t: (3, 0)),
                  pl.BlockSpec((tile, width), lambda t: (4 * width // tile + t, 0)),
                  pl.BlockSpec((tile, width), lambda t: (8 * width // tile + t, 0)),
                  pl.BlockSpec((1, tile), lambda t: (0, t))],
        out_specs=[big, big, big, pl.BlockSpec((8, width), whole), pl.BlockSpec((1, tile), lambda t: (0, t)), hbm, hbm],
        out_shape=[
            jax.ShapeDtypeStruct((count, width), BF16),
            jax.ShapeDtypeStruct((count, width), F32),
            jax.ShapeDtypeStruct((count, width), BF16),
            jax.ShapeDtypeStruct((8, width), F32),
            jax.ShapeDtypeStruct((1, units), F32),
        ] + grad_shapes(block_rows, stack - 3 * width, width),
        scratch_shapes=[
            pltpu.VMEM((count, width), F32),
            pltpu.VMEM((count, width), BF16),
            pltpu.VMEM((count, width), F32),
            pltpu.VMEM((2, 2, tile, width), BF16),
            pltpu.VMEM((width, width), BF16),
            pltpu.SemaphoreType.DMA((3,)),
        ],
        compiler_params=pltpu.CompilerParams(vmem_limit_bytes=60 * 2**20),
        cost_estimate=SHORT,
        name="mlp",
    )(core, x, attn, dz, vectors, weights, weights, weights, b1)


def back_kernel(first, q_ref, k_ref, v_ref, da_ref, at_ref, stat_ref, cos_ref, sin_ref,
                qm_ref, km_ref, pos_ref, *rest):
    dq_ref, dk_ref, dv_ref, gb_ref, gf_ref = rest if first else rest[5:]
    count = q_ref.shape[0]
    lane = lax.broadcasted_iota(jnp.int32, (1, 128), 1)
    zero = jnp.zeros((), BF16)
    q = q_ref[...]
    k = k_ref[...]
    v = v_ref[...]
    da = da_ref[...]
    prod = da.astype(F32) * at_ref[...].astype(F32)
    qm = qm_ref[...].astype(F32)
    k_aug = jnp.concatenate([k, km_ref[...]], axis=1)
    v_aug = jnp.concatenate([v, jnp.broadcast_to((lane < 2).astype(BF16), (count, 128))], axis=1)
    tile = 256
    dq = dk = dv = None
    for h in (0, 1):
        mine = (lane // 64) == h
        qh = jnp.where(mine, q, zero)
        kh = jnp.where(mine, k, zero)
        dah = jnp.where(mine, da, zero)
        delta = jnp.sum(jnp.where(mine, prod, 0.0), axis=-1, keepdims=True)
        d1, d2, _ = split3(delta)
        l1, l2, l3 = split3(stat_ref[:, 64 * h:64 * h + 1])
        extra = jnp.where(lane == 8, -l1, jnp.where(lane == 9, -l2, jnp.where(lane == 10, -l3, qm)))
        q_aug = jnp.concatenate([qh, extra.astype(BF16)], axis=1)
        da_aug = jnp.concatenate(
            [dah, jnp.where(lane == 0, -d1, jnp.where(lane == 1, -d2, 0.0)).astype(BF16)], axis=1)
        dks, dvs, dqh = [], [], None
        for i in range(count // tile):
            sl = slice(i * tile, (i + 1) * tile)
            p = jnp.exp(mm(k_aug[sl], q_aug, LAST))
            dp = mm(v_aug[sl], da_aug, LAST)
            ds = (p * dp).astype(BF16)
            dvs.append(mm(p.astype(BF16), dah, PLAIN))
            dks.append(mm(ds, qh, PLAIN))
            part = mm(ds, kh[sl], FIRST)
            dqh = part if dqh is None else dqh + part
        dkh = jnp.concatenate(dks, axis=0)
        dvh = jnp.concatenate(dvs, axis=0)
        dq = dqh if dq is None else dq + dqh
        dk = dkh if dk is None else dk + dkh
        dv = dvh if dv is None else dv + dvh
    dq = dq * 0.125
    c = cos_ref[...]
    s = sin_ref[...]
    turned = dq * swap_halves(q.astype(F32) * 8.0) + dk * swap_halves(k.astype(F32))
    turned = jnp.where(lane % 64 < 32, -turned, turned)
    row = lambda a: jnp.sum(a, axis=0, keepdims=True)
    gf_ref[...] = jnp.concatenate(
        [row(turned * pos_ref[:, 0:1]), row(turned * pos_ref[:, 1:2]), jnp.zeros((6, 128), F32)], axis=0)
    dqp = (dq * c - swap_halves(dq) * s).astype(BF16)
    dkp = (dk * c - swap_halves(dk) * s).astype(BF16)
    dvp = dv.astype(BF16)
    gb_ref[...] = jnp.concatenate(
        [row(dqp.astype(F32)), row(dkp.astype(F32)), row(dvp.astype(F32)), jnp.zeros((5, 128), F32)], axis=0)
    dq_ref[...] = dqp
    dk_ref[...] = dkp
    dv_ref[...] = dvp


def attend_back(start, stop, before, q, k, v, da, attn, stat, cos, sin, qm, km, pos):
    count, width = q.shape
    whole = lambda p: (0, 0)
    col = lambda p: (0, p + start)
    tall = pl.BlockSpec((count, 128), col)
    fixed = pl.BlockSpec((count, 128), whole)
    small = pl.BlockSpec((8, 128), col)
    in_specs = [tall] * 8 + [fixed] * 2 + [pl.BlockSpec((count, 2), whole)]
    operands = [q, k, v, da, attn, stat, cos, sin, qm, km, pos]
    aliases = {}
    if before is not None:
        aliases = {len(operands) + i: i for i in range(5)}
        in_specs += [pl.BlockSpec(memory_space=pl.ANY)] * 5
        operands += list(before)
    return pl.pallas_call(
        functools.partial(back_kernel, before is None),
        grid=(stop - start,),
        in_specs=in_specs,
        out_specs=[tall] * 3 + [small] * 2,
        out_shape=[jax.ShapeDtypeStruct((count, width), BF16)] * 3 + [jax.ShapeDtypeStruct((8, width), F32)] * 2,
        input_output_aliases=aliases,
        compiler_params=pltpu.CompilerParams(vmem_limit_bytes=56 * 2**20),
        cost_estimate=SHORT,
        name="attend_back",
    )(*operands)


def qkv_grad_kernel(block_rows, core_ref, dq_ref, dk_ref, dv_ref, n1_ref, keep_ref, give_ref, stage_s, sem):
    width = n1_ref.shape[1]
    cols = dq_ref.shape[1]
    step = pl.program_id(0)
    n1 = n1_ref[...]
    for j, ref in enumerate((dq_ref, dk_ref, dv_ref)):
        stage_s[step, j] = mm(ref[...], n1, FIRST).astype(BF16)
        send_rows(core_ref[0], block_rows, stage_s.at[step, j], j * width + step * cols, 0, keep_ref, give_ref, sem)

    @pl.when(step == pl.num_programs(0) - 1)
    def _():
        pltpu.make_async_copy(stage_s, stage_s, sem).wait()


def qkv_grad(core, dq, dk, dv, n1, block_rows):
    count, width = n1.shape
    cols = width // 2
    tall = pl.BlockSpec((count, cols), lambda p: (0, p))
    hbm = pl.BlockSpec(memory_space=pl.ANY)
    return pl.pallas_call(
        functools.partial(qkv_grad_kernel, block_rows),
        grid=(2,),
        in_specs=[pl.BlockSpec(memory_space=pltpu.SMEM)] + [tall] * 3 + [pl.BlockSpec((count, width), lambda p: (0, 0))],
        out_specs=[hbm, hbm],
        out_shape=grad_shapes(block_rows, 3 * width, width),
        scratch_shapes=[pltpu.VMEM((2, 3, cols, width), BF16), pltpu.SemaphoreType.DMA],
        compiler_params=pltpu.CompilerParams(vmem_limit_bytes=56 * 2**20),
        cost_estimate=SHORT,
        name="qkv_grad",
    )(core, dq, dk, dv, n1)


def input_kernel(dq_ref, dk_ref, dv_ref, w_ref, x_ref, dm_ref, vec_ref, sums_ref, gb_ref, gf_ref, up_ref, ig_ref, out_ref):
    step = pl.program_id(0)
    d = jnp.concatenate([dq_ref[...], dk_ref[...], dv_ref[...]], axis=1)
    dn = mm(d, w_ref[...], PLAIN)
    unit, inverse = norm_parts(x_ref[...].astype(F32))
    ig_ref[...] = dm_ref[...] + norm_back(unit, inverse, dn, vec_ref[0:1, :])
    row = lambda a: jnp.sum(a, axis=0, keepdims=True)
    sums = jnp.concatenate([row(dn * unit), row(dn)], axis=0)

    @pl.when(step == 0)
    def _():
        width = dn.shape[1]
        half = width // 2
        out_ref[0:2] = sums
        out_ref[2:4] = sums_ref[0:2]
        out_ref[4:7] = gb_ref[0:3]
        out_ref[7:8] = sums_ref[2:3]
        for i in range(4):
            out_ref[8 + i:9 + i] = up_ref[:, i * width:(i + 1) * width]
        out_ref[12:13] = sums_ref[3:4]
        lane = lax.broadcasted_iota(jnp.int32, (width, half), 0)
        slot = lax.broadcasted_iota(jnp.int32, (width, half), 1)
        pick = jnp.where((lane // 64 == slot // 32) & (lane % 32 == slot % 32), 1.0, 0.0)
        both = lax.dot_general(gf_ref[...], pick, PLAIN, precision=lax.Precision.HIGHEST, preferred_element_type=F32)
        out_ref[13:14, :half] = both[0:1]
        out_ref[13:14, half:] = both[1:2]

    @pl.when(step > 0)
    def _():
        out_ref[0:2] += sums


def input_back(dq, dk, dv, weights, x, dm, vectors, sums, grad_bias, grad_freq, bias_up):
    count, width = x.shape
    tile = 256
    part = pl.BlockSpec((tile, width), lambda i: (i, 0))
    whole = lambda i: (0, 0)
    fixed = lambda a: pl.BlockSpec(a.shape, whole)
    return pl.pallas_call(
        input_kernel,
        grid=(count // tile,),
        in_specs=[part] * 3 + [pl.BlockSpec((3 * width, width), whole), part, part]
        + [fixed(a) for a in (vectors, sums, grad_bias, grad_freq, bias_up)],
        out_specs=[part, fixed(vectors)],
        out_shape=[jax.ShapeDtypeStruct((count, width), F32), jax.ShapeDtypeStruct(vectors.shape, F32)],
        compiler_params=pltpu.CompilerParams(vmem_limit_bytes=56 * 2**20),
        cost_estimate=SHORT,
        name="input_back",
    )(dq, dk, dv, weights, x, dm, vectors, sums, grad_bias, grad_freq, bias_up)


def fold_kernel(count, pos_ref, *refs):
    out_ref = refs[-1]
    ways = out_ref.shape[0]
    for k in range(ways):
        total = refs[k][...].astype(F32) + refs[ways + k][...].astype(F32)
        for more in refs[2 * ways:-1]:
            total = total + more[0].astype(F32)
        out_ref[k] = total.astype(BF16)


def fold(pos, keep, got, ways, more=()):
    count, rows, width = keep.shape
    some = count // 2
    quarter = [pl.BlockSpec((some, rows // 2, width // 2), lambda i, pos, k=k: (i, pos[k, 0], pos[k, 1])) for k in ways]
    extra = [pl.BlockSpec((1, some, rows // 2, width // 2), lambda i, pos, at=at: (at, i, 0, 0)) for _, at in more]
    out = pl.BlockSpec((len(ways), some, rows // 2, width // 2), lambda i, pos: (0, i, 0, 0))
    shape = jax.ShapeDtypeStruct((len(ways), count, rows // 2, width // 2), BF16)
    return pl.pallas_call(
        functools.partial(fold_kernel, len(more)),
        grid_spec=pltpu.PrefetchScalarGridSpec(
            num_scalar_prefetch=1, grid=(count // some,), in_specs=quarter * 2 + extra, out_specs=out),
        compiler_params=pltpu.CompilerParams(vmem_limit_bytes=40 * 2**20),
        out_shape=shape,
        cost_estimate=SHORT,
        name="fold",
    )(pos, *([keep] * len(ways)), *([got] * len(ways)), *[a for a, _ in more])


def pack_kernel(owner_ref, *refs):
    early, late, out_ref, total_s = refs[:4], refs[4:8], refs[8], refs[9]
    square = None
    start = 0
    for parts in (early, late):
        total = parts[0][...].astype(F32)
        for part in parts[1:]:
            total = total + part[...].astype(F32)
        total_s[start:start + total.shape[0]] = total.astype(BF16)
        start += total.shape[0]
        more = jnp.sum(total * total).reshape(1, 1)
        square = more if square is None else square + more
    rows = total_s.shape[1]
    lane = lax.broadcasted_iota(jnp.int32, (8, out_ref.shape[2]), 1)
    one, two, three = split3(square)
    extra = jnp.where(lane == 0, one, jnp.where(lane == 1, two, jnp.where(lane == 2, three, 0.0))).astype(BF16)
    for p in range(out_ref.shape[0]):
        out_ref[p, :rows] = total_s[lax.div(owner_ref[p], 2)]
        out_ref[p, rows:] = extra


def pack(owner, early, late):
    blocks = early[0].shape[0] + late[0].shape[0]
    rows, cols = early[0].shape[1:]
    vmem = pl.BlockSpec(memory_space=pltpu.VMEM)
    return pl.pallas_call(
        pack_kernel,
        in_specs=[pl.BlockSpec(memory_space=pltpu.SMEM)] + [vmem] * 8,
        out_specs=vmem,
        out_shape=jax.ShapeDtypeStruct((owner.shape[0], rows + 8, cols), BF16),
        scratch_shapes=[pltpu.VMEM((blocks, rows, cols), BF16)],
        compiler_params=pltpu.CompilerParams(vmem_limit_bytes=32 * 2**20),
        cost_estimate=SHORT,
        name="pack",
    )(owner, *early, *late)


def clip_of(square, vec):
    norm = jnp.sqrt(square + jnp.sum(vec * vec).reshape(1, 1))
    return norm, jnp.minimum(1.0, 1.0 / (norm + 1e-06))


def adam_kernel(own_ref, a_ref, b_ref, as_ref, bs_ref, vt_ref, vw_ref, vm_ref, vv_ref, w_ref, m_ref, v_ref,
                g_out, v_out, w_out, vg_out, vv_out, vw_out, norm_out):
    def squares(ref):
        block = ref[...].astype(F32)
        lane = lax.broadcasted_iota(jnp.int32, block.shape, 4)
        row = lax.broadcasted_iota(jnp.int32, block.shape, 3)
        return jnp.sum(jnp.where((lane < 3) & (row == 0), block, 0.0)).reshape(1, 1)

    norm, clip = clip_of(squares(as_ref) + squares(bs_ref), vt_ref[...])
    own = own_ref[0] > 0
    grad = jnp.where(own, a_ref[:, 0, 0].astype(F32), b_ref[:, 0, 0].astype(F32))
    grad = grad[:, :w_ref.shape[0] // grad.shape[0]].reshape(w_ref.shape) * clip
    second, weight = adam(w_ref[...], m_ref[...], v_ref[...], grad, 0.02, 0.05)
    g_out[...] = grad
    v_out[...] = second
    w_out[...] = weight

    @pl.when((pl.program_id(0) == 0) & (pl.program_id(1) == 0))
    def _():
        vec_grad = vt_ref[...] * clip
        second, weight = adam(vw_ref[...], vm_ref[...], vv_ref[...], vec_grad, 0.2, 0.0)
        vg_out[...] = vec_grad
        vv_out[...] = second
        vw_out[...] = weight
        norm_out[...] = norm


def adam_rows(own, mine, other, vec_total, vectors, vec_first, vec_second, weight, first, second):
    rows, width = weight.shape
    deep, tall, wide, piece, cols = mine.shape
    part = pl.BlockSpec((deep, 1, 1, piece, cols), lambda y, x: (0, y, x, 0, 0))
    marks = pl.BlockSpec((deep, tall, wide, 8, 128), lambda y, x: (0, 0, 0, piece // 8 - 1, 0))
    flat = pl.BlockSpec((rows // tall, width // wide), lambda y, x: (y, x))
    vec = pl.BlockSpec(vectors.shape, lambda y, x: (0, 0))
    shape = jax.ShapeDtypeStruct((rows, width), F32)
    small = jax.ShapeDtypeStruct(vectors.shape, F32)
    return pl.pallas_call(
        adam_kernel,
        grid=(tall, wide),
        in_specs=[pl.BlockSpec(memory_space=pltpu.SMEM), part, part, marks, marks] + [vec] * 4 + [flat] * 3,
        out_specs=[flat] * 3 + [vec] * 3 + [pl.BlockSpec((1, 1), lambda y, x: (0, 0))],
        out_shape=[shape] * 3 + [small] * 3 + [jax.ShapeDtypeStruct((1, 1), F32)],
        compiler_params=pltpu.CompilerParams(vmem_limit_bytes=60 * 2**20),
        cost_estimate=SHORT,
        name="adam",
    )(own, mine, other, mine, other, vec_total, vectors, vec_first, vec_second, weight, first, second)


from jax.sharding import PartitionSpec as P

HEADS = 12
STEP = 7


def place_tokens(heights, widths, count):
    sizes = heights * widths
    ends = jnp.cumsum(sizes)
    starts = ends - sizes
    places = jnp.arange(count, dtype=jnp.int32)
    segment = jnp.sum((places[:, None] >= ends[None, :]).astype(jnp.int32), axis=1)
    slots = jnp.arange(heights.shape[0], dtype=jnp.int32)
    picks = (segment[:, None] == slots[None, :]).astype(jnp.int32)
    begin = jnp.sum(picks * starts[None, :], axis=1)
    across = jnp.maximum(jnp.sum(picks * widths[None, :], axis=1), 1)
    offset = places - begin
    live = places < ends[-1]
    return (segment, offset // across, offset % across, live)


def adam(weight, first, second, grad, rate, decay):
    first_new = 0.5 * first + 0.5 * grad
    second_new = 0.5 * second + 0.5 * grad * grad
    correct = 1.0 - 0.5**STEP
    direction = first_new / correct / (jnp.sqrt(second_new / correct) + 1e-08)
    return (second_new, weight - rate * (direction + decay * weight))


def pairwise(bits, total):
    return [(i, i ^ bits) for i in range(total)]


def sum_part(value, devices, step, stop):
    while step < stop:
        value = value + lax.ppermute(value, "dp", pairwise(step, devices))
        step *= 2
    return value


CORES = ("group", "dp")
SWAP = [(0, 1), (1, 0)]


def cross(value, bit0, bit1, devices):
    perm = [(i, i ^ (bit0 if i < devices else bit1)) for i in range(2 * devices)]
    return lax.ppermute(value, CORES, perm)


def along_z(values, devices):
    return [
        lax.ppermute(v, "dp", [(i, (i + 4 * (s + 1)) % devices) for i in range(devices)])
        for s, v in enumerate(values)
    ]


def along_line(value, devices, step, up):
    last = devices // 4
    perm = []
    for z in range(last):
        near = z - 1 if up else z + 1
        far = z - step if up else z + step
        if 0 <= far < last:
            perm += [(4 * near + i, 4 * z + i) for i in range(4)]
    return lax.ppermute(value, "dp", perm)


def gather_pieces(master, inverse, core, me, devices, freqs, make_tables):
    tie = lax.optimization_barrier
    block_rows, width = master.shape
    half = block_rows // 2
    mine = lax.dynamic_slice_in_dim(master, core * half, half, 0).astype(BF16)
    large = mine[:LARGE]
    small = mine[LARGE:]
    z = me // 4
    deep = lax.rem(z - inverse // 4 + 4, 4)
    apart = me ^ inverse
    one = jnp.where(core == 0, apart & 1, (apart >> 1) & 1)
    two = jnp.where(core == 0, (apart >> 1) & 1, apart & 1)
    slots = jnp.stack([
        8 * two + 4 * one + deep,
        4 * deep + 2 * two + one,
        8 * one + 4 * two + deep,
        4 * deep + 2 * one + two,
    ]).astype(jnp.int32)
    up = along_z([large] * 3, devices)
    small = jnp.stack([small, cross(small, 1, 2, devices)])
    small, freqs = tie((small, freqs))
    small = jnp.concatenate([small, cross(small, 2, 1, devices)])
    large = jnp.stack([large] + up)
    large, small, tables, slots = tie((large, small, make_tables(freqs), slots))
    first = cross(large, 1, 2, devices)
    ups = [along_line(small, devices, 1, True)]
    downs = [along_line(small, devices, 1, False)]
    first, ups[0], downs[0] = tie((first, ups[0], downs[0]))
    first = jnp.concatenate([large, first])
    second = cross(first, 2, 1, devices)
    for step in (2, 3):
        ups.append(along_line(ups[-1], devices, step, True))
        downs.append(along_line(downs[-1], devices, step, False))
    small = jnp.concatenate([small] + [jnp.where(z >= s, ups[s - 1], downs[3 - s]) for s in (1, 2, 3)])
    other = [lax.ppermute(a, "group", SWAP) for a in (first, second, small)]
    return (first, second, small, *other), slots, tables


def quarters(core, me):
    x, y = me & 1, (me >> 1) & 1
    one = jnp.where(core == 0, x, y)
    two = jnp.where(core == 0, y, x)
    pairs = [(1 - one, 1 - two), (1 - one, two), (one, 1 - two), (one, two)]
    return jnp.stack([
        jnp.stack([jnp.where(core == 0, b, a), jnp.where(core == 0, a, b)]) for a, b in pairs
    ]).astype(jnp.int32)


def sum_z(low, me, devices):
    count, rows, cols = low.shape
    z = me // 4
    low = low.reshape(count, 4, rows // 4, cols)
    pick = lambda at: lax.dynamic_index_in_dim(low, at, 1, keepdims=False)
    return (pick(z), *along_z([pick(lax.rem(z + s, 4)) for s in (1, 2, 3)], devices))


def reduce_plain(local_mat, owner_block, devices):
    rows, width = local_mat.shape
    block_rows = rows // devices
    term = local_mat.reshape(devices, block_rows, width)[owner_block].reshape(rows, width)
    share = lax.psum_scatter(term.astype(F32), "dp", scatter_dimension=0, tiled=True)
    return lax.psum(share.astype(BF16), "group").astype(F32)


def local(
    tokens,
    cotangent,
    grid_h,
    grid_w,
    owner_block,
    master,
    first_mom,
    second_mom,
    vectors,
    vec_first,
    vec_second,
):
    devices = lax.axis_size("dp")
    core = lax.axis_index("group")
    me = lax.axis_index("dp")
    count = tokens.shape[1]
    width = tokens.shape[2]
    heads = HEADS
    head_dim = width // heads
    half = head_dim // 2
    block_rows = master.shape[0]
    stack = devices * block_rows
    quick = devices == 16 and block_rows == 2 * (LARGE + SMALL) and width % 256 == 0
    inverse = jnp.argsort(owner_block)
    segment, rows_pos, cols_pos, live = place_tokens(grid_h[0], grid_w[0], count)
    x = tokens[0]

    def make_tables(freqs):
        def spread(part):
            return jnp.broadcast_to(part.reshape(heads, 1, half), (heads, 2, half)).reshape(1, width)

        down = rows_pos.astype(F32)[:, None]
        right = cols_pos.astype(F32)[:, None]
        angle = down * spread(freqs[: width // 2]) + right * spread(freqs[width // 2 :])
        lower = (jnp.arange(width) % head_dim < half)[None]
        cosine = jnp.cos(angle)
        sine = jnp.sin(angle)
        sine = jnp.where(lower, -sine, sine)
        ids = jnp.arange(128)[None]
        match = segment[:, None] == ids
        key_mask = jnp.where(match | ((ids >= 8) & (ids < 11)), 1.0, 0.0).astype(BF16)
        query_mask = jnp.where((ids < 8) & ~match, MASKED, 0.0).astype(BF16)
        places = jnp.stack([rows_pos, cols_pos], axis=1).astype(F32)
        grad_two = jnp.where(live[:, None], cotangent[0], jnp.zeros((), BF16))
        unit, _ = norm_parts(x.astype(F32))
        first_in = (unit * vectors[0] + vectors[1]).astype(BF16)
        return (cosine, sine, key_mask, query_mask, places, grad_two, first_in,
                vectors[4:7].reshape(1, 3 * width), vectors[8:12].reshape(1, 4 * width))

    if quick:
        weights, slots, tables = gather_pieces(master, inverse, core, me, devices, vectors[13], make_tables)
    else:
        low = lax.all_gather(master.astype(BF16), "dp", axis=0, tiled=True)
        weights = low.reshape(devices, block_rows, width)[inverse].reshape(stack, width)
        slots = jnp.zeros((4, devices), jnp.int32)
        tables = make_tables(vectors[13])
    cosine, sine, key_mask, query_mask, places, grad_two, first_in, bias_qkv, bias_one = tables
    here = core.reshape(1).astype(jnp.int32)
    query, key, value, attn, stat, *placed = attend(
        here, slots, first_in, bias_qkv,
        cosine, sine, query_mask, key_mask, weights, stack,
    )
    if quick:
        weights = placed[0]
    whole_rows = block_rows if quick else 0
    block_out, grad_middle, grad_attn, sums, bias_up, keep_mlp, give_mlp = mlp(
        here, x, attn, grad_two, vectors, weights, bias_one, whole_rows
    )
    pairs = width // 128
    tie = lax.optimization_barrier
    if quick:
        pos = quarters(core, me)
        got = lax.ppermute(give_mlp, "group", SWAP)
    back = None
    cuts = (0, 1, pairs - 1, pairs)
    for start, stop in zip(cuts[:-1], cuts[1:]):
        back = attend_back(
            start, stop, back, query, key, value, grad_attn, attn, stat, cosine, sine, query_mask, key_mask, places
        )
        if quick and start == 0:
            send, back = tie((fold(pos, keep_mlp, got, (0, 1)), back))
            came = cross(send, 1, 2, devices)
        if quick and start == 1:
            send, back = tie((fold(pos, keep_mlp, got, (2,), ((came, 0),)), back))
            again = cross(send, 2, 1, devices)
    grad_q, grad_k, grad_v, grad_bias, grad_freq = back
    keep_qkv, give_qkv = qkv_grad(here, grad_q, grad_k, grad_v, first_in, whole_rows)
    if quick:
        again, give_qkv = tie((again, give_qkv))
        low, grad_v, give_qkv = tie((fold(pos, keep_mlp, got, (3,), ((came, 1), (again, 0)))[0], grad_v, give_qkv))
        late = sum_z(low, me, devices)
    if quick:
        got_qkv = lax.ppermute(give_qkv, "group", SWAP)
        send = fold(pos, keep_qkv, got_qkv, (0, 1))
        third = send.shape[2] // 3
        send = [send[:, :, third * i:third * (i + 1)] for i in range(3)]
        send, grad_v = tie((send, grad_v))
    input_grad, local_vec = input_back(
        grad_q, grad_k, grad_v, weights, x, grad_middle, vectors, sums, grad_bias, grad_freq, bias_up
    )
    if quick:
        send[2], local_vec = tie((send[2], local_vec))
        came = [cross(a, 1, 2, devices) for a in send]
        came, local_vec, late = tie((came, local_vec, late))
        came = jnp.concatenate(came, axis=2)
        again = cross(fold(pos, keep_qkv, got_qkv, (2,), ((came, 0),)), 2, 1, devices)
        vec_total = sum_part(local_vec + lax.ppermute(local_vec, "group", SWAP), devices, 4, devices)
        again, vec_total = tie((again, vec_total))
        early = sum_z(fold(pos, keep_qkv, got_qkv, (3,), ((came, 1), (again, 0)))[0], me, devices)
        early, vec_total = tie((early, sum_part(vec_total, devices, 1, 4)))
        load = pack(owner_block, early, late)
        mine = lax.all_to_all(load, "dp", 0, 0, tiled=True)
        other = lax.ppermute(mine, "group", SWAP)
        shape = (devices // 4, 2, 2, *load.shape[1:])
        own = (owner_block[me] % 2 == core).astype(jnp.int32).reshape(1)
        mat_grad, mat_second, mat_weight, vec_grad, vec_second_new, vec_weight, norm = adam_rows(
            own, mine.reshape(shape), other.reshape(shape), vec_total, vectors, vec_first, vec_second,
            master, first_mom, second_mom,
        )
        grad_norm = norm.reshape(())
    else:
        vec_total = lax.psum(local_vec, CORES)
        share = reduce_plain(jnp.concatenate([keep_qkv, keep_mlp]), owner_block, devices)
        square = lax.psum(jnp.sum(share * share), "dp")
        grad_norm = jnp.sqrt(square + jnp.sum(vec_total * vec_total))
        clip = jnp.minimum(1.0, 1.0 / (grad_norm + 1e-06))
        mat_grad = share * clip
        mat_second, mat_weight = adam(master, first_mom, second_mom, mat_grad, 0.02, 0.05)
        vec_grad = vec_total * clip
        vec_second_new, vec_weight = adam(vectors, vec_first, vec_second, vec_grad, 0.2, 0.0)
    return (
        block_out[None],
        input_grad[None],
        mat_grad,
        mat_second,
        mat_weight,
        vec_grad,
        vec_second_new,
        vec_weight,
        grad_norm,
    )


def solution(mesh):
    return jax.shard_map(
        local,
        mesh=mesh,
        in_specs=(
            P("group", "dp", None),
            P("group", "dp", None),
            P("group", "dp"),
            P("group", "dp"),
            P(),
            P("dp", None),
            P("dp", None),
            P("dp", None),
            P(),
            P(),
            P(),
        ),
        out_specs=(
            P("group", "dp", None),
            P("group", "dp", None),
            P("dp", None),
            P("dp", None),
            P("dp", None),
            P(),
            P(),
            P(),
            P(),
        ),
        check_vma=False,
    )
```

```python
import functools
import jax
import jax.numpy as jnp
from jax import lax
from jax.experimental import pallas as pl
from jax.experimental.pallas import tpu as pltpu

F32 = jnp.float32
BF16 = jnp.bfloat16
LAST = (((1,), (1,)), ((), ()))
FIRST = (((0,), (0,)), ((), ()))
PLAIN = (((1,), (0,)), ((), ()))
MASKED = -1e9
SHORT = pl.CostEstimate(flops=1000, bytes_accessed=1000, transcendentals=0)


def mm(left, right, dims):
    return lax.dot_general(left, right, dims, preferred_element_type=F32)


def norm_parts(value):
    centre = value - jnp.mean(value, axis=-1, keepdims=True)
    spread = jnp.mean(centre * centre, axis=-1, keepdims=True)
    inverse = lax.rsqrt(spread + 1e-6)
    return centre * inverse, inverse


def norm_back(unit, inverse, grad, gain):
    scaled = grad * gain
    first = jnp.mean(scaled, axis=-1, keepdims=True)
    second = jnp.mean(scaled * unit, axis=-1, keepdims=True)
    return inverse * (scaled - first - unit * second)


def swap_halves(value):
    lane = lax.broadcasted_iota(jnp.int32, value.shape, 1)
    return jnp.where(
        lane % 64 < 32, pltpu.roll(value, 96, 1), pltpu.roll(value, 32, 1)
    )


def split3(value):
    one = value.astype(BF16).astype(F32)
    rest = value - one
    two = rest.astype(BF16).astype(F32)
    return one, two, rest - two


LARGE = 208
SMALL = 80


def place_pieces(core, slot_ref, mine, other, block, side, dst, sem):
    for which, (first, second, small) in enumerate((mine, other)):
        @pl.when((core == side) if which == 0 else (core != side))
        def _():
            large_slot = slot_ref[2 * which, block]
            small_slot = slot_ref[2 * which + 1, block]

            @pl.when(large_slot < 8)
            def _():
                pltpu.make_async_copy(first.at[large_slot], dst(0, LARGE), sem).start()

            @pl.when(large_slot >= 8)
            def _():
                pltpu.make_async_copy(second.at[large_slot - 8], dst(0, LARGE), sem).start()

            pltpu.make_async_copy(small.at[small_slot], dst(LARGE, SMALL), sem).start()


def attend_kernel(blocks, core_ref, slot_ref, n1_ref, bq_ref, bk_ref, bv_ref,
                  cos_ref, sin_ref, qm_ref, km_ref, *rest):
    if blocks:
        mine, other = rest[0:3], rest[3:6]
        q_ref, k_ref, v_ref, attn_ref, stat_ref, w_ref, w_s, near, far, back = rest[6:]
    else:
        w_ref, q_ref, k_ref, v_ref, attn_ref, stat_ref, w_s, near = rest
    count, width = n1_ref.shape
    step = pl.program_id(0)

    @pl.when(step == 0)
    def _():
        if blocks:
            core = core_ref[0]
            rows = w_ref.shape[0] // blocks

            def start(block, sem):
                for side in (0, 1):
                    def dst(offset, size):
                        base = block * rows + side * (rows // 2) + offset
                        return w_s.at[pl.ds(pl.multiple_of(base, 16), size)]
                    place_pieces(core, slot_ref, mine, other, block, side, dst, sem)

            def near_block(block, carry):
                start(block, near)
                return carry

            def far_block(block, carry):
                start(block, far)
                return carry

            lax.fori_loop(0, 3 * width // rows, near_block, 0)
            lax.fori_loop(3 * width // rows, blocks, far_block, 0)
        else:
            pltpu.make_async_copy(w_ref.at[pl.ds(0, 3 * width)], w_s, near).start()
        head = w_s.at[pl.ds(0, 3 * width)]
        pltpu.make_async_copy(head, head, near).wait()

    if blocks:
        @pl.when(step == 1)
        def _():
            tail = w_s.at[pl.ds(3 * width, w_s.shape[0] - 3 * width)]
            pltpu.make_async_copy(tail, tail, far).wait()
            pltpu.make_async_copy(w_s, w_ref, back).start()

    def third(j):
        return w_s[pl.ds(pl.multiple_of(j * width + step * 128, 128), 128), :]

    w = jnp.concatenate([third(0), third(1), third(2)], axis=0)
    qkv = mm(n1_ref[...], w, LAST)
    q = qkv[:, :128] + bq_ref[...]
    k = qkv[:, 128:256] + bk_ref[...]
    v = (qkv[:, 256:] + bv_ref[...]).astype(BF16)
    c = cos_ref[...]
    s = sin_ref[...]
    qr = ((q * c + swap_halves(q) * s).astype(BF16).astype(F32) * 0.125).astype(BF16)
    kr = (k * c + swap_halves(k) * s).astype(BF16)
    q_ref[...] = qr
    k_ref[...] = kr
    v_ref[...] = v
    lane = lax.broadcasted_iota(jnp.int32, (1, 128), 1)
    k_aug = jnp.concatenate([kr, km_ref[...]], axis=1)
    v_aug = jnp.concatenate([v, jnp.ones((count, 128), BF16)], axis=1)
    zero = jnp.zeros((), BF16)
    tile = 256
    for i in range(count // tile):
        rows = pl.ds(i * tile, tile)
        out = None
        stats = []
        for h in (0, 1):
            mine_lanes = (lane // 64) == h
            qa = jnp.concatenate(
                [jnp.where(mine_lanes, qr[i * tile:(i + 1) * tile], zero), qm_ref[rows, :]], axis=1)
            scores = mm(qa, k_aug, LAST)
            top = jnp.max(scores, axis=-1, keepdims=True)
            e = jnp.exp(scores - top).astype(BF16)
            o = mm(e, v_aug, PLAIN)
            total = o[:, 128:]
            o = o[:, :128] / total
            out = o if out is None else jnp.where(lane < 64, out, o)
            stats.append(top + jnp.log(total[:, :1]))
        attn_ref[rows, :] = out.astype(BF16)
        stat_ref[rows, :] = jnp.where(lane < 64, stats[0], stats[1])

    if blocks:
        @pl.when(step == pl.num_programs(0) - 1)
        def _():
            pltpu.make_async_copy(w_s, w_ref, back).wait()


def attend(core, slots, n1, bqkv, cos, sin, qm, km, weights, stack):
    count, width = n1.shape
    pairs = width // 128
    pieces = isinstance(weights, tuple)
    blocks = slots.shape[1] if pieces else 0
    whole = lambda p: (0, 0)
    col = lambda p: (0, p)
    smem = pl.BlockSpec(memory_space=pltpu.SMEM)
    hbm = pl.BlockSpec(memory_space=pl.ANY)
    given = weights if pieces else (weights,)
    specs = [smem, smem] + [
        pl.BlockSpec((count, width), whole),
        pl.BlockSpec((1, 128), col),
        pl.BlockSpec((1, 128), lambda p: (0, p + pairs)),
        pl.BlockSpec((1, 128), lambda p: (0, p + 2 * pairs)),
        pl.BlockSpec((count, 128), col),
        pl.BlockSpec((count, 128), col),
        pl.BlockSpec((count, 128), whole),
        pl.BlockSpec((count, 128), whole),
    ] + [hbm] * len(given)
    outs = [pl.BlockSpec((count, 128), col)] * 5
    shape = lambda d: jax.ShapeDtypeStruct((count, width), d)
    shapes = [shape(BF16)] * 4 + [shape(F32)]
    scratch = [pltpu.VMEM((stack if pieces else 3 * width, width), BF16), pltpu.SemaphoreType.DMA]
    if pieces:
        outs.append(hbm)
        shapes.append(jax.ShapeDtypeStruct((stack, width), BF16))
        scratch += [pltpu.SemaphoreType.DMA] * 2
    return pl.pallas_call(
        functools.partial(attend_kernel, blocks),
        grid=(pairs,),
        in_specs=specs,
        out_specs=outs,
        out_shape=shapes,
        scratch_shapes=scratch,
        compiler_params=pltpu.CompilerParams(vmem_limit_bytes=56 * 2**20),
        cost_estimate=SHORT,
        name="attend",
    )(core, slots, n1, bqkv, bqkv, bqkv, cos, sin, qm, km, *given)


def gelu_both(x):
    cdf = 0.5 + 0.5 * lax.erf(x * 0.7071067811865476)
    return x * cdf, cdf + x * jnp.exp(x * x * -0.5) * 0.3989422804014327


def send_rows(core, block_rows, stage, row, base, keep_ref, give_ref, sem):
    if not block_rows:
        rows = stage.shape[0]
        pltpu.make_async_copy(
            stage, keep_ref.at[pl.ds(pl.multiple_of(row - base, 64), rows)], sem
        ).start()
        return

    def one(index, carry):
        at = row + 64 * index
        block = lax.div(at, block_rows)
        inner = pl.ds(pl.multiple_of(at - block * block_rows, 64), 64)
        slot = lax.div(block, 2) - base // 2
        source = stage.at[pl.ds(pl.multiple_of(64 * index, 64), 64)]
        own = lax.rem(block, 2) == core

        @pl.when(own)
        def _():
            pltpu.make_async_copy(source, keep_ref.at[slot, inner], sem).start()

        @pl.when(jnp.logical_not(own))
        def _():
            pltpu.make_async_copy(source, give_ref.at[slot, inner], sem).start()

        return carry

    lax.fori_loop(0, stage.shape[0] // 64, one, 0)


def mlp_kernel(block_rows, base, core_ref, x_ref, at_ref, dz_ref, vec_ref, wo_ref, w1_ref, w2_ref, b1_ref,
               out_ref, dm_ref, da_ref, sums_ref, gb_ref, keep_ref, give_ref,
               middle_s, n2_s, acc_s, stage_s, proj_s, sems):
    step = pl.program_id(0)
    last = pl.num_programs(0) - 1
    count, width = x_ref.shape
    core = core_ref[0]
    tile = w1_ref.shape[0]

    @pl.when(step == 0)
    def _():
        middle = x_ref[...].astype(F32) + mm(at_ref[...], wo_ref[...], LAST) + vec_ref[7:8, :]
        middle_s[...] = middle
        unit, _ = norm_parts(middle)
        n2_s[...] = (unit * vec_ref[2:3, :] + vec_ref[3:4, :]).astype(BF16)
        acc_s[...] = jnp.zeros_like(acc_s)
        dm_ref[...] = jnp.zeros_like(dm_ref)

    slot = lax.rem(step, 2)

    @pl.when(step >= 2)
    def _():
        pltpu.make_async_copy(stage_s.at[slot], stage_s.at[slot], sems.at[slot]).wait()

    n2 = n2_s[...]
    dz = dz_ref[...]
    w1 = w1_ref[...]
    w2 = w2_ref[...]
    pre = mm(w1, n2, LAST) + b1_ref[...].reshape(tile, 1)
    back = mm(w2, dz, LAST)
    act, slope = gelu_both(pre)
    hidden = act.astype(BF16)
    stage_s[slot, 1] = mm(hidden, dz, PLAIN).astype(BF16)
    dpre = (back * slope).astype(BF16)
    gb_ref[...] = jnp.sum(dpre.astype(F32), axis=1, keepdims=True).reshape(1, tile)
    stage_s[slot, 0] = mm(dpre, n2, PLAIN).astype(BF16)
    acc_s[...] += mm(hidden, w2, FIRST)
    dm_ref[...] += mm(dpre, w1, FIRST)
    for j in (0, 1):
        send_rows(core, block_rows, stage_s.at[slot, j], (4 + 4 * j) * width + step * tile,
                  base, keep_ref, give_ref, sems.at[slot])

    @pl.when(step == last)
    def _():
        middle = middle_s[...]
        out_ref[...] = (middle + acc_s[...] + vec_ref[12:13, :]).astype(BF16)
        unit, inverse = norm_parts(middle)
        dn = dm_ref[...]
        dy = dz_ref[...].astype(F32)
        dm = dy + norm_back(unit, inverse, dn, vec_ref[2:3, :])
        dm_ref[...] = dm
        low = dm.astype(BF16)
        row = lambda a: jnp.sum(a, axis=0, keepdims=True)
        sums_ref[...] = jnp.concatenate(
            [row(dn * unit), row(dn), row(low.astype(F32)), row(dy), jnp.zeros((4, width), F32)], axis=0)
        proj_s[...] = mm(low, at_ref[...], FIRST).astype(BF16)
        send_rows(core, block_rows, proj_s, 3 * width, base, keep_ref, give_ref, sems.at[2])
        da_ref[...] = mm(low, wo_ref[...], PLAIN).astype(BF16)
        pltpu.make_async_copy(stage_s.at[slot], stage_s.at[slot], sems.at[slot]).wait()
        pltpu.make_async_copy(stage_s.at[1 - slot], stage_s.at[1 - slot], sems.at[1 - slot]).wait()
        pltpu.make_async_copy(proj_s, proj_s, sems.at[2]).wait()


def grad_shapes(block_rows, rows, width):
    if block_rows:
        half = jax.ShapeDtypeStruct((rows // block_rows // 2, block_rows, width), BF16)
        return [half, half]
    return [jax.ShapeDtypeStruct((rows, width), BF16), jax.ShapeDtypeStruct((16, width), BF16)]


def mlp(core, x, attn, dz, vectors, weights, b1, block_rows, tile=512):
    count, width = x.shape
    units = 4 * width
    stack = weights.shape[0]
    base = 3 * width // block_rows if block_rows else 3 * width
    whole = lambda t: (0, 0)
    big = pl.BlockSpec((count, width), whole)
    hbm = pl.BlockSpec(memory_space=pl.ANY)
    return pl.pallas_call(
        functools.partial(mlp_kernel, block_rows, base),
        grid=(units // tile,),
        in_specs=[pl.BlockSpec(memory_space=pltpu.SMEM), big, big, big, pl.BlockSpec(vectors.shape, whole),
                  pl.BlockSpec((width, width), lambda t: (3, 0)),
                  pl.BlockSpec((tile, width), lambda t: (4 * width // tile + t, 0)),
                  pl.BlockSpec((tile, width), lambda t: (8 * width // tile + t, 0)),
                  pl.BlockSpec((1, tile), lambda t: (0, t))],
        out_specs=[big, big, big, pl.BlockSpec((8, width), whole), pl.BlockSpec((1, tile), lambda t: (0, t)), hbm, hbm],
        out_shape=[
            jax.ShapeDtypeStruct((count, width), BF16),
            jax.ShapeDtypeStruct((count, width), F32),
            jax.ShapeDtypeStruct((count, width), BF16),
            jax.ShapeDtypeStruct((8, width), F32),
            jax.ShapeDtypeStruct((1, units), F32),
        ] + grad_shapes(block_rows, stack - 3 * width, width),
        scratch_shapes=[
            pltpu.VMEM((count, width), F32),
            pltpu.VMEM((count, width), BF16),
            pltpu.VMEM((count, width), F32),
            pltpu.VMEM((2, 2, tile, width), BF16),
            pltpu.VMEM((width, width), BF16),
            pltpu.SemaphoreType.DMA((3,)),
        ],
        compiler_params=pltpu.CompilerParams(vmem_limit_bytes=60 * 2**20),
        cost_estimate=SHORT,
        name="mlp",
    )(core, x, attn, dz, vectors, weights, weights, weights, b1)


def back_kernel(first, q_ref, k_ref, v_ref, da_ref, at_ref, stat_ref, cos_ref, sin_ref,
                qm_ref, km_ref, pos_ref, *rest):
    dq_ref, dk_ref, dv_ref, gb_ref, gf_ref = rest if first else rest[5:]
    count = q_ref.shape[0]
    lane = lax.broadcasted_iota(jnp.int32, (1, 128), 1)
    zero = jnp.zeros((), BF16)
    q = q_ref[...]
    k = k_ref[...]
    v = v_ref[...]
    da = da_ref[...]
    prod = da.astype(F32) * at_ref[...].astype(F32)
    qm = qm_ref[...].astype(F32)
    k_aug = jnp.concatenate([k, km_ref[...]], axis=1)
    v_aug = jnp.concatenate([v, jnp.broadcast_to((lane < 2).astype(BF16), (count, 128))], axis=1)
    tile = 256
    dq = dk = dv = None
    for h in (0, 1):
        mine = (lane // 64) == h
        qh = jnp.where(mine, q, zero)
        kh = jnp.where(mine, k, zero)
        dah = jnp.where(mine, da, zero)
        delta = jnp.sum(jnp.where(mine, prod, 0.0), axis=-1, keepdims=True)
        d1, d2, _ = split3(delta)
        l1, l2, l3 = split3(stat_ref[:, 64 * h:64 * h + 1])
        extra = jnp.where(lane == 8, -l1, jnp.where(lane == 9, -l2, jnp.where(lane == 10, -l3, qm)))
        q_aug = jnp.concatenate([qh, extra.astype(BF16)], axis=1)
        da_aug = jnp.concatenate(
            [dah, jnp.where(lane == 0, -d1, jnp.where(lane == 1, -d2, 0.0)).astype(BF16)], axis=1)
        dks, dvs, dqh = [], [], None
        for i in range(count // tile):
            sl = slice(i * tile, (i + 1) * tile)
            p = jnp.exp(mm(k_aug[sl], q_aug, LAST))
            dp = mm(v_aug[sl], da_aug, LAST)
            ds = (p * dp).astype(BF16)
            dvs.append(mm(p.astype(BF16), dah, PLAIN))
            dks.append(mm(ds, qh, PLAIN))
            part = mm(ds, kh[sl], FIRST)
            dqh = part if dqh is None else dqh + part
        dkh = jnp.concatenate(dks, axis=0)
        dvh = jnp.concatenate(dvs, axis=0)
        dq = dqh if dq is None else dq + dqh
        dk = dkh if dk is None else dk + dkh
        dv = dvh if dv is None else dv + dvh
    dq = dq * 0.125
    c = cos_ref[...]
    s = sin_ref[...]
    turned = dq * swap_halves(q.astype(F32) * 8.0) + dk * swap_halves(k.astype(F32))
    turned = jnp.where(lane % 64 < 32, -turned, turned)
    row = lambda a: jnp.sum(a, axis=0, keepdims=True)
    gf_ref[...] = jnp.concatenate(
        [row(turned * pos_ref[:, 0:1]), row(turned * pos_ref[:, 1:2]), jnp.zeros((6, 128), F32)], axis=0)
    dqp = (dq * c - swap_halves(dq) * s).astype(BF16)
    dkp = (dk * c - swap_halves(dk) * s).astype(BF16)
    dvp = dv.astype(BF16)
    gb_ref[...] = jnp.concatenate(
        [row(dqp.astype(F32)), row(dkp.astype(F32)), row(dvp.astype(F32)), jnp.zeros((5, 128), F32)], axis=0)
    dq_ref[...] = dqp
    dk_ref[...] = dkp
    dv_ref[...] = dvp


def attend_back(start, stop, before, q, k, v, da, attn, stat, cos, sin, qm, km, pos):
    count, width = q.shape
    whole = lambda p: (0, 0)
    col = lambda p: (0, p + start)
    tall = pl.BlockSpec((count, 128), col)
    fixed = pl.BlockSpec((count, 128), whole)
    small = pl.BlockSpec((8, 128), col)
    in_specs = [tall] * 8 + [fixed] * 2 + [pl.BlockSpec((count, 2), whole)]
    operands = [q, k, v, da, attn, stat, cos, sin, qm, km, pos]
    aliases = {}
    if before is not None:
        aliases = {len(operands) + i: i for i in range(5)}
        in_specs += [pl.BlockSpec(memory_space=pl.ANY)] * 5
        operands += list(before)
    return pl.pallas_call(
        functools.partial(back_kernel, before is None),
        grid=(stop - start,),
        in_specs=in_specs,
        out_specs=[tall] * 3 + [small] * 2,
        out_shape=[jax.ShapeDtypeStruct((count, width), BF16)] * 3 + [jax.ShapeDtypeStruct((8, width), F32)] * 2,
        input_output_aliases=aliases,
        compiler_params=pltpu.CompilerParams(vmem_limit_bytes=56 * 2**20),
        cost_estimate=SHORT,
        name="attend_back",
    )(*operands)


def qkv_grad_kernel(block_rows, core_ref, dq_ref, dk_ref, dv_ref, n1_ref, keep_ref, give_ref, stage_s, sem):
    width = n1_ref.shape[1]
    cols = dq_ref.shape[1]
    step = pl.program_id(0)
    n1 = n1_ref[...]
    for j, ref in enumerate((dq_ref, dk_ref, dv_ref)):
        stage_s[step, j] = mm(ref[...], n1, FIRST).astype(BF16)
        send_rows(core_ref[0], block_rows, stage_s.at[step, j], j * width + step * cols, 0, keep_ref, give_ref, sem)

    @pl.when(step == pl.num_programs(0) - 1)
    def _():
        pltpu.make_async_copy(stage_s, stage_s, sem).wait()


def qkv_grad(core, dq, dk, dv, n1, block_rows):
    count, width = n1.shape
    cols = width // 2
    tall = pl.BlockSpec((count, cols), lambda p: (0, p))
    hbm = pl.BlockSpec(memory_space=pl.ANY)
    return pl.pallas_call(
        functools.partial(qkv_grad_kernel, block_rows),
        grid=(2,),
        in_specs=[pl.BlockSpec(memory_space=pltpu.SMEM)] + [tall] * 3 + [pl.BlockSpec((count, width), lambda p: (0, 0))],
        out_specs=[hbm, hbm],
        out_shape=grad_shapes(block_rows, 3 * width, width),
        scratch_shapes=[pltpu.VMEM((2, 3, cols, width), BF16), pltpu.SemaphoreType.DMA],
        compiler_params=pltpu.CompilerParams(vmem_limit_bytes=56 * 2**20),
        cost_estimate=SHORT,
        name="qkv_grad",
    )(core, dq, dk, dv, n1)


def input_kernel(dq_ref, dk_ref, dv_ref, w_ref, x_ref, dm_ref, vec_ref, sums_ref, gb_ref, gf_ref, up_ref, ig_ref, out_ref):
    step = pl.program_id(0)
    d = jnp.concatenate([dq_ref[...], dk_ref[...], dv_ref[...]], axis=1)
    dn = mm(d, w_ref[...], PLAIN)
    unit, inverse = norm_parts(x_ref[...].astype(F32))
    ig_ref[...] = dm_ref[...] + norm_back(unit, inverse, dn, vec_ref[0:1, :])
    row = lambda a: jnp.sum(a, axis=0, keepdims=True)
    sums = jnp.concatenate([row(dn * unit), row(dn)], axis=0)

    @pl.when(step == 0)
    def _():
        width = dn.shape[1]
        half = width // 2
        out_ref[0:2] = sums
        out_ref[2:4] = sums_ref[0:2]
        out_ref[4:7] = gb_ref[0:3]
        out_ref[7:8] = sums_ref[2:3]
        for i in range(4):
            out_ref[8 + i:9 + i] = up_ref[:, i * width:(i + 1) * width]
        out_ref[12:13] = sums_ref[3:4]
        lane = lax.broadcasted_iota(jnp.int32, (width, half), 0)
        slot = lax.broadcasted_iota(jnp.int32, (width, half), 1)
        pick = jnp.where((lane // 64 == slot // 32) & (lane % 32 == slot % 32), 1.0, 0.0)
        both = lax.dot_general(gf_ref[...], pick, PLAIN, precision=lax.Precision.HIGHEST, preferred_element_type=F32)
        out_ref[13:14, :half] = both[0:1]
        out_ref[13:14, half:] = both[1:2]

    @pl.when(step > 0)
    def _():
        out_ref[0:2] += sums


def input_back(dq, dk, dv, weights, x, dm, vectors, sums, grad_bias, grad_freq, bias_up):
    count, width = x.shape
    tile = 256
    part = pl.BlockSpec((tile, width), lambda i: (i, 0))
    whole = lambda i: (0, 0)
    fixed = lambda a: pl.BlockSpec(a.shape, whole)
    return pl.pallas_call(
        input_kernel,
        grid=(count // tile,),
        in_specs=[part] * 3 + [pl.BlockSpec((3 * width, width), whole), part, part]
        + [fixed(a) for a in (vectors, sums, grad_bias, grad_freq, bias_up)],
        out_specs=[part, fixed(vectors)],
        out_shape=[jax.ShapeDtypeStruct((count, width), F32), jax.ShapeDtypeStruct(vectors.shape, F32)],
        compiler_params=pltpu.CompilerParams(vmem_limit_bytes=56 * 2**20),
        cost_estimate=SHORT,
        name="input_back",
    )(dq, dk, dv, weights, x, dm, vectors, sums, grad_bias, grad_freq, bias_up)


def fold_kernel(count, pos_ref, *refs):
    out_ref = refs[-1]
    ways = out_ref.shape[0]
    for k in range(ways):
        total = refs[k][...].astype(F32) + refs[ways + k][...].astype(F32)
        for more in refs[2 * ways:-1]:
            total = total + more[0].astype(F32)
        out_ref[k] = total.astype(BF16)


def fold(pos, keep, got, ways, more=()):
    count, rows, width = keep.shape
    some = count // 2
    quarter = [pl.BlockSpec((some, rows // 2, width // 2), lambda i, pos, k=k: (i, pos[k, 0], pos[k, 1])) for k in ways]
    extra = [pl.BlockSpec((1, some, rows // 2, width // 2), lambda i, pos, at=at: (at, i, 0, 0)) for _, at in more]
    out = pl.BlockSpec((len(ways), some, rows // 2, width // 2), lambda i, pos: (0, i, 0, 0))
    shape = jax.ShapeDtypeStruct((len(ways), count, rows // 2, width // 2), BF16)
    return pl.pallas_call(
        functools.partial(fold_kernel, len(more)),
        grid_spec=pltpu.PrefetchScalarGridSpec(
            num_scalar_prefetch=1, grid=(count // some,), in_specs=quarter * 2 + extra, out_specs=out),
        compiler_params=pltpu.CompilerParams(vmem_limit_bytes=40 * 2**20),
        out_shape=shape,
        cost_estimate=SHORT,
        name="fold",
    )(pos, *([keep] * len(ways)), *([got] * len(ways)), *[a for a, _ in more])


def pack_kernel(owner_ref, *refs):
    early, late, out_ref, total_s = refs[:4], refs[4:8], refs[8], refs[9]
    square = None
    start = 0
    for parts in (early, late):
        total = parts[0][...].astype(F32)
        for part in parts[1:]:
            total = total + part[...].astype(F32)
        total_s[start:start + total.shape[0]] = total.astype(BF16)
        start += total.shape[0]
        more = jnp.sum(total * total).reshape(1, 1)
        square = more if square is None else square + more
    rows = total_s.shape[1]
    lane = lax.broadcasted_iota(jnp.int32, (8, out_ref.shape[2]), 1)
    one, two, three = split3(square)
    extra = jnp.where(lane == 0, one, jnp.where(lane == 1, two, jnp.where(lane == 2, three, 0.0))).astype(BF16)
    for p in range(out_ref.shape[0]):
        out_ref[p, :rows] = total_s[lax.div(owner_ref[p], 2)]
        out_ref[p, rows:] = extra


def pack(owner, early, late):
    blocks = early[0].shape[0] + late[0].shape[0]
    rows, cols = early[0].shape[1:]
    vmem = pl.BlockSpec(memory_space=pltpu.VMEM)
    return pl.pallas_call(
        pack_kernel,
        in_specs=[pl.BlockSpec(memory_space=pltpu.SMEM)] + [vmem] * 8,
        out_specs=vmem,
        out_shape=jax.ShapeDtypeStruct((owner.shape[0], rows + 8, cols), BF16),
        scratch_shapes=[pltpu.VMEM((blocks, rows, cols), BF16)],
        compiler_params=pltpu.CompilerParams(vmem_limit_bytes=32 * 2**20),
        cost_estimate=SHORT,
        name="pack",
    )(owner, *early, *late)


def clip_of(square, vec):
    norm = jnp.sqrt(square + jnp.sum(vec * vec).reshape(1, 1))
    return norm, jnp.minimum(1.0, 1.0 / (norm + 1e-06))


def adam_kernel(own_ref, a_ref, b_ref, as_ref, bs_ref, vt_ref, vw_ref, vm_ref, vv_ref, w_ref, m_ref, v_ref,
                g_out, v_out, w_out, vg_out, vv_out, vw_out, norm_out):
    def squares(ref):
        block = ref[...].astype(F32)
        lane = lax.broadcasted_iota(jnp.int32, block.shape, 4)
        row = lax.broadcasted_iota(jnp.int32, block.shape, 3)
        return jnp.sum(jnp.where((lane < 3) & (row == 0), block, 0.0)).reshape(1, 1)

    norm, clip = clip_of(squares(as_ref) + squares(bs_ref), vt_ref[...])
    own = own_ref[0] > 0
    grad = jnp.where(own, a_ref[:, 0, 0].astype(F32), b_ref[:, 0, 0].astype(F32))
    grad = grad[:, :w_ref.shape[0] // grad.shape[0]].reshape(w_ref.shape) * clip
    second, weight = adam(w_ref[...], m_ref[...], v_ref[...], grad, 0.02, 0.05)
    g_out[...] = grad
    v_out[...] = second
    w_out[...] = weight

    @pl.when((pl.program_id(0) == 0) & (pl.program_id(1) == 0))
    def _():
        vec_grad = vt_ref[...] * clip
        second, weight = adam(vw_ref[...], vm_ref[...], vv_ref[...], vec_grad, 0.2, 0.0)
        vg_out[...] = vec_grad
        vv_out[...] = second
        vw_out[...] = weight
        norm_out[...] = norm


def adam_rows(own, mine, other, vec_total, vectors, vec_first, vec_second, weight, first, second):
    rows, width = weight.shape
    deep, tall, wide, piece, cols = mine.shape
    part = pl.BlockSpec((deep, 1, 1, piece, cols), lambda y, x: (0, y, x, 0, 0))
    marks = pl.BlockSpec((deep, tall, wide, 8, 128), lambda y, x: (0, 0, 0, piece // 8 - 1, 0))
    flat = pl.BlockSpec((rows // tall, width // wide), lambda y, x: (y, x))
    vec = pl.BlockSpec(vectors.shape, lambda y, x: (0, 0))
    shape = jax.ShapeDtypeStruct((rows, width), F32)
    small = jax.ShapeDtypeStruct(vectors.shape, F32)
    return pl.pallas_call(
        adam_kernel,
        grid=(tall, wide),
        in_specs=[pl.BlockSpec(memory_space=pltpu.SMEM), part, part, marks, marks] + [vec] * 4 + [flat] * 3,
        out_specs=[flat] * 3 + [vec] * 3 + [pl.BlockSpec((1, 1), lambda y, x: (0, 0))],
        out_shape=[shape] * 3 + [small] * 3 + [jax.ShapeDtypeStruct((1, 1), F32)],
        compiler_params=pltpu.CompilerParams(vmem_limit_bytes=60 * 2**20),
        cost_estimate=SHORT,
        name="adam",
    )(own, mine, other, mine, other, vec_total, vectors, vec_first, vec_second, weight, first, second)


from jax.sharding import PartitionSpec as P

HEADS = 12
STEP = 7


def place_tokens(heights, widths, count):
    sizes = heights * widths
    ends = jnp.cumsum(sizes)
    starts = ends - sizes
    places = jnp.arange(count, dtype=jnp.int32)
    segment = jnp.sum((places[:, None] >= ends[None, :]).astype(jnp.int32), axis=1)
    slots = jnp.arange(heights.shape[0], dtype=jnp.int32)
    picks = (segment[:, None] == slots[None, :]).astype(jnp.int32)
    begin = jnp.sum(picks * starts[None, :], axis=1)
    across = jnp.maximum(jnp.sum(picks * widths[None, :], axis=1), 1)
    offset = places - begin
    live = places < ends[-1]
    return (segment, offset // across, offset % across, live)


def adam(weight, first, second, grad, rate, decay):
    first_new = 0.5 * first + 0.5 * grad
    second_new = 0.5 * second + 0.5 * grad * grad
    correct = 1.0 - 0.5**STEP
    direction = first_new / correct / (jnp.sqrt(second_new / correct) + 1e-08)
    return (second_new, weight - rate * (direction + decay * weight))


def pairwise(bits, total):
    return [(i, i ^ bits) for i in range(total)]


def sum_part(value, devices, step, stop):
    while step < stop:
        value = value + lax.ppermute(value, "dp", pairwise(step, devices))
        step *= 2
    return value


CORES = ("group", "dp")
SWAP = [(0, 1), (1, 0)]


def cross(value, bit0, bit1, devices):
    perm = [(i, i ^ (bit0 if i < devices else bit1)) for i in range(2 * devices)]
    return lax.ppermute(value, CORES, perm)


def along_z(values, devices):
    return [
        lax.ppermute(v, "dp", [(i, (i + 4 * (s + 1)) % devices) for i in range(devices)])
        for s, v in enumerate(values)
    ]


def along_line(value, devices, step, up):
    last = devices // 4
    perm = []
    for z in range(last):
        near = z - 1 if up else z + 1
        far = z - step if up else z + step
        if 0 <= far < last:
            perm += [(4 * near + i, 4 * z + i) for i in range(4)]
    return lax.ppermute(value, "dp", perm)


def gather_pieces(master, inverse, core, me, devices, freqs, make_angles, tables):
    tie = lax.optimization_barrier
    block_rows, width = master.shape
    half = block_rows // 2
    mine = lax.dynamic_slice_in_dim(master, core * half, half, 0).astype(BF16)
    large = mine[:LARGE]
    small = mine[LARGE:]
    z = me // 4
    deep = lax.rem(z - inverse // 4 + 4, 4)
    apart = me ^ inverse
    one = jnp.where(core == 0, apart & 1, (apart >> 1) & 1)
    two = jnp.where(core == 0, (apart >> 1) & 1, apart & 1)
    slots = jnp.stack([
        8 * two + 4 * one + deep,
        4 * deep + 2 * two + one,
        8 * one + 4 * two + deep,
        4 * deep + 2 * one + two,
    ]).astype(jnp.int32)
    up = along_z([large] * 3, devices)
    small = jnp.stack([small, cross(small, 1, 2, devices)])
    small = jnp.concatenate([small, cross(small, 2, 1, devices)])
    large = jnp.stack([large] + up)
    large, small, tables, slots = tie((large, small, tables, slots))
    first = cross(large, 1, 2, devices)
    ups = [along_line(small, devices, 1, True)]
    downs = [along_line(small, devices, 1, False)]
    first, ups[0], downs[0], freqs = tie((first, ups[0], downs[0], freqs))
    angles = make_angles(freqs)
    first = jnp.concatenate([large, first])
    second = cross(first, 2, 1, devices)
    for step in (2, 3):
        ups.append(along_line(ups[-1], devices, step, True))
        downs.append(along_line(downs[-1], devices, step, False))
        if step == 2:
            ups[1], downs[1], angles = tie((ups[1], downs[1], angles))
    small = jnp.concatenate([small] + [jnp.where(z >= s, ups[s - 1], downs[3 - s]) for s in (1, 2, 3)])
    other = [lax.ppermute(a, "group", SWAP) for a in (first, second, small)]
    return (first, second, small, *other), slots, angles + tables


def quarters(core, me):
    x, y = me & 1, (me >> 1) & 1
    one = jnp.where(core == 0, x, y)
    two = jnp.where(core == 0, y, x)
    pairs = [(1 - one, 1 - two), (1 - one, two), (one, 1 - two), (one, two)]
    return jnp.stack([
        jnp.stack([jnp.where(core == 0, b, a), jnp.where(core == 0, a, b)]) for a, b in pairs
    ]).astype(jnp.int32)


def sum_z(low, me, devices):
    count, rows, cols = low.shape
    z = me // 4
    low = low.reshape(count, 4, rows // 4, cols)
    pick = lambda at: lax.dynamic_index_in_dim(low, at, 1, keepdims=False)
    return (pick(z), *along_z([pick(lax.rem(z + s, 4)) for s in (1, 2, 3)], devices))


def reduce_plain(local_mat, owner_block, devices):
    rows, width = local_mat.shape
    block_rows = rows // devices
    term = local_mat.reshape(devices, block_rows, width)[owner_block].reshape(rows, width)
    share = lax.psum_scatter(term.astype(F32), "dp", scatter_dimension=0, tiled=True)
    return lax.psum(share.astype(BF16), "group").astype(F32)


def local(
    tokens,
    cotangent,
    grid_h,
    grid_w,
    owner_block,
    master,
    first_mom,
    second_mom,
    vectors,
    vec_first,
    vec_second,
):
    devices = lax.axis_size("dp")
    core = lax.axis_index("group")
    me = lax.axis_index("dp")
    count = tokens.shape[1]
    width = tokens.shape[2]
    heads = HEADS
    head_dim = width // heads
    half = head_dim // 2
    block_rows = master.shape[0]
    stack = devices * block_rows
    quick = devices == 16 and block_rows == 2 * (LARGE + SMALL) and width % 256 == 0
    inverse = jnp.argsort(owner_block)
    segment, rows_pos, cols_pos, live = place_tokens(grid_h[0], grid_w[0], count)
    x = tokens[0]

    def make_angles(freqs):
        def spread(part):
            return jnp.broadcast_to(part.reshape(heads, 1, half), (heads, 2, half)).reshape(1, width)

        down = rows_pos.astype(F32)[:, None]
        right = cols_pos.astype(F32)[:, None]
        angle = down * spread(freqs[: width // 2]) + right * spread(freqs[width // 2 :])
        lower = (jnp.arange(width) % head_dim < half)[None]
        cosine = jnp.cos(angle)
        sine = jnp.sin(angle)
        return (cosine, jnp.where(lower, -sine, sine))

    def make_tables():
        ids = jnp.arange(128)[None]
        match = segment[:, None] == ids
        key_mask = jnp.where(match | ((ids >= 8) & (ids < 11)), 1.0, 0.0).astype(BF16)
        query_mask = jnp.where((ids < 8) & ~match, MASKED, 0.0).astype(BF16)
        places = jnp.stack([rows_pos, cols_pos], axis=1).astype(F32)
        grad_two = jnp.where(live[:, None], cotangent[0], jnp.zeros((), BF16))
        unit, _ = norm_parts(x.astype(F32))
        first_in = (unit * vectors[0] + vectors[1]).astype(BF16)
        return (key_mask, query_mask, places, grad_two, first_in,
                vectors[4:7].reshape(1, 3 * width), vectors[8:12].reshape(1, 4 * width))

    if quick:
        weights, slots, tables = gather_pieces(master, inverse, core, me, devices, vectors[13], make_angles, make_tables())
    else:
        low = lax.all_gather(master.astype(BF16), "dp", axis=0, tiled=True)
        weights = low.reshape(devices, block_rows, width)[inverse].reshape(stack, width)
        slots = jnp.zeros((4, devices), jnp.int32)
        tables = make_angles(vectors[13]) + make_tables()
    cosine, sine, key_mask, query_mask, places, grad_two, first_in, bias_qkv, bias_one = tables
    here = core.reshape(1).astype(jnp.int32)
    query, key, value, attn, stat, *placed = attend(
        here, slots, first_in, bias_qkv,
        cosine, sine, query_mask, key_mask, weights, stack,
    )
    if quick:
        weights = placed[0]
    whole_rows = block_rows if quick else 0
    block_out, grad_middle, grad_attn, sums, bias_up, keep_mlp, give_mlp = mlp(
        here, x, attn, grad_two, vectors, weights, bias_one, whole_rows
    )
    pairs = width // 128
    tie = lax.optimization_barrier
    if quick:
        pos = quarters(core, me)
        got = lax.ppermute(give_mlp, "group", SWAP)
    back = None
    cuts = (0, 1, pairs - 1, pairs)
    for start, stop in zip(cuts[:-1], cuts[1:]):
        back = attend_back(
            start, stop, back, query, key, value, grad_attn, attn, stat, cosine, sine, query_mask, key_mask, places
        )
        if quick and start == 0:
            send, back = tie((fold(pos, keep_mlp, got, (0, 1)), back))
            came = cross(send, 1, 2, devices)
        if quick and start == 1:
            send, back = tie((fold(pos, keep_mlp, got, (2,), ((came, 0),)), back))
            again = cross(send, 2, 1, devices)
    grad_q, grad_k, grad_v, grad_bias, grad_freq = back
    keep_qkv, give_qkv = qkv_grad(here, grad_q, grad_k, grad_v, first_in, whole_rows)
    if quick:
        again, give_qkv = tie((again, give_qkv))
        low, grad_v, give_qkv = tie((fold(pos, keep_mlp, got, (3,), ((came, 1), (again, 0)))[0], grad_v, give_qkv))
        late = sum_z(low, me, devices)
    if quick:
        got_qkv = lax.ppermute(give_qkv, "group", SWAP)
        send = fold(pos, keep_qkv, got_qkv, (0, 1))
        third = send.shape[2] // 3
        send = [send[:, :, third * i:third * (i + 1)] for i in range(3)]
        send, grad_v = tie((send, grad_v))
    input_grad, local_vec = input_back(
        grad_q, grad_k, grad_v, weights, x, grad_middle, vectors, sums, grad_bias, grad_freq, bias_up
    )
    if quick:
        send[2], local_vec = tie((send[2], local_vec))
        came = [cross(a, 1, 2, devices) for a in send]
        came, local_vec, late = tie((came, local_vec, late))
        came = jnp.concatenate(came, axis=2)
        again = cross(fold(pos, keep_qkv, got_qkv, (2,), ((came, 0),)), 2, 1, devices)
        vec_total = sum_part(local_vec + lax.ppermute(local_vec, "group", SWAP), devices, 4, devices)
        again, vec_total = tie((again, vec_total))
        early = sum_z(fold(pos, keep_qkv, got_qkv, (3,), ((came, 1), (again, 0)))[0], me, devices)
        early, vec_total = tie((early, sum_part(vec_total, devices, 1, 4)))
        load = pack(owner_block, early, late)
        mine = lax.all_to_all(load, "dp", 0, 0, tiled=True)
        other = lax.ppermute(mine, "group", SWAP)
        shape = (devices // 4, 2, 2, *load.shape[1:])
        own = (owner_block[me] % 2 == core).astype(jnp.int32).reshape(1)
        mat_grad, mat_second, mat_weight, vec_grad, vec_second_new, vec_weight, norm = adam_rows(
            own, mine.reshape(shape), other.reshape(shape), vec_total, vectors, vec_first, vec_second,
            master, first_mom, second_mom,
        )
        grad_norm = norm.reshape(())
    else:
        vec_total = lax.psum(local_vec, CORES)
        share = reduce_plain(jnp.concatenate([keep_qkv, keep_mlp]), owner_block, devices)
        square = lax.psum(jnp.sum(share * share), "dp")
        grad_norm = jnp.sqrt(square + jnp.sum(vec_total * vec_total))
        clip = jnp.minimum(1.0, 1.0 / (grad_norm + 1e-06))
        mat_grad = share * clip
        mat_second, mat_weight = adam(master, first_mom, second_mom, mat_grad, 0.02, 0.05)
        vec_grad = vec_total * clip
        vec_second_new, vec_weight = adam(vectors, vec_first, vec_second, vec_grad, 0.2, 0.0)
    return (
        block_out[None],
        input_grad[None],
        mat_grad,
        mat_second,
        mat_weight,
        vec_grad,
        vec_second_new,
        vec_weight,
        grad_norm,
    )


def solution(mesh):
    return jax.shard_map(
        local,
        mesh=mesh,
        in_specs=(
            P("group", "dp", None),
            P("group", "dp", None),
            P("group", "dp"),
            P("group", "dp"),
            P(),
            P("dp", None),
            P("dp", None),
            P("dp", None),
            P(),
            P(),
            P(),
        ),
        out_specs=(
            P("group", "dp", None),
            P("group", "dp", None),
            P("dp", None),
            P("dp", None),
            P("dp", None),
            P(),
            P(),
            P(),
            P(),
        ),
        check_vma=False,
    )
```

```python
import functools
import jax
import jax.numpy as jnp
from jax import lax
from jax.experimental import pallas as pl
from jax.experimental.pallas import tpu as pltpu

F32 = jnp.float32
BF16 = jnp.bfloat16
LAST = (((1,), (1,)), ((), ()))
FIRST = (((0,), (0,)), ((), ()))
PLAIN = (((1,), (0,)), ((), ()))
MASKED = -1e9
SHORT = pl.CostEstimate(flops=1000, bytes_accessed=1000, transcendentals=0)


def mm(left, right, dims):
    return lax.dot_general(left, right, dims, preferred_element_type=F32)


def norm_parts(value):
    centre = value - jnp.mean(value, axis=-1, keepdims=True)
    spread = jnp.mean(centre * centre, axis=-1, keepdims=True)
    inverse = lax.rsqrt(spread + 1e-6)
    return centre * inverse, inverse


def norm_back(unit, inverse, grad, gain):
    scaled = grad * gain
    first = jnp.mean(scaled, axis=-1, keepdims=True)
    second = jnp.mean(scaled * unit, axis=-1, keepdims=True)
    return inverse * (scaled - first - unit * second)


def swap_halves(value):
    lane = lax.broadcasted_iota(jnp.int32, value.shape, 1)
    return jnp.where(
        lane % 64 < 32, pltpu.roll(value, 96, 1), pltpu.roll(value, 32, 1)
    )


def split3(value):
    one = value.astype(BF16).astype(F32)
    rest = value - one
    two = rest.astype(BF16).astype(F32)
    return one, two, rest - two


LARGE = 208
SMALL = 80


def place_pieces(core, slot_ref, mine, other, block, side, dst, sem):
    for which, (first, second, small) in enumerate((mine, other)):
        @pl.when((core == side) if which == 0 else (core != side))
        def _():
            large_slot = slot_ref[2 * which, block]
            small_slot = slot_ref[2 * which + 1, block]

            @pl.when(large_slot < 8)
            def _():
                pltpu.make_async_copy(first.at[large_slot], dst(0, LARGE), sem).start()

            @pl.when(large_slot >= 8)
            def _():
                pltpu.make_async_copy(second.at[large_slot - 8], dst(0, LARGE), sem).start()

            pltpu.make_async_copy(small.at[small_slot], dst(LARGE, SMALL), sem).start()


def attend_kernel(blocks, core_ref, slot_ref, n1_ref, bq_ref, bk_ref, bv_ref,
                  cos_ref, sin_ref, qm_ref, km_ref, *rest):
    if blocks:
        mine, other = rest[0:3], rest[3:6]
        q_ref, k_ref, v_ref, attn_ref, stat_ref, w_ref, w_s, near, far, back = rest[6:]
    else:
        w_ref, q_ref, k_ref, v_ref, attn_ref, stat_ref, w_s, near = rest
    count, width = n1_ref.shape
    step = pl.program_id(0)

    @pl.when(step == 0)
    def _():
        if blocks:
            core = core_ref[0]
            rows = w_ref.shape[0] // blocks

            def start(block, sem):
                for side in (0, 1):
                    def dst(offset, size):
                        base = block * rows + side * (rows // 2) + offset
                        return w_s.at[pl.ds(pl.multiple_of(base, 16), size)]
                    place_pieces(core, slot_ref, mine, other, block, side, dst, sem)

            def near_block(block, carry):
                start(block, near)
                return carry

            def far_block(block, carry):
                start(block, far)
                return carry

            lax.fori_loop(0, 3 * width // rows, near_block, 0)
            lax.fori_loop(3 * width // rows, blocks, far_block, 0)
        else:
            pltpu.make_async_copy(w_ref.at[pl.ds(0, 3 * width)], w_s, near).start()
        head = w_s.at[pl.ds(0, 3 * width)]
        pltpu.make_async_copy(head, head, near).wait()

    if blocks:
        @pl.when(step == 1)
        def _():
            tail = w_s.at[pl.ds(3 * width, w_s.shape[0] - 3 * width)]
            pltpu.make_async_copy(tail, tail, far).wait()
            pltpu.make_async_copy(w_s, w_ref, back).start()

    def third(j):
        return w_s[pl.ds(pl.multiple_of(j * width + step * 128, 128), 128), :]

    w = jnp.concatenate([third(0), third(1), third(2)], axis=0)
    qkv = mm(n1_ref[...], w, LAST)
    q = qkv[:, :128] + bq_ref[...]
    k = qkv[:, 128:256] + bk_ref[...]
    v = (qkv[:, 256:] + bv_ref[...]).astype(BF16)
    c = cos_ref[...]
    s = sin_ref[...]
    qr = ((q * c + swap_halves(q) * s).astype(BF16).astype(F32) * 0.125).astype(BF16)
    kr = (k * c + swap_halves(k) * s).astype(BF16)
    q_ref[...] = qr
    k_ref[...] = kr
    v_ref[...] = v
    lane = lax.broadcasted_iota(jnp.int32, (1, 128), 1)
    k_aug = jnp.concatenate([kr, km_ref[...]], axis=1)
    v_aug = jnp.concatenate([v, jnp.ones((count, 128), BF16)], axis=1)
    zero = jnp.zeros((), BF16)
    tile = 256
    for i in range(count // tile):
        rows = pl.ds(i * tile, tile)
        out = None
        stats = []
        for h in (0, 1):
            mine_lanes = (lane // 64) == h
            qa = jnp.concatenate(
                [jnp.where(mine_lanes, qr[i * tile:(i + 1) * tile], zero), qm_ref[rows, :]], axis=1)
            scores = mm(qa, k_aug, LAST)
            top = jnp.max(scores, axis=-1, keepdims=True)
            e = jnp.exp(scores - top).astype(BF16)
            o = mm(e, v_aug, PLAIN)
            total = o[:, 128:]
            o = o[:, :128] / total
            out = o if out is None else jnp.where(lane < 64, out, o)
            stats.append(top + jnp.log(total[:, :1]))
        attn_ref[rows, :] = out.astype(BF16)
        stat_ref[rows, :] = jnp.where(lane < 64, stats[0], stats[1])

    if blocks:
        @pl.when(step == pl.num_programs(0) - 1)
        def _():
            pltpu.make_async_copy(w_s, w_ref, back).wait()


def attend(core, slots, n1, bqkv, cos, sin, qm, km, weights, stack):
    count, width = n1.shape
    pairs = width // 128
    pieces = isinstance(weights, tuple)
    blocks = slots.shape[1] if pieces else 0
    whole = lambda p: (0, 0)
    col = lambda p: (0, p)
    smem = pl.BlockSpec(memory_space=pltpu.SMEM)
    hbm = pl.BlockSpec(memory_space=pl.ANY)
    given = weights if pieces else (weights,)
    specs = [smem, smem] + [
        pl.BlockSpec((count, width), whole),
        pl.BlockSpec((1, 128), col),
        pl.BlockSpec((1, 128), lambda p: (0, p + pairs)),
        pl.BlockSpec((1, 128), lambda p: (0, p + 2 * pairs)),
        pl.BlockSpec((count, 128), col),
        pl.BlockSpec((count, 128), col),
        pl.BlockSpec((count, 128), whole),
        pl.BlockSpec((count, 128), whole),
    ] + [hbm] * len(given)
    outs = [pl.BlockSpec((count, 128), col)] * 5
    shape = lambda d: jax.ShapeDtypeStruct((count, width), d)
    shapes = [shape(BF16)] * 4 + [shape(F32)]
    scratch = [pltpu.VMEM((stack if pieces else 3 * width, width), BF16), pltpu.SemaphoreType.DMA]
    if pieces:
        outs.append(hbm)
        shapes.append(jax.ShapeDtypeStruct((stack, width), BF16))
        scratch += [pltpu.SemaphoreType.DMA] * 2
    return pl.pallas_call(
        functools.partial(attend_kernel, blocks),
        grid=(pairs,),
        in_specs=specs,
        out_specs=outs,
        out_shape=shapes,
        scratch_shapes=scratch,
        compiler_params=pltpu.CompilerParams(vmem_limit_bytes=56 * 2**20),
        cost_estimate=SHORT,
        name="attend",
    )(core, slots, n1, bqkv, bqkv, bqkv, cos, sin, qm, km, *given)


def gelu_both(x):
    cdf = 0.5 + 0.5 * lax.erf(x * 0.7071067811865476)
    return x * cdf, cdf + x * jnp.exp(x * x * -0.5) * 0.3989422804014327


def send_rows(core, block_rows, stage, row, base, keep_ref, give_ref, sem):
    if not block_rows:
        rows = stage.shape[0]
        pltpu.make_async_copy(
            stage, keep_ref.at[pl.ds(pl.multiple_of(row - base, 64), rows)], sem
        ).start()
        return

    def one(index, carry):
        at = row + 64 * index
        block = lax.div(at, block_rows)
        inner = pl.ds(pl.multiple_of(at - block * block_rows, 64), 64)
        slot = lax.div(block, 2) - base // 2
        source = stage.at[pl.ds(pl.multiple_of(64 * index, 64), 64)]
        own = lax.rem(block, 2) == core

        @pl.when(own)
        def _():
            pltpu.make_async_copy(source, keep_ref.at[slot, inner], sem).start()

        @pl.when(jnp.logical_not(own))
        def _():
            pltpu.make_async_copy(source, give_ref.at[slot, inner], sem).start()

        return carry

    lax.fori_loop(0, stage.shape[0] // 64, one, 0)


def mlp_kernel(block_rows, base, core_ref, x_ref, at_ref, dz_ref, vec_ref, wo_ref, w1_ref, w2_ref, b1_ref,
               out_ref, dm_ref, da_ref, sums_ref, gb_ref, keep_ref, give_ref,
               middle_s, n2_s, acc_s, stage_s, proj_s, sems):
    step = pl.program_id(0)
    last = pl.num_programs(0) - 1
    count, width = x_ref.shape
    core = core_ref[0]
    tile = w1_ref.shape[0]

    @pl.when(step == 0)
    def _():
        middle = x_ref[...].astype(F32) + mm(at_ref[...], wo_ref[...], LAST) + vec_ref[7:8, :]
        middle_s[...] = middle
        unit, _ = norm_parts(middle)
        n2_s[...] = (unit * vec_ref[2:3, :] + vec_ref[3:4, :]).astype(BF16)
        acc_s[...] = jnp.zeros_like(acc_s)
        dm_ref[...] = jnp.zeros_like(dm_ref)

    slot = lax.rem(step, 2)

    @pl.when(step >= 2)
    def _():
        pltpu.make_async_copy(stage_s.at[slot], stage_s.at[slot], sems.at[slot]).wait()

    n2 = n2_s[...]
    dz = dz_ref[...]
    w1 = w1_ref[...]
    w2 = w2_ref[...]
    pre = mm(w1, n2, LAST) + b1_ref[...].reshape(tile, 1)
    back = mm(w2, dz, LAST)
    act, slope = gelu_both(pre)
    hidden = act.astype(BF16)
    stage_s[slot, 1] = mm(hidden, dz, PLAIN).astype(BF16)
    dpre = (back * slope).astype(BF16)
    gb_ref[...] = jnp.sum(dpre.astype(F32), axis=1, keepdims=True).reshape(1, tile)
    stage_s[slot, 0] = mm(dpre, n2, PLAIN).astype(BF16)
    acc_s[...] += mm(hidden, w2, FIRST)
    dm_ref[...] += mm(dpre, w1, FIRST)
    for j in (0, 1):
        send_rows(core, block_rows, stage_s.at[slot, j], (4 + 4 * j) * width + step * tile,
                  base, keep_ref, give_ref, sems.at[slot])

    @pl.when(step == last)
    def _():
        middle = middle_s[...]
        out_ref[...] = (middle + acc_s[...] + vec_ref[12:13, :]).astype(BF16)
        unit, inverse = norm_parts(middle)
        dn = dm_ref[...]
        dy = dz_ref[...].astype(F32)
        dm = dy + norm_back(unit, inverse, dn, vec_ref[2:3, :])
        dm_ref[...] = dm
        low = dm.astype(BF16)
        row = lambda a: jnp.sum(a, axis=0, keepdims=True)
        sums_ref[...] = jnp.concatenate(
            [row(dn * unit), row(dn), row(low.astype(F32)), row(dy), jnp.zeros((4, width), F32)], axis=0)
        proj_s[...] = mm(low, at_ref[...], FIRST).astype(BF16)
        send_rows(core, block_rows, proj_s, 3 * width, base, keep_ref, give_ref, sems.at[2])
        da_ref[...] = mm(low, wo_ref[...], PLAIN).astype(BF16)
        pltpu.make_async_copy(stage_s.at[slot], stage_s.at[slot], sems.at[slot]).wait()
        pltpu.make_async_copy(stage_s.at[1 - slot], stage_s.at[1 - slot], sems.at[1 - slot]).wait()
        pltpu.make_async_copy(proj_s, proj_s, sems.at[2]).wait()


def grad_shapes(block_rows, rows, width):
    if block_rows:
        half = jax.ShapeDtypeStruct((rows // block_rows // 2, block_rows, width), BF16)
        return [half, half]
    return [jax.ShapeDtypeStruct((rows, width), BF16), jax.ShapeDtypeStruct((16, width), BF16)]


def mlp(core, x, attn, dz, vectors, weights, b1, block_rows, tile=512):
    count, width = x.shape
    units = 4 * width
    stack = weights.shape[0]
    base = 3 * width // block_rows if block_rows else 3 * width
    whole = lambda t: (0, 0)
    big = pl.BlockSpec((count, width), whole)
    hbm = pl.BlockSpec(memory_space=pl.ANY)
    return pl.pallas_call(
        functools.partial(mlp_kernel, block_rows, base),
        grid=(units // tile,),
        in_specs=[pl.BlockSpec(memory_space=pltpu.SMEM), big, big, big, pl.BlockSpec(vectors.shape, whole),
                  pl.BlockSpec((width, width), lambda t: (3, 0)),
                  pl.BlockSpec((tile, width), lambda t: (4 * width // tile + t, 0)),
                  pl.BlockSpec((tile, width), lambda t: (8 * width // tile + t, 0)),
                  pl.BlockSpec((1, tile), lambda t: (0, t))],
        out_specs=[big, big, big, pl.BlockSpec((8, width), whole), pl.BlockSpec((1, tile), lambda t: (0, t)), hbm, hbm],
        out_shape=[
            jax.ShapeDtypeStruct((count, width), BF16),
            jax.ShapeDtypeStruct((count, width), F32),
            jax.ShapeDtypeStruct((count, width), BF16),
            jax.ShapeDtypeStruct((8, width), F32),
            jax.ShapeDtypeStruct((1, units), F32),
        ] + grad_shapes(block_rows, stack - 3 * width, width),
        scratch_shapes=[
            pltpu.VMEM((count, width), F32),
            pltpu.VMEM((count, width), BF16),
            pltpu.VMEM((count, width), F32),
            pltpu.VMEM((2, 2, tile, width), BF16),
            pltpu.VMEM((width, width), BF16),
            pltpu.SemaphoreType.DMA((3,)),
        ],
        compiler_params=pltpu.CompilerParams(vmem_limit_bytes=60 * 2**20),
        cost_estimate=SHORT,
        name="mlp",
    )(core, x, attn, dz, vectors, weights, weights, weights, b1)


def back_kernel(first, q_ref, k_ref, v_ref, da_ref, at_ref, stat_ref, cos_ref, sin_ref,
                qm_ref, km_ref, pos_ref, *rest):
    dq_ref, dk_ref, dv_ref, gb_ref, gf_ref = rest if first else rest[5:]
    count = q_ref.shape[0]
    lane = lax.broadcasted_iota(jnp.int32, (1, 128), 1)
    zero = jnp.zeros((), BF16)
    q = q_ref[...]
    k = k_ref[...]
    v = v_ref[...]
    da = da_ref[...]
    prod = da.astype(F32) * at_ref[...].astype(F32)
    qm = qm_ref[...].astype(F32)
    k_aug = jnp.concatenate([k, km_ref[...]], axis=1)
    v_aug = jnp.concatenate([v, jnp.broadcast_to((lane < 2).astype(BF16), (count, 128))], axis=1)
    tile = 256
    dq = dk = dv = None
    for h in (0, 1):
        mine = (lane // 64) == h
        qh = jnp.where(mine, q, zero)
        kh = jnp.where(mine, k, zero)
        dah = jnp.where(mine, da, zero)
        delta = jnp.sum(jnp.where(mine, prod, 0.0), axis=-1, keepdims=True)
        d1, d2, _ = split3(delta)
        l1, l2, l3 = split3(stat_ref[:, 64 * h:64 * h + 1])
        extra = jnp.where(lane == 8, -l1, jnp.where(lane == 9, -l2, jnp.where(lane == 10, -l3, qm)))
        q_aug = jnp.concatenate([qh, extra.astype(BF16)], axis=1)
        da_aug = jnp.concatenate(
            [dah, jnp.where(lane == 0, -d1, jnp.where(lane == 1, -d2, 0.0)).astype(BF16)], axis=1)
        dks, dvs, dqh = [], [], None
        for i in range(count // tile):
            sl = slice(i * tile, (i + 1) * tile)
            p = jnp.exp(mm(k_aug[sl], q_aug, LAST))
            dp = mm(v_aug[sl], da_aug, LAST)
            ds = (p * dp).astype(BF16)
            dvs.append(mm(p.astype(BF16), dah, PLAIN))
            dks.append(mm(ds, qh, PLAIN))
            part = mm(ds, kh[sl], FIRST)
            dqh = part if dqh is None else dqh + part
        dkh = jnp.concatenate(dks, axis=0)
        dvh = jnp.concatenate(dvs, axis=0)
        dq = dqh if dq is None else dq + dqh
        dk = dkh if dk is None else dk + dkh
        dv = dvh if dv is None else dv + dvh
    dq = dq * 0.125
    c = cos_ref[...]
    s = sin_ref[...]
    turned = dq * swap_halves(q.astype(F32) * 8.0) + dk * swap_halves(k.astype(F32))
    turned = jnp.where(lane % 64 < 32, -turned, turned)
    row = lambda a: jnp.sum(a, axis=0, keepdims=True)
    gf_ref[...] = jnp.concatenate(
        [row(turned * pos_ref[:, 0:1]), row(turned * pos_ref[:, 1:2]), jnp.zeros((6, 128), F32)], axis=0)
    dqp = (dq * c - swap_halves(dq) * s).astype(BF16)
    dkp = (dk * c - swap_halves(dk) * s).astype(BF16)
    dvp = dv.astype(BF16)
    gb_ref[...] = jnp.concatenate(
        [row(dqp.astype(F32)), row(dkp.astype(F32)), row(dvp.astype(F32)), jnp.zeros((5, 128), F32)], axis=0)
    dq_ref[...] = dqp
    dk_ref[...] = dkp
    dv_ref[...] = dvp


def attend_back(start, stop, before, q, k, v, da, attn, stat, cos, sin, qm, km, pos):
    count, width = q.shape
    whole = lambda p: (0, 0)
    col = lambda p: (0, p + start)
    tall = pl.BlockSpec((count, 128), col)
    fixed = pl.BlockSpec((count, 128), whole)
    small = pl.BlockSpec((8, 128), col)
    in_specs = [tall] * 8 + [fixed] * 2 + [pl.BlockSpec((count, 2), whole)]
    operands = [q, k, v, da, attn, stat, cos, sin, qm, km, pos]
    aliases = {}
    if before is not None:
        aliases = {len(operands) + i: i for i in range(5)}
        in_specs += [pl.BlockSpec(memory_space=pl.ANY)] * 5
        operands += list(before)
    return pl.pallas_call(
        functools.partial(back_kernel, before is None),
        grid=(stop - start,),
        in_specs=in_specs,
        out_specs=[tall] * 3 + [small] * 2,
        out_shape=[jax.ShapeDtypeStruct((count, width), BF16)] * 3 + [jax.ShapeDtypeStruct((8, width), F32)] * 2,
        input_output_aliases=aliases,
        compiler_params=pltpu.CompilerParams(vmem_limit_bytes=56 * 2**20),
        cost_estimate=SHORT,
        name="attend_back",
    )(*operands)


def qkv_grad_kernel(block_rows, core_ref, dq_ref, dk_ref, dv_ref, n1_ref, keep_ref, give_ref, stage_s, sem):
    width = n1_ref.shape[1]
    cols = dq_ref.shape[1]
    step = pl.program_id(0)
    n1 = n1_ref[...]
    for j, ref in enumerate((dq_ref, dk_ref, dv_ref)):
        stage_s[step, j] = mm(ref[...], n1, FIRST).astype(BF16)
        send_rows(core_ref[0], block_rows, stage_s.at[step, j], j * width + step * cols, 0, keep_ref, give_ref, sem)

    @pl.when(step == pl.num_programs(0) - 1)
    def _():
        pltpu.make_async_copy(stage_s, stage_s, sem).wait()


def qkv_grad(core, dq, dk, dv, n1, block_rows):
    count, width = n1.shape
    cols = width // 2
    tall = pl.BlockSpec((count, cols), lambda p: (0, p))
    hbm = pl.BlockSpec(memory_space=pl.ANY)
    return pl.pallas_call(
        functools.partial(qkv_grad_kernel, block_rows),
        grid=(2,),
        in_specs=[pl.BlockSpec(memory_space=pltpu.SMEM)] + [tall] * 3 + [pl.BlockSpec((count, width), lambda p: (0, 0))],
        out_specs=[hbm, hbm],
        out_shape=grad_shapes(block_rows, 3 * width, width),
        scratch_shapes=[pltpu.VMEM((2, 3, cols, width), BF16), pltpu.SemaphoreType.DMA],
        compiler_params=pltpu.CompilerParams(vmem_limit_bytes=56 * 2**20),
        cost_estimate=SHORT,
        name="qkv_grad",
    )(core, dq, dk, dv, n1)


def input_kernel(dq_ref, dk_ref, dv_ref, w_ref, x_ref, dm_ref, vec_ref, sums_ref, gb_ref, gf_ref, up_ref, ig_ref, out_ref):
    step = pl.program_id(0)
    d = jnp.concatenate([dq_ref[...], dk_ref[...], dv_ref[...]], axis=1)
    dn = mm(d, w_ref[...], PLAIN)
    unit, inverse = norm_parts(x_ref[...].astype(F32))
    ig_ref[...] = dm_ref[...] + norm_back(unit, inverse, dn, vec_ref[0:1, :])
    row = lambda a: jnp.sum(a, axis=0, keepdims=True)
    sums = jnp.concatenate([row(dn * unit), row(dn)], axis=0)

    @pl.when(step == 0)
    def _():
        width = dn.shape[1]
        half = width // 2
        out_ref[0:2] = sums
        out_ref[2:4] = sums_ref[0:2]
        out_ref[4:7] = gb_ref[0:3]
        out_ref[7:8] = sums_ref[2:3]
        for i in range(4):
            out_ref[8 + i:9 + i] = up_ref[:, i * width:(i + 1) * width]
        out_ref[12:13] = sums_ref[3:4]
        lane = lax.broadcasted_iota(jnp.int32, (width, half), 0)
        slot = lax.broadcasted_iota(jnp.int32, (width, half), 1)
        pick = jnp.where((lane // 64 == slot // 32) & (lane % 32 == slot % 32), 1.0, 0.0)
        both = lax.dot_general(gf_ref[...], pick, PLAIN, precision=lax.Precision.HIGHEST, preferred_element_type=F32)
        out_ref[13:14, :half] = both[0:1]
        out_ref[13:14, half:] = both[1:2]

    @pl.when(step > 0)
    def _():
        out_ref[0:2] += sums


def input_back(dq, dk, dv, weights, x, dm, vectors, sums, grad_bias, grad_freq, bias_up):
    count, width = x.shape
    tile = 256
    part = pl.BlockSpec((tile, width), lambda i: (i, 0))
    whole = lambda i: (0, 0)
    fixed = lambda a: pl.BlockSpec(a.shape, whole)
    return pl.pallas_call(
        input_kernel,
        grid=(count // tile,),
        in_specs=[part] * 3 + [pl.BlockSpec((3 * width, width), whole), part, part]
        + [fixed(a) for a in (vectors, sums, grad_bias, grad_freq, bias_up)],
        out_specs=[part, fixed(vectors)],
        out_shape=[jax.ShapeDtypeStruct((count, width), F32), jax.ShapeDtypeStruct(vectors.shape, F32)],
        compiler_params=pltpu.CompilerParams(vmem_limit_bytes=56 * 2**20),
        cost_estimate=SHORT,
        name="input_back",
    )(dq, dk, dv, weights, x, dm, vectors, sums, grad_bias, grad_freq, bias_up)


def fold_kernel(count, pos_ref, *refs):
    out_ref = refs[-1]
    ways = out_ref.shape[0]
    for k in range(ways):
        total = refs[k][...].astype(F32) + refs[ways + k][...].astype(F32)
        for more in refs[2 * ways:-1]:
            total = total + more[0].astype(F32)
        out_ref[k] = total.astype(BF16)


def fold(pos, keep, got, ways, more=()):
    count, rows, width = keep.shape
    some = count // 2
    quarter = [pl.BlockSpec((some, rows // 2, width // 2), lambda i, pos, k=k: (i, pos[k, 0], pos[k, 1])) for k in ways]
    extra = [pl.BlockSpec((1, some, rows // 2, width // 2), lambda i, pos, at=at: (at, i, 0, 0)) for _, at in more]
    out = pl.BlockSpec((len(ways), some, rows // 2, width // 2), lambda i, pos: (0, i, 0, 0))
    shape = jax.ShapeDtypeStruct((len(ways), count, rows // 2, width // 2), BF16)
    return pl.pallas_call(
        functools.partial(fold_kernel, len(more)),
        grid_spec=pltpu.PrefetchScalarGridSpec(
            num_scalar_prefetch=1, grid=(count // some,), in_specs=quarter * 2 + extra, out_specs=out),
        compiler_params=pltpu.CompilerParams(vmem_limit_bytes=40 * 2**20),
        out_shape=shape,
        cost_estimate=SHORT,
        name="fold",
    )(pos, *([keep] * len(ways)), *([got] * len(ways)), *[a for a, _ in more])


def pack_kernel(owner_ref, *refs):
    early, late, out_ref, total_s = refs[:4], refs[4:8], refs[8], refs[9]
    square = None
    start = 0
    for parts in (early, late):
        total = parts[0][...].astype(F32)
        for part in parts[1:]:
            total = total + part[...].astype(F32)
        total_s[start:start + total.shape[0]] = total.astype(BF16)
        start += total.shape[0]
        more = jnp.sum(total * total).reshape(1, 1)
        square = more if square is None else square + more
    rows = total_s.shape[1]
    lane = lax.broadcasted_iota(jnp.int32, (8, out_ref.shape[2]), 1)
    one, two, three = split3(square)
    extra = jnp.where(lane == 0, one, jnp.where(lane == 1, two, jnp.where(lane == 2, three, 0.0))).astype(BF16)
    for p in range(out_ref.shape[0]):
        out_ref[p, :rows] = total_s[lax.div(owner_ref[p], 2)]
        out_ref[p, rows:] = extra


def pack(owner, early, late):
    blocks = early[0].shape[0] + late[0].shape[0]
    rows, cols = early[0].shape[1:]
    vmem = pl.BlockSpec(memory_space=pltpu.VMEM)
    return pl.pallas_call(
        pack_kernel,
        in_specs=[pl.BlockSpec(memory_space=pltpu.SMEM)] + [vmem] * 8,
        out_specs=vmem,
        out_shape=jax.ShapeDtypeStruct((owner.shape[0], rows + 8, cols), BF16),
        scratch_shapes=[pltpu.VMEM((blocks, rows, cols), BF16)],
        compiler_params=pltpu.CompilerParams(vmem_limit_bytes=32 * 2**20),
        cost_estimate=SHORT,
        name="pack",
    )(owner, *early, *late)


def clip_of(square, vec):
    norm = jnp.sqrt(square + jnp.sum(vec * vec).reshape(1, 1))
    return norm, jnp.minimum(1.0, 1.0 / (norm + 1e-06))


def adam_kernel(own_ref, a_ref, b_ref, as_ref, bs_ref, vt_ref, vw_ref, vm_ref, vv_ref, w_ref, m_ref, v_ref,
                g_out, v_out, w_out, vg_out, vv_out, vw_out, norm_out):
    def squares(ref):
        block = ref[...].astype(F32)
        lane = lax.broadcasted_iota(jnp.int32, block.shape, 4)
        row = lax.broadcasted_iota(jnp.int32, block.shape, 3)
        return jnp.sum(jnp.where((lane < 3) & (row == 0), block, 0.0)).reshape(1, 1)

    norm, clip = clip_of(squares(as_ref) + squares(bs_ref), vt_ref[...])
    own = own_ref[0] > 0
    grad = jnp.where(own, a_ref[:, 0, 0].astype(F32), b_ref[:, 0, 0].astype(F32))
    grad = grad[:, :w_ref.shape[0] // grad.shape[0]].reshape(w_ref.shape) * clip
    second, weight = adam(w_ref[...], m_ref[...], v_ref[...], grad, 0.02, 0.05)
    g_out[...] = grad
    v_out[...] = second
    w_out[...] = weight

    @pl.when((pl.program_id(0) == 0) & (pl.program_id(1) == 0))
    def _():
        vec_grad = vt_ref[...] * clip
        second, weight = adam(vw_ref[...], vm_ref[...], vv_ref[...], vec_grad, 0.2, 0.0)
        vg_out[...] = vec_grad
        vv_out[...] = second
        vw_out[...] = weight
        norm_out[...] = norm


def adam_rows(own, mine, other, vec_total, vectors, vec_first, vec_second, weight, first, second):
    rows, width = weight.shape
    deep, tall, wide, piece, cols = mine.shape
    part = pl.BlockSpec((deep, 1, 1, piece, cols), lambda y, x: (0, y, x, 0, 0))
    marks = pl.BlockSpec((deep, tall, wide, 8, 128), lambda y, x: (0, 0, 0, piece // 8 - 1, 0))
    flat = pl.BlockSpec((rows // tall, width // wide), lambda y, x: (y, x))
    vec = pl.BlockSpec(vectors.shape, lambda y, x: (0, 0))
    shape = jax.ShapeDtypeStruct((rows, width), F32)
    small = jax.ShapeDtypeStruct(vectors.shape, F32)
    return pl.pallas_call(
        adam_kernel,
        grid=(tall, wide),
        in_specs=[pl.BlockSpec(memory_space=pltpu.SMEM), part, part, marks, marks] + [vec] * 4 + [flat] * 3,
        out_specs=[flat] * 3 + [vec] * 3 + [pl.BlockSpec((1, 1), lambda y, x: (0, 0))],
        out_shape=[shape] * 3 + [small] * 3 + [jax.ShapeDtypeStruct((1, 1), F32)],
        compiler_params=pltpu.CompilerParams(vmem_limit_bytes=60 * 2**20),
        cost_estimate=SHORT,
        name="adam",
    )(own, mine, other, mine, other, vec_total, vectors, vec_first, vec_second, weight, first, second)


from jax.sharding import PartitionSpec as P

HEADS = 12
STEP = 7


def place_tokens(heights, widths, count):
    sizes = heights * widths
    ends = jnp.cumsum(sizes)
    starts = ends - sizes
    places = jnp.arange(count, dtype=jnp.int32)
    segment = jnp.sum((places[:, None] >= ends[None, :]).astype(jnp.int32), axis=1)
    slots = jnp.arange(heights.shape[0], dtype=jnp.int32)
    picks = (segment[:, None] == slots[None, :]).astype(jnp.int32)
    begin = jnp.sum(picks * starts[None, :], axis=1)
    across = jnp.maximum(jnp.sum(picks * widths[None, :], axis=1), 1)
    offset = places - begin
    live = places < ends[-1]
    return (segment, offset // across, offset % across, live)


def adam(weight, first, second, grad, rate, decay):
    first_new = 0.5 * first + 0.5 * grad
    second_new = 0.5 * second + 0.5 * grad * grad
    correct = 1.0 - 0.5**STEP
    direction = first_new / correct / (jnp.sqrt(second_new / correct) + 1e-08)
    return (second_new, weight - rate * (direction + decay * weight))


def pairwise(bits, total):
    return [(i, i ^ bits) for i in range(total)]


def sum_part(value, devices, step, stop):
    while step < stop:
        value = value + lax.ppermute(value, "dp", pairwise(step, devices))
        step *= 2
    return value


CORES = ("group", "dp")
SWAP = [(0, 1), (1, 0)]


def cross(value, bit0, bit1, devices):
    perm = [(i, i ^ (bit0 if i < devices else bit1)) for i in range(2 * devices)]
    return lax.ppermute(value, CORES, perm)


def along_z(values, devices):
    return [
        lax.ppermute(v, "dp", [(i, (i + 4 * (s + 1)) % devices) for i in range(devices)])
        for s, v in enumerate(values)
    ]


def along_line(value, devices, step, up):
    last = devices // 4
    perm = []
    for z in range(last):
        near = z - 1 if up else z + 1
        far = z - step if up else z + step
        if 0 <= far < last:
            perm += [(4 * near + i, 4 * z + i) for i in range(4)]
    return lax.ppermute(value, "dp", perm)


def gather_pieces(master, inverse, core, me, devices, freqs, make_angles, x, make_norm, tables):
    tie = lax.optimization_barrier
    block_rows, width = master.shape
    half = block_rows // 2
    mine = lax.dynamic_slice_in_dim(master, core * half, half, 0).astype(BF16)
    large = mine[:LARGE]
    small = mine[LARGE:]
    z = me // 4
    deep = lax.rem(z - inverse // 4 + 4, 4)
    apart = me ^ inverse
    one = jnp.where(core == 0, apart & 1, (apart >> 1) & 1)
    two = jnp.where(core == 0, (apart >> 1) & 1, apart & 1)
    slots = jnp.stack([
        8 * two + 4 * one + deep,
        4 * deep + 2 * two + one,
        8 * one + 4 * two + deep,
        4 * deep + 2 * one + two,
    ]).astype(jnp.int32)
    up = along_z([large] * 3, devices)
    small = jnp.stack([small, cross(small, 1, 2, devices)])
    small = jnp.concatenate([small, cross(small, 2, 1, devices)])
    large = jnp.stack([large] + up)
    large, small, tables, slots, freqs = tie((large, small, tables, slots, freqs))
    angles = make_angles(freqs)
    first = cross(large, 1, 2, devices)
    ups = [along_line(small, devices, 1, True)]
    downs = [along_line(small, devices, 1, False)]
    first, ups[0], downs[0], angles, x = tie((first, ups[0], downs[0], angles, x))
    normed = make_norm(x)
    first = jnp.concatenate([large, first])
    second = cross(first, 2, 1, devices)
    for step in (2, 3):
        ups.append(along_line(ups[-1], devices, step, True))
        downs.append(along_line(downs[-1], devices, step, False))
        if step == 2:
            ups[1], downs[1], normed = tie((ups[1], downs[1], normed))
    small = jnp.concatenate([small] + [jnp.where(z >= s, ups[s - 1], downs[3 - s]) for s in (1, 2, 3)])
    other = [lax.ppermute(a, "group", SWAP) for a in (first, second, small)]
    return (first, second, small, *other), slots, angles + (normed,) + tables


def quarters(core, me):
    x, y = me & 1, (me >> 1) & 1
    one = jnp.where(core == 0, x, y)
    two = jnp.where(core == 0, y, x)
    pairs = [(1 - one, 1 - two), (1 - one, two), (one, 1 - two), (one, two)]
    return jnp.stack([
        jnp.stack([jnp.where(core == 0, b, a), jnp.where(core == 0, a, b)]) for a, b in pairs
    ]).astype(jnp.int32)


def sum_z(low, me, devices):
    count, rows, cols = low.shape
    z = me // 4
    low = low.reshape(count, 4, rows // 4, cols)
    pick = lambda at: lax.dynamic_index_in_dim(low, at, 1, keepdims=False)
    return (pick(z), *along_z([pick(lax.rem(z + s, 4)) for s in (1, 2, 3)], devices))


def reduce_plain(local_mat, owner_block, devices):
    rows, width = local_mat.shape
    block_rows = rows // devices
    term = local_mat.reshape(devices, block_rows, width)[owner_block].reshape(rows, width)
    share = lax.psum_scatter(term.astype(F32), "dp", scatter_dimension=0, tiled=True)
    return lax.psum(share.astype(BF16), "group").astype(F32)


def local(
    tokens,
    cotangent,
    grid_h,
    grid_w,
    owner_block,
    master,
    first_mom,
    second_mom,
    vectors,
    vec_first,
    vec_second,
):
    devices = lax.axis_size("dp")
    core = lax.axis_index("group")
    me = lax.axis_index("dp")
    count = tokens.shape[1]
    width = tokens.shape[2]
    heads = HEADS
    head_dim = width // heads
    half = head_dim // 2
    block_rows = master.shape[0]
    stack = devices * block_rows
    quick = devices == 16 and block_rows == 2 * (LARGE + SMALL) and width % 256 == 0
    inverse = jnp.argsort(owner_block)
    segment, rows_pos, cols_pos, live = place_tokens(grid_h[0], grid_w[0], count)
    x = tokens[0]

    def spread(part):
        return jnp.broadcast_to(part.reshape(heads, 1, half), (heads, 2, half)).reshape(1, width)

    freqs = (spread(vectors[13, : width // 2]), spread(vectors[13, width // 2 :]))

    def make_angles(freqs):
        down = rows_pos.astype(F32)[:, None]
        right = cols_pos.astype(F32)[:, None]
        angle = down * freqs[0] + right * freqs[1]
        lower = (jnp.arange(width) % head_dim < half)[None]
        cosine = jnp.cos(angle)
        sine = jnp.sin(angle)
        return (cosine, jnp.where(lower, -sine, sine))

    def make_norm(x):
        unit, _ = norm_parts(x.astype(F32))
        return (unit * vectors[0] + vectors[1]).astype(BF16)

    def make_tables():
        ids = jnp.arange(128)[None]
        match = segment[:, None] == ids
        key_mask = jnp.where(match | ((ids >= 8) & (ids < 11)), 1.0, 0.0).astype(BF16)
        query_mask = jnp.where((ids < 8) & ~match, MASKED, 0.0).astype(BF16)
        places = jnp.stack([rows_pos, cols_pos], axis=1).astype(F32)
        grad_two = jnp.where(live[:, None], cotangent[0], jnp.zeros((), BF16))
        return (key_mask, query_mask, places, grad_two,
                vectors[4:7].reshape(1, 3 * width), vectors[8:12].reshape(1, 4 * width))

    if quick:
        weights, slots, tables = gather_pieces(master, inverse, core, me, devices, freqs, make_angles, x, make_norm, make_tables())
    else:
        low = lax.all_gather(master.astype(BF16), "dp", axis=0, tiled=True)
        weights = low.reshape(devices, block_rows, width)[inverse].reshape(stack, width)
        slots = jnp.zeros((4, devices), jnp.int32)
        tables = make_angles(freqs) + (make_norm(x),) + make_tables()
    cosine, sine, first_in, key_mask, query_mask, places, grad_two, bias_qkv, bias_one = tables
    here = core.reshape(1).astype(jnp.int32)
    query, key, value, attn, stat, *placed = attend(
        here, slots, first_in, bias_qkv,
        cosine, sine, query_mask, key_mask, weights, stack,
    )
    if quick:
        weights = placed[0]
    whole_rows = block_rows if quick else 0
    block_out, grad_middle, grad_attn, sums, bias_up, keep_mlp, give_mlp = mlp(
        here, x, attn, grad_two, vectors, weights, bias_one, whole_rows
    )
    pairs = width // 128
    tie = lax.optimization_barrier
    if quick:
        pos = quarters(core, me)
        got = lax.ppermute(give_mlp, "group", SWAP)
    back = None
    cuts = (0, 1, pairs - 1, pairs)
    for start, stop in zip(cuts[:-1], cuts[1:]):
        back = attend_back(
            start, stop, back, query, key, value, grad_attn, attn, stat, cosine, sine, query_mask, key_mask, places
        )
        if quick and start == 0:
            send, back = tie((fold(pos, keep_mlp, got, (0, 1)), back))
            came = cross(send, 1, 2, devices)
        if quick and start == 1:
            send, back = tie((fold(pos, keep_mlp, got, (2,), ((came, 0),)), back))
            again = cross(send, 2, 1, devices)
    grad_q, grad_k, grad_v, grad_bias, grad_freq = back
    keep_qkv, give_qkv = qkv_grad(here, grad_q, grad_k, grad_v, first_in, whole_rows)
    if quick:
        again, give_qkv = tie((again, give_qkv))
        low, grad_v, give_qkv = tie((fold(pos, keep_mlp, got, (3,), ((came, 1), (again, 0)))[0], grad_v, give_qkv))
        late = sum_z(low, me, devices)
    if quick:
        got_qkv = lax.ppermute(give_qkv, "group", SWAP)
        send = fold(pos, keep_qkv, got_qkv, (0, 1))
        third = send.shape[2] // 3
        send = [send[:, :, third * i:third * (i + 1)] for i in range(3)]
        send, grad_v = tie((send, grad_v))
    input_grad, local_vec = input_back(
        grad_q, grad_k, grad_v, weights, x, grad_middle, vectors, sums, grad_bias, grad_freq, bias_up
    )
    if quick:
        send[2], local_vec = tie((send[2], local_vec))
        came = [cross(a, 1, 2, devices) for a in send]
        came, local_vec, late = tie((came, local_vec, late))
        came = jnp.concatenate(came, axis=2)
        again = cross(fold(pos, keep_qkv, got_qkv, (2,), ((came, 0),)), 2, 1, devices)
        vec_total = sum_part(local_vec + lax.ppermute(local_vec, "group", SWAP), devices, 4, devices)
        again, vec_total = tie((again, vec_total))
        early = sum_z(fold(pos, keep_qkv, got_qkv, (3,), ((came, 1), (again, 0)))[0], me, devices)
        early, vec_total = tie((early, sum_part(vec_total, devices, 1, 4)))
        load = pack(owner_block, early, late)
        mine = lax.all_to_all(load, "dp", 0, 0, tiled=True)
        other = lax.ppermute(mine, "group", SWAP)
        shape = (devices // 4, 2, 2, *load.shape[1:])
        own = (owner_block[me] % 2 == core).astype(jnp.int32).reshape(1)
        mat_grad, mat_second, mat_weight, vec_grad, vec_second_new, vec_weight, norm = adam_rows(
            own, mine.reshape(shape), other.reshape(shape), vec_total, vectors, vec_first, vec_second,
            master, first_mom, second_mom,
        )
        grad_norm = norm.reshape(())
    else:
        vec_total = lax.psum(local_vec, CORES)
        share = reduce_plain(jnp.concatenate([keep_qkv, keep_mlp]), owner_block, devices)
        square = lax.psum(jnp.sum(share * share), "dp")
        grad_norm = jnp.sqrt(square + jnp.sum(vec_total * vec_total))
        clip = jnp.minimum(1.0, 1.0 / (grad_norm + 1e-06))
        mat_grad = share * clip
        mat_second, mat_weight = adam(master, first_mom, second_mom, mat_grad, 0.02, 0.05)
        vec_grad = vec_total * clip
        vec_second_new, vec_weight = adam(vectors, vec_first, vec_second, vec_grad, 0.2, 0.0)
    return (
        block_out[None],
        input_grad[None],
        mat_grad,
        mat_second,
        mat_weight,
        vec_grad,
        vec_second_new,
        vec_weight,
        grad_norm,
    )


def solution(mesh):
    return jax.shard_map(
        local,
        mesh=mesh,
        in_specs=(
            P("group", "dp", None),
            P("group", "dp", None),
            P("group", "dp"),
            P("group", "dp"),
            P(),
            P("dp", None),
            P("dp", None),
            P("dp", None),
            P(),
            P(),
            P(),
        ),
        out_specs=(
            P("group", "dp", None),
            P("group", "dp", None),
            P("dp", None),
            P("dp", None),
            P("dp", None),
            P(),
            P(),
            P(),
            P(),
        ),
        check_vma=False,
    )
```

```python
import functools
import jax
import jax.numpy as jnp
from jax import lax
from jax.experimental import pallas as pl
from jax.experimental.pallas import tpu as pltpu

F32 = jnp.float32
BF16 = jnp.bfloat16
LAST = (((1,), (1,)), ((), ()))
FIRST = (((0,), (0,)), ((), ()))
PLAIN = (((1,), (0,)), ((), ()))
MASKED = -1e9
SHORT = pl.CostEstimate(flops=1000, bytes_accessed=1000, transcendentals=0)


def mm(left, right, dims):
    return lax.dot_general(left, right, dims, preferred_element_type=F32)


def norm_parts(value):
    centre = value - jnp.mean(value, axis=-1, keepdims=True)
    spread = jnp.mean(centre * centre, axis=-1, keepdims=True)
    inverse = lax.rsqrt(spread + 1e-6)
    return centre * inverse, inverse


def norm_back(unit, inverse, grad, gain):
    scaled = grad * gain
    first = jnp.mean(scaled, axis=-1, keepdims=True)
    second = jnp.mean(scaled * unit, axis=-1, keepdims=True)
    return inverse * (scaled - first - unit * second)


def swap_halves(value):
    lane = lax.broadcasted_iota(jnp.int32, value.shape, 1)
    return jnp.where(
        lane % 64 < 32, pltpu.roll(value, 96, 1), pltpu.roll(value, 32, 1)
    )


def split3(value):
    one = value.astype(BF16).astype(F32)
    rest = value - one
    two = rest.astype(BF16).astype(F32)
    return one, two, rest - two


LARGE = 208
SMALL = 80


def place_pieces(core, slot_ref, mine, other, block, side, dst, sem):
    for which, (first, second, small) in enumerate((mine, other)):
        @pl.when((core == side) if which == 0 else (core != side))
        def _():
            large_slot = slot_ref[2 * which, block]
            small_slot = slot_ref[2 * which + 1, block]

            @pl.when(large_slot < 8)
            def _():
                pltpu.make_async_copy(first.at[large_slot], dst(0, LARGE), sem).start()

            @pl.when(large_slot >= 8)
            def _():
                pltpu.make_async_copy(second.at[large_slot - 8], dst(0, LARGE), sem).start()

            pltpu.make_async_copy(small.at[small_slot], dst(LARGE, SMALL), sem).start()


def attend_kernel(blocks, core_ref, slot_ref, n1_ref, bq_ref, bk_ref, bv_ref,
                  cos_ref, sin_ref, qm_ref, km_ref, *rest):
    if blocks:
        mine, other = rest[0:3], rest[3:6]
        q_ref, k_ref, v_ref, attn_ref, stat_ref, w_ref, w_s, near, far, back = rest[6:]
    else:
        w_ref, q_ref, k_ref, v_ref, attn_ref, stat_ref, w_s, near = rest
    count, width = n1_ref.shape
    step = pl.program_id(0)

    @pl.when(step == 0)
    def _():
        if blocks:
            core = core_ref[0]
            rows = w_ref.shape[0] // blocks

            def start(block, sem):
                for side in (0, 1):
                    def dst(offset, size):
                        base = block * rows + side * (rows // 2) + offset
                        return w_s.at[pl.ds(pl.multiple_of(base, 16), size)]
                    place_pieces(core, slot_ref, mine, other, block, side, dst, sem)

            def near_block(block, carry):
                start(block, near)
                return carry

            def far_block(block, carry):
                start(block, far)
                return carry

            lax.fori_loop(0, 3 * width // rows, near_block, 0)
            lax.fori_loop(3 * width // rows, blocks, far_block, 0)
        else:
            pltpu.make_async_copy(w_ref.at[pl.ds(0, 3 * width)], w_s, near).start()
        head = w_s.at[pl.ds(0, 3 * width)]
        pltpu.make_async_copy(head, head, near).wait()

    if blocks:
        @pl.when(step == 1)
        def _():
            tail = w_s.at[pl.ds(3 * width, w_s.shape[0] - 3 * width)]
            pltpu.make_async_copy(tail, tail, far).wait()
            pltpu.make_async_copy(w_s, w_ref, back).start()

    def third(j):
        return w_s[pl.ds(pl.multiple_of(j * width + step * 128, 128), 128), :]

    w = jnp.concatenate([third(0), third(1), third(2)], axis=0)
    qkv = mm(n1_ref[...], w, LAST)
    q = qkv[:, :128] + bq_ref[...]
    k = qkv[:, 128:256] + bk_ref[...]
    v = (qkv[:, 256:] + bv_ref[...]).astype(BF16)
    c = cos_ref[...]
    s = sin_ref[...]
    qr = ((q * c + swap_halves(q) * s).astype(BF16).astype(F32) * 0.125).astype(BF16)
    kr = (k * c + swap_halves(k) * s).astype(BF16)
    q_ref[...] = qr
    k_ref[...] = kr
    v_ref[...] = v
    lane = lax.broadcasted_iota(jnp.int32, (1, 128), 1)
    k_aug = jnp.concatenate([kr, km_ref[...]], axis=1)
    v_aug = jnp.concatenate([v, jnp.ones((count, 128), BF16)], axis=1)
    zero = jnp.zeros((), BF16)
    tile = 256
    for i in range(count // tile):
        rows = pl.ds(i * tile, tile)
        out = None
        stats = []
        for h in (0, 1):
            mine_lanes = (lane // 64) == h
            qa = jnp.concatenate(
                [jnp.where(mine_lanes, qr[i * tile:(i + 1) * tile], zero), qm_ref[rows, :]], axis=1)
            scores = mm(qa, k_aug, LAST)
            top = jnp.max(scores, axis=-1, keepdims=True)
            e = jnp.exp(scores - top).astype(BF16)
            o = mm(e, v_aug, PLAIN)
            total = o[:, 128:]
            o = o[:, :128] / total
            out = o if out is None else jnp.where(lane < 64, out, o)
            stats.append(top + jnp.log(total[:, :1]))
        attn_ref[rows, :] = out.astype(BF16)
        stat_ref[rows, :] = jnp.where(lane < 64, stats[0], stats[1])

    if blocks:
        @pl.when(step == pl.num_programs(0) - 1)
        def _():
            pltpu.make_async_copy(w_s, w_ref, back).wait()


def attend(core, slots, n1, bqkv, cos, sin, qm, km, weights, stack):
    count, width = n1.shape
    pairs = width // 128
    pieces = isinstance(weights, tuple)
    blocks = slots.shape[1] if pieces else 0
    whole = lambda p: (0, 0)
    col = lambda p: (0, p)
    smem = pl.BlockSpec(memory_space=pltpu.SMEM)
    hbm = pl.BlockSpec(memory_space=pl.ANY)
    given = weights if pieces else (weights,)
    specs = [smem, smem] + [
        pl.BlockSpec((count, width), whole),
        pl.BlockSpec((1, 128), col),
        pl.BlockSpec((1, 128), lambda p: (0, p + pairs)),
        pl.BlockSpec((1, 128), lambda p: (0, p + 2 * pairs)),
        pl.BlockSpec((count, 128), col),
        pl.BlockSpec((count, 128), col),
        pl.BlockSpec((count, 128), whole),
        pl.BlockSpec((count, 128), whole),
    ] + [hbm] * len(given)
    outs = [pl.BlockSpec((count, 128), col)] * 5
    shape = lambda d: jax.ShapeDtypeStruct((count, width), d)
    shapes = [shape(BF16)] * 4 + [shape(F32)]
    scratch = [pltpu.VMEM((stack if pieces else 3 * width, width), BF16), pltpu.SemaphoreType.DMA]
    if pieces:
        outs.append(hbm)
        shapes.append(jax.ShapeDtypeStruct((stack, width), BF16))
        scratch += [pltpu.SemaphoreType.DMA] * 2
    return pl.pallas_call(
        functools.partial(attend_kernel, blocks),
        grid=(pairs,),
        in_specs=specs,
        out_specs=outs,
        out_shape=shapes,
        scratch_shapes=scratch,
        compiler_params=pltpu.CompilerParams(vmem_limit_bytes=28 * 2**20),
        cost_estimate=SHORT,
        name="attend",
    )(core, slots, n1, bqkv, bqkv, bqkv, cos, sin, qm, km, *given)


def gelu_both(x):
    cdf = 0.5 + 0.5 * lax.erf(x * 0.7071067811865476)
    return x * cdf, cdf + x * jnp.exp(x * x * -0.5) * 0.3989422804014327


def send_rows(core, block_rows, stage, row, base, keep_ref, give_ref, sem):
    if not block_rows:
        rows = stage.shape[0]
        pltpu.make_async_copy(
            stage, keep_ref.at[pl.ds(pl.multiple_of(row - base, 64), rows)], sem
        ).start()
        return

    def one(index, carry):
        at = row + 64 * index
        block = lax.div(at, block_rows)
        inner = pl.ds(pl.multiple_of(at - block * block_rows, 64), 64)
        slot = lax.div(block, 2) - base // 2
        source = stage.at[pl.ds(pl.multiple_of(64 * index, 64), 64)]
        own = lax.rem(block, 2) == core

        @pl.when(own)
        def _():
            pltpu.make_async_copy(source, keep_ref.at[slot, inner], sem).start()

        @pl.when(jnp.logical_not(own))
        def _():
            pltpu.make_async_copy(source, give_ref.at[slot, inner], sem).start()

        return carry

    lax.fori_loop(0, stage.shape[0] // 64, one, 0)


def mlp_kernel(block_rows, base, core_ref, x_ref, at_ref, dz_ref, vec_ref, wo_ref, w1_ref, w2_ref, b1_ref,
               out_ref, dm_ref, da_ref, sums_ref, gb_ref, keep_ref, give_ref,
               middle_s, n2_s, acc_s, stage_s, proj_s, sems):
    step = pl.program_id(0)
    last = pl.num_programs(0) - 1
    count, width = x_ref.shape
    core = core_ref[0]
    tile = w1_ref.shape[0]

    @pl.when(step == 0)
    def _():
        middle = x_ref[...].astype(F32) + mm(at_ref[...], wo_ref[...], LAST) + vec_ref[7:8, :]
        middle_s[...] = middle
        unit, _ = norm_parts(middle)
        n2_s[...] = (unit * vec_ref[2:3, :] + vec_ref[3:4, :]).astype(BF16)
        acc_s[...] = jnp.zeros_like(acc_s)
        dm_ref[...] = jnp.zeros_like(dm_ref)

    slot = lax.rem(step, 2)

    @pl.when(step >= 2)
    def _():
        pltpu.make_async_copy(stage_s.at[slot], stage_s.at[slot], sems.at[slot]).wait()

    n2 = n2_s[...]
    dz = dz_ref[...]
    w1 = w1_ref[...]
    w2 = w2_ref[...]
    pre = mm(w1, n2, LAST) + b1_ref[...].reshape(tile, 1)
    back = mm(w2, dz, LAST)
    act, slope = gelu_both(pre)
    hidden = act.astype(BF16)
    stage_s[slot, 1] = mm(hidden, dz, PLAIN).astype(BF16)
    dpre = (back * slope).astype(BF16)
    gb_ref[...] = jnp.sum(dpre.astype(F32), axis=1, keepdims=True).reshape(1, tile)
    stage_s[slot, 0] = mm(dpre, n2, PLAIN).astype(BF16)
    acc_s[...] += mm(hidden, w2, FIRST)
    dm_ref[...] += mm(dpre, w1, FIRST)
    for j in (0, 1):
        send_rows(core, block_rows, stage_s.at[slot, j], (4 + 4 * j) * width + step * tile,
                  base, keep_ref, give_ref, sems.at[slot])

    @pl.when(step == last)
    def _():
        middle = middle_s[...]
        out_ref[...] = (middle + acc_s[...] + vec_ref[12:13, :]).astype(BF16)
        unit, inverse = norm_parts(middle)
        dn = dm_ref[...]
        dy = dz_ref[...].astype(F32)
        dm = dy + norm_back(unit, inverse, dn, vec_ref[2:3, :])
        dm_ref[...] = dm
        low = dm.astype(BF16)
        row = lambda a: jnp.sum(a, axis=0, keepdims=True)
        sums_ref[...] = jnp.concatenate(
            [row(dn * unit), row(dn), row(low.astype(F32)), row(dy), jnp.zeros((4, width), F32)], axis=0)
        proj_s[...] = mm(low, at_ref[...], FIRST).astype(BF16)
        send_rows(core, block_rows, proj_s, 3 * width, base, keep_ref, give_ref, sems.at[2])
        da_ref[...] = mm(low, wo_ref[...], PLAIN).astype(BF16)
        pltpu.make_async_copy(stage_s.at[slot], stage_s.at[slot], sems.at[slot]).wait()
        pltpu.make_async_copy(stage_s.at[1 - slot], stage_s.at[1 - slot], sems.at[1 - slot]).wait()
        pltpu.make_async_copy(proj_s, proj_s, sems.at[2]).wait()


def grad_shapes(block_rows, rows, width):
    if block_rows:
        half = jax.ShapeDtypeStruct((rows // block_rows // 2, block_rows, width), BF16)
        return [half, half]
    return [jax.ShapeDtypeStruct((rows, width), BF16), jax.ShapeDtypeStruct((16, width), BF16)]


def mlp(core, x, attn, dz, vectors, weights, b1, block_rows, tile=512):
    count, width = x.shape
    units = 4 * width
    stack = weights.shape[0]
    base = 3 * width // block_rows if block_rows else 3 * width
    whole = lambda t: (0, 0)
    big = pl.BlockSpec((count, width), whole)
    hbm = pl.BlockSpec(memory_space=pl.ANY)
    return pl.pallas_call(
        functools.partial(mlp_kernel, block_rows, base),
        grid=(units // tile,),
        in_specs=[pl.BlockSpec(memory_space=pltpu.SMEM), big, big, big, pl.BlockSpec(vectors.shape, whole),
                  pl.BlockSpec((width, width), lambda t: (3, 0)),
                  pl.BlockSpec((tile, width), lambda t: (4 * width // tile + t, 0)),
                  pl.BlockSpec((tile, width), lambda t: (8 * width // tile + t, 0)),
                  pl.BlockSpec((1, tile), lambda t: (0, t))],
        out_specs=[big, big, big, pl.BlockSpec((8, width), whole), pl.BlockSpec((1, tile), lambda t: (0, t)), hbm, hbm],
        out_shape=[
            jax.ShapeDtypeStruct((count, width), BF16),
            jax.ShapeDtypeStruct((count, width), F32),
            jax.ShapeDtypeStruct((count, width), BF16),
            jax.ShapeDtypeStruct((8, width), F32),
            jax.ShapeDtypeStruct((1, units), F32),
        ] + grad_shapes(block_rows, stack - 3 * width, width),
        scratch_shapes=[
            pltpu.VMEM((count, width), F32),
            pltpu.VMEM((count, width), BF16),
            pltpu.VMEM((count, width), F32),
            pltpu.VMEM((2, 2, tile, width), BF16),
            pltpu.VMEM((width, width), BF16),
            pltpu.SemaphoreType.DMA((3,)),
        ],
        compiler_params=pltpu.CompilerParams(vmem_limit_bytes=60 * 2**20),
        cost_estimate=SHORT,
        name="mlp",
    )(core, x, attn, dz, vectors, weights, weights, weights, b1)


def back_kernel(first, q_ref, k_ref, v_ref, da_ref, at_ref, stat_ref, cos_ref, sin_ref,
                qm_ref, km_ref, pos_ref, *rest):
    dq_ref, dk_ref, dv_ref, gb_ref, gf_ref = rest if first else rest[5:]
    count = q_ref.shape[0]
    lane = lax.broadcasted_iota(jnp.int32, (1, 128), 1)
    zero = jnp.zeros((), BF16)
    q = q_ref[...]
    k = k_ref[...]
    v = v_ref[...]
    da = da_ref[...]
    prod = da.astype(F32) * at_ref[...].astype(F32)
    qm = qm_ref[...].astype(F32)
    k_aug = jnp.concatenate([k, km_ref[...]], axis=1)
    v_aug = jnp.concatenate([v, jnp.broadcast_to((lane < 2).astype(BF16), (count, 128))], axis=1)
    tile = 256
    dq = dk = dv = None
    for h in (0, 1):
        mine = (lane // 64) == h
        qh = jnp.where(mine, q, zero)
        kh = jnp.where(mine, k, zero)
        dah = jnp.where(mine, da, zero)
        delta = jnp.sum(jnp.where(mine, prod, 0.0), axis=-1, keepdims=True)
        d1, d2, _ = split3(delta)
        l1, l2, l3 = split3(stat_ref[:, 64 * h:64 * h + 1])
        extra = jnp.where(lane == 8, -l1, jnp.where(lane == 9, -l2, jnp.where(lane == 10, -l3, qm)))
        q_aug = jnp.concatenate([qh, extra.astype(BF16)], axis=1)
        da_aug = jnp.concatenate(
            [dah, jnp.where(lane == 0, -d1, jnp.where(lane == 1, -d2, 0.0)).astype(BF16)], axis=1)
        dks, dvs, dqh = [], [], None
        for i in range(count // tile):
            sl = slice(i * tile, (i + 1) * tile)
            p = jnp.exp(mm(k_aug[sl], q_aug, LAST))
            dp = mm(v_aug[sl], da_aug, LAST)
            ds = (p * dp).astype(BF16)
            dvs.append(mm(p.astype(BF16), dah, PLAIN))
            dks.append(mm(ds, qh, PLAIN))
            part = mm(ds, kh[sl], FIRST)
            dqh = part if dqh is None else dqh + part
        dkh = jnp.concatenate(dks, axis=0)
        dvh = jnp.concatenate(dvs, axis=0)
        dq = dqh if dq is None else dq + dqh
        dk = dkh if dk is None else dk + dkh
        dv = dvh if dv is None else dv + dvh
    dq = dq * 0.125
    c = cos_ref[...]
    s = sin_ref[...]
    turned = dq * swap_halves(q.astype(F32) * 8.0) + dk * swap_halves(k.astype(F32))
    turned = jnp.where(lane % 64 < 32, -turned, turned)
    row = lambda a: jnp.sum(a, axis=0, keepdims=True)
    gf_ref[...] = jnp.concatenate(
        [row(turned * pos_ref[:, 0:1]), row(turned * pos_ref[:, 1:2]), jnp.zeros((6, 128), F32)], axis=0)
    dqp = (dq * c - swap_halves(dq) * s).astype(BF16)
    dkp = (dk * c - swap_halves(dk) * s).astype(BF16)
    dvp = dv.astype(BF16)
    gb_ref[...] = jnp.concatenate(
        [row(dqp.astype(F32)), row(dkp.astype(F32)), row(dvp.astype(F32)), jnp.zeros((5, 128), F32)], axis=0)
    dq_ref[...] = dqp
    dk_ref[...] = dkp
    dv_ref[...] = dvp


def attend_back(start, stop, before, q, k, v, da, attn, stat, cos, sin, qm, km, pos):
    count, width = q.shape
    whole = lambda p: (0, 0)
    col = lambda p: (0, p + start)
    tall = pl.BlockSpec((count, 128), col)
    fixed = pl.BlockSpec((count, 128), whole)
    small = pl.BlockSpec((8, 128), col)
    in_specs = [tall] * 8 + [fixed] * 2 + [pl.BlockSpec((count, 2), whole)]
    operands = [q, k, v, da, attn, stat, cos, sin, qm, km, pos]
    aliases = {}
    if before is not None:
        aliases = {len(operands) + i: i for i in range(5)}
        in_specs += [pl.BlockSpec(memory_space=pl.ANY)] * 5
        operands += list(before)
    return pl.pallas_call(
        functools.partial(back_kernel, before is None),
        grid=(stop - start,),
        in_specs=in_specs,
        out_specs=[tall] * 3 + [small] * 2,
        out_shape=[jax.ShapeDtypeStruct((count, width), BF16)] * 3 + [jax.ShapeDtypeStruct((8, width), F32)] * 2,
        input_output_aliases=aliases,
        compiler_params=pltpu.CompilerParams(vmem_limit_bytes=56 * 2**20),
        cost_estimate=SHORT,
        name="attend_back",
    )(*operands)


def qkv_grad_kernel(block_rows, core_ref, dq_ref, dk_ref, dv_ref, n1_ref, keep_ref, give_ref, stage_s, sem):
    width = n1_ref.shape[1]
    cols = dq_ref.shape[1]
    step = pl.program_id(0)
    n1 = n1_ref[...]
    for j, ref in enumerate((dq_ref, dk_ref, dv_ref)):
        stage_s[step, j] = mm(ref[...], n1, FIRST).astype(BF16)
        send_rows(core_ref[0], block_rows, stage_s.at[step, j], j * width + step * cols, 0, keep_ref, give_ref, sem)

    @pl.when(step == pl.num_programs(0) - 1)
    def _():
        pltpu.make_async_copy(stage_s, stage_s, sem).wait()


def qkv_grad(core, dq, dk, dv, n1, block_rows):
    count, width = n1.shape
    cols = width // 2
    tall = pl.BlockSpec((count, cols), lambda p: (0, p))
    hbm = pl.BlockSpec(memory_space=pl.ANY)
    return pl.pallas_call(
        functools.partial(qkv_grad_kernel, block_rows),
        grid=(2,),
        in_specs=[pl.BlockSpec(memory_space=pltpu.SMEM)] + [tall] * 3 + [pl.BlockSpec((count, width), lambda p: (0, 0))],
        out_specs=[hbm, hbm],
        out_shape=grad_shapes(block_rows, 3 * width, width),
        scratch_shapes=[pltpu.VMEM((2, 3, cols, width), BF16), pltpu.SemaphoreType.DMA],
        compiler_params=pltpu.CompilerParams(vmem_limit_bytes=56 * 2**20),
        cost_estimate=SHORT,
        name="qkv_grad",
    )(core, dq, dk, dv, n1)


def input_kernel(dq_ref, dk_ref, dv_ref, w_ref, x_ref, dm_ref, vec_ref, sums_ref, gb_ref, gf_ref, up_ref, ig_ref, out_ref):
    step = pl.program_id(0)
    d = jnp.concatenate([dq_ref[...], dk_ref[...], dv_ref[...]], axis=1)
    dn = mm(d, w_ref[...], PLAIN)
    unit, inverse = norm_parts(x_ref[...].astype(F32))
    ig_ref[...] = dm_ref[...] + norm_back(unit, inverse, dn, vec_ref[0:1, :])
    row = lambda a: jnp.sum(a, axis=0, keepdims=True)
    sums = jnp.concatenate([row(dn * unit), row(dn)], axis=0)

    @pl.when(step == 0)
    def _():
        width = dn.shape[1]
        half = width // 2
        out_ref[0:2] = sums
        out_ref[2:4] = sums_ref[0:2]
        out_ref[4:7] = gb_ref[0:3]
        out_ref[7:8] = sums_ref[2:3]
        for i in range(4):
            out_ref[8 + i:9 + i] = up_ref[:, i * width:(i + 1) * width]
        out_ref[12:13] = sums_ref[3:4]
        lane = lax.broadcasted_iota(jnp.int32, (width, half), 0)
        slot = lax.broadcasted_iota(jnp.int32, (width, half), 1)
        pick = jnp.where((lane // 64 == slot // 32) & (lane % 32 == slot % 32), 1.0, 0.0)
        both = lax.dot_general(gf_ref[...], pick, PLAIN, precision=lax.Precision.HIGHEST, preferred_element_type=F32)
        out_ref[13:14, :half] = both[0:1]
        out_ref[13:14, half:] = both[1:2]

    @pl.when(step > 0)
    def _():
        out_ref[0:2] += sums


def input_back(dq, dk, dv, weights, x, dm, vectors, sums, grad_bias, grad_freq, bias_up):
    count, width = x.shape
    tile = 256
    part = pl.BlockSpec((tile, width), lambda i: (i, 0))
    whole = lambda i: (0, 0)
    fixed = lambda a: pl.BlockSpec(a.shape, whole)
    return pl.pallas_call(
        input_kernel,
        grid=(count // tile,),
        in_specs=[part] * 3 + [pl.BlockSpec((3 * width, width), whole), part, part]
        + [fixed(a) for a in (vectors, sums, grad_bias, grad_freq, bias_up)],
        out_specs=[part, fixed(vectors)],
        out_shape=[jax.ShapeDtypeStruct((count, width), F32), jax.ShapeDtypeStruct(vectors.shape, F32)],
        compiler_params=pltpu.CompilerParams(vmem_limit_bytes=56 * 2**20),
        cost_estimate=SHORT,
        name="input_back",
    )(dq, dk, dv, weights, x, dm, vectors, sums, grad_bias, grad_freq, bias_up)


def fold_kernel(count, pos_ref, *refs):
    out_ref = refs[-1]
    ways = out_ref.shape[0]
    for k in range(ways):
        total = refs[k][...].astype(F32) + refs[ways + k][...].astype(F32)
        for more in refs[2 * ways:-1]:
            total = total + more[0].astype(F32)
        out_ref[k] = total.astype(BF16)


def fold(pos, keep, got, ways, more=()):
    count, rows, width = keep.shape
    some = count // 2
    quarter = [pl.BlockSpec((some, rows // 2, width // 2), lambda i, pos, k=k: (i, pos[k, 0], pos[k, 1])) for k in ways]
    extra = [pl.BlockSpec((1, some, rows // 2, width // 2), lambda i, pos, at=at: (at, i, 0, 0)) for _, at in more]
    out = pl.BlockSpec((len(ways), some, rows // 2, width // 2), lambda i, pos: (0, i, 0, 0))
    shape = jax.ShapeDtypeStruct((len(ways), count, rows // 2, width // 2), BF16)
    return pl.pallas_call(
        functools.partial(fold_kernel, len(more)),
        grid_spec=pltpu.PrefetchScalarGridSpec(
            num_scalar_prefetch=1, grid=(count // some,), in_specs=quarter * 2 + extra, out_specs=out),
        compiler_params=pltpu.CompilerParams(vmem_limit_bytes=40 * 2**20),
        out_shape=shape,
        cost_estimate=SHORT,
        name="fold",
    )(pos, *([keep] * len(ways)), *([got] * len(ways)), *[a for a, _ in more])


def pack_kernel(owner_ref, *refs):
    early, late, out_ref, total_s = refs[:4], refs[4:8], refs[8], refs[9]
    square = None
    start = 0
    for parts in (early, late):
        total = parts[0][...].astype(F32)
        for part in parts[1:]:
            total = total + part[...].astype(F32)
        total_s[start:start + total.shape[0]] = total.astype(BF16)
        start += total.shape[0]
        more = jnp.sum(total * total).reshape(1, 1)
        square = more if square is None else square + more
    rows = total_s.shape[1]
    lane = lax.broadcasted_iota(jnp.int32, (8, out_ref.shape[2]), 1)
    one, two, three = split3(square)
    extra = jnp.where(lane == 0, one, jnp.where(lane == 1, two, jnp.where(lane == 2, three, 0.0))).astype(BF16)
    for p in range(out_ref.shape[0]):
        out_ref[p, :rows] = total_s[lax.div(owner_ref[p], 2)]
        out_ref[p, rows:] = extra


def pack(owner, early, late):
    blocks = early[0].shape[0] + late[0].shape[0]
    rows, cols = early[0].shape[1:]
    vmem = pl.BlockSpec(memory_space=pltpu.VMEM)
    return pl.pallas_call(
        pack_kernel,
        in_specs=[pl.BlockSpec(memory_space=pltpu.SMEM)] + [vmem] * 8,
        out_specs=vmem,
        out_shape=jax.ShapeDtypeStruct((owner.shape[0], rows + 8, cols), BF16),
        scratch_shapes=[pltpu.VMEM((blocks, rows, cols), BF16)],
        compiler_params=pltpu.CompilerParams(vmem_limit_bytes=32 * 2**20),
        cost_estimate=SHORT,
        name="pack",
    )(owner, *early, *late)


def clip_of(square, vec):
    norm = jnp.sqrt(square + jnp.sum(vec * vec).reshape(1, 1))
    return norm, jnp.minimum(1.0, 1.0 / (norm + 1e-06))


def adam_kernel(own_ref, a_ref, b_ref, as_ref, bs_ref, vt_ref, vw_ref, vm_ref, vv_ref, w_ref, m_ref, v_ref,
                g_out, v_out, w_out, vg_out, vv_out, vw_out, norm_out):
    def squares(ref):
        block = ref[...].astype(F32)
        lane = lax.broadcasted_iota(jnp.int32, block.shape, 4)
        row = lax.broadcasted_iota(jnp.int32, block.shape, 3)
        return jnp.sum(jnp.where((lane < 3) & (row == 0), block, 0.0)).reshape(1, 1)

    norm, clip = clip_of(squares(as_ref) + squares(bs_ref), vt_ref[...])
    own = own_ref[0] > 0
    grad = jnp.where(own, a_ref[:, 0, 0].astype(F32), b_ref[:, 0, 0].astype(F32))
    grad = grad[:, :w_ref.shape[0] // grad.shape[0]].reshape(w_ref.shape) * clip
    second, weight = adam(w_ref[...], m_ref[...], v_ref[...], grad, 0.02, 0.05)
    g_out[...] = grad
    v_out[...] = second
    w_out[...] = weight

    @pl.when((pl.program_id(0) == 0) & (pl.program_id(1) == 0))
    def _():
        vec_grad = vt_ref[...] * clip
        second, weight = adam(vw_ref[...], vm_ref[...], vv_ref[...], vec_grad, 0.2, 0.0)
        vg_out[...] = vec_grad
        vv_out[...] = second
        vw_out[...] = weight
        norm_out[...] = norm


def adam_rows(own, mine, other, vec_total, vectors, vec_first, vec_second, weight, first, second):
    rows, width = weight.shape
    deep, tall, wide, piece, cols = mine.shape
    part = pl.BlockSpec((deep, 1, 1, piece, cols), lambda y, x: (0, y, x, 0, 0))
    marks = pl.BlockSpec((deep, tall, wide, 8, 128), lambda y, x: (0, 0, 0, piece // 8 - 1, 0))
    flat = pl.BlockSpec((rows // tall, width // wide), lambda y, x: (y, x))
    vec = pl.BlockSpec(vectors.shape, lambda y, x: (0, 0))
    shape = jax.ShapeDtypeStruct((rows, width), F32)
    small = jax.ShapeDtypeStruct(vectors.shape, F32)
    return pl.pallas_call(
        adam_kernel,
        grid=(tall, wide),
        in_specs=[pl.BlockSpec(memory_space=pltpu.SMEM), part, part, marks, marks] + [vec] * 4 + [flat] * 3,
        out_specs=[flat] * 3 + [vec] * 3 + [pl.BlockSpec((1, 1), lambda y, x: (0, 0))],
        out_shape=[shape] * 3 + [small] * 3 + [jax.ShapeDtypeStruct((1, 1), F32)],
        compiler_params=pltpu.CompilerParams(vmem_limit_bytes=60 * 2**20),
        cost_estimate=SHORT,
        name="adam",
    )(own, mine, other, mine, other, vec_total, vectors, vec_first, vec_second, weight, first, second)


from jax.sharding import PartitionSpec as P

HEADS = 12
STEP = 7


def place_tokens(heights, widths, count):
    sizes = heights * widths
    ends = jnp.cumsum(sizes)
    starts = ends - sizes
    places = jnp.arange(count, dtype=jnp.int32)
    segment = jnp.sum((places[:, None] >= ends[None, :]).astype(jnp.int32), axis=1)
    slots = jnp.arange(heights.shape[0], dtype=jnp.int32)
    picks = (segment[:, None] == slots[None, :]).astype(jnp.int32)
    begin = jnp.sum(picks * starts[None, :], axis=1)
    across = jnp.maximum(jnp.sum(picks * widths[None, :], axis=1), 1)
    offset = places - begin
    live = places < ends[-1]
    return (segment, offset // across, offset % across, live)


def adam(weight, first, second, grad, rate, decay):
    first_new = 0.5 * first + 0.5 * grad
    second_new = 0.5 * second + 0.5 * grad * grad
    correct = 1.0 - 0.5**STEP
    direction = first_new / correct / (jnp.sqrt(second_new / correct) + 1e-08)
    return (second_new, weight - rate * (direction + decay * weight))


def pairwise(bits, total):
    return [(i, i ^ bits) for i in range(total)]


def sum_part(value, devices, step, stop):
    while step < stop:
        value = value + lax.ppermute(value, "dp", pairwise(step, devices))
        step *= 2
    return value


CORES = ("group", "dp")
SWAP = [(0, 1), (1, 0)]


def cross(value, bit0, bit1, devices):
    perm = [(i, i ^ (bit0 if i < devices else bit1)) for i in range(2 * devices)]
    return lax.ppermute(value, CORES, perm)


def along_z(values, devices):
    return [
        lax.ppermute(v, "dp", [(i, (i + 4 * (s + 1)) % devices) for i in range(devices)])
        for s, v in enumerate(values)
    ]


def along_line(value, devices, step, up):
    last = devices // 4
    perm = []
    for z in range(last):
        near = z - 1 if up else z + 1
        far = z - step if up else z + step
        if 0 <= far < last:
            perm += [(4 * near + i, 4 * z + i) for i in range(4)]
    return lax.ppermute(value, "dp", perm)


def gather_pieces(master, inverse, core, me, devices, freqs, make_angles, late, make_late, tables):
    tie = lax.optimization_barrier
    block_rows, width = master.shape
    half = block_rows // 2
    mine = lax.dynamic_slice_in_dim(master, core * half, half, 0).astype(BF16)
    large = mine[:LARGE]
    small = mine[LARGE:]
    z = me // 4
    deep = lax.rem(z - inverse // 4 + 4, 4)
    apart = me ^ inverse
    one = jnp.where(core == 0, apart & 1, (apart >> 1) & 1)
    two = jnp.where(core == 0, (apart >> 1) & 1, apart & 1)
    slots = jnp.stack([
        8 * two + 4 * one + deep,
        4 * deep + 2 * two + one,
        8 * one + 4 * two + deep,
        4 * deep + 2 * one + two,
    ]).astype(jnp.int32)
    up = along_z([large] * 3, devices)
    small = jnp.stack([small, cross(small, 1, 2, devices)])
    small, freqs = tie((small, freqs))
    small = jnp.concatenate([small, cross(small, 2, 1, devices)])
    large = jnp.stack([large] + up)
    large, small, tables, slots, angles = tie((large, small, tables, slots, make_angles(freqs)))
    first = cross(large, 1, 2, devices)
    ups = [along_line(small, devices, 1, True)]
    downs = [along_line(small, devices, 1, False)]
    first, ups[0], downs[0], late = tie((first, ups[0], downs[0], late))
    done = make_late(*late)
    first = jnp.concatenate([large, first])
    second = cross(first, 2, 1, devices)
    for step in (2, 3):
        ups.append(along_line(ups[-1], devices, step, True))
        downs.append(along_line(downs[-1], devices, step, False))
        if step == 2:
            ups[1], downs[1], done = tie((ups[1], downs[1], done))
    small = jnp.concatenate([small] + [jnp.where(z >= s, ups[s - 1], downs[3 - s]) for s in (1, 2, 3)])
    other = [lax.ppermute(a, "group", SWAP) for a in (first, second, small)]
    return (first, second, small, *other), slots, angles + done + tables


def quarters(core, me):
    x, y = me & 1, (me >> 1) & 1
    one = jnp.where(core == 0, x, y)
    two = jnp.where(core == 0, y, x)
    pairs = [(1 - one, 1 - two), (1 - one, two), (one, 1 - two), (one, two)]
    return jnp.stack([
        jnp.stack([jnp.where(core == 0, b, a), jnp.where(core == 0, a, b)]) for a, b in pairs
    ]).astype(jnp.int32)


def sum_z(low, me, devices):
    count, rows, cols = low.shape
    z = me // 4
    low = low.reshape(count, 4, rows // 4, cols)
    pick = lambda at: lax.dynamic_index_in_dim(low, at, 1, keepdims=False)
    return (pick(z), *along_z([pick(lax.rem(z + s, 4)) for s in (1, 2, 3)], devices))


def reduce_plain(local_mat, owner_block, devices):
    rows, width = local_mat.shape
    block_rows = rows // devices
    term = local_mat.reshape(devices, block_rows, width)[owner_block].reshape(rows, width)
    share = lax.psum_scatter(term.astype(F32), "dp", scatter_dimension=0, tiled=True)
    return lax.psum(share.astype(BF16), "group").astype(F32)


def local(
    tokens,
    cotangent,
    grid_h,
    grid_w,
    owner_block,
    master,
    first_mom,
    second_mom,
    vectors,
    vec_first,
    vec_second,
):
    devices = lax.axis_size("dp")
    core = lax.axis_index("group")
    me = lax.axis_index("dp")
    count = tokens.shape[1]
    width = tokens.shape[2]
    heads = HEADS
    head_dim = width // heads
    half = head_dim // 2
    block_rows = master.shape[0]
    stack = devices * block_rows
    quick = devices == 16 and block_rows == 2 * (LARGE + SMALL) and width % 256 == 0
    inverse = jnp.argsort(owner_block)
    segment, rows_pos, cols_pos, live = place_tokens(grid_h[0], grid_w[0], count)
    x = tokens[0]

    def spread(part):
        return jnp.broadcast_to(part.reshape(heads, 1, half), (heads, 2, half)).reshape(1, width)

    freqs = (spread(vectors[13, : width // 2]), spread(vectors[13, width // 2 :]))

    def make_angles(freqs):
        down = rows_pos.astype(F32)[:, None]
        right = cols_pos.astype(F32)[:, None]
        angle = down * freqs[0] + right * freqs[1]
        lower = (jnp.arange(width) % head_dim < half)[None]
        cosine = jnp.cos(angle)
        sine = jnp.sin(angle)
        return (cosine, jnp.where(lower, -sine, sine))

    late = (x, cotangent[0])

    def make_late(x, cot):
        unit, _ = norm_parts(x.astype(F32))
        grad_two = jnp.where(live[:, None], cot, jnp.zeros((), BF16))
        return ((unit * vectors[0] + vectors[1]).astype(BF16), grad_two)

    def make_tables():
        ids = jnp.arange(128)[None]
        match = segment[:, None] == ids
        key_mask = jnp.where(match | ((ids >= 8) & (ids < 11)), 1.0, 0.0).astype(BF16)
        query_mask = jnp.where((ids < 8) & ~match, MASKED, 0.0).astype(BF16)
        places = jnp.stack([rows_pos, cols_pos], axis=1).astype(F32)
        return (key_mask, query_mask, places,
                vectors[4:7].reshape(1, 3 * width), vectors[8:12].reshape(1, 4 * width))

    if quick:
        weights, slots, tables = gather_pieces(master, inverse, core, me, devices, freqs, make_angles, late, make_late, make_tables())
    else:
        low = lax.all_gather(master.astype(BF16), "dp", axis=0, tiled=True)
        weights = low.reshape(devices, block_rows, width)[inverse].reshape(stack, width)
        slots = jnp.zeros((4, devices), jnp.int32)
        tables = make_angles(freqs) + make_late(*late) + make_tables()
    cosine, sine, first_in, grad_two, key_mask, query_mask, places, bias_qkv, bias_one = tables
    here = core.reshape(1).astype(jnp.int32)
    query, key, value, attn, stat, *placed = attend(
        here, slots, first_in, bias_qkv,
        cosine, sine, query_mask, key_mask, weights, stack,
    )
    if quick:
        weights = placed[0]
    whole_rows = block_rows if quick else 0
    block_out, grad_middle, grad_attn, sums, bias_up, keep_mlp, give_mlp = mlp(
        here, x, attn, grad_two, vectors, weights, bias_one, whole_rows
    )
    pairs = width // 128
    tie = lax.optimization_barrier
    if quick:
        pos = quarters(core, me)
        got = lax.ppermute(give_mlp, "group", SWAP)
    back = None
    cuts = (0, 1, pairs - 1, pairs)
    for start, stop in zip(cuts[:-1], cuts[1:]):
        back = attend_back(
            start, stop, back, query, key, value, grad_attn, attn, stat, cosine, sine, query_mask, key_mask, places
        )
        if quick and start == 0:
            send, back = tie((fold(pos, keep_mlp, got, (0, 1)), back))
            came = cross(send, 1, 2, devices)
        if quick and start == 1:
            send, back = tie((fold(pos, keep_mlp, got, (2,), ((came, 0),)), back))
            again = cross(send, 2, 1, devices)
    grad_q, grad_k, grad_v, grad_bias, grad_freq = back
    keep_qkv, give_qkv = qkv_grad(here, grad_q, grad_k, grad_v, first_in, whole_rows)
    if quick:
        again, give_qkv = tie((again, give_qkv))
        low, grad_v, give_qkv = tie((fold(pos, keep_mlp, got, (3,), ((came, 1), (again, 0)))[0], grad_v, give_qkv))
        late = sum_z(low, me, devices)
    if quick:
        got_qkv = lax.ppermute(give_qkv, "group", SWAP)
        send = fold(pos, keep_qkv, got_qkv, (0, 1))
        third = send.shape[2] // 3
        send = [send[:, :, third * i:third * (i + 1)] for i in range(3)]
        send, grad_v = tie((send, grad_v))
    input_grad, local_vec = input_back(
        grad_q, grad_k, grad_v, weights, x, grad_middle, vectors, sums, grad_bias, grad_freq, bias_up
    )
    if quick:
        send[2], local_vec = tie((send[2], local_vec))
        came = [cross(a, 1, 2, devices) for a in send]
        came, local_vec, late = tie((came, local_vec, late))
        came = jnp.concatenate(came, axis=2)
        again = cross(fold(pos, keep_qkv, got_qkv, (2,), ((came, 0),)), 2, 1, devices)
        vec_total = sum_part(local_vec + lax.ppermute(local_vec, "group", SWAP), devices, 4, devices)
        again, vec_total = tie((again, vec_total))
        early = sum_z(fold(pos, keep_qkv, got_qkv, (3,), ((came, 1), (again, 0)))[0], me, devices)
        early, vec_total = tie((early, sum_part(vec_total, devices, 1, 4)))
        load = pack(owner_block, early, late)
        mine = lax.all_to_all(load, "dp", 0, 0, tiled=True)
        other = lax.ppermute(mine, "group", SWAP)
        shape = (devices // 4, 2, 2, *load.shape[1:])
        own = (owner_block[me] % 2 == core).astype(jnp.int32).reshape(1)
        mat_grad, mat_second, mat_weight, vec_grad, vec_second_new, vec_weight, norm = adam_rows(
            own, mine.reshape(shape), other.reshape(shape), vec_total, vectors, vec_first, vec_second,
            master, first_mom, second_mom,
        )
        grad_norm = norm.reshape(())
    else:
        vec_total = lax.psum(local_vec, CORES)
        share = reduce_plain(jnp.concatenate([keep_qkv, keep_mlp]), owner_block, devices)
        square = lax.psum(jnp.sum(share * share), "dp")
        grad_norm = jnp.sqrt(square + jnp.sum(vec_total * vec_total))
        clip = jnp.minimum(1.0, 1.0 / (grad_norm + 1e-06))
        mat_grad = share * clip
        mat_second, mat_weight = adam(master, first_mom, second_mom, mat_grad, 0.02, 0.05)
        vec_grad = vec_total * clip
        vec_second_new, vec_weight = adam(vectors, vec_first, vec_second, vec_grad, 0.2, 0.0)
    return (
        block_out[None],
        input_grad[None],
        mat_grad,
        mat_second,
        mat_weight,
        vec_grad,
        vec_second_new,
        vec_weight,
        grad_norm,
    )


def solution(mesh):
    return jax.shard_map(
        local,
        mesh=mesh,
        in_specs=(
            P("group", "dp", None),
            P("group", "dp", None),
            P("group", "dp"),
            P("group", "dp"),
            P(),
            P("dp", None),
            P("dp", None),
            P("dp", None),
            P(),
            P(),
            P(),
        ),
        out_specs=(
            P("group", "dp", None),
            P("group", "dp", None),
            P("dp", None),
            P("dp", None),
            P("dp", None),
            P(),
            P(),
            P(),
            P(),
        ),
        check_vma=False,
    )
```

```python
import functools
import jax
import jax.numpy as jnp
from jax import lax
from jax.experimental import pallas as pl
from jax.experimental.pallas import tpu as pltpu

F32 = jnp.float32
BF16 = jnp.bfloat16
LAST = (((1,), (1,)), ((), ()))
FIRST = (((0,), (0,)), ((), ()))
PLAIN = (((1,), (0,)), ((), ()))
MASKED = -1e9
MORE = 40
SHORT = pl.CostEstimate(flops=1000, bytes_accessed=1000, transcendentals=0)


def mm(left, right, dims):
    return lax.dot_general(left, right, dims, preferred_element_type=F32)


def norm_parts(value):
    centre = value - jnp.mean(value, axis=-1, keepdims=True)
    spread = jnp.mean(centre * centre, axis=-1, keepdims=True)
    inverse = lax.rsqrt(spread + 1e-6)
    return centre * inverse, inverse


def norm_back(unit, inverse, grad, gain):
    scaled = grad * gain
    first = jnp.mean(scaled, axis=-1, keepdims=True)
    second = jnp.mean(scaled * unit, axis=-1, keepdims=True)
    return inverse * (scaled - first - unit * second)


def swap_halves(value):
    lane = lax.broadcasted_iota(jnp.int32, value.shape, 1)
    return jnp.where(
        lane % 64 < 32, pltpu.roll(value, 96, 1), pltpu.roll(value, 32, 1)
    )


def split3(value):
    one = value.astype(BF16).astype(F32)
    rest = value - one
    two = rest.astype(BF16).astype(F32)
    return one, two, rest - two


LARGE = 208
SMALL = 80


def place_pieces(core, slot_ref, mine, other, block, side, dst, sem):
    for which, (first, second, small) in enumerate((mine, other)):
        @pl.when((core == side) if which == 0 else (core != side))
        def _():
            large_slot = slot_ref[2 * which, block]
            small_slot = slot_ref[2 * which + 1, block]

            @pl.when(large_slot < 8)
            def _():
                pltpu.make_async_copy(first.at[large_slot], dst(0, LARGE), sem).start()

            @pl.when(large_slot >= 8)
            def _():
                pltpu.make_async_copy(second.at[large_slot - 8], dst(0, LARGE), sem).start()

            pltpu.make_async_copy(small.at[small_slot], dst(LARGE, SMALL), sem).start()


def attend_kernel(blocks, core_ref, slot_ref, n1_ref, bq_ref, bk_ref, bv_ref,
                  cos_ref, sin_ref, qm_ref, km_ref, *rest):
    if blocks:
        mine, other = rest[0:3], rest[3:6]
        q_ref, k_ref, v_ref, attn_ref, stat_ref, w_ref, w_s, near, far, back = rest[6:]
    else:
        w_ref, q_ref, k_ref, v_ref, attn_ref, stat_ref, w_s, near = rest
    count, width = n1_ref.shape
    step = pl.program_id(0)

    @pl.when(step == 0)
    def _():
        if blocks:
            core = core_ref[0]
            rows = w_ref.shape[0] // blocks

            def start(block, sem):
                for side in (0, 1):
                    def dst(offset, size):
                        base = block * rows + side * (rows // 2) + offset
                        return w_s.at[pl.ds(pl.multiple_of(base, 16), size)]
                    place_pieces(core, slot_ref, mine, other, block, side, dst, sem)

            def near_block(block, carry):
                start(block, near)
                return carry

            def far_block(block, carry):
                start(block, far)
                return carry

            lax.fori_loop(0, 3 * width // rows, near_block, 0)
            lax.fori_loop(3 * width // rows, blocks, far_block, 0)
        else:
            pltpu.make_async_copy(w_ref.at[pl.ds(0, 3 * width)], w_s, near).start()
        head = w_s.at[pl.ds(0, 3 * width)]
        pltpu.make_async_copy(head, head, near).wait()

    if blocks:
        @pl.when(step == 1)
        def _():
            tail = w_s.at[pl.ds(3 * width, w_s.shape[0] - 3 * width)]
            pltpu.make_async_copy(tail, tail, far).wait()
            pltpu.make_async_copy(w_s, w_ref, back).start()

    def third(j):
        return w_s[pl.ds(pl.multiple_of(j * width + step * 128, 128), 128), :]

    w = jnp.concatenate([third(0), third(1), third(2)], axis=0)
    qkv = mm(n1_ref[...], w, LAST)
    q = qkv[:, :128] + bq_ref[...]
    k = qkv[:, 128:256] + bk_ref[...]
    v = (qkv[:, 256:] + bv_ref[...]).astype(BF16)
    c = cos_ref[...]
    s = sin_ref[...]
    qr = ((q * c + swap_halves(q) * s).astype(BF16).astype(F32) * 0.125).astype(BF16)
    kr = (k * c + swap_halves(k) * s).astype(BF16)
    q_ref[...] = qr
    k_ref[...] = kr
    v_ref[...] = v
    lane = lax.broadcasted_iota(jnp.int32, (1, 128), 1)
    k_aug = jnp.concatenate([kr, km_ref[...]], axis=1)
    v_aug = jnp.concatenate([v, jnp.ones((count, 128), BF16)], axis=1)
    zero = jnp.zeros((), BF16)
    tile = 256
    for i in range(count // tile):
        rows = pl.ds(i * tile, tile)
        out = None
        stats = []
        for h in (0, 1):
            mine_lanes = (lane // 64) == h
            qa = jnp.concatenate(
                [jnp.where(mine_lanes, qr[i * tile:(i + 1) * tile], zero), qm_ref[rows, :]], axis=1)
            scores = mm(qa, k_aug, LAST)
            top = jnp.max(scores, axis=-1, keepdims=True)
            e = jnp.exp(scores - top).astype(BF16)
            o = mm(e, v_aug, PLAIN)
            total = o[:, 128:]
            o = o[:, :128] / total
            out = o if out is None else jnp.where(lane < 64, out, o)
            stats.append(top + jnp.log(total[:, :1]))
        attn_ref[rows, :] = out.astype(BF16)
        stat_ref[rows, :] = jnp.where(lane < 64, stats[0], stats[1])

    if blocks:
        @pl.when(step == pl.num_programs(0) - 1)
        def _():
            pltpu.make_async_copy(w_s, w_ref, back).wait()


def attend(core, slots, n1, bqkv, cos, sin, qm, km, weights, stack):
    count, width = n1.shape
    pairs = width // 128
    pieces = isinstance(weights, tuple)
    blocks = slots.shape[1] if pieces else 0
    whole = lambda p: (0, 0)
    col = lambda p: (0, p)
    smem = pl.BlockSpec(memory_space=pltpu.SMEM)
    hbm = pl.BlockSpec(memory_space=pl.ANY)
    given = weights if pieces else (weights,)
    specs = [smem, smem] + [
        pl.BlockSpec((count, width), whole),
        pl.BlockSpec((1, 128), col),
        pl.BlockSpec((1, 128), lambda p: (0, p + pairs)),
        pl.BlockSpec((1, 128), lambda p: (0, p + 2 * pairs)),
        pl.BlockSpec((count, 128), col),
        pl.BlockSpec((count, 128), col),
        pl.BlockSpec((count, 128), whole),
        pl.BlockSpec((count, 128), whole),
    ] + [hbm] * len(given)
    outs = [pl.BlockSpec((count, 128), col)] * 5
    shape = lambda d: jax.ShapeDtypeStruct((count, width), d)
    shapes = [shape(BF16)] * 4 + [shape(F32)]
    scratch = [pltpu.VMEM((stack if pieces else 3 * width, width), BF16), pltpu.SemaphoreType.DMA]
    if pieces:
        outs.append(hbm)
        shapes.append(jax.ShapeDtypeStruct((stack, width), BF16))
        scratch += [pltpu.SemaphoreType.DMA] * 2
    return pl.pallas_call(
        functools.partial(attend_kernel, blocks),
        grid=(pairs,),
        in_specs=specs,
        out_specs=outs,
        out_shape=shapes,
        scratch_shapes=scratch,
        compiler_params=pltpu.CompilerParams(vmem_limit_bytes=56 * 2**20),
        cost_estimate=SHORT,
        name="attend",
    )(core, slots, n1, bqkv, bqkv, bqkv, cos, sin, qm, km, *given)


def gelu_both(x):
    cdf = 0.5 + 0.5 * lax.erf(x * 0.7071067811865476)
    return x * cdf, cdf + x * jnp.exp(x * x * -0.5) * 0.3989422804014327


def send_rows(core, block_rows, stage, row, base, keep_ref, give_ref, sem):
    if not block_rows:
        rows = stage.shape[0]
        pltpu.make_async_copy(
            stage, keep_ref.at[pl.ds(pl.multiple_of(row - base, 64), rows)], sem
        ).start()
        return

    half = stage.shape[1] // 2

    def one(index, carry):
        at = row + 64 * index
        block = lax.div(at, block_rows)
        inner = pl.ds(pl.multiple_of(at - block * block_rows, 64), 64)
        rows = pl.ds(pl.multiple_of(64 * index, 64), 64)
        for c in (0, 1):
            @pl.when(core == c)
            def _():
                for own, target in ((c, keep_ref), (1 - c, give_ref)):
                    source = stage.at[rows, pl.ds(own * half, half)]
                    pltpu.make_async_copy(source, target.at[block - base, inner], sem).start()

        return carry

    lax.fori_loop(0, stage.shape[0] // 64, one, 0)


def mlp_kernel(block_rows, base, core_ref, x_ref, at_ref, dz_ref, vec_ref, wo_ref, w1_ref, w2_ref, b1_ref,
               out_ref, dm_ref, da_ref, sums_ref, gb_ref, keep_ref, give_ref,
               middle_s, n2_s, acc_s, stage_s, proj_s, sems):
    step = pl.program_id(0)
    last = pl.num_programs(0) - 1
    count, width = x_ref.shape
    core = core_ref[0]
    tile = w1_ref.shape[0]

    @pl.when(step == 0)
    def _():
        middle = x_ref[...].astype(F32) + mm(at_ref[...], wo_ref[...], LAST) + vec_ref[7:8, :]
        middle_s[...] = middle
        unit, _ = norm_parts(middle)
        n2_s[...] = (unit * vec_ref[2:3, :] + vec_ref[3:4, :]).astype(BF16)
        acc_s[...] = jnp.zeros_like(acc_s)
        dm_ref[...] = jnp.zeros_like(dm_ref)

    slot = lax.rem(step, 2)

    @pl.when(step >= 2)
    def _():
        pltpu.make_async_copy(stage_s.at[slot], stage_s.at[slot], sems.at[slot]).wait()

    n2 = n2_s[...]
    dz = dz_ref[...]
    w1 = w1_ref[...]
    w2 = w2_ref[...]
    pre = mm(w1, n2, LAST) + b1_ref[...].reshape(tile, 1)
    back = mm(w2, dz, LAST)
    act, slope = gelu_both(pre)
    hidden = act.astype(BF16)
    stage_s[slot, 1] = mm(hidden, dz, PLAIN).astype(BF16)
    dpre = (back * slope).astype(BF16)
    gb_ref[...] = jnp.sum(dpre.astype(F32), axis=1, keepdims=True).reshape(1, tile)
    stage_s[slot, 0] = mm(dpre, n2, PLAIN).astype(BF16)
    acc_s[...] += mm(hidden, w2, FIRST)
    dm_ref[...] += mm(dpre, w1, FIRST)
    for j in (0, 1):
        send_rows(core, block_rows, stage_s.at[slot, j], (4 + 4 * j) * width + step * tile,
                  base, keep_ref, give_ref, sems.at[slot])

    @pl.when(step == last)
    def _():
        middle = middle_s[...]
        out_ref[...] = (middle + acc_s[...] + vec_ref[12:13, :]).astype(BF16)
        unit, inverse = norm_parts(middle)
        dn = dm_ref[...]
        dy = dz_ref[...].astype(F32)
        dm = dy + norm_back(unit, inverse, dn, vec_ref[2:3, :])
        dm_ref[...] = dm
        low = dm.astype(BF16)
        row = lambda a: jnp.sum(a, axis=0, keepdims=True)
        sums_ref[...] = jnp.concatenate(
            [row(dn * unit), row(dn), row(low.astype(F32)), row(dy), jnp.zeros((4, width), F32)], axis=0)
        proj_s[...] = mm(low, at_ref[...], FIRST).astype(BF16)
        send_rows(core, block_rows, proj_s, 3 * width, base, keep_ref, give_ref, sems.at[2])
        da_ref[...] = mm(low, wo_ref[...], PLAIN).astype(BF16)
        pltpu.make_async_copy(stage_s.at[slot], stage_s.at[slot], sems.at[slot]).wait()
        pltpu.make_async_copy(stage_s.at[1 - slot], stage_s.at[1 - slot], sems.at[1 - slot]).wait()
        pltpu.make_async_copy(proj_s, proj_s, sems.at[2]).wait()


def grad_shapes(block_rows, rows, width):
    if block_rows:
        half = jax.ShapeDtypeStruct((rows // block_rows, block_rows, width // 2), BF16)
        return [half, half]
    return [jax.ShapeDtypeStruct((rows, width), BF16), jax.ShapeDtypeStruct((16, width), BF16)]


def mlp(core, x, attn, dz, vectors, weights, b1, block_rows, tile=512):
    count, width = x.shape
    units = 4 * width
    stack = weights.shape[0]
    base = 3 * width // block_rows if block_rows else 3 * width
    whole = lambda t: (0, 0)
    big = pl.BlockSpec((count, width), whole)
    hbm = pl.BlockSpec(memory_space=pl.ANY)
    return pl.pallas_call(
        functools.partial(mlp_kernel, block_rows, base),
        grid=(units // tile,),
        in_specs=[pl.BlockSpec(memory_space=pltpu.SMEM), big, big, big, pl.BlockSpec(vectors.shape, whole),
                  pl.BlockSpec((width, width), lambda t: (3, 0)),
                  pl.BlockSpec((tile, width), lambda t: (4 * width // tile + t, 0)),
                  pl.BlockSpec((tile, width), lambda t: (8 * width // tile + t, 0)),
                  pl.BlockSpec((1, tile), lambda t: (0, t))],
        out_specs=[big, big, big, pl.BlockSpec((8, width), whole), pl.BlockSpec((1, tile), lambda t: (0, t)), hbm, hbm],
        out_shape=[
            jax.ShapeDtypeStruct((count, width), BF16),
            jax.ShapeDtypeStruct((count, width), F32),
            jax.ShapeDtypeStruct((count, width), BF16),
            jax.ShapeDtypeStruct((8, width), F32),
            jax.ShapeDtypeStruct((1, units), F32),
        ] + grad_shapes(block_rows, stack - 3 * width, width),
        scratch_shapes=[
            pltpu.VMEM((count, width), F32),
            pltpu.VMEM((count, width), BF16),
            pltpu.VMEM((count, width), F32),
            pltpu.VMEM((2, 2, tile, width), BF16),
            pltpu.VMEM((width, width), BF16),
            pltpu.SemaphoreType.DMA((3,)),
        ],
        compiler_params=pltpu.CompilerParams(vmem_limit_bytes=60 * 2**20),
        cost_estimate=SHORT,
        name="mlp",
    )(core, x, attn, dz, vectors, weights, weights, weights, b1)


def back_kernel(first, q_ref, k_ref, v_ref, da_ref, at_ref, stat_ref, cos_ref, sin_ref,
                qm_ref, km_ref, pos_ref, *rest):
    dq_ref, dk_ref, dv_ref, gb_ref, gf_ref = rest if first else rest[5:]
    count = q_ref.shape[0]
    lane = lax.broadcasted_iota(jnp.int32, (1, 128), 1)
    zero = jnp.zeros((), BF16)
    q = q_ref[...]
    k = k_ref[...]
    v = v_ref[...]
    da = da_ref[...]
    prod = da.astype(F32) * at_ref[...].astype(F32)
    qm = qm_ref[...].astype(F32)
    k_aug = jnp.concatenate([k, km_ref[...]], axis=1)
    v_aug = jnp.concatenate([v, jnp.broadcast_to((lane < 2).astype(BF16), (count, 128))], axis=1)
    tile = 256
    dq = dk = dv = None
    for h in (0, 1):
        mine = (lane // 64) == h
        qh = jnp.where(mine, q, zero)
        kh = jnp.where(mine, k, zero)
        dah = jnp.where(mine, da, zero)
        delta = jnp.sum(jnp.where(mine, prod, 0.0), axis=-1, keepdims=True)
        d1, d2, _ = split3(delta)
        l1, l2, l3 = split3(stat_ref[:, 64 * h:64 * h + 1])
        extra = jnp.where(lane == 8, -l1, jnp.where(lane == 9, -l2, jnp.where(lane == 10, -l3, qm)))
        q_aug = jnp.concatenate([qh, extra.astype(BF16)], axis=1)
        da_aug = jnp.concatenate(
            [dah, jnp.where(lane == 0, -d1, jnp.where(lane == 1, -d2, 0.0)).astype(BF16)], axis=1)
        dks, dvs, dqh = [], [], None
        for i in range(count // tile):
            sl = slice(i * tile, (i + 1) * tile)
            p = jnp.exp(mm(k_aug[sl], q_aug, LAST))
            dp = mm(v_aug[sl], da_aug, LAST)
            ds = (p * dp).astype(BF16)
            dvs.append(mm(p.astype(BF16), dah, PLAIN))
            dks.append(mm(ds, qh, PLAIN))
            part = mm(ds, kh[sl], FIRST)
            dqh = part if dqh is None else dqh + part
        dkh = jnp.concatenate(dks, axis=0)
        dvh = jnp.concatenate(dvs, axis=0)
        dq = dqh if dq is None else dq + dqh
        dk = dkh if dk is None else dk + dkh
        dv = dvh if dv is None else dv + dvh
    dq = dq * 0.125
    c = cos_ref[...]
    s = sin_ref[...]
    turned = dq * swap_halves(q.astype(F32) * 8.0) + dk * swap_halves(k.astype(F32))
    turned = jnp.where(lane % 64 < 32, -turned, turned)
    row = lambda a: jnp.sum(a, axis=0, keepdims=True)
    gf_ref[...] = jnp.concatenate(
        [row(turned * pos_ref[:, 0:1]), row(turned * pos_ref[:, 1:2]), jnp.zeros((6, 128), F32)], axis=0)
    dqp = (dq * c - swap_halves(dq) * s).astype(BF16)
    dkp = (dk * c - swap_halves(dk) * s).astype(BF16)
    dvp = dv.astype(BF16)
    gb_ref[...] = jnp.concatenate(
        [row(dqp.astype(F32)), row(dkp.astype(F32)), row(dvp.astype(F32)), jnp.zeros((5, 128), F32)], axis=0)
    dq_ref[...] = dqp
    dk_ref[...] = dkp
    dv_ref[...] = dvp


def attend_back(start, stop, before, q, k, v, da, attn, stat, cos, sin, qm, km, pos):
    count, width = q.shape
    whole = lambda p: (0, 0)
    col = lambda p: (0, p + start)
    tall = pl.BlockSpec((count, 128), col)
    fixed = pl.BlockSpec((count, 128), whole)
    small = pl.BlockSpec((8, 128), col)
    in_specs = [tall] * 8 + [fixed] * 2 + [pl.BlockSpec((count, 2), whole)]
    operands = [q, k, v, da, attn, stat, cos, sin, qm, km, pos]
    aliases = {}
    if before is not None:
        aliases = {len(operands) + i: i for i in range(5)}
        in_specs += [pl.BlockSpec(memory_space=pl.ANY)] * 5
        operands += list(before)
    return pl.pallas_call(
        functools.partial(back_kernel, before is None),
        grid=(stop - start,),
        in_specs=in_specs,
        out_specs=[tall] * 3 + [small] * 2,
        out_shape=[jax.ShapeDtypeStruct((count, width), BF16)] * 3 + [jax.ShapeDtypeStruct((8, width), F32)] * 2,
        input_output_aliases=aliases,
        compiler_params=pltpu.CompilerParams(vmem_limit_bytes=56 * 2**20),
        cost_estimate=SHORT,
        name="attend_back",
    )(*operands)


def qkv_grad_kernel(block_rows, core_ref, dq_ref, dk_ref, dv_ref, n1_ref, keep_ref, give_ref, stage_s, sem):
    width = n1_ref.shape[1]
    cols = dq_ref.shape[1]
    step = pl.program_id(0)
    n1 = n1_ref[...]
    for j, ref in enumerate((dq_ref, dk_ref, dv_ref)):
        stage_s[step, j] = mm(ref[...], n1, FIRST).astype(BF16)
        send_rows(core_ref[0], block_rows, stage_s.at[step, j], j * width + step * cols, 0, keep_ref, give_ref, sem)

    @pl.when(step == pl.num_programs(0) - 1)
    def _():
        pltpu.make_async_copy(stage_s, stage_s, sem).wait()


def qkv_grad(core, dq, dk, dv, n1, block_rows):
    count, width = n1.shape
    cols = width // 2
    tall = pl.BlockSpec((count, cols), lambda p: (0, p))
    hbm = pl.BlockSpec(memory_space=pl.ANY)
    return pl.pallas_call(
        functools.partial(qkv_grad_kernel, block_rows),
        grid=(2,),
        in_specs=[pl.BlockSpec(memory_space=pltpu.SMEM)] + [tall] * 3 + [pl.BlockSpec((count, width), lambda p: (0, 0))],
        out_specs=[hbm, hbm],
        out_shape=grad_shapes(block_rows, 3 * width, width),
        scratch_shapes=[pltpu.VMEM((2, 3, cols, width), BF16), pltpu.SemaphoreType.DMA],
        compiler_params=pltpu.CompilerParams(vmem_limit_bytes=56 * 2**20),
        cost_estimate=SHORT,
        name="qkv_grad",
    )(core, dq, dk, dv, n1)


def input_kernel(dq_ref, dk_ref, dv_ref, w_ref, x_ref, dm_ref, vec_ref, sums_ref, gb_ref, gf_ref, up_ref, ig_ref, out_ref):
    step = pl.program_id(0)
    d = jnp.concatenate([dq_ref[...], dk_ref[...], dv_ref[...]], axis=1)
    dn = mm(d, w_ref[...], PLAIN)
    unit, inverse = norm_parts(x_ref[...].astype(F32))
    ig_ref[...] = dm_ref[...] + norm_back(unit, inverse, dn, vec_ref[0:1, :])
    row = lambda a: jnp.sum(a, axis=0, keepdims=True)
    sums = jnp.concatenate([row(dn * unit), row(dn)], axis=0)

    @pl.when(step == 0)
    def _():
        width = dn.shape[1]
        half = width // 2
        out_ref[0:2] = sums
        out_ref[2:4] = sums_ref[0:2]
        out_ref[4:7] = gb_ref[0:3]
        out_ref[7:8] = sums_ref[2:3]
        for i in range(4):
            out_ref[8 + i:9 + i] = up_ref[:, i * width:(i + 1) * width]
        out_ref[12:13] = sums_ref[3:4]
        lane = lax.broadcasted_iota(jnp.int32, (width, half), 0)
        slot = lax.broadcasted_iota(jnp.int32, (width, half), 1)
        pick = jnp.where((lane // 64 == slot // 32) & (lane % 32 == slot % 32), 1.0, 0.0)
        both = lax.dot_general(gf_ref[...], pick, PLAIN, precision=lax.Precision.HIGHEST, preferred_element_type=F32)
        out_ref[13:14, :half] = both[0:1]
        out_ref[13:14, half:] = both[1:2]

    @pl.when(step > 0)
    def _():
        out_ref[0:2] += sums


def input_back(dq, dk, dv, weights, x, dm, vectors, sums, grad_bias, grad_freq, bias_up):
    count, width = x.shape
    tile = 256
    part = pl.BlockSpec((tile, width), lambda i: (i, 0))
    whole = lambda i: (0, 0)
    fixed = lambda a: pl.BlockSpec(a.shape, whole)
    return pl.pallas_call(
        input_kernel,
        grid=(count // tile,),
        in_specs=[part] * 3 + [pl.BlockSpec((3 * width, width), whole), part, part]
        + [fixed(a) for a in (vectors, sums, grad_bias, grad_freq, bias_up)],
        out_specs=[part, fixed(vectors)],
        out_shape=[jax.ShapeDtypeStruct((count, width), F32), jax.ShapeDtypeStruct(vectors.shape, F32)],
        compiler_params=pltpu.CompilerParams(vmem_limit_bytes=56 * 2**20),
        cost_estimate=SHORT,
        name="input_back",
    )(dq, dk, dv, weights, x, dm, vectors, sums, grad_bias, grad_freq, bias_up)


def fold_kernel(pos_ref, keep_ref, got_ref, send_ref, hold_ref):
    rows = keep_ref.shape[1] // 2
    deep = 4
    piece = rows // deep
    more, less = MORE, piece - MORE
    for m in range(keep_ref.shape[0] // 2):
        for way in range(4):
            here = pl.ds(pl.multiple_of(pos_ref[way, 0] * rows, 16), rows)
            even, odd = (
                keep_ref[2 * m + e, here, :].astype(F32) + got_ref[2 * m + e, here, :].astype(F32) for e in (0, 1)
            )
            parts = []
            for z in range(deep):
                at = z * piece
                parts.append((
                    jnp.concatenate([even[at:at + more], odd[at:at + less]], axis=0),
                    jnp.concatenate([even[at + more:at + piece], odd[at + less:at + piece]], axis=0),
                ))
            left = jnp.concatenate([a for a, _ in parts], axis=0)
            right = jnp.concatenate([a for _, a in parts], axis=0)
            out = (send_ref, hold_ref)[way // 2]
            out[way % 2, m] = jnp.where(pos_ref[way, 1] == 0, left, right).astype(BF16)


def fold(pos, keep, got):
    count, rows, cols = keep.shape
    some = 4 if count % 4 == 0 else 2
    whole = pl.BlockSpec((some, rows, cols), lambda i, pos: (i, 0, 0))
    out = pl.BlockSpec((2, some // 2, rows // 2, cols), lambda i, pos: (0, i, 0, 0))
    shape = jax.ShapeDtypeStruct((2, count // 2, rows // 2, cols), BF16)
    return pl.pallas_call(
        fold_kernel,
        grid_spec=pltpu.PrefetchScalarGridSpec(
            num_scalar_prefetch=1, grid=(count // some,), in_specs=[whole, whole], out_specs=[out, out]),
        compiler_params=pltpu.CompilerParams(vmem_limit_bytes=40 * 2**20),
        out_shape=[shape, shape],
        cost_estimate=SHORT,
        name="fold",
    )(pos, keep, got)


def pack_kernel(owner_ref, *refs):
    early, late, out_ref, total_s = refs[:4], refs[4:8], refs[8], refs[9]
    square = None
    start = 0
    rows = early[0].shape[1]
    for parts in (early, late):
        total = parts[0][...].astype(F32)
        for part in parts[1:]:
            total = total + part[...].astype(F32)
        total_s[start:start + total.shape[0], :rows] = total
        start += total.shape[0]
        more = jnp.sum(total * total).reshape(1, 1)
        square = more if square is None else square + more
    total_s[:, rows:] = jnp.zeros((start, total_s.shape[1] - rows, total_s.shape[2]), F32)
    lane = lax.broadcasted_iota(jnp.int32, (8, out_ref.shape[2]), 1)
    one, two, three = split3(square)
    extra = jnp.where(lane == 0, one, jnp.where(lane == 1, two, jnp.where(lane == 2, three, 0.0)))
    devices = out_ref.shape[0]
    skip = jnp.where(owner_ref[devices] == 0, MORE, rows - MORE)
    for p in range(devices):
        block = owner_ref[p]
        at = lax.rem(block, 2) * skip
        mine = total_s[lax.div(block, 2), pl.ds(pl.multiple_of(at, 8), MORE), :]
        out_ref[p] = jnp.concatenate([mine, extra], axis=0).astype(BF16)


def pack(owner, x, early, late):
    blocks = early[0].shape[0] + late[0].shape[0]
    rows, cols = early[0].shape[1:]
    vmem = pl.BlockSpec(memory_space=pltpu.VMEM)
    return pl.pallas_call(
        pack_kernel,
        in_specs=[pl.BlockSpec(memory_space=pltpu.SMEM)] + [vmem] * 8,
        out_specs=vmem,
        out_shape=jax.ShapeDtypeStruct((owner.shape[0], MORE + 8, cols), BF16),
        scratch_shapes=[pltpu.VMEM((blocks, rows + 8, cols), F32)],
        compiler_params=pltpu.CompilerParams(vmem_limit_bytes=32 * 2**20),
        cost_estimate=SHORT,
        name="pack",
    )(jnp.concatenate([owner, x.reshape(1).astype(owner.dtype)]), *early, *late)


def clip_of(square, vec):
    norm = jnp.sqrt(square + jnp.sum(vec * vec).reshape(1, 1))
    return norm, jnp.minimum(1.0, 1.0 / (norm + 1e-06))


def adam_kernel(own_ref, a_ref, b_ref, as_ref, bs_ref, vt_ref, vw_ref, vm_ref, vv_ref, w_ref, m_ref, v_ref,
                g_out, v_out, w_out, vg_out, vv_out, vw_out, norm_out):
    def squares(ref):
        block = ref[...].astype(F32)
        lane = lax.broadcasted_iota(jnp.int32, block.shape, 4)
        row = lax.broadcasted_iota(jnp.int32, block.shape, 3)
        return jnp.sum(jnp.where((lane < 3) & (row == 0), block, 0.0)).reshape(1, 1)

    norm, clip = clip_of(squares(as_ref) + squares(bs_ref), vt_ref[...])
    mine = pl.program_id(1) == own_ref[0]
    even = own_ref[1] == 0
    deep = a_ref.shape[0]
    piece = w_ref.shape[0] // deep
    runs = []
    for z in range(deep):
        left, right = (jnp.where(mine, a_ref[z, 0, x].astype(F32), b_ref[z, 0, x].astype(F32)) for x in (0, 1))
        runs.append(jnp.where(
            even,
            jnp.concatenate([left[:MORE], right[:piece - MORE]], axis=0),
            jnp.concatenate([left[:piece - MORE], right[:MORE]], axis=0),
        ))
    grad = jnp.concatenate(runs, axis=0) * clip
    second, weight = adam(w_ref[...], m_ref[...], v_ref[...], grad, 0.02, 0.05)
    g_out[...] = grad
    v_out[...] = second
    w_out[...] = weight

    @pl.when((pl.program_id(0) == 0) & (pl.program_id(1) == 0))
    def _():
        vec_grad = vt_ref[...] * clip
        second, weight = adam(vw_ref[...], vm_ref[...], vv_ref[...], vec_grad, 0.2, 0.0)
        vg_out[...] = vec_grad
        vv_out[...] = second
        vw_out[...] = weight
        norm_out[...] = norm


def adam_rows(own, mine, other, vec_total, vectors, vec_first, vec_second, weight, first, second):
    rows, width = weight.shape
    deep, tall, wide, piece, cols = mine.shape
    part = pl.BlockSpec((deep, 1, wide, piece, cols), lambda y, h: (0, y, 0, 0, 0))
    marks = pl.BlockSpec((deep, tall, wide, 8, 128), lambda y, x: (0, 0, 0, piece // 8 - 1, 0))
    flat = pl.BlockSpec((rows // tall, cols), lambda y, h: (y, h))
    vec = pl.BlockSpec(vectors.shape, lambda y, x: (0, 0))
    shape = jax.ShapeDtypeStruct((rows, width), F32)
    small = jax.ShapeDtypeStruct(vectors.shape, F32)
    return pl.pallas_call(
        adam_kernel,
        grid=(tall, width // cols),
        in_specs=[pl.BlockSpec(memory_space=pltpu.SMEM), part, part, marks, marks] + [vec] * 4 + [flat] * 3,
        out_specs=[flat] * 3 + [vec] * 3 + [pl.BlockSpec((1, 1), lambda y, x: (0, 0))],
        out_shape=[shape] * 3 + [small] * 3 + [jax.ShapeDtypeStruct((1, 1), F32)],
        compiler_params=pltpu.CompilerParams(vmem_limit_bytes=60 * 2**20),
        cost_estimate=SHORT,
        name="adam",
    )(own, mine, other, mine, other, vec_total, vectors, vec_first, vec_second, weight, first, second)


from jax.sharding import PartitionSpec as P

HEADS = 12
STEP = 7


def place_tokens(heights, widths, count):
    sizes = heights * widths
    ends = jnp.cumsum(sizes)
    starts = ends - sizes
    places = jnp.arange(count, dtype=jnp.int32)
    segment = jnp.sum((places[:, None] >= ends[None, :]).astype(jnp.int32), axis=1)
    slots = jnp.arange(heights.shape[0], dtype=jnp.int32)
    picks = (segment[:, None] == slots[None, :]).astype(jnp.int32)
    begin = jnp.sum(picks * starts[None, :], axis=1)
    across = jnp.maximum(jnp.sum(picks * widths[None, :], axis=1), 1)
    offset = places - begin
    live = places < ends[-1]
    return (segment, offset // across, offset % across, live)


def adam(weight, first, second, grad, rate, decay):
    first_new = 0.5 * first + 0.5 * grad
    second_new = 0.5 * second + 0.5 * grad * grad
    correct = 1.0 - 0.5**STEP
    direction = first_new / correct / (jnp.sqrt(second_new / correct) + 1e-08)
    return (second_new, weight - rate * (direction + decay * weight))


def pairwise(bits, total):
    return [(i, i ^ bits) for i in range(total)]


def sum_part(value, devices, step, stop):
    while step < stop:
        value = value + lax.ppermute(value, "dp", pairwise(step, devices))
        step *= 2
    return value


CORES = ("group", "dp")
SWAP = [(0, 1), (1, 0)]


def cross(value, bit0, bit1, devices):
    perm = [(i, i ^ (bit0 if i < devices else bit1)) for i in range(2 * devices)]
    return lax.ppermute(value, CORES, perm)


def along_z(values, devices):
    return [
        lax.ppermute(v, "dp", [(i, (i + 4 * (s + 1)) % devices) for i in range(devices)])
        for s, v in enumerate(values)
    ]


def along_line(value, devices, step, up):
    last = devices // 4
    perm = []
    for z in range(last):
        near = z - 1 if up else z + 1
        far = z - step if up else z + step
        if 0 <= far < last:
            perm += [(4 * near + i, 4 * z + i) for i in range(4)]
    return lax.ppermute(value, "dp", perm)


def gather_pieces(master, inverse, core, me, devices, freqs, make_angles, late, make_late, tables):
    tie = lax.optimization_barrier
    block_rows, width = master.shape
    half = block_rows // 2
    mine = lax.dynamic_slice_in_dim(master, core * half, half, 0).astype(BF16)
    large = mine[:LARGE]
    small = mine[LARGE:]
    z = me // 4
    deep = lax.rem(z - inverse // 4 + 4, 4)
    apart = me ^ inverse
    one = jnp.where(core == 0, apart & 1, (apart >> 1) & 1)
    two = jnp.where(core == 0, (apart >> 1) & 1, apart & 1)
    slots = jnp.stack([
        8 * two + 4 * one + deep,
        4 * deep + 2 * two + one,
        8 * one + 4 * two + deep,
        4 * deep + 2 * one + two,
    ]).astype(jnp.int32)
    up = along_z([large] * 3, devices)
    small = jnp.stack([small, cross(small, 1, 2, devices)])
    small, freqs = tie((small, freqs))
    small = jnp.concatenate([small, cross(small, 2, 1, devices)])
    large = jnp.stack([large] + up)
    large, small, tables, slots, angles = tie((large, small, tables, slots, make_angles(freqs)))
    first = cross(large, 1, 2, devices)
    ups = [along_line(small, devices, 1, True)]
    downs = [along_line(small, devices, 1, False)]
    first, ups[0], downs[0], late = tie((first, ups[0], downs[0], late))
    done = make_late(*late)
    first = jnp.concatenate([large, first])
    second = cross(first, 2, 1, devices)
    for step in (2, 3):
        ups.append(along_line(ups[-1], devices, step, True))
        downs.append(along_line(downs[-1], devices, step, False))
        if step == 2:
            ups[1], downs[1], done = tie((ups[1], downs[1], done))
    small = jnp.concatenate([small] + [jnp.where(z >= s, ups[s - 1], downs[3 - s]) for s in (1, 2, 3)])
    other = [lax.ppermute(a, "group", SWAP) for a in (first, second, small)]
    return (first, second, small, *other), slots, angles + done + tables


def quarters(core, me):
    x, y = me & 1, (me >> 1) & 1
    one = jnp.where(core == 0, x, y)
    two = jnp.where(core == 0, y, x)
    pairs = [(1 - one, 1 - two), (1 - one, two), (one, 1 - two), (one, two)]
    return jnp.stack([
        jnp.stack([jnp.where(core == 0, b, a), jnp.where(core == 0, a, b)]) for a, b in pairs
    ]).astype(jnp.int32)


def add_low(*terms):
    total = terms[0].astype(F32)
    for term in terms[1:]:
        total = total + term.astype(F32)
    return total.astype(BF16)


def sum_z(low, me, devices):
    count, rows, cols = low.shape
    z = me // 4
    low = low.reshape(count, 4, rows // 4, cols)
    pick = lambda at: lax.dynamic_index_in_dim(low, at, 1, keepdims=False)
    return (pick(z), *along_z([pick(lax.rem(z + s, 4)) for s in (1, 2, 3)], devices))


def reduce_plain(local_mat, owner_block, devices):
    rows, width = local_mat.shape
    block_rows = rows // devices
    term = local_mat.reshape(devices, block_rows, width)[owner_block].reshape(rows, width)
    share = lax.psum_scatter(term.astype(F32), "dp", scatter_dimension=0, tiled=True)
    return lax.psum(share.astype(BF16), "group").astype(F32)


def local(
    tokens,
    cotangent,
    grid_h,
    grid_w,
    owner_block,
    master,
    first_mom,
    second_mom,
    vectors,
    vec_first,
    vec_second,
):
    devices = lax.axis_size("dp")
    core = lax.axis_index("group")
    me = lax.axis_index("dp")
    count = tokens.shape[1]
    width = tokens.shape[2]
    heads = HEADS
    head_dim = width // heads
    half = head_dim // 2
    block_rows = master.shape[0]
    stack = devices * block_rows
    quick = devices == 16 and block_rows == 2 * (LARGE + SMALL) and width % 256 == 0
    inverse = jnp.argsort(owner_block)
    segment, rows_pos, cols_pos, live = place_tokens(grid_h[0], grid_w[0], count)
    x = tokens[0]

    def spread(part):
        return jnp.broadcast_to(part.reshape(heads, 1, half), (heads, 2, half)).reshape(1, width)

    freqs = (spread(vectors[13, : width // 2]), spread(vectors[13, width // 2 :]))

    def make_angles(freqs):
        down = rows_pos.astype(F32)[:, None]
        right = cols_pos.astype(F32)[:, None]
        angle = down * freqs[0] + right * freqs[1]
        lower = (jnp.arange(width) % head_dim < half)[None]
        cosine = jnp.cos(angle)
        sine = jnp.sin(angle)
        return (cosine, jnp.where(lower, -sine, sine))

    late = (x, cotangent[0])

    def make_late(x, cot):
        unit, _ = norm_parts(x.astype(F32))
        grad_two = jnp.where(live[:, None], cot, jnp.zeros((), BF16))
        return ((unit * vectors[0] + vectors[1]).astype(BF16), grad_two)

    def make_tables():
        ids = jnp.arange(128)[None]
        match = segment[:, None] == ids
        key_mask = jnp.where(match | ((ids >= 8) & (ids < 11)), 1.0, 0.0).astype(BF16)
        query_mask = jnp.where((ids < 8) & ~match, MASKED, 0.0).astype(BF16)
        places = jnp.stack([rows_pos, cols_pos], axis=1).astype(F32)
        return (key_mask, query_mask, places,
                vectors[4:7].reshape(1, 3 * width), vectors[8:12].reshape(1, 4 * width))

    if quick:
        weights, slots, tables = gather_pieces(master, inverse, core, me, devices, freqs, make_angles, late, make_late, make_tables())
    else:
        low = lax.all_gather(master.astype(BF16), "dp", axis=0, tiled=True)
        weights = low.reshape(devices, block_rows, width)[inverse].reshape(stack, width)
        slots = jnp.zeros((4, devices), jnp.int32)
        tables = make_angles(freqs) + make_late(*late) + make_tables()
    cosine, sine, first_in, grad_two, key_mask, query_mask, places, bias_qkv, bias_one = tables
    here = core.reshape(1).astype(jnp.int32)
    query, key, value, attn, stat, *placed = attend(
        here, slots, first_in, bias_qkv,
        cosine, sine, query_mask, key_mask, weights, stack,
    )
    if quick:
        weights = placed[0]
    whole_rows = block_rows if quick else 0
    block_out, grad_middle, grad_attn, sums, bias_up, keep_mlp, give_mlp = mlp(
        here, x, attn, grad_two, vectors, weights, bias_one, whole_rows
    )
    pairs = width // 128
    tie = lax.optimization_barrier
    if quick:
        pos = quarters(core, me)
        got = lax.ppermute(give_mlp, "group", SWAP)
    back = None
    cuts = (0, 1, pairs - 1, pairs)
    for start, stop in zip(cuts[:-1], cuts[1:]):
        back = attend_back(
            start, stop, back, query, key, value, grad_attn, attn, stat, cosine, sine, query_mask, key_mask, places
        )
        if quick and start == 0:
            (send, hold), back = tie((fold(pos, keep_mlp, got), back))
            came = cross(send, 1, 2, devices)
        if quick and start == 1:
            send, back = tie((add_low(hold[0], came[0]), back))
            again = cross(send, 2, 1, devices)
    grad_q, grad_k, grad_v, grad_bias, grad_freq = back
    keep_qkv, give_qkv = qkv_grad(here, grad_q, grad_k, grad_v, first_in, whole_rows)
    if quick:
        again, give_qkv = tie((again, give_qkv))
        low, grad_v, give_qkv = tie((add_low(hold[1], came[1], again), grad_v, give_qkv))
        late = sum_z(low, me, devices)
    if quick:
        got_qkv = lax.ppermute(give_qkv, "group", SWAP)
        send, hold = fold(pos, keep_qkv, got_qkv)
        third = send.shape[2] // 3
        send = [send[:, :, third * i:third * (i + 1)] for i in range(3)]
        send, grad_v = tie((send, grad_v))
    input_grad, local_vec = input_back(
        grad_q, grad_k, grad_v, weights, x, grad_middle, vectors, sums, grad_bias, grad_freq, bias_up
    )
    if quick:
        send[2], local_vec = tie((send[2], local_vec))
        came = [cross(a, 1, 2, devices) for a in send]
        came, local_vec, late = tie((came, local_vec, late))
        came = jnp.concatenate(came, axis=2)
        again = cross(add_low(hold[0], came[0]), 2, 1, devices)
        vec_total = sum_part(local_vec + lax.ppermute(local_vec, "group", SWAP), devices, 4, devices)
        again, vec_total = tie((again, vec_total))
        early = sum_z(add_low(hold[1], came[1], again), me, devices)
        early, vec_total = tie((early, sum_part(vec_total, devices, 1, 4)))
        load = pack(owner_block, me & 1, early, late)
        mine = lax.all_to_all(load, "dp", 0, 0, tiled=True)
        other = lax.ppermute(mine, "group", SWAP)
        shape = (devices // 4, 2, 2, *load.shape[1:])
        own = jnp.stack([core, owner_block[me] % 2]).astype(jnp.int32)
        mat_grad, mat_second, mat_weight, vec_grad, vec_second_new, vec_weight, norm = adam_rows(
            own, mine.reshape(shape), other.reshape(shape), vec_total, vectors, vec_first, vec_second,
            master, first_mom, second_mom,
        )
        grad_norm = norm.reshape(())
    else:
        vec_total = lax.psum(local_vec, CORES)
        share = reduce_plain(jnp.concatenate([keep_qkv, keep_mlp]), owner_block, devices)
        square = lax.psum(jnp.sum(share * share), "dp")
        grad_norm = jnp.sqrt(square + jnp.sum(vec_total * vec_total))
        clip = jnp.minimum(1.0, 1.0 / (grad_norm + 1e-06))
        mat_grad = share * clip
        mat_second, mat_weight = adam(master, first_mom, second_mom, mat_grad, 0.02, 0.05)
        vec_grad = vec_total * clip
        vec_second_new, vec_weight = adam(vectors, vec_first, vec_second, vec_grad, 0.2, 0.0)
    return (
        block_out[None],
        input_grad[None],
        mat_grad,
        mat_second,
        mat_weight,
        vec_grad,
        vec_second_new,
        vec_weight,
        grad_norm,
    )


def solution(mesh):
    return jax.shard_map(
        local,
        mesh=mesh,
        in_specs=(
            P("group", "dp", None),
            P("group", "dp", None),
            P("group", "dp"),
            P("group", "dp"),
            P(),
            P("dp", None),
            P("dp", None),
            P("dp", None),
            P(),
            P(),
            P(),
        ),
        out_specs=(
            P("group", "dp", None),
            P("group", "dp", None),
            P("dp", None),
            P("dp", None),
            P("dp", None),
            P(),
            P(),
            P(),
            P(),
        ),
        check_vma=False,
    )
```

```python
import functools
import jax
import jax.numpy as jnp
from jax import lax
from jax.experimental import pallas as pl
from jax.experimental.pallas import tpu as pltpu

F32 = jnp.float32
BF16 = jnp.bfloat16
LAST = (((1,), (1,)), ((), ()))
FIRST = (((0,), (0,)), ((), ()))
PLAIN = (((1,), (0,)), ((), ()))
MASKED = -1e9
MORE = 40
SHORT = pl.CostEstimate(flops=1000, bytes_accessed=1000, transcendentals=0)


def mm(left, right, dims):
    return lax.dot_general(left, right, dims, preferred_element_type=F32)


def norm_parts(value):
    centre = value - jnp.mean(value, axis=-1, keepdims=True)
    spread = jnp.mean(centre * centre, axis=-1, keepdims=True)
    inverse = lax.rsqrt(spread + 1e-6)
    return centre * inverse, inverse


def norm_back(unit, inverse, grad, gain):
    scaled = grad * gain
    first = jnp.mean(scaled, axis=-1, keepdims=True)
    second = jnp.mean(scaled * unit, axis=-1, keepdims=True)
    return inverse * (scaled - first - unit * second)


def swap_halves(value):
    lane = lax.broadcasted_iota(jnp.int32, value.shape, 1)
    return jnp.where(
        lane % 64 < 32, pltpu.roll(value, 96, 1), pltpu.roll(value, 32, 1)
    )


def split3(value):
    one = value.astype(BF16).astype(F32)
    rest = value - one
    two = rest.astype(BF16).astype(F32)
    return one, two, rest - two


LARGE = 208
SMALL = 80


def place_pieces(core, slot_ref, mine, other, block, side, dst, sem):
    for which, (first, second, small) in enumerate((mine, other)):
        @pl.when((core == side) if which == 0 else (core != side))
        def _():
            large_slot = slot_ref[2 * which, block]
            small_slot = slot_ref[2 * which + 1, block]

            @pl.when(large_slot < 8)
            def _():
                pltpu.make_async_copy(first.at[large_slot], dst(0, LARGE), sem).start()

            @pl.when(large_slot >= 8)
            def _():
                pltpu.make_async_copy(second.at[large_slot - 8], dst(0, LARGE), sem).start()

            pltpu.make_async_copy(small.at[small_slot], dst(LARGE, SMALL), sem).start()


def attend_kernel(blocks, core_ref, slot_ref, n1_ref, bq_ref, bk_ref, bv_ref,
                  cos_ref, sin_ref, qm_ref, km_ref, *rest):
    if blocks:
        mine, other = rest[0:3], rest[3:6]
        q_ref, k_ref, v_ref, attn_ref, stat_ref, w_ref, w_s, near, far, back = rest[6:]
    else:
        w_ref, q_ref, k_ref, v_ref, attn_ref, stat_ref, w_s, near = rest
    count, width = n1_ref.shape
    step = pl.program_id(0)

    @pl.when(step == 0)
    def _():
        if blocks:
            core = core_ref[0]
            rows = w_ref.shape[0] // blocks

            def start(block, sem):
                for side in (0, 1):
                    def dst(offset, size):
                        base = block * rows + side * (rows // 2) + offset
                        return w_s.at[pl.ds(pl.multiple_of(base, 16), size)]
                    place_pieces(core, slot_ref, mine, other, block, side, dst, sem)

            def near_block(block, carry):
                start(block, near)
                return carry

            def far_block(block, carry):
                start(block, far)
                return carry

            lax.fori_loop(0, 3 * width // rows, near_block, 0)
            lax.fori_loop(3 * width // rows, blocks, far_block, 0)
        else:
            pltpu.make_async_copy(w_ref.at[pl.ds(0, 3 * width)], w_s, near).start()
        head = w_s.at[pl.ds(0, 3 * width)]
        pltpu.make_async_copy(head, head, near).wait()

    if blocks:
        @pl.when(step == 1)
        def _():
            tail = w_s.at[pl.ds(3 * width, w_s.shape[0] - 3 * width)]
            pltpu.make_async_copy(tail, tail, far).wait()
            pltpu.make_async_copy(w_s, w_ref, back).start()

    def third(j):
        return w_s[pl.ds(pl.multiple_of(j * width + step * 128, 128), 128), :]

    w = jnp.concatenate([third(0), third(1), third(2)], axis=0)
    qkv = mm(n1_ref[...], w, LAST)
    q = qkv[:, :128] + bq_ref[...]
    k = qkv[:, 128:256] + bk_ref[...]
    v = (qkv[:, 256:] + bv_ref[...]).astype(BF16)
    c = cos_ref[...]
    s = sin_ref[...]
    qr = ((q * c + swap_halves(q) * s).astype(BF16).astype(F32) * 0.125).astype(BF16)
    kr = (k * c + swap_halves(k) * s).astype(BF16)
    q_ref[...] = qr
    k_ref[...] = kr
    v_ref[...] = v
    lane = lax.broadcasted_iota(jnp.int32, (1, 128), 1)
    k_aug = jnp.concatenate([kr, km_ref[...]], axis=1)
    v_aug = jnp.concatenate([v, jnp.ones((count, 128), BF16)], axis=1)
    zero = jnp.zeros((), BF16)
    tile = 256
    for i in range(count // tile):
        rows = pl.ds(i * tile, tile)
        out = None
        stats = []
        for h in (0, 1):
            mine_lanes = (lane // 64) == h
            qa = jnp.concatenate(
                [jnp.where(mine_lanes, qr[i * tile:(i + 1) * tile], zero), qm_ref[rows, :]], axis=1)
            scores = mm(qa, k_aug, LAST)
            top = jnp.max(scores, axis=-1, keepdims=True)
            e = jnp.exp(scores - top).astype(BF16)
            o = mm(e, v_aug, PLAIN)
            total = o[:, 128:]
            o = o[:, :128] / total
            out = o if out is None else jnp.where(lane < 64, out, o)
            stats.append(top + jnp.log(total[:, :1]))
        attn_ref[rows, :] = out.astype(BF16)
        stat_ref[rows, :] = jnp.where(lane < 64, stats[0], stats[1])

    if blocks:
        @pl.when(step == pl.num_programs(0) - 1)
        def _():
            pltpu.make_async_copy(w_s, w_ref, back).wait()


def attend(core, slots, n1, bqkv, cos, sin, qm, km, weights, stack):
    count, width = n1.shape
    pairs = width // 128
    pieces = isinstance(weights, tuple)
    blocks = slots.shape[1] if pieces else 0
    whole = lambda p: (0, 0)
    col = lambda p: (0, p)
    smem = pl.BlockSpec(memory_space=pltpu.SMEM)
    hbm = pl.BlockSpec(memory_space=pl.ANY)
    given = weights if pieces else (weights,)
    specs = [smem, smem] + [
        pl.BlockSpec((count, width), whole),
        pl.BlockSpec((1, 128), col),
        pl.BlockSpec((1, 128), lambda p: (0, p + pairs)),
        pl.BlockSpec((1, 128), lambda p: (0, p + 2 * pairs)),
        pl.BlockSpec((count, 128), col),
        pl.BlockSpec((count, 128), col),
        pl.BlockSpec((count, 128), whole),
        pl.BlockSpec((count, 128), whole),
    ] + [hbm] * len(given)
    outs = [pl.BlockSpec((count, 128), col)] * 5
    shape = lambda d: jax.ShapeDtypeStruct((count, width), d)
    shapes = [shape(BF16)] * 4 + [shape(F32)]
    scratch = [pltpu.VMEM((stack if pieces else 3 * width, width), BF16), pltpu.SemaphoreType.DMA]
    if pieces:
        outs.append(hbm)
        shapes.append(jax.ShapeDtypeStruct((stack, width), BF16))
        scratch += [pltpu.SemaphoreType.DMA] * 2
    return pl.pallas_call(
        functools.partial(attend_kernel, blocks),
        grid=(pairs,),
        in_specs=specs,
        out_specs=outs,
        out_shape=shapes,
        scratch_shapes=scratch,
        compiler_params=pltpu.CompilerParams(vmem_limit_bytes=56 * 2**20),
        cost_estimate=SHORT,
        name="attend",
    )(core, slots, n1, bqkv, bqkv, bqkv, cos, sin, qm, km, *given)


def gelu_both(x):
    cdf = 0.5 + 0.5 * lax.erf(x * 0.7071067811865476)
    return x * cdf, cdf + x * jnp.exp(x * x * -0.5) * 0.3989422804014327


def put_halves(stage, value):
    half = value.shape[1] // 2
    low = value.astype(BF16)
    stage[0] = low[:, :half]
    stage[1] = low[:, half:]


def send_rows(core, block_rows, stage, row, base, keep_ref, give_ref, sem):
    rows, half = stage.shape[1:]
    if not block_rows:
        for c in (0, 1):
            target = keep_ref.at[pl.ds(pl.multiple_of(row - base, 64), rows), pl.ds(c * half, half)]
            pltpu.make_async_copy(stage.at[c], target, sem).start()
        return
    for piece in range(rows // 64):
        at = row + 64 * piece
        block = lax.div(at, block_rows)
        inner = pl.ds(pl.multiple_of(at - block * block_rows, 64), 64)
        here = pl.ds(64 * piece, 64)
        pltpu.make_async_copy(stage.at[core, here], keep_ref.at[block - base, inner], sem).start()
        pltpu.make_async_copy(stage.at[1 - core, here], give_ref.at[block - base, inner], sem).start()


def mlp_kernel(block_rows, base, core_ref, x_ref, at_ref, dz_ref, vec_ref, wo_ref, w1_ref, w2_ref, b1_ref,
               out_ref, dm_ref, da_ref, sums_ref, gb_ref, keep_ref, give_ref,
               middle_s, n2_s, acc_s, stage_s, proj_s, sems):
    step = pl.program_id(0)
    last = pl.num_programs(0) - 1
    count, width = x_ref.shape
    core = core_ref[0]
    tile = w1_ref.shape[0]

    @pl.when(step == 0)
    def _():
        middle = x_ref[...].astype(F32) + mm(at_ref[...], wo_ref[...], LAST) + vec_ref[7:8, :]
        middle_s[...] = middle
        unit, _ = norm_parts(middle)
        n2_s[...] = (unit * vec_ref[2:3, :] + vec_ref[3:4, :]).astype(BF16)
        acc_s[...] = jnp.zeros_like(acc_s)
        dm_ref[...] = jnp.zeros_like(dm_ref)

    slot = lax.rem(step, 2)

    @pl.when(step >= 2)
    def _():
        pltpu.make_async_copy(stage_s.at[slot], stage_s.at[slot], sems.at[slot]).wait()

    n2 = n2_s[...]
    dz = dz_ref[...]
    w1 = w1_ref[...]
    w2 = w2_ref[...]
    pre = mm(w1, n2, LAST) + b1_ref[...].reshape(tile, 1)
    back = mm(w2, dz, LAST)
    act, slope = gelu_both(pre)
    hidden = act.astype(BF16)
    put_halves(stage_s.at[slot, 1], mm(hidden, dz, PLAIN))
    dpre = (back * slope).astype(BF16)
    gb_ref[...] = jnp.sum(dpre.astype(F32), axis=1, keepdims=True).reshape(1, tile)
    put_halves(stage_s.at[slot, 0], mm(dpre, n2, PLAIN))
    acc_s[...] += mm(hidden, w2, FIRST)
    dm_ref[...] += mm(dpre, w1, FIRST)
    for j in (0, 1):
        send_rows(core, block_rows, stage_s.at[slot, j], (4 + 4 * j) * width + step * tile,
                  base, keep_ref, give_ref, sems.at[slot])

    @pl.when(step == last)
    def _():
        middle = middle_s[...]
        out_ref[...] = (middle + acc_s[...] + vec_ref[12:13, :]).astype(BF16)
        unit, inverse = norm_parts(middle)
        dn = dm_ref[...]
        dy = dz_ref[...].astype(F32)
        dm = dy + norm_back(unit, inverse, dn, vec_ref[2:3, :])
        dm_ref[...] = dm
        low = dm.astype(BF16)
        row = lambda a: jnp.sum(a, axis=0, keepdims=True)
        sums_ref[...] = jnp.concatenate(
            [row(dn * unit), row(dn), row(low.astype(F32)), row(dy), jnp.zeros((4, width), F32)], axis=0)
        put_halves(proj_s, mm(low, at_ref[...], FIRST))
        send_rows(core, block_rows, proj_s, 3 * width, base, keep_ref, give_ref, sems.at[2])
        da_ref[...] = mm(low, wo_ref[...], PLAIN).astype(BF16)
        pltpu.make_async_copy(stage_s.at[slot], stage_s.at[slot], sems.at[slot]).wait()
        pltpu.make_async_copy(stage_s.at[1 - slot], stage_s.at[1 - slot], sems.at[1 - slot]).wait()
        pltpu.make_async_copy(proj_s, proj_s, sems.at[2]).wait()


def grad_shapes(block_rows, rows, width):
    if block_rows:
        half = jax.ShapeDtypeStruct((rows // block_rows, block_rows, width // 2), BF16)
        return [half, half]
    return [jax.ShapeDtypeStruct((rows, width), BF16), jax.ShapeDtypeStruct((16, width), BF16)]


def mlp(core, x, attn, dz, vectors, weights, b1, block_rows, tile=512):
    count, width = x.shape
    units = 4 * width
    stack = weights.shape[0]
    base = 3 * width // block_rows if block_rows else 3 * width
    whole = lambda t: (0, 0)
    big = pl.BlockSpec((count, width), whole)
    hbm = pl.BlockSpec(memory_space=pl.ANY)
    return pl.pallas_call(
        functools.partial(mlp_kernel, block_rows, base),
        grid=(units // tile,),
        in_specs=[pl.BlockSpec(memory_space=pltpu.SMEM), big, big, big, pl.BlockSpec(vectors.shape, whole),
                  pl.BlockSpec((width, width), lambda t: (3, 0)),
                  pl.BlockSpec((tile, width), lambda t: (4 * width // tile + t, 0)),
                  pl.BlockSpec((tile, width), lambda t: (8 * width // tile + t, 0)),
                  pl.BlockSpec((1, tile), lambda t: (0, t))],
        out_specs=[big, big, big, pl.BlockSpec((8, width), whole), pl.BlockSpec((1, tile), lambda t: (0, t)), hbm, hbm],
        out_shape=[
            jax.ShapeDtypeStruct((count, width), BF16),
            jax.ShapeDtypeStruct((count, width), F32),
            jax.ShapeDtypeStruct((count, width), BF16),
            jax.ShapeDtypeStruct((8, width), F32),
            jax.ShapeDtypeStruct((1, units), F32),
        ] + grad_shapes(block_rows, stack - 3 * width, width),
        scratch_shapes=[
            pltpu.VMEM((count, width), F32),
            pltpu.VMEM((count, width), BF16),
            pltpu.VMEM((count, width), F32),
            pltpu.VMEM((2, 2, 2, tile, width // 2), BF16),
            pltpu.VMEM((2, width, width // 2), BF16),
            pltpu.SemaphoreType.DMA((3,)),
        ],
        compiler_params=pltpu.CompilerParams(vmem_limit_bytes=60 * 2**20),
        cost_estimate=SHORT,
        name="mlp",
    )(core, x, attn, dz, vectors, weights, weights, weights, b1)


def back_kernel(first, q_ref, k_ref, v_ref, da_ref, at_ref, stat_ref, cos_ref, sin_ref,
                qm_ref, km_ref, pos_ref, *rest):
    dq_ref, dk_ref, dv_ref, gb_ref, gf_ref = rest if first else rest[5:]
    count = q_ref.shape[0]
    lane = lax.broadcasted_iota(jnp.int32, (1, 128), 1)
    zero = jnp.zeros((), BF16)
    q = q_ref[...]
    k = k_ref[...]
    v = v_ref[...]
    da = da_ref[...]
    prod = da.astype(F32) * at_ref[...].astype(F32)
    qm = qm_ref[...].astype(F32)
    k_aug = jnp.concatenate([k, km_ref[...]], axis=1)
    v_aug = jnp.concatenate([v, jnp.broadcast_to((lane < 2).astype(BF16), (count, 128))], axis=1)
    tile = 256
    dq = dk = dv = None
    for h in (0, 1):
        mine = (lane // 64) == h
        qh = jnp.where(mine, q, zero)
        kh = jnp.where(mine, k, zero)
        dah = jnp.where(mine, da, zero)
        delta = jnp.sum(jnp.where(mine, prod, 0.0), axis=-1, keepdims=True)
        d1, d2, _ = split3(delta)
        l1, l2, l3 = split3(stat_ref[:, 64 * h:64 * h + 1])
        extra = jnp.where(lane == 8, -l1, jnp.where(lane == 9, -l2, jnp.where(lane == 10, -l3, qm)))
        q_aug = jnp.concatenate([qh, extra.astype(BF16)], axis=1)
        da_aug = jnp.concatenate(
            [dah, jnp.where(lane == 0, -d1, jnp.where(lane == 1, -d2, 0.0)).astype(BF16)], axis=1)
        dks, dvs, dqh = [], [], None
        for i in range(count // tile):
            sl = slice(i * tile, (i + 1) * tile)
            p = jnp.exp(mm(k_aug[sl], q_aug, LAST))
            dp = mm(v_aug[sl], da_aug, LAST)
            ds = (p * dp).astype(BF16)
            dvs.append(mm(p.astype(BF16), dah, PLAIN))
            dks.append(mm(ds, qh, PLAIN))
            part = mm(ds, kh[sl], FIRST)
            dqh = part if dqh is None else dqh + part
        dkh = jnp.concatenate(dks, axis=0)
        dvh = jnp.concatenate(dvs, axis=0)
        dq = dqh if dq is None else dq + dqh
        dk = dkh if dk is None else dk + dkh
        dv = dvh if dv is None else dv + dvh
    dq = dq * 0.125
    c = cos_ref[...]
    s = sin_ref[...]
    turned = dq * swap_halves(q.astype(F32) * 8.0) + dk * swap_halves(k.astype(F32))
    turned = jnp.where(lane % 64 < 32, -turned, turned)
    row = lambda a: jnp.sum(a, axis=0, keepdims=True)
    gf_ref[...] = jnp.concatenate(
        [row(turned * pos_ref[:, 0:1]), row(turned * pos_ref[:, 1:2]), jnp.zeros((6, 128), F32)], axis=0)
    dqp = (dq * c - swap_halves(dq) * s).astype(BF16)
    dkp = (dk * c - swap_halves(dk) * s).astype(BF16)
    dvp = dv.astype(BF16)
    gb_ref[...] = jnp.concatenate(
        [row(dqp.astype(F32)), row(dkp.astype(F32)), row(dvp.astype(F32)), jnp.zeros((5, 128), F32)], axis=0)
    dq_ref[...] = dqp
    dk_ref[...] = dkp
    dv_ref[...] = dvp


def attend_back(start, stop, before, q, k, v, da, attn, stat, cos, sin, qm, km, pos):
    count, width = q.shape
    whole = lambda p: (0, 0)
    col = lambda p: (0, p + start)
    tall = pl.BlockSpec((count, 128), col)
    fixed = pl.BlockSpec((count, 128), whole)
    small = pl.BlockSpec((8, 128), col)
    in_specs = [tall] * 8 + [fixed] * 2 + [pl.BlockSpec((count, 2), whole)]
    operands = [q, k, v, da, attn, stat, cos, sin, qm, km, pos]
    aliases = {}
    if before is not None:
        aliases = {len(operands) + i: i for i in range(5)}
        in_specs += [pl.BlockSpec(memory_space=pl.ANY)] * 5
        operands += list(before)
    return pl.pallas_call(
        functools.partial(back_kernel, before is None),
        grid=(stop - start,),
        in_specs=in_specs,
        out_specs=[tall] * 3 + [small] * 2,
        out_shape=[jax.ShapeDtypeStruct((count, width), BF16)] * 3 + [jax.ShapeDtypeStruct((8, width), F32)] * 2,
        input_output_aliases=aliases,
        compiler_params=pltpu.CompilerParams(vmem_limit_bytes=56 * 2**20),
        cost_estimate=SHORT,
        name="attend_back",
    )(*operands)


def qkv_grad_kernel(block_rows, core_ref, dq_ref, dk_ref, dv_ref, n1_ref, keep_ref, give_ref, stage_s, sem):
    width = n1_ref.shape[1]
    cols = dq_ref.shape[1]
    step = pl.program_id(0)
    n1 = n1_ref[...]
    for j, ref in enumerate((dq_ref, dk_ref, dv_ref)):
        put_halves(stage_s.at[step, j], mm(ref[...], n1, FIRST))
        send_rows(core_ref[0], block_rows, stage_s.at[step, j], j * width + step * cols, 0, keep_ref, give_ref, sem)

    @pl.when(step == pl.num_programs(0) - 1)
    def _():
        pltpu.make_async_copy(stage_s, stage_s, sem).wait()


def qkv_grad(core, dq, dk, dv, n1, block_rows):
    count, width = n1.shape
    cols = width // 2
    tall = pl.BlockSpec((count, cols), lambda p: (0, p))
    hbm = pl.BlockSpec(memory_space=pl.ANY)
    return pl.pallas_call(
        functools.partial(qkv_grad_kernel, block_rows),
        grid=(2,),
        in_specs=[pl.BlockSpec(memory_space=pltpu.SMEM)] + [tall] * 3 + [pl.BlockSpec((count, width), lambda p: (0, 0))],
        out_specs=[hbm, hbm],
        out_shape=grad_shapes(block_rows, 3 * width, width),
        scratch_shapes=[pltpu.VMEM((2, 3, 2, cols, width // 2), BF16), pltpu.SemaphoreType.DMA],
        compiler_params=pltpu.CompilerParams(vmem_limit_bytes=56 * 2**20),
        cost_estimate=SHORT,
        name="qkv_grad",
    )(core, dq, dk, dv, n1)


def input_kernel(dq_ref, dk_ref, dv_ref, w_ref, x_ref, dm_ref, vec_ref, sums_ref, gb_ref, gf_ref, up_ref, ig_ref, out_ref):
    step = pl.program_id(0)
    d = jnp.concatenate([dq_ref[...], dk_ref[...], dv_ref[...]], axis=1)
    dn = mm(d, w_ref[...], PLAIN)
    unit, inverse = norm_parts(x_ref[...].astype(F32))
    ig_ref[...] = dm_ref[...] + norm_back(unit, inverse, dn, vec_ref[0:1, :])
    row = lambda a: jnp.sum(a, axis=0, keepdims=True)
    sums = jnp.concatenate([row(dn * unit), row(dn)], axis=0)

    @pl.when(step == 0)
    def _():
        width = dn.shape[1]
        half = width // 2
        out_ref[0:2] = sums
        out_ref[2:4] = sums_ref[0:2]
        out_ref[4:7] = gb_ref[0:3]
        out_ref[7:8] = sums_ref[2:3]
        for i in range(4):
            out_ref[8 + i:9 + i] = up_ref[:, i * width:(i + 1) * width]
        out_ref[12:13] = sums_ref[3:4]
        lane = lax.broadcasted_iota(jnp.int32, (width, half), 0)
        slot = lax.broadcasted_iota(jnp.int32, (width, half), 1)
        pick = jnp.where((lane // 64 == slot // 32) & (lane % 32 == slot % 32), 1.0, 0.0)
        both = lax.dot_general(gf_ref[...], pick, PLAIN, precision=lax.Precision.HIGHEST, preferred_element_type=F32)
        out_ref[13:14, :half] = both[0:1]
        out_ref[13:14, half:] = both[1:2]

    @pl.when(step > 0)
    def _():
        out_ref[0:2] += sums


def input_back(dq, dk, dv, weights, x, dm, vectors, sums, grad_bias, grad_freq, bias_up):
    count, width = x.shape
    tile = 256
    part = pl.BlockSpec((tile, width), lambda i: (i, 0))
    whole = lambda i: (0, 0)
    fixed = lambda a: pl.BlockSpec(a.shape, whole)
    return pl.pallas_call(
        input_kernel,
        grid=(count // tile,),
        in_specs=[part] * 3 + [pl.BlockSpec((3 * width, width), whole), part, part]
        + [fixed(a) for a in (vectors, sums, grad_bias, grad_freq, bias_up)],
        out_specs=[part, fixed(vectors)],
        out_shape=[jax.ShapeDtypeStruct((count, width), F32), jax.ShapeDtypeStruct(vectors.shape, F32)],
        compiler_params=pltpu.CompilerParams(vmem_limit_bytes=56 * 2**20),
        cost_estimate=SHORT,
        name="input_back",
    )(dq, dk, dv, weights, x, dm, vectors, sums, grad_bias, grad_freq, bias_up)


def fold_kernel(pos_ref, keep_ref, got_ref, send_ref, hold_ref):
    rows = keep_ref.shape[1] // 2
    deep = 4
    piece = rows // deep
    more, less = MORE, piece - MORE
    for m in range(keep_ref.shape[0] // 2):
        both = []
        for y in (0, 1):
            here = slice(y * rows, y * rows + rows)
            even, odd = (
                keep_ref[2 * m + e, here, :].astype(F32) + got_ref[2 * m + e, here, :].astype(F32) for e in (0, 1)
            )
            parts = []
            for z in range(deep):
                at = z * piece
                parts.append((
                    jnp.concatenate([even[at:at + more], odd[at:at + less]], axis=0),
                    jnp.concatenate([even[at + more:at + piece], odd[at + less:at + piece]], axis=0),
                ))
            both.append([jnp.concatenate([p[x] for p in parts], axis=0).astype(BF16) for x in (0, 1)])
        for y in (0, 1):
            for x in (0, 1):
                for way in range(4):
                    @pl.when((pos_ref[way, 0] == y) & (pos_ref[way, 1] == x))
                    def _(way=way, y=y, x=x):
                        (send_ref, hold_ref)[way // 2][way % 2, m] = both[y][x]


def fold(pos, keep, got):
    count, rows, cols = keep.shape
    some = 4 if count % 4 == 0 else 2
    whole = pl.BlockSpec((some, rows, cols), lambda i, pos: (i, 0, 0))
    out = pl.BlockSpec((2, some // 2, rows // 2, cols), lambda i, pos: (0, i, 0, 0))
    shape = jax.ShapeDtypeStruct((2, count // 2, rows // 2, cols), BF16)
    return pl.pallas_call(
        fold_kernel,
        grid_spec=pltpu.PrefetchScalarGridSpec(
            num_scalar_prefetch=1, grid=(count // some,), in_specs=[whole, whole], out_specs=[out, out]),
        compiler_params=pltpu.CompilerParams(vmem_limit_bytes=40 * 2**20),
        out_shape=[shape, shape],
        cost_estimate=SHORT,
        name="fold",
    )(pos, keep, got)


def pack_kernel(owner_ref, *refs):
    early, late, out_ref, total_s = refs[:4], refs[4:8], refs[8], refs[9]
    square = None
    start = 0
    rows = early[0].shape[1]
    for parts in (early, late):
        total = parts[0][...].astype(F32)
        for part in parts[1:]:
            total = total + part[...].astype(F32)
        total_s[start:start + total.shape[0], :rows] = total
        start += total.shape[0]
        more = jnp.sum(total * total).reshape(1, 1)
        square = more if square is None else square + more
    total_s[:, rows:] = jnp.zeros((start, total_s.shape[1] - rows, total_s.shape[2]), F32)
    lane = lax.broadcasted_iota(jnp.int32, (8, out_ref.shape[2]), 1)
    one, two, three = split3(square)
    extra = jnp.where(lane == 0, one, jnp.where(lane == 1, two, jnp.where(lane == 2, three, 0.0)))
    devices = out_ref.shape[0]
    skip = jnp.where(owner_ref[devices] == 0, MORE, rows - MORE)
    for p in range(devices):
        block = owner_ref[p]
        at = lax.rem(block, 2) * skip
        mine = total_s[lax.div(block, 2), pl.ds(pl.multiple_of(at, 8), MORE), :]
        out_ref[p] = jnp.concatenate([mine, extra], axis=0).astype(BF16)


def pack(owner, x, early, late):
    blocks = early[0].shape[0] + late[0].shape[0]
    rows, cols = early[0].shape[1:]
    vmem = pl.BlockSpec(memory_space=pltpu.VMEM)
    return pl.pallas_call(
        pack_kernel,
        in_specs=[pl.BlockSpec(memory_space=pltpu.SMEM)] + [vmem] * 8,
        out_specs=vmem,
        out_shape=jax.ShapeDtypeStruct((owner.shape[0], MORE + 8, cols), BF16),
        scratch_shapes=[pltpu.VMEM((blocks, rows + 8, cols), F32)],
        compiler_params=pltpu.CompilerParams(vmem_limit_bytes=32 * 2**20),
        cost_estimate=SHORT,
        name="pack",
    )(jnp.concatenate([owner, x.reshape(1).astype(owner.dtype)]), *early, *late)


def clip_of(square, vec):
    norm = jnp.sqrt(square + jnp.sum(vec * vec).reshape(1, 1))
    return norm, jnp.minimum(1.0, 1.0 / (norm + 1e-06))


def adam_kernel(own_ref, a_ref, b_ref, as_ref, bs_ref, vt_ref, vw_ref, vm_ref, vv_ref, w_ref, m_ref, v_ref,
                g_out, v_out, w_out, vg_out, vv_out, vw_out, norm_out):
    def squares(ref):
        block = ref[...].astype(F32)
        lane = lax.broadcasted_iota(jnp.int32, block.shape, 4)
        row = lax.broadcasted_iota(jnp.int32, block.shape, 3)
        return jnp.sum(jnp.where((lane < 3) & (row == 0), block, 0.0)).reshape(1, 1)

    norm, clip = clip_of(squares(as_ref) + squares(bs_ref), vt_ref[...])
    mine = pl.program_id(1) == own_ref[0]
    even = own_ref[1] == 0
    deep = a_ref.shape[0]
    piece = w_ref.shape[0] // deep
    runs = []
    for z in range(deep):
        left, right = (jnp.where(mine, a_ref[z, 0, x].astype(F32), b_ref[z, 0, x].astype(F32)) for x in (0, 1))
        runs.append(jnp.where(
            even,
            jnp.concatenate([left[:MORE], right[:piece - MORE]], axis=0),
            jnp.concatenate([left[:piece - MORE], right[:MORE]], axis=0),
        ))
    grad = jnp.concatenate(runs, axis=0) * clip
    second, weight = adam(w_ref[...], m_ref[...], v_ref[...], grad, 0.02, 0.05)
    g_out[...] = grad
    v_out[...] = second
    w_out[...] = weight

    @pl.when((pl.program_id(0) == 0) & (pl.program_id(1) == 0))
    def _():
        vec_grad = vt_ref[...] * clip
        second, weight = adam(vw_ref[...], vm_ref[...], vv_ref[...], vec_grad, 0.2, 0.0)
        vg_out[...] = vec_grad
        vv_out[...] = second
        vw_out[...] = weight
        norm_out[...] = norm


def adam_rows(own, mine, other, vec_total, vectors, vec_first, vec_second, weight, first, second):
    rows, width = weight.shape
    deep, tall, wide, piece, cols = mine.shape
    part = pl.BlockSpec((deep, 1, wide, piece, cols), lambda y, h: (0, y, 0, 0, 0))
    marks = pl.BlockSpec((deep, tall, wide, 8, 128), lambda y, x: (0, 0, 0, piece // 8 - 1, 0))
    flat = pl.BlockSpec((rows // tall, cols), lambda y, h: (y, h))
    vec = pl.BlockSpec(vectors.shape, lambda y, x: (0, 0))
    shape = jax.ShapeDtypeStruct((rows, width), F32)
    small = jax.ShapeDtypeStruct(vectors.shape, F32)
    return pl.pallas_call(
        adam_kernel,
        grid=(tall, width // cols),
        in_specs=[pl.BlockSpec(memory_space=pltpu.SMEM), part, part, marks, marks] + [vec] * 4 + [flat] * 3,
        out_specs=[flat] * 3 + [vec] * 3 + [pl.BlockSpec((1, 1), lambda y, x: (0, 0))],
        out_shape=[shape] * 3 + [small] * 3 + [jax.ShapeDtypeStruct((1, 1), F32)],
        compiler_params=pltpu.CompilerParams(vmem_limit_bytes=60 * 2**20),
        cost_estimate=SHORT,
        name="adam",
    )(own, mine, other, mine, other, vec_total, vectors, vec_first, vec_second, weight, first, second)


from jax.sharding import PartitionSpec as P

HEADS = 12
STEP = 7


def place_tokens(heights, widths, count):
    sizes = heights * widths
    ends = jnp.cumsum(sizes)
    starts = ends - sizes
    places = jnp.arange(count, dtype=jnp.int32)
    segment = jnp.sum((places[:, None] >= ends[None, :]).astype(jnp.int32), axis=1)
    slots = jnp.arange(heights.shape[0], dtype=jnp.int32)
    picks = (segment[:, None] == slots[None, :]).astype(jnp.int32)
    begin = jnp.sum(picks * starts[None, :], axis=1)
    across = jnp.maximum(jnp.sum(picks * widths[None, :], axis=1), 1)
    offset = places - begin
    live = places < ends[-1]
    return (segment, offset // across, offset % across, live)


def adam(weight, first, second, grad, rate, decay):
    first_new = 0.5 * first + 0.5 * grad
    second_new = 0.5 * second + 0.5 * grad * grad
    correct = 1.0 - 0.5**STEP
    direction = first_new / correct / (jnp.sqrt(second_new / correct) + 1e-08)
    return (second_new, weight - rate * (direction + decay * weight))


def pairwise(bits, total):
    return [(i, i ^ bits) for i in range(total)]


def sum_part(value, devices, step, stop):
    while step < stop:
        value = value + lax.ppermute(value, "dp", pairwise(step, devices))
        step *= 2
    return value


CORES = ("group", "dp")
SWAP = [(0, 1), (1, 0)]


def cross(value, bit0, bit1, devices):
    perm = [(i, i ^ (bit0 if i < devices else bit1)) for i in range(2 * devices)]
    return lax.ppermute(value, CORES, perm)


def along_z(values, devices):
    return [
        lax.ppermute(v, "dp", [(i, (i + 4 * (s + 1)) % devices) for i in range(devices)])
        for s, v in enumerate(values)
    ]


def along_line(value, devices, step, up):
    last = devices // 4
    perm = []
    for z in range(last):
        near = z - 1 if up else z + 1
        far = z - step if up else z + step
        if 0 <= far < last:
            perm += [(4 * near + i, 4 * z + i) for i in range(4)]
    return lax.ppermute(value, "dp", perm)


def gather_pieces(master, inverse, core, me, devices, freqs, make_angles, late, make_late, tables):
    tie = lax.optimization_barrier
    block_rows, width = master.shape
    half = block_rows // 2
    mine = lax.dynamic_slice_in_dim(master, core * half, half, 0).astype(BF16)
    large = mine[:LARGE]
    small = mine[LARGE:]
    z = me // 4
    deep = lax.rem(z - inverse // 4 + 4, 4)
    apart = me ^ inverse
    one = jnp.where(core == 0, apart & 1, (apart >> 1) & 1)
    two = jnp.where(core == 0, (apart >> 1) & 1, apart & 1)
    slots = jnp.stack([
        8 * two + 4 * one + deep,
        4 * deep + 2 * two + one,
        8 * one + 4 * two + deep,
        4 * deep + 2 * one + two,
    ]).astype(jnp.int32)
    up = along_z([large] * 3, devices)
    small = jnp.stack([small, cross(small, 1, 2, devices)])
    small, freqs = tie((small, freqs))
    small = jnp.concatenate([small, cross(small, 2, 1, devices)])
    large = jnp.stack([large] + up)
    large, small, tables, slots, angles = tie((large, small, tables, slots, make_angles(freqs)))
    first = cross(large, 1, 2, devices)
    ups = [along_line(small, devices, 1, True)]
    downs = [along_line(small, devices, 1, False)]
    first, ups[0], downs[0], late = tie((first, ups[0], downs[0], late))
    done = make_late(*late)
    first = jnp.concatenate([large, first])
    second = cross(first, 2, 1, devices)
    for step in (2, 3):
        ups.append(along_line(ups[-1], devices, step, True))
        downs.append(along_line(downs[-1], devices, step, False))
        if step == 2:
            ups[1], downs[1], done = tie((ups[1], downs[1], done))
    small = jnp.concatenate([small] + [jnp.where(z >= s, ups[s - 1], downs[3 - s]) for s in (1, 2, 3)])
    other = [lax.ppermute(a, "group", SWAP) for a in (first, second, small)]
    return (first, second, small, *other), slots, angles + done + tables


def quarters(core, me):
    x, y = me & 1, (me >> 1) & 1
    one = jnp.where(core == 0, x, y)
    two = jnp.where(core == 0, y, x)
    pairs = [(1 - one, 1 - two), (1 - one, two), (one, 1 - two), (one, two)]
    return jnp.stack([
        jnp.stack([jnp.where(core == 0, b, a), jnp.where(core == 0, a, b)]) for a, b in pairs
    ]).astype(jnp.int32)


def add_low(*terms):
    total = terms[0].astype(F32)
    for term in terms[1:]:
        total = total + term.astype(F32)
    return total.astype(BF16)


def sum_z(low, me, devices):
    count, rows, cols = low.shape
    z = me // 4
    low = low.reshape(count, 4, rows // 4, cols)
    pick = lambda at: lax.dynamic_index_in_dim(low, at, 1, keepdims=False)
    return (pick(z), *along_z([pick(lax.rem(z + s, 4)) for s in (1, 2, 3)], devices))


def reduce_plain(local_mat, owner_block, devices):
    rows, width = local_mat.shape
    block_rows = rows // devices
    term = local_mat.reshape(devices, block_rows, width)[owner_block].reshape(rows, width)
    share = lax.psum_scatter(term.astype(F32), "dp", scatter_dimension=0, tiled=True)
    return lax.psum(share.astype(BF16), "group").astype(F32)


def local(
    tokens,
    cotangent,
    grid_h,
    grid_w,
    owner_block,
    master,
    first_mom,
    second_mom,
    vectors,
    vec_first,
    vec_second,
):
    devices = lax.axis_size("dp")
    core = lax.axis_index("group")
    me = lax.axis_index("dp")
    count = tokens.shape[1]
    width = tokens.shape[2]
    heads = HEADS
    head_dim = width // heads
    half = head_dim // 2
    block_rows = master.shape[0]
    stack = devices * block_rows
    quick = devices == 16 and block_rows == 2 * (LARGE + SMALL) and width % 256 == 0
    inverse = jnp.argsort(owner_block)
    segment, rows_pos, cols_pos, live = place_tokens(grid_h[0], grid_w[0], count)
    x = tokens[0]

    def spread(part):
        return jnp.broadcast_to(part.reshape(heads, 1, half), (heads, 2, half)).reshape(1, width)

    freqs = (spread(vectors[13, : width // 2]), spread(vectors[13, width // 2 :]))

    def make_angles(freqs):
        down = rows_pos.astype(F32)[:, None]
        right = cols_pos.astype(F32)[:, None]
        angle = down * freqs[0] + right * freqs[1]
        lower = (jnp.arange(width) % head_dim < half)[None]
        cosine = jnp.cos(angle)
        sine = jnp.sin(angle)
        return (cosine, jnp.where(lower, -sine, sine))

    late = (x, cotangent[0])

    def make_late(x, cot):
        unit, _ = norm_parts(x.astype(F32))
        grad_two = jnp.where(live[:, None], cot, jnp.zeros((), BF16))
        return ((unit * vectors[0] + vectors[1]).astype(BF16), grad_two)

    def make_tables():
        ids = jnp.arange(128)[None]
        match = segment[:, None] == ids
        key_mask = jnp.where(match | ((ids >= 8) & (ids < 11)), 1.0, 0.0).astype(BF16)
        query_mask = jnp.where((ids < 8) & ~match, MASKED, 0.0).astype(BF16)
        places = jnp.stack([rows_pos, cols_pos], axis=1).astype(F32)
        return (key_mask, query_mask, places,
                vectors[4:7].reshape(1, 3 * width), vectors[8:12].reshape(1, 4 * width))

    if quick:
        weights, slots, tables = gather_pieces(master, inverse, core, me, devices, freqs, make_angles, late, make_late, make_tables())
    else:
        low = lax.all_gather(master.astype(BF16), "dp", axis=0, tiled=True)
        weights = low.reshape(devices, block_rows, width)[inverse].reshape(stack, width)
        slots = jnp.zeros((4, devices), jnp.int32)
        tables = make_angles(freqs) + make_late(*late) + make_tables()
    cosine, sine, first_in, grad_two, key_mask, query_mask, places, bias_qkv, bias_one = tables
    here = core.reshape(1).astype(jnp.int32)
    query, key, value, attn, stat, *placed = attend(
        here, slots, first_in, bias_qkv,
        cosine, sine, query_mask, key_mask, weights, stack,
    )
    if quick:
        weights = placed[0]
    whole_rows = block_rows if quick else 0
    block_out, grad_middle, grad_attn, sums, bias_up, keep_mlp, give_mlp = mlp(
        here, x, attn, grad_two, vectors, weights, bias_one, whole_rows
    )
    pairs = width // 128
    tie = lax.optimization_barrier
    if quick:
        pos = quarters(core, me)
        got = lax.ppermute(give_mlp, "group", SWAP)
    back = None
    cuts = (0, 1, pairs - 1, pairs)
    for start, stop in zip(cuts[:-1], cuts[1:]):
        back = attend_back(
            start, stop, back, query, key, value, grad_attn, attn, stat, cosine, sine, query_mask, key_mask, places
        )
        if quick and start == 0:
            (send, hold), back = tie((fold(pos, keep_mlp, got), back))
            came = cross(send, 1, 2, devices)
        if quick and start == 1:
            send, back = tie((add_low(hold[0], came[0]), back))
            again = cross(send, 2, 1, devices)
    grad_q, grad_k, grad_v, grad_bias, grad_freq = back
    keep_qkv, give_qkv = qkv_grad(here, grad_q, grad_k, grad_v, first_in, whole_rows)
    if quick:
        again, give_qkv = tie((again, give_qkv))
        low, grad_v, give_qkv = tie((add_low(hold[1], came[1], again), grad_v, give_qkv))
        late = sum_z(low, me, devices)
    if quick:
        got_qkv = lax.ppermute(give_qkv, "group", SWAP)
        send, hold = fold(pos, keep_qkv, got_qkv)
        third = send.shape[2] // 3
        send = [send[:, :, third * i:third * (i + 1)] for i in range(3)]
        send, grad_v = tie((send, grad_v))
    input_grad, local_vec = input_back(
        grad_q, grad_k, grad_v, weights, x, grad_middle, vectors, sums, grad_bias, grad_freq, bias_up
    )
    if quick:
        send[2], local_vec = tie((send[2], local_vec))
        came = [cross(a, 1, 2, devices) for a in send]
        came, local_vec, late = tie((came, local_vec, late))
        came = jnp.concatenate(came, axis=2)
        again = cross(add_low(hold[0], came[0]), 2, 1, devices)
        vec_total = sum_part(local_vec + lax.ppermute(local_vec, "group", SWAP), devices, 4, devices)
        again, vec_total = tie((again, vec_total))
        early = sum_z(add_low(hold[1], came[1], again), me, devices)
        early, vec_total = tie((early, sum_part(vec_total, devices, 1, 4)))
        load = pack(owner_block, me & 1, early, late)
        mine = lax.all_to_all(load, "dp", 0, 0, tiled=True)
        other = lax.ppermute(mine, "group", SWAP)
        shape = (devices // 4, 2, 2, *load.shape[1:])
        own = jnp.stack([core, owner_block[me] % 2]).astype(jnp.int32)
        mat_grad, mat_second, mat_weight, vec_grad, vec_second_new, vec_weight, norm = adam_rows(
            own, mine.reshape(shape), other.reshape(shape), vec_total, vectors, vec_first, vec_second,
            master, first_mom, second_mom,
        )
        grad_norm = norm.reshape(())
    else:
        vec_total = lax.psum(local_vec, CORES)
        share = reduce_plain(jnp.concatenate([keep_qkv, keep_mlp]), owner_block, devices)
        square = lax.psum(jnp.sum(share * share), "dp")
        grad_norm = jnp.sqrt(square + jnp.sum(vec_total * vec_total))
        clip = jnp.minimum(1.0, 1.0 / (grad_norm + 1e-06))
        mat_grad = share * clip
        mat_second, mat_weight = adam(master, first_mom, second_mom, mat_grad, 0.02, 0.05)
        vec_grad = vec_total * clip
        vec_second_new, vec_weight = adam(vectors, vec_first, vec_second, vec_grad, 0.2, 0.0)
    return (
        block_out[None],
        input_grad[None],
        mat_grad,
        mat_second,
        mat_weight,
        vec_grad,
        vec_second_new,
        vec_weight,
        grad_norm,
    )


def solution(mesh):
    return jax.shard_map(
        local,
        mesh=mesh,
        in_specs=(
            P("group", "dp", None),
            P("group", "dp", None),
            P("group", "dp"),
            P("group", "dp"),
            P(),
            P("dp", None),
            P("dp", None),
            P("dp", None),
            P(),
            P(),
            P(),
        ),
        out_specs=(
            P("group", "dp", None),
            P("group", "dp", None),
            P("dp", None),
            P("dp", None),
            P("dp", None),
            P(),
            P(),
            P(),
            P(),
        ),
        check_vma=False,
    )
```

```python
import functools
import jax
import jax.numpy as jnp
from jax import lax
from jax.experimental import pallas as pl
from jax.experimental.pallas import tpu as pltpu

F32 = jnp.float32
BF16 = jnp.bfloat16
LAST = (((1,), (1,)), ((), ()))
FIRST = (((0,), (0,)), ((), ()))
PLAIN = (((1,), (0,)), ((), ()))
MASKED = -1e9
MORE = 40
SHORT = pl.CostEstimate(flops=1000, bytes_accessed=1000, transcendentals=0)


def mm(left, right, dims):
    return lax.dot_general(left, right, dims, preferred_element_type=F32)


def norm_parts(value):
    centre = value - jnp.mean(value, axis=-1, keepdims=True)
    spread = jnp.mean(centre * centre, axis=-1, keepdims=True)
    inverse = lax.rsqrt(spread + 1e-6)
    return centre * inverse, inverse


def norm_back(unit, inverse, grad, gain):
    scaled = grad * gain
    first = jnp.mean(scaled, axis=-1, keepdims=True)
    second = jnp.mean(scaled * unit, axis=-1, keepdims=True)
    return inverse * (scaled - first - unit * second)


def swap_halves(value):
    lane = lax.broadcasted_iota(jnp.int32, value.shape, 1)
    return jnp.where(
        lane % 64 < 32, pltpu.roll(value, 96, 1), pltpu.roll(value, 32, 1)
    )


def split3(value):
    one = value.astype(BF16).astype(F32)
    rest = value - one
    two = rest.astype(BF16).astype(F32)
    return one, two, rest - two


LARGE = 208
SMALL = 80


def place_pieces(core, slot_ref, mine, other, block, side, dst, sem):
    for which, (first, second, small) in enumerate((mine, other)):
        @pl.when((core == side) if which == 0 else (core != side))
        def _():
            large_slot = slot_ref[2 * which, block]
            small_slot = slot_ref[2 * which + 1, block]

            @pl.when(large_slot < 8)
            def _():
                pltpu.make_async_copy(first.at[large_slot], dst(0, LARGE), sem).start()

            @pl.when(large_slot >= 8)
            def _():
                pltpu.make_async_copy(second.at[large_slot - 8], dst(0, LARGE), sem).start()

            pltpu.make_async_copy(small.at[small_slot], dst(LARGE, SMALL), sem).start()


def attend_kernel(blocks, core_ref, slot_ref, n1_ref, bq_ref, bk_ref, bv_ref,
                  cos_ref, sin_ref, qm_ref, km_ref, *rest):
    if blocks:
        mine, other = rest[0:3], rest[3:6]
        q_ref, k_ref, v_ref, attn_ref, stat_ref, w_ref, w_s, near, far, back = rest[6:]
    else:
        w_ref, q_ref, k_ref, v_ref, attn_ref, stat_ref, w_s, near = rest
    count, width = n1_ref.shape
    step = pl.program_id(0)

    @pl.when(step == 0)
    def _():
        if blocks:
            core = core_ref[0]
            rows = w_ref.shape[0] // blocks

            def start(block, sem):
                for side in (0, 1):
                    def dst(offset, size):
                        base = block * rows + side * (rows // 2) + offset
                        return w_s.at[pl.ds(pl.multiple_of(base, 16), size)]
                    place_pieces(core, slot_ref, mine, other, block, side, dst, sem)

            def near_block(block, carry):
                start(block, near)
                return carry

            def far_block(block, carry):
                start(block, far)
                return carry

            lax.fori_loop(0, 3 * width // rows, near_block, 0)
            lax.fori_loop(3 * width // rows, blocks, far_block, 0)
        else:
            pltpu.make_async_copy(w_ref.at[pl.ds(0, 3 * width)], w_s, near).start()
        head = w_s.at[pl.ds(0, 3 * width)]
        pltpu.make_async_copy(head, head, near).wait()

    if blocks:
        @pl.when(step == 1)
        def _():
            tail = w_s.at[pl.ds(3 * width, w_s.shape[0] - 3 * width)]
            pltpu.make_async_copy(tail, tail, far).wait()
            pltpu.make_async_copy(w_s, w_ref, back).start()

    def third(j):
        return w_s[pl.ds(pl.multiple_of(j * width + step * 128, 128), 128), :]

    w = jnp.concatenate([third(0), third(1), third(2)], axis=0)
    qkv = mm(n1_ref[...], w, LAST)
    q = qkv[:, :128] + bq_ref[...]
    k = qkv[:, 128:256] + bk_ref[...]
    v = (qkv[:, 256:] + bv_ref[...]).astype(BF16)
    c = cos_ref[...]
    s = sin_ref[...]
    qr = ((q * c + swap_halves(q) * s).astype(BF16).astype(F32) * 0.125).astype(BF16)
    kr = (k * c + swap_halves(k) * s).astype(BF16)
    q_ref[...] = qr
    k_ref[...] = kr
    v_ref[...] = v
    lane = lax.broadcasted_iota(jnp.int32, (1, 128), 1)
    k_aug = jnp.concatenate([kr, km_ref[...]], axis=1)
    v_aug = jnp.concatenate([v, jnp.ones((count, 128), BF16)], axis=1)
    zero = jnp.zeros((), BF16)
    tile = 256
    for i in range(count // tile):
        rows = pl.ds(i * tile, tile)
        out = None
        stats = []
        for h in (0, 1):
            mine_lanes = (lane // 64) == h
            qa = jnp.concatenate(
                [jnp.where(mine_lanes, qr[i * tile:(i + 1) * tile], zero), qm_ref[rows, :]], axis=1)
            scores = mm(qa, k_aug, LAST)
            top = jnp.max(scores, axis=-1, keepdims=True)
            e = jnp.exp(scores - top).astype(BF16)
            o = mm(e, v_aug, PLAIN)
            total = o[:, 128:]
            o = o[:, :128] / total
            out = o if out is None else jnp.where(lane < 64, out, o)
            stats.append(top + jnp.log(total[:, :1]))
        attn_ref[rows, :] = out.astype(BF16)
        stat_ref[rows, :] = jnp.where(lane < 64, stats[0], stats[1])

    if blocks:
        @pl.when(step == pl.num_programs(0) - 1)
        def _():
            pltpu.make_async_copy(w_s, w_ref, back).wait()


def attend(core, slots, n1, bqkv, cos, sin, qm, km, weights, stack):
    count, width = n1.shape
    pairs = width // 128
    pieces = isinstance(weights, tuple)
    blocks = slots.shape[1] if pieces else 0
    whole = lambda p: (0, 0)
    col = lambda p: (0, p)
    smem = pl.BlockSpec(memory_space=pltpu.SMEM)
    hbm = pl.BlockSpec(memory_space=pl.ANY)
    given = weights if pieces else (weights,)
    specs = [smem, smem] + [
        pl.BlockSpec((count, width), whole),
        pl.BlockSpec((1, 128), col),
        pl.BlockSpec((1, 128), lambda p: (0, p + pairs)),
        pl.BlockSpec((1, 128), lambda p: (0, p + 2 * pairs)),
        pl.BlockSpec((count, 128), col),
        pl.BlockSpec((count, 128), col),
        pl.BlockSpec((count, 128), whole),
        pl.BlockSpec((count, 128), whole),
    ] + [hbm] * len(given)
    outs = [pl.BlockSpec((count, 128), col)] * 5
    shape = lambda d: jax.ShapeDtypeStruct((count, width), d)
    shapes = [shape(BF16)] * 4 + [shape(F32)]
    scratch = [pltpu.VMEM((stack if pieces else 3 * width, width), BF16), pltpu.SemaphoreType.DMA]
    if pieces:
        outs.append(hbm)
        shapes.append(jax.ShapeDtypeStruct((stack, width), BF16))
        scratch += [pltpu.SemaphoreType.DMA] * 2
    return pl.pallas_call(
        functools.partial(attend_kernel, blocks),
        grid=(pairs,),
        in_specs=specs,
        out_specs=outs,
        out_shape=shapes,
        scratch_shapes=scratch,
        compiler_params=pltpu.CompilerParams(vmem_limit_bytes=56 * 2**20),
        cost_estimate=SHORT,
        name="attend",
    )(core, slots, n1, bqkv, bqkv, bqkv, cos, sin, qm, km, *given)


def gelu_both(x):
    cdf = 0.5 + 0.5 * lax.erf(x * 0.7071067811865476)
    return x * cdf, cdf + x * jnp.exp(x * x * -0.5) * 0.3989422804014327


def put_halves(stage, value):
    half = value.shape[1] // 2
    low = value.astype(BF16)
    stage[0] = low[:, :half]
    stage[1] = low[:, half:]


def send_rows(core, block_rows, stage, row, base, keep_ref, give_ref, sem):
    rows, half = stage.shape[1:]
    here = pl.ds(pl.multiple_of(row - base, 64), rows)
    if block_rows:
        pltpu.make_async_copy(stage.at[core], keep_ref.at[here], sem).start()
        pltpu.make_async_copy(stage.at[1 - core], give_ref.at[here], sem).start()
    else:
        for c in (0, 1):
            pltpu.make_async_copy(stage.at[c], keep_ref.at[here, pl.ds(c * half, half)], sem).start()


def mlp_kernel(block_rows, base, core_ref, x_ref, at_ref, dz_ref, vec_ref, wo_ref, w1_ref, w2_ref, b1_ref,
               out_ref, dm_ref, da_ref, sums_ref, gb_ref, keep_ref, give_ref,
               middle_s, n2_s, acc_s, stage_s, proj_s, sems):
    step = pl.program_id(0)
    last = pl.num_programs(0) - 1
    count, width = x_ref.shape
    core = core_ref[0]
    tile = w1_ref.shape[0]

    @pl.when(step == 0)
    def _():
        middle = x_ref[...].astype(F32) + mm(at_ref[...], wo_ref[...], LAST) + vec_ref[7:8, :]
        middle_s[...] = middle
        unit, _ = norm_parts(middle)
        n2_s[...] = (unit * vec_ref[2:3, :] + vec_ref[3:4, :]).astype(BF16)
        acc_s[...] = jnp.zeros_like(acc_s)
        dm_ref[...] = jnp.zeros_like(dm_ref)

    slot = lax.rem(step, 2)

    @pl.when(step >= 2)
    def _():
        pltpu.make_async_copy(stage_s.at[slot], stage_s.at[slot], sems.at[slot]).wait()

    n2 = n2_s[...]
    dz = dz_ref[...]
    w1 = w1_ref[...]
    w2 = w2_ref[...]
    pre = mm(w1, n2, LAST) + b1_ref[...].reshape(tile, 1)
    back = mm(w2, dz, LAST)
    act, slope = gelu_both(pre)
    hidden = act.astype(BF16)
    put_halves(stage_s.at[slot, 1], mm(hidden, dz, PLAIN))
    dpre = (back * slope).astype(BF16)
    gb_ref[...] = jnp.sum(dpre.astype(F32), axis=1, keepdims=True).reshape(1, tile)
    put_halves(stage_s.at[slot, 0], mm(dpre, n2, PLAIN))
    acc_s[...] += mm(hidden, w2, FIRST)
    dm_ref[...] += mm(dpre, w1, FIRST)
    for j in (0, 1):
        send_rows(core, block_rows, stage_s.at[slot, j], (4 + 4 * j) * width + step * tile,
                  base, keep_ref, give_ref, sems.at[slot])

    @pl.when(step == last)
    def _():
        middle = middle_s[...]
        out_ref[...] = (middle + acc_s[...] + vec_ref[12:13, :]).astype(BF16)
        unit, inverse = norm_parts(middle)
        dn = dm_ref[...]
        dy = dz_ref[...].astype(F32)
        dm = dy + norm_back(unit, inverse, dn, vec_ref[2:3, :])
        dm_ref[...] = dm
        low = dm.astype(BF16)
        row = lambda a: jnp.sum(a, axis=0, keepdims=True)
        sums_ref[...] = jnp.concatenate(
            [row(dn * unit), row(dn), row(low.astype(F32)), row(dy), jnp.zeros((4, width), F32)], axis=0)
        put_halves(proj_s, mm(low, at_ref[...], FIRST))
        send_rows(core, block_rows, proj_s, 3 * width, base, keep_ref, give_ref, sems.at[2])
        da_ref[...] = mm(low, wo_ref[...], PLAIN).astype(BF16)
        pltpu.make_async_copy(stage_s.at[slot], stage_s.at[slot], sems.at[slot]).wait()
        pltpu.make_async_copy(stage_s.at[1 - slot], stage_s.at[1 - slot], sems.at[1 - slot]).wait()
        pltpu.make_async_copy(proj_s, proj_s, sems.at[2]).wait()


def grad_shapes(block_rows, rows, width):
    if block_rows:
        half = jax.ShapeDtypeStruct((rows, width // 2), BF16)
        return [half, half]
    return [jax.ShapeDtypeStruct((rows, width), BF16), jax.ShapeDtypeStruct((16, width), BF16)]


def mlp(core, x, attn, dz, vectors, weights, b1, block_rows, tile=256):
    count, width = x.shape
    units = 4 * width
    stack = weights.shape[0]
    base = 3 * width
    whole = lambda t: (0, 0)
    big = pl.BlockSpec((count, width), whole)
    hbm = pl.BlockSpec(memory_space=pl.ANY)
    return pl.pallas_call(
        functools.partial(mlp_kernel, block_rows, base),
        grid=(units // tile,),
        in_specs=[pl.BlockSpec(memory_space=pltpu.SMEM), big, big, big, pl.BlockSpec(vectors.shape, whole),
                  pl.BlockSpec((width, width), lambda t: (3, 0)),
                  pl.BlockSpec((tile, width), lambda t: (4 * width // tile + t, 0)),
                  pl.BlockSpec((tile, width), lambda t: (8 * width // tile + t, 0)),
                  pl.BlockSpec((1, tile), lambda t: (0, t))],
        out_specs=[big, big, big, pl.BlockSpec((8, width), whole), pl.BlockSpec((1, tile), lambda t: (0, t)), hbm, hbm],
        out_shape=[
            jax.ShapeDtypeStruct((count, width), BF16),
            jax.ShapeDtypeStruct((count, width), F32),
            jax.ShapeDtypeStruct((count, width), BF16),
            jax.ShapeDtypeStruct((8, width), F32),
            jax.ShapeDtypeStruct((1, units), F32),
        ] + grad_shapes(block_rows, stack - 3 * width, width),
        scratch_shapes=[
            pltpu.VMEM((count, width), F32),
            pltpu.VMEM((count, width), BF16),
            pltpu.VMEM((count, width), F32),
            pltpu.VMEM((2, 2, 2, tile, width // 2), BF16),
            pltpu.VMEM((2, width, width // 2), BF16),
            pltpu.SemaphoreType.DMA((3,)),
        ],
        compiler_params=pltpu.CompilerParams(vmem_limit_bytes=60 * 2**20),
        cost_estimate=SHORT,
        name="mlp",
    )(core, x, attn, dz, vectors, weights, weights, weights, b1)


def back_kernel(first, q_ref, k_ref, v_ref, da_ref, at_ref, stat_ref, cos_ref, sin_ref,
                qm_ref, km_ref, pos_ref, *rest):
    dq_ref, dk_ref, dv_ref, gb_ref, gf_ref = rest if first else rest[5:]
    count = q_ref.shape[0]
    lane = lax.broadcasted_iota(jnp.int32, (1, 128), 1)
    zero = jnp.zeros((), BF16)
    q = q_ref[...]
    k = k_ref[...]
    v = v_ref[...]
    da = da_ref[...]
    prod = da.astype(F32) * at_ref[...].astype(F32)
    qm = qm_ref[...].astype(F32)
    k_aug = jnp.concatenate([k, km_ref[...]], axis=1)
    v_aug = jnp.concatenate([v, jnp.broadcast_to((lane < 2).astype(BF16), (count, 128))], axis=1)
    tile = 256
    dq = dk = dv = None
    for h in (0, 1):
        mine = (lane // 64) == h
        qh = jnp.where(mine, q, zero)
        kh = jnp.where(mine, k, zero)
        dah = jnp.where(mine, da, zero)
        delta = jnp.sum(jnp.where(mine, prod, 0.0), axis=-1, keepdims=True)
        d1, d2, _ = split3(delta)
        l1, l2, l3 = split3(stat_ref[:, 64 * h:64 * h + 1])
        extra = jnp.where(lane == 8, -l1, jnp.where(lane == 9, -l2, jnp.where(lane == 10, -l3, qm)))
        q_aug = jnp.concatenate([qh, extra.astype(BF16)], axis=1)
        da_aug = jnp.concatenate(
            [dah, jnp.where(lane == 0, -d1, jnp.where(lane == 1, -d2, 0.0)).astype(BF16)], axis=1)
        dks, dvs, dqh = [], [], None
        for i in range(count // tile):
            sl = slice(i * tile, (i + 1) * tile)
            p = jnp.exp(mm(k_aug[sl], q_aug, LAST))
            dp = mm(v_aug[sl], da_aug, LAST)
            ds = (p * dp).astype(BF16)
            dvs.append(mm(p.astype(BF16), dah, PLAIN))
            dks.append(mm(ds, qh, PLAIN))
            part = mm(ds, kh[sl], FIRST)
            dqh = part if dqh is None else dqh + part
        dkh = jnp.concatenate(dks, axis=0)
        dvh = jnp.concatenate(dvs, axis=0)
        dq = dqh if dq is None else dq + dqh
        dk = dkh if dk is None else dk + dkh
        dv = dvh if dv is None else dv + dvh
    dq = dq * 0.125
    c = cos_ref[...]
    s = sin_ref[...]
    turned = dq * swap_halves(q.astype(F32) * 8.0) + dk * swap_halves(k.astype(F32))
    turned = jnp.where(lane % 64 < 32, -turned, turned)
    row = lambda a: jnp.sum(a, axis=0, keepdims=True)
    gf_ref[...] = jnp.concatenate(
        [row(turned * pos_ref[:, 0:1]), row(turned * pos_ref[:, 1:2]), jnp.zeros((6, 128), F32)], axis=0)
    dqp = (dq * c - swap_halves(dq) * s).astype(BF16)
    dkp = (dk * c - swap_halves(dk) * s).astype(BF16)
    dvp = dv.astype(BF16)
    gb_ref[...] = jnp.concatenate(
        [row(dqp.astype(F32)), row(dkp.astype(F32)), row(dvp.astype(F32)), jnp.zeros((5, 128), F32)], axis=0)
    dq_ref[...] = dqp
    dk_ref[...] = dkp
    dv_ref[...] = dvp


def attend_back(start, stop, before, q, k, v, da, attn, stat, cos, sin, qm, km, pos):
    count, width = q.shape
    whole = lambda p: (0, 0)
    col = lambda p: (0, p + start)
    tall = pl.BlockSpec((count, 128), col)
    fixed = pl.BlockSpec((count, 128), whole)
    small = pl.BlockSpec((8, 128), col)
    in_specs = [tall] * 8 + [fixed] * 2 + [pl.BlockSpec((count, 2), whole)]
    operands = [q, k, v, da, attn, stat, cos, sin, qm, km, pos]
    aliases = {}
    if before is not None:
        aliases = {len(operands) + i: i for i in range(5)}
        in_specs += [pl.BlockSpec(memory_space=pl.ANY)] * 5
        operands += list(before)
    return pl.pallas_call(
        functools.partial(back_kernel, before is None),
        grid=(stop - start,),
        in_specs=in_specs,
        out_specs=[tall] * 3 + [small] * 2,
        out_shape=[jax.ShapeDtypeStruct((count, width), BF16)] * 3 + [jax.ShapeDtypeStruct((8, width), F32)] * 2,
        input_output_aliases=aliases,
        compiler_params=pltpu.CompilerParams(vmem_limit_bytes=56 * 2**20),
        cost_estimate=SHORT,
        name="attend_back",
    )(*operands)


def qkv_grad_kernel(block_rows, core_ref, dq_ref, dk_ref, dv_ref, n1_ref, keep_ref, give_ref, stage_s, sem):
    width = n1_ref.shape[1]
    cols = dq_ref.shape[1]
    step = pl.program_id(0)
    n1 = n1_ref[...]
    for j, ref in enumerate((dq_ref, dk_ref, dv_ref)):
        put_halves(stage_s.at[step, j], mm(ref[...], n1, FIRST))
        send_rows(core_ref[0], block_rows, stage_s.at[step, j], j * width + step * cols, 0, keep_ref, give_ref, sem)

    @pl.when(step == pl.num_programs(0) - 1)
    def _():
        pltpu.make_async_copy(stage_s, stage_s, sem).wait()


def qkv_grad(core, dq, dk, dv, n1, block_rows):
    count, width = n1.shape
    cols = width // 2
    tall = pl.BlockSpec((count, cols), lambda p: (0, p))
    hbm = pl.BlockSpec(memory_space=pl.ANY)
    return pl.pallas_call(
        functools.partial(qkv_grad_kernel, block_rows),
        grid=(2,),
        in_specs=[pl.BlockSpec(memory_space=pltpu.SMEM)] + [tall] * 3 + [pl.BlockSpec((count, width), lambda p: (0, 0))],
        out_specs=[hbm, hbm],
        out_shape=grad_shapes(block_rows, 3 * width, width),
        scratch_shapes=[pltpu.VMEM((2, 3, 2, cols, width // 2), BF16), pltpu.SemaphoreType.DMA],
        compiler_params=pltpu.CompilerParams(vmem_limit_bytes=56 * 2**20),
        cost_estimate=SHORT,
        name="qkv_grad",
    )(core, dq, dk, dv, n1)


def input_kernel(dq_ref, dk_ref, dv_ref, w_ref, x_ref, dm_ref, vec_ref, sums_ref, gb_ref, gf_ref, up_ref, ig_ref, out_ref):
    step = pl.program_id(0)
    d = jnp.concatenate([dq_ref[...], dk_ref[...], dv_ref[...]], axis=1)
    dn = mm(d, w_ref[...], PLAIN)
    unit, inverse = norm_parts(x_ref[...].astype(F32))
    ig_ref[...] = dm_ref[...] + norm_back(unit, inverse, dn, vec_ref[0:1, :])
    row = lambda a: jnp.sum(a, axis=0, keepdims=True)
    sums = jnp.concatenate([row(dn * unit), row(dn)], axis=0)

    @pl.when(step == 0)
    def _():
        width = dn.shape[1]
        half = width // 2
        out_ref[0:2] = sums
        out_ref[2:4] = sums_ref[0:2]
        out_ref[4:7] = gb_ref[0:3]
        out_ref[7:8] = sums_ref[2:3]
        for i in range(4):
            out_ref[8 + i:9 + i] = up_ref[:, i * width:(i + 1) * width]
        out_ref[12:13] = sums_ref[3:4]
        lane = lax.broadcasted_iota(jnp.int32, (width, half), 0)
        slot = lax.broadcasted_iota(jnp.int32, (width, half), 1)
        pick = jnp.where((lane // 64 == slot // 32) & (lane % 32 == slot % 32), 1.0, 0.0)
        both = lax.dot_general(gf_ref[...], pick, PLAIN, precision=lax.Precision.HIGHEST, preferred_element_type=F32)
        out_ref[13:14, :half] = both[0:1]
        out_ref[13:14, half:] = both[1:2]

    @pl.when(step > 0)
    def _():
        out_ref[0:2] += sums


def input_back(dq, dk, dv, weights, x, dm, vectors, sums, grad_bias, grad_freq, bias_up):
    count, width = x.shape
    tile = 256
    part = pl.BlockSpec((tile, width), lambda i: (i, 0))
    whole = lambda i: (0, 0)
    fixed = lambda a: pl.BlockSpec(a.shape, whole)
    return pl.pallas_call(
        input_kernel,
        grid=(count // tile,),
        in_specs=[part] * 3 + [pl.BlockSpec((3 * width, width), whole), part, part]
        + [fixed(a) for a in (vectors, sums, grad_bias, grad_freq, bias_up)],
        out_specs=[part, fixed(vectors)],
        out_shape=[jax.ShapeDtypeStruct((count, width), F32), jax.ShapeDtypeStruct(vectors.shape, F32)],
        compiler_params=pltpu.CompilerParams(vmem_limit_bytes=56 * 2**20),
        cost_estimate=SHORT,
        name="input_back",
    )(dq, dk, dv, weights, x, dm, vectors, sums, grad_bias, grad_freq, bias_up)


def fold_kernel(pos_ref, keep_ref, got_ref, send_ref, hold_ref):
    rows = keep_ref.shape[1] // 2
    deep = 4
    piece = rows // deep
    more, less = MORE, piece - MORE
    for m in range(keep_ref.shape[0] // 2):
        both = []
        for y in (0, 1):
            here = slice(y * rows, y * rows + rows)
            even, odd = (
                keep_ref[2 * m + e, here, :].astype(F32) + got_ref[2 * m + e, here, :].astype(F32) for e in (0, 1)
            )
            parts = []
            for z in range(deep):
                at = z * piece
                parts.append((
                    jnp.concatenate([even[at:at + more], odd[at:at + less]], axis=0),
                    jnp.concatenate([even[at + more:at + piece], odd[at + less:at + piece]], axis=0),
                ))
            both.append([jnp.concatenate([p[x] for p in parts], axis=0).astype(BF16) for x in (0, 1)])
        for y in (0, 1):
            for x in (0, 1):
                for way in range(4):
                    @pl.when((pos_ref[way, 0] == y) & (pos_ref[way, 1] == x))
                    def _(way=way, y=y, x=x):
                        (send_ref, hold_ref)[way // 2][way % 2, m] = both[y][x]


def fold(pos, keep, got):
    count, rows, cols = keep.shape
    some = 4 if count % 4 == 0 else 2
    whole = pl.BlockSpec((some, rows, cols), lambda i, pos: (i, 0, 0))
    out = pl.BlockSpec((2, some // 2, rows // 2, cols), lambda i, pos: (0, i, 0, 0))
    shape = jax.ShapeDtypeStruct((2, count // 2, rows // 2, cols), BF16)
    return pl.pallas_call(
        fold_kernel,
        grid_spec=pltpu.PrefetchScalarGridSpec(
            num_scalar_prefetch=1, grid=(count // some,), in_specs=[whole, whole], out_specs=[out, out]),
        compiler_params=pltpu.CompilerParams(vmem_limit_bytes=40 * 2**20),
        out_shape=[shape, shape],
        cost_estimate=SHORT,
        name="fold",
    )(pos, keep, got)


def pack_kernel(owner_ref, *refs):
    early, late, out_ref, total_s = refs[:4], refs[4:8], refs[8], refs[9]
    square = None
    start = 0
    rows = early[0].shape[1]
    for parts in (early, late):
        total = parts[0][...].astype(F32)
        for part in parts[1:]:
            total = total + part[...].astype(F32)
        total_s[start:start + total.shape[0], :rows] = total
        start += total.shape[0]
        more = jnp.sum(total * total).reshape(1, 1)
        square = more if square is None else square + more
    total_s[:, rows:] = jnp.zeros((start, total_s.shape[1] - rows, total_s.shape[2]), F32)
    lane = lax.broadcasted_iota(jnp.int32, (8, out_ref.shape[2]), 1)
    one, two, three = split3(square)
    extra = jnp.where(lane == 0, one, jnp.where(lane == 1, two, jnp.where(lane == 2, three, 0.0)))
    devices = out_ref.shape[0]
    skip = jnp.where(owner_ref[devices] == 0, MORE, rows - MORE)
    for p in range(devices):
        block = owner_ref[p]
        at = lax.rem(block, 2) * skip
        mine = total_s[lax.div(block, 2), pl.ds(pl.multiple_of(at, 8), MORE), :]
        out_ref[p] = jnp.concatenate([mine, extra], axis=0).astype(BF16)


def pack(owner, x, early, late):
    blocks = early[0].shape[0] + late[0].shape[0]
    rows, cols = early[0].shape[1:]
    vmem = pl.BlockSpec(memory_space=pltpu.VMEM)
    return pl.pallas_call(
        pack_kernel,
        in_specs=[pl.BlockSpec(memory_space=pltpu.SMEM)] + [vmem] * 8,
        out_specs=vmem,
        out_shape=jax.ShapeDtypeStruct((owner.shape[0], MORE + 8, cols), BF16),
        scratch_shapes=[pltpu.VMEM((blocks, rows + 8, cols), F32)],
        compiler_params=pltpu.CompilerParams(vmem_limit_bytes=32 * 2**20),
        cost_estimate=SHORT,
        name="pack",
    )(jnp.concatenate([owner, x.reshape(1).astype(owner.dtype)]), *early, *late)


def clip_of(square, vec):
    norm = jnp.sqrt(square + jnp.sum(vec * vec).reshape(1, 1))
    return norm, jnp.minimum(1.0, 1.0 / (norm + 1e-06))


def adam_kernel(own_ref, a_ref, b_ref, as_ref, bs_ref, vt_ref, vw_ref, vm_ref, vv_ref, w_ref, m_ref, v_ref,
                g_out, v_out, w_out, vg_out, vv_out, vw_out, norm_out):
    def squares(ref):
        block = ref[...].astype(F32)
        lane = lax.broadcasted_iota(jnp.int32, block.shape, 4)
        row = lax.broadcasted_iota(jnp.int32, block.shape, 3)
        return jnp.sum(jnp.where((lane < 3) & (row == 0), block, 0.0)).reshape(1, 1)

    norm, clip = clip_of(squares(as_ref) + squares(bs_ref), vt_ref[...])
    mine = pl.program_id(1) == own_ref[0]
    even = own_ref[1] == 0
    deep = a_ref.shape[0]
    piece = w_ref.shape[0] // deep
    runs = []
    for z in range(deep):
        left, right = (jnp.where(mine, a_ref[z, 0, x].astype(F32), b_ref[z, 0, x].astype(F32)) for x in (0, 1))
        runs.append(jnp.where(
            even,
            jnp.concatenate([left[:MORE], right[:piece - MORE]], axis=0),
            jnp.concatenate([left[:piece - MORE], right[:MORE]], axis=0),
        ))
    grad = jnp.concatenate(runs, axis=0) * clip
    second, weight = adam(w_ref[...], m_ref[...], v_ref[...], grad, 0.02, 0.05)
    g_out[...] = grad
    v_out[...] = second
    w_out[...] = weight

    @pl.when((pl.program_id(0) == 0) & (pl.program_id(1) == 0))
    def _():
        vec_grad = vt_ref[...] * clip
        second, weight = adam(vw_ref[...], vm_ref[...], vv_ref[...], vec_grad, 0.2, 0.0)
        vg_out[...] = vec_grad
        vv_out[...] = second
        vw_out[...] = weight
        norm_out[...] = norm


def adam_rows(own, mine, other, vec_total, vectors, vec_first, vec_second, weight, first, second):
    rows, width = weight.shape
    deep, tall, wide, piece, cols = mine.shape
    part = pl.BlockSpec((deep, 1, wide, piece, cols), lambda y, h: (0, y, 0, 0, 0))
    marks = pl.BlockSpec((deep, tall, wide, 8, 128), lambda y, x: (0, 0, 0, piece // 8 - 1, 0))
    flat = pl.BlockSpec((rows // tall, cols), lambda y, h: (y, h))
    vec = pl.BlockSpec(vectors.shape, lambda y, x: (0, 0))
    shape = jax.ShapeDtypeStruct((rows, width), F32)
    small = jax.ShapeDtypeStruct(vectors.shape, F32)
    return pl.pallas_call(
        adam_kernel,
        grid=(tall, width // cols),
        in_specs=[pl.BlockSpec(memory_space=pltpu.SMEM), part, part, marks, marks] + [vec] * 4 + [flat] * 3,
        out_specs=[flat] * 3 + [vec] * 3 + [pl.BlockSpec((1, 1), lambda y, x: (0, 0))],
        out_shape=[shape] * 3 + [small] * 3 + [jax.ShapeDtypeStruct((1, 1), F32)],
        compiler_params=pltpu.CompilerParams(vmem_limit_bytes=60 * 2**20),
        cost_estimate=SHORT,
        name="adam",
    )(own, mine, other, mine, other, vec_total, vectors, vec_first, vec_second, weight, first, second)


from jax.sharding import PartitionSpec as P

HEADS = 12
STEP = 7


def place_tokens(heights, widths, count):
    sizes = heights * widths
    ends = jnp.cumsum(sizes)
    starts = ends - sizes
    places = jnp.arange(count, dtype=jnp.int32)
    segment = jnp.sum((places[:, None] >= ends[None, :]).astype(jnp.int32), axis=1)
    slots = jnp.arange(heights.shape[0], dtype=jnp.int32)
    picks = (segment[:, None] == slots[None, :]).astype(jnp.int32)
    begin = jnp.sum(picks * starts[None, :], axis=1)
    across = jnp.maximum(jnp.sum(picks * widths[None, :], axis=1), 1)
    offset = places - begin
    live = places < ends[-1]
    return (segment, offset // across, offset % across, live)


def adam(weight, first, second, grad, rate, decay):
    first_new = 0.5 * first + 0.5 * grad
    second_new = 0.5 * second + 0.5 * grad * grad
    correct = 1.0 - 0.5**STEP
    direction = first_new / correct / (jnp.sqrt(second_new / correct) + 1e-08)
    return (second_new, weight - rate * (direction + decay * weight))


def pairwise(bits, total):
    return [(i, i ^ bits) for i in range(total)]


def sum_part(value, devices, step, stop):
    while step < stop:
        value = value + lax.ppermute(value, "dp", pairwise(step, devices))
        step *= 2
    return value


CORES = ("group", "dp")
SWAP = [(0, 1), (1, 0)]


def cross(value, bit0, bit1, devices):
    perm = [(i, i ^ (bit0 if i < devices else bit1)) for i in range(2 * devices)]
    return lax.ppermute(value, CORES, perm)


def along_z(values, devices):
    return [
        lax.ppermute(v, "dp", [(i, (i + 4 * (s + 1)) % devices) for i in range(devices)])
        for s, v in enumerate(values)
    ]


def along_line(value, devices, step, up):
    last = devices // 4
    perm = []
    for z in range(last):
        near = z - 1 if up else z + 1
        far = z - step if up else z + step
        if 0 <= far < last:
            perm += [(4 * near + i, 4 * z + i) for i in range(4)]
    return lax.ppermute(value, "dp", perm)


def gather_pieces(master, inverse, core, me, devices, freqs, make_angles, late, make_late, tables):
    tie = lax.optimization_barrier
    block_rows, width = master.shape
    half = block_rows // 2
    mine = lax.dynamic_slice_in_dim(master, core * half, half, 0).astype(BF16)
    large = mine[:LARGE]
    small = mine[LARGE:]
    z = me // 4
    deep = lax.rem(z - inverse // 4 + 4, 4)
    apart = me ^ inverse
    one = jnp.where(core == 0, apart & 1, (apart >> 1) & 1)
    two = jnp.where(core == 0, (apart >> 1) & 1, apart & 1)
    slots = jnp.stack([
        8 * two + 4 * one + deep,
        4 * deep + 2 * two + one,
        8 * one + 4 * two + deep,
        4 * deep + 2 * one + two,
    ]).astype(jnp.int32)
    up = along_z([large] * 3, devices)
    small = jnp.stack([small, cross(small, 1, 2, devices)])
    small, freqs = tie((small, freqs))
    small = jnp.concatenate([small, cross(small, 2, 1, devices)])
    large = jnp.stack([large] + up)
    large, small, tables, slots, angles = tie((large, small, tables, slots, make_angles(freqs)))
    first = cross(large, 1, 2, devices)
    ups = [along_line(small, devices, 1, True)]
    downs = [along_line(small, devices, 1, False)]
    first, ups[0], downs[0], late = tie((first, ups[0], downs[0], late))
    done = make_late(*late)
    first = jnp.concatenate([large, first])
    second = cross(first, 2, 1, devices)
    for step in (2, 3):
        ups.append(along_line(ups[-1], devices, step, True))
        downs.append(along_line(downs[-1], devices, step, False))
        if step == 2:
            ups[1], downs[1], done = tie((ups[1], downs[1], done))
    small = jnp.concatenate([small] + [jnp.where(z >= s, ups[s - 1], downs[3 - s]) for s in (1, 2, 3)])
    other = [lax.ppermute(a, "group", SWAP) for a in (first, second, small)]
    return (first, second, small, *other), slots, angles + done + tables


def quarters(core, me):
    x, y = me & 1, (me >> 1) & 1
    one = jnp.where(core == 0, x, y)
    two = jnp.where(core == 0, y, x)
    pairs = [(1 - one, 1 - two), (1 - one, two), (one, 1 - two), (one, two)]
    return jnp.stack([
        jnp.stack([jnp.where(core == 0, b, a), jnp.where(core == 0, a, b)]) for a, b in pairs
    ]).astype(jnp.int32)


def add_low(*terms):
    total = terms[0].astype(F32)
    for term in terms[1:]:
        total = total + term.astype(F32)
    return total.astype(BF16)


def sum_z(low, me, devices):
    count, rows, cols = low.shape
    z = me // 4
    low = low.reshape(count, 4, rows // 4, cols)
    pick = lambda at: lax.dynamic_index_in_dim(low, at, 1, keepdims=False)
    return (pick(z), *along_z([pick(lax.rem(z + s, 4)) for s in (1, 2, 3)], devices))


def reduce_plain(local_mat, owner_block, devices):
    rows, width = local_mat.shape
    block_rows = rows // devices
    term = local_mat.reshape(devices, block_rows, width)[owner_block].reshape(rows, width)
    share = lax.psum_scatter(term.astype(F32), "dp", scatter_dimension=0, tiled=True)
    return lax.psum(share.astype(BF16), "group").astype(F32)


def local(
    tokens,
    cotangent,
    grid_h,
    grid_w,
    owner_block,
    master,
    first_mom,
    second_mom,
    vectors,
    vec_first,
    vec_second,
):
    devices = lax.axis_size("dp")
    core = lax.axis_index("group")
    me = lax.axis_index("dp")
    count = tokens.shape[1]
    width = tokens.shape[2]
    heads = HEADS
    head_dim = width // heads
    half = head_dim // 2
    block_rows = master.shape[0]
    stack = devices * block_rows
    quick = devices == 16 and block_rows == 2 * (LARGE + SMALL) and width % 256 == 0
    inverse = jnp.argsort(owner_block)
    segment, rows_pos, cols_pos, live = place_tokens(grid_h[0], grid_w[0], count)
    x = tokens[0]

    def spread(part):
        return jnp.broadcast_to(part.reshape(heads, 1, half), (heads, 2, half)).reshape(1, width)

    freqs = (spread(vectors[13, : width // 2]), spread(vectors[13, width // 2 :]))

    def make_angles(freqs):
        down = rows_pos.astype(F32)[:, None]
        right = cols_pos.astype(F32)[:, None]
        angle = down * freqs[0] + right * freqs[1]
        lower = (jnp.arange(width) % head_dim < half)[None]
        cosine = jnp.cos(angle)
        sine = jnp.sin(angle)
        return (cosine, jnp.where(lower, -sine, sine))

    late = (x, cotangent[0])

    def make_late(x, cot):
        unit, _ = norm_parts(x.astype(F32))
        grad_two = jnp.where(live[:, None], cot, jnp.zeros((), BF16))
        return ((unit * vectors[0] + vectors[1]).astype(BF16), grad_two)

    def make_tables():
        ids = jnp.arange(128)[None]
        match = segment[:, None] == ids
        key_mask = jnp.where(match | ((ids >= 8) & (ids < 11)), 1.0, 0.0).astype(BF16)
        query_mask = jnp.where((ids < 8) & ~match, MASKED, 0.0).astype(BF16)
        places = jnp.stack([rows_pos, cols_pos], axis=1).astype(F32)
        return (key_mask, query_mask, places,
                vectors[4:7].reshape(1, 3 * width), vectors[8:12].reshape(1, 4 * width))

    if quick:
        weights, slots, tables = gather_pieces(master, inverse, core, me, devices, freqs, make_angles, late, make_late, make_tables())
    else:
        low = lax.all_gather(master.astype(BF16), "dp", axis=0, tiled=True)
        weights = low.reshape(devices, block_rows, width)[inverse].reshape(stack, width)
        slots = jnp.zeros((4, devices), jnp.int32)
        tables = make_angles(freqs) + make_late(*late) + make_tables()
    cosine, sine, first_in, grad_two, key_mask, query_mask, places, bias_qkv, bias_one = tables
    here = core.reshape(1).astype(jnp.int32)
    query, key, value, attn, stat, *placed = attend(
        here, slots, first_in, bias_qkv,
        cosine, sine, query_mask, key_mask, weights, stack,
    )
    if quick:
        weights = placed[0]
    whole_rows = block_rows if quick else 0
    block_out, grad_middle, grad_attn, sums, bias_up, keep_mlp, give_mlp = mlp(
        here, x, attn, grad_two, vectors, weights, bias_one, whole_rows
    )
    pairs = width // 128
    blocked = lambda a: a.reshape(-1, block_rows, width // 2)
    tie = lax.optimization_barrier
    if quick:
        pos = quarters(core, me)
        got = lax.ppermute(give_mlp, "group", SWAP)
    back = None
    cuts = (0, 1, pairs - 1, pairs)
    for start, stop in zip(cuts[:-1], cuts[1:]):
        back = attend_back(
            start, stop, back, query, key, value, grad_attn, attn, stat, cosine, sine, query_mask, key_mask, places
        )
        if quick and start == 0:
            (send, hold), back = tie((fold(pos, blocked(keep_mlp), blocked(got)), back))
            came = cross(send, 1, 2, devices)
        if quick and start == 1:
            send, back = tie((add_low(hold[0], came[0]), back))
            again = cross(send, 2, 1, devices)
    grad_q, grad_k, grad_v, grad_bias, grad_freq = back
    keep_qkv, give_qkv = qkv_grad(here, grad_q, grad_k, grad_v, first_in, whole_rows)
    if quick:
        again, give_qkv = tie((again, give_qkv))
        low, grad_v, give_qkv = tie((add_low(hold[1], came[1], again), grad_v, give_qkv))
        late = sum_z(low, me, devices)
    if quick:
        got_qkv = lax.ppermute(give_qkv, "group", SWAP)
        send, hold = fold(pos, blocked(keep_qkv), blocked(got_qkv))
        third = send.shape[2] // 3
        send = [send[:, :, third * i:third * (i + 1)] for i in range(3)]
        send, grad_v = tie((send, grad_v))
    input_grad, local_vec = input_back(
        grad_q, grad_k, grad_v, weights, x, grad_middle, vectors, sums, grad_bias, grad_freq, bias_up
    )
    if quick:
        send[2], local_vec = tie((send[2], local_vec))
        came = [cross(a, 1, 2, devices) for a in send]
        came, local_vec, late = tie((came, local_vec, late))
        came = jnp.concatenate(came, axis=2)
        again = cross(add_low(hold[0], came[0]), 2, 1, devices)
        vec_total = sum_part(local_vec + lax.ppermute(local_vec, "group", SWAP), devices, 4, devices)
        again, vec_total = tie((again, vec_total))
        early = sum_z(add_low(hold[1], came[1], again), me, devices)
        early, vec_total = tie((early, sum_part(vec_total, devices, 1, 4)))
        load = pack(owner_block, me & 1, early, late)
        mine = lax.all_to_all(load, "dp", 0, 0, tiled=True)
        other = lax.ppermute(mine, "group", SWAP)
        shape = (devices // 4, 2, 2, *load.shape[1:])
        own = jnp.stack([core, owner_block[me] % 2]).astype(jnp.int32)
        mat_grad, mat_second, mat_weight, vec_grad, vec_second_new, vec_weight, norm = adam_rows(
            own, mine.reshape(shape), other.reshape(shape), vec_total, vectors, vec_first, vec_second,
            master, first_mom, second_mom,
        )
        grad_norm = norm.reshape(())
    else:
        vec_total = lax.psum(local_vec, CORES)
        share = reduce_plain(jnp.concatenate([keep_qkv, keep_mlp]), owner_block, devices)
        square = lax.psum(jnp.sum(share * share), "dp")
        grad_norm = jnp.sqrt(square + jnp.sum(vec_total * vec_total))
        clip = jnp.minimum(1.0, 1.0 / (grad_norm + 1e-06))
        mat_grad = share * clip
        mat_second, mat_weight = adam(master, first_mom, second_mom, mat_grad, 0.02, 0.05)
        vec_grad = vec_total * clip
        vec_second_new, vec_weight = adam(vectors, vec_first, vec_second, vec_grad, 0.2, 0.0)
    return (
        block_out[None],
        input_grad[None],
        mat_grad,
        mat_second,
        mat_weight,
        vec_grad,
        vec_second_new,
        vec_weight,
        grad_norm,
    )


def solution(mesh):
    return jax.shard_map(
        local,
        mesh=mesh,
        in_specs=(
            P("group", "dp", None),
            P("group", "dp", None),
            P("group", "dp"),
            P("group", "dp"),
            P(),
            P("dp", None),
            P("dp", None),
            P("dp", None),
            P(),
            P(),
            P(),
        ),
        out_specs=(
            P("group", "dp", None),
            P("group", "dp", None),
            P("dp", None),
            P("dp", None),
            P("dp", None),
            P(),
            P(),
            P(),
            P(),
        ),
        check_vma=False,
    )
```

```python
import functools
import jax
import jax.numpy as jnp
from jax import lax
from jax.experimental import pallas as pl
from jax.experimental.pallas import tpu as pltpu

F32 = jnp.float32
BF16 = jnp.bfloat16
LAST = (((1,), (1,)), ((), ()))
FIRST = (((0,), (0,)), ((), ()))
PLAIN = (((1,), (0,)), ((), ()))
MASKED = -1e9
MORE = 40
SHORT = pl.CostEstimate(flops=1000, bytes_accessed=1000, transcendentals=0)


def mm(left, right, dims):
    return lax.dot_general(left, right, dims, preferred_element_type=F32)


def norm_parts(value):
    centre = value - jnp.mean(value, axis=-1, keepdims=True)
    spread = jnp.mean(centre * centre, axis=-1, keepdims=True)
    inverse = lax.rsqrt(spread + 1e-6)
    return centre * inverse, inverse


def norm_back(unit, inverse, grad, gain):
    scaled = grad * gain
    first = jnp.mean(scaled, axis=-1, keepdims=True)
    second = jnp.mean(scaled * unit, axis=-1, keepdims=True)
    return inverse * (scaled - first - unit * second)


def swap_halves(value):
    lane = lax.broadcasted_iota(jnp.int32, value.shape, 1)
    return jnp.where(
        lane % 64 < 32, pltpu.roll(value, 96, 1), pltpu.roll(value, 32, 1)
    )


def split3(value):
    one = value.astype(BF16).astype(F32)
    rest = value - one
    two = rest.astype(BF16).astype(F32)
    return one, two, rest - two


LARGE = 192
SMALL = 96


def place_pieces(core, slot_ref, mine, other, block, side, dst, sem):
    for which, (first, second, small) in enumerate((mine, other)):
        @pl.when((core == side) if which == 0 else (core != side))
        def _():
            large_slot = slot_ref[2 * which, block]
            small_slot = slot_ref[2 * which + 1, block]

            @pl.when(large_slot < 8)
            def _():
                pltpu.make_async_copy(first.at[large_slot], dst(0, LARGE), sem).start()

            @pl.when(large_slot >= 8)
            def _():
                pltpu.make_async_copy(second.at[large_slot - 8], dst(0, LARGE), sem).start()

            pltpu.make_async_copy(small.at[small_slot], dst(LARGE, SMALL), sem).start()


def attend_kernel(blocks, core_ref, slot_ref, n1_ref, bq_ref, bk_ref, bv_ref,
                  cos_ref, sin_ref, qm_ref, km_ref, *rest):
    if blocks:
        mine, other = rest[0:3], rest[3:6]
        q_ref, k_ref, v_ref, attn_ref, stat_ref, w_ref, w_s, near, far, back = rest[6:]
    else:
        w_ref, q_ref, k_ref, v_ref, attn_ref, stat_ref, w_s, near = rest
    count, width = n1_ref.shape
    step = pl.program_id(0)

    @pl.when(step == 0)
    def _():
        if blocks:
            core = core_ref[0]
            rows = w_ref.shape[0] // blocks

            def start(block, sem):
                for side in (0, 1):
                    def dst(offset, size):
                        base = block * rows + side * (rows // 2) + offset
                        return w_s.at[pl.ds(pl.multiple_of(base, 16), size)]
                    place_pieces(core, slot_ref, mine, other, block, side, dst, sem)

            def near_block(block, carry):
                start(block, near)
                return carry

            def far_block(block, carry):
                start(block, far)
                return carry

            lax.fori_loop(0, 3 * width // rows, near_block, 0)
            lax.fori_loop(3 * width // rows, blocks, far_block, 0)
        else:
            pltpu.make_async_copy(w_ref.at[pl.ds(0, 3 * width)], w_s, near).start()
        head = w_s.at[pl.ds(0, 3 * width)]
        pltpu.make_async_copy(head, head, near).wait()

    if blocks:
        @pl.when(step == 1)
        def _():
            tail = w_s.at[pl.ds(3 * width, w_s.shape[0] - 3 * width)]
            pltpu.make_async_copy(tail, tail, far).wait()
            pltpu.make_async_copy(w_s, w_ref, back).start()

    def third(j):
        return w_s[pl.ds(pl.multiple_of(j * width + step * 128, 128), 128), :]

    w = jnp.concatenate([third(0), third(1), third(2)], axis=0)
    qkv = mm(n1_ref[...], w, LAST)
    q = qkv[:, :128] + bq_ref[...]
    k = qkv[:, 128:256] + bk_ref[...]
    v = (qkv[:, 256:] + bv_ref[...]).astype(BF16)
    c = cos_ref[...]
    s = sin_ref[...]
    qr = ((q * c + swap_halves(q) * s).astype(BF16).astype(F32) * 0.125).astype(BF16)
    kr = (k * c + swap_halves(k) * s).astype(BF16)
    q_ref[...] = qr
    k_ref[...] = kr
    v_ref[...] = v
    lane = lax.broadcasted_iota(jnp.int32, (1, 128), 1)
    k_aug = jnp.concatenate([kr, km_ref[...]], axis=1)
    v_aug = jnp.concatenate([v, jnp.ones((count, 128), BF16)], axis=1)
    zero = jnp.zeros((), BF16)
    tile = 256
    for i in range(count // tile):
        rows = pl.ds(i * tile, tile)
        out = None
        stats = []
        for h in (0, 1):
            mine_lanes = (lane // 64) == h
            qa = jnp.concatenate(
                [jnp.where(mine_lanes, qr[i * tile:(i + 1) * tile], zero), qm_ref[rows, :]], axis=1)
            scores = mm(qa, k_aug, LAST)
            top = jnp.max(scores, axis=-1, keepdims=True)
            e = jnp.exp(scores - top).astype(BF16)
            o = mm(e, v_aug, PLAIN)
            total = o[:, 128:]
            o = o[:, :128] / total
            out = o if out is None else jnp.where(lane < 64, out, o)
            stats.append(top + jnp.log(total[:, :1]))
        attn_ref[rows, :] = out.astype(BF16)
        stat_ref[rows, :] = jnp.where(lane < 64, stats[0], stats[1])

    if blocks:
        @pl.when(step == pl.num_programs(0) - 1)
        def _():
            pltpu.make_async_copy(w_s, w_ref, back).wait()


def attend(core, slots, n1, bqkv, cos, sin, qm, km, weights, stack):
    count, width = n1.shape
    pairs = width // 128
    pieces = isinstance(weights, tuple)
    blocks = slots.shape[1] if pieces else 0
    whole = lambda p: (0, 0)
    col = lambda p: (0, p)
    smem = pl.BlockSpec(memory_space=pltpu.SMEM)
    hbm = pl.BlockSpec(memory_space=pl.ANY)
    given = weights if pieces else (weights,)
    specs = [smem, smem] + [
        pl.BlockSpec((count, width), whole),
        pl.BlockSpec((1, 128), col),
        pl.BlockSpec((1, 128), lambda p: (0, p + pairs)),
        pl.BlockSpec((1, 128), lambda p: (0, p + 2 * pairs)),
        pl.BlockSpec((count, 128), col),
        pl.BlockSpec((count, 128), col),
        pl.BlockSpec((count, 128), whole),
        pl.BlockSpec((count, 128), whole),
    ] + [hbm] * len(given)
    outs = [pl.BlockSpec((count, 128), col)] * 5
    shape = lambda d: jax.ShapeDtypeStruct((count, width), d)
    shapes = [shape(BF16)] * 4 + [shape(F32)]
    scratch = [pltpu.VMEM((stack if pieces else 3 * width, width), BF16), pltpu.SemaphoreType.DMA]
    if pieces:
        outs.append(hbm)
        shapes.append(jax.ShapeDtypeStruct((stack, width), BF16))
        scratch += [pltpu.SemaphoreType.DMA] * 2
    return pl.pallas_call(
        functools.partial(attend_kernel, blocks),
        grid=(pairs,),
        in_specs=specs,
        out_specs=outs,
        out_shape=shapes,
        scratch_shapes=scratch,
        compiler_params=pltpu.CompilerParams(vmem_limit_bytes=56 * 2**20),
        cost_estimate=SHORT,
        name="attend",
    )(core, slots, n1, bqkv, bqkv, bqkv, cos, sin, qm, km, *given)


def gelu_both(x):
    cdf = 0.5 + 0.5 * lax.erf(x * 0.7071067811865476)
    return x * cdf, cdf + x * jnp.exp(x * x * -0.5) * 0.3989422804014327


def put_halves(stage, value):
    half = value.shape[1] // 2
    low = value.astype(BF16)
    stage[0] = low[:, :half]
    stage[1] = low[:, half:]


def send_rows(core, block_rows, stage, row, base, keep_ref, give_ref, sem):
    rows, half = stage.shape[1:]
    here = pl.ds(pl.multiple_of(row - base, 64), rows)
    if block_rows:
        pltpu.make_async_copy(stage.at[core], keep_ref.at[here], sem).start()
        pltpu.make_async_copy(stage.at[1 - core], give_ref.at[here], sem).start()
    else:
        for c in (0, 1):
            pltpu.make_async_copy(stage.at[c], keep_ref.at[here, pl.ds(c * half, half)], sem).start()


def mlp_kernel(block_rows, base, core_ref, x_ref, at_ref, dz_ref, vec_ref, wo_ref, w1_ref, w2_ref, b1_ref,
               out_ref, dm_ref, da_ref, sums_ref, gb_ref, keep_ref, give_ref,
               middle_s, n2_s, acc_s, stage_s, proj_s, sems):
    step = pl.program_id(0)
    last = pl.num_programs(0) - 1
    count, width = x_ref.shape
    core = core_ref[0]
    tile = w1_ref.shape[0]

    @pl.when(step == 0)
    def _():
        middle = x_ref[...].astype(F32) + mm(at_ref[...], wo_ref[...], LAST) + vec_ref[7:8, :]
        middle_s[...] = middle
        unit, _ = norm_parts(middle)
        n2_s[...] = (unit * vec_ref[2:3, :] + vec_ref[3:4, :]).astype(BF16)
        acc_s[...] = jnp.zeros_like(acc_s)
        dm_ref[...] = jnp.zeros_like(dm_ref)

    slot = lax.rem(step, 2)

    @pl.when(step >= 2)
    def _():
        pltpu.make_async_copy(stage_s.at[slot], stage_s.at[slot], sems.at[slot]).wait()

    n2 = n2_s[...]
    dz = dz_ref[...]
    w1 = w1_ref[...]
    w2 = w2_ref[...]
    pre = mm(w1, n2, LAST) + b1_ref[...].reshape(tile, 1)
    back = mm(w2, dz, LAST)
    act, slope = gelu_both(pre)
    hidden = act.astype(BF16)
    put_halves(stage_s.at[slot, 1], mm(hidden, dz, PLAIN))
    dpre = (back * slope).astype(BF16)
    gb_ref[...] = jnp.sum(dpre.astype(F32), axis=1, keepdims=True).reshape(1, tile)
    put_halves(stage_s.at[slot, 0], mm(dpre, n2, PLAIN))
    acc_s[...] += mm(hidden, w2, FIRST)
    dm_ref[...] += mm(dpre, w1, FIRST)
    for j in (0, 1):
        send_rows(core, block_rows, stage_s.at[slot, j], (4 + 4 * j) * width + step * tile,
                  base, keep_ref, give_ref, sems.at[slot])

    @pl.when(step == last)
    def _():
        middle = middle_s[...]
        out_ref[...] = (middle + acc_s[...] + vec_ref[12:13, :]).astype(BF16)
        unit, inverse = norm_parts(middle)
        dn = dm_ref[...]
        dy = dz_ref[...].astype(F32)
        dm = dy + norm_back(unit, inverse, dn, vec_ref[2:3, :])
        dm_ref[...] = dm
        low = dm.astype(BF16)
        row = lambda a: jnp.sum(a, axis=0, keepdims=True)
        sums_ref[...] = jnp.concatenate(
            [row(dn * unit), row(dn), row(low.astype(F32)), row(dy), jnp.zeros((4, width), F32)], axis=0)
        put_halves(proj_s, mm(low, at_ref[...], FIRST))
        send_rows(core, block_rows, proj_s, 3 * width, base, keep_ref, give_ref, sems.at[2])
        da_ref[...] = mm(low, wo_ref[...], PLAIN).astype(BF16)
        pltpu.make_async_copy(stage_s.at[slot], stage_s.at[slot], sems.at[slot]).wait()
        pltpu.make_async_copy(stage_s.at[1 - slot], stage_s.at[1 - slot], sems.at[1 - slot]).wait()
        pltpu.make_async_copy(proj_s, proj_s, sems.at[2]).wait()


def grad_shapes(block_rows, rows, width):
    if block_rows:
        half = jax.ShapeDtypeStruct((rows, width // 2), BF16)
        return [half, half]
    return [jax.ShapeDtypeStruct((rows, width), BF16), jax.ShapeDtypeStruct((16, width), BF16)]


def mlp(core, x, attn, dz, vectors, weights, b1, block_rows, tile=256):
    count, width = x.shape
    units = 4 * width
    stack = weights.shape[0]
    base = 3 * width
    whole = lambda t: (0, 0)
    big = pl.BlockSpec((count, width), whole)
    hbm = pl.BlockSpec(memory_space=pl.ANY)
    return pl.pallas_call(
        functools.partial(mlp_kernel, block_rows, base),
        grid=(units // tile,),
        in_specs=[pl.BlockSpec(memory_space=pltpu.SMEM), big, big, big, pl.BlockSpec(vectors.shape, whole),
                  pl.BlockSpec((width, width), lambda t: (3, 0)),
                  pl.BlockSpec((tile, width), lambda t: (4 * width // tile + t, 0)),
                  pl.BlockSpec((tile, width), lambda t: (8 * width // tile + t, 0)),
                  pl.BlockSpec((1, tile), lambda t: (0, t))],
        out_specs=[big, big, big, pl.BlockSpec((8, width), whole), pl.BlockSpec((1, tile), lambda t: (0, t)), hbm, hbm],
        out_shape=[
            jax.ShapeDtypeStruct((count, width), BF16),
            jax.ShapeDtypeStruct((count, width), F32),
            jax.ShapeDtypeStruct((count, width), BF16),
            jax.ShapeDtypeStruct((8, width), F32),
            jax.ShapeDtypeStruct((1, units), F32),
        ] + grad_shapes(block_rows, stack - 3 * width, width),
        scratch_shapes=[
            pltpu.VMEM((count, width), F32),
            pltpu.VMEM((count, width), BF16),
            pltpu.VMEM((count, width), F32),
            pltpu.VMEM((2, 2, 2, tile, width // 2), BF16),
            pltpu.VMEM((2, width, width // 2), BF16),
            pltpu.SemaphoreType.DMA((3,)),
        ],
        compiler_params=pltpu.CompilerParams(vmem_limit_bytes=60 * 2**20),
        cost_estimate=SHORT,
        name="mlp",
    )(core, x, attn, dz, vectors, weights, weights, weights, b1)


def back_kernel(first, q_ref, k_ref, v_ref, da_ref, at_ref, stat_ref, cos_ref, sin_ref,
                qm_ref, km_ref, pos_ref, *rest):
    dq_ref, dk_ref, dv_ref, gb_ref, gf_ref = rest if first else rest[5:]
    count = q_ref.shape[0]
    lane = lax.broadcasted_iota(jnp.int32, (1, 128), 1)
    zero = jnp.zeros((), BF16)
    q = q_ref[...]
    k = k_ref[...]
    v = v_ref[...]
    da = da_ref[...]
    prod = da.astype(F32) * at_ref[...].astype(F32)
    qm = qm_ref[...].astype(F32)
    k_aug = jnp.concatenate([k, km_ref[...]], axis=1)
    v_aug = jnp.concatenate([v, jnp.broadcast_to((lane < 2).astype(BF16), (count, 128))], axis=1)
    tile = 256
    dq = dk = dv = None
    for h in (0, 1):
        mine = (lane // 64) == h
        qh = jnp.where(mine, q, zero)
        kh = jnp.where(mine, k, zero)
        dah = jnp.where(mine, da, zero)
        delta = jnp.sum(jnp.where(mine, prod, 0.0), axis=-1, keepdims=True)
        d1, d2, _ = split3(delta)
        l1, l2, l3 = split3(stat_ref[:, 64 * h:64 * h + 1])
        extra = jnp.where(lane == 8, -l1, jnp.where(lane == 9, -l2, jnp.where(lane == 10, -l3, qm)))
        q_aug = jnp.concatenate([qh, extra.astype(BF16)], axis=1)
        da_aug = jnp.concatenate(
            [dah, jnp.where(lane == 0, -d1, jnp.where(lane == 1, -d2, 0.0)).astype(BF16)], axis=1)
        dks, dvs, dqh = [], [], None
        for i in range(count // tile):
            sl = slice(i * tile, (i + 1) * tile)
            p = jnp.exp(mm(k_aug[sl], q_aug, LAST))
            dp = mm(v_aug[sl], da_aug, LAST)
            ds = (p * dp).astype(BF16)
            dvs.append(mm(p.astype(BF16), dah, PLAIN))
            dks.append(mm(ds, qh, PLAIN))
            part = mm(ds, kh[sl], FIRST)
            dqh = part if dqh is None else dqh + part
        dkh = jnp.concatenate(dks, axis=0)
        dvh = jnp.concatenate(dvs, axis=0)
        dq = dqh if dq is None else dq + dqh
        dk = dkh if dk is None else dk + dkh
        dv = dvh if dv is None else dv + dvh
    dq = dq * 0.125
    c = cos_ref[...]
    s = sin_ref[...]
    turned = dq * swap_halves(q.astype(F32) * 8.0) + dk * swap_halves(k.astype(F32))
    turned = jnp.where(lane % 64 < 32, -turned, turned)
    row = lambda a: jnp.sum(a, axis=0, keepdims=True)
    gf_ref[...] = jnp.concatenate(
        [row(turned * pos_ref[:, 0:1]), row(turned * pos_ref[:, 1:2]), jnp.zeros((6, 128), F32)], axis=0)
    dqp = (dq * c - swap_halves(dq) * s).astype(BF16)
    dkp = (dk * c - swap_halves(dk) * s).astype(BF16)
    dvp = dv.astype(BF16)
    gb_ref[...] = jnp.concatenate(
        [row(dqp.astype(F32)), row(dkp.astype(F32)), row(dvp.astype(F32)), jnp.zeros((5, 128), F32)], axis=0)
    dq_ref[...] = dqp
    dk_ref[...] = dkp
    dv_ref[...] = dvp


def attend_back(start, stop, before, q, k, v, da, attn, stat, cos, sin, qm, km, pos):
    count, width = q.shape
    whole = lambda p: (0, 0)
    col = lambda p: (0, p + start)
    tall = pl.BlockSpec((count, 128), col)
    fixed = pl.BlockSpec((count, 128), whole)
    small = pl.BlockSpec((8, 128), col)
    in_specs = [tall] * 8 + [fixed] * 2 + [pl.BlockSpec((count, 2), whole)]
    operands = [q, k, v, da, attn, stat, cos, sin, qm, km, pos]
    aliases = {}
    if before is not None:
        aliases = {len(operands) + i: i for i in range(5)}
        in_specs += [pl.BlockSpec(memory_space=pl.ANY)] * 5
        operands += list(before)
    return pl.pallas_call(
        functools.partial(back_kernel, before is None),
        grid=(stop - start,),
        in_specs=in_specs,
        out_specs=[tall] * 3 + [small] * 2,
        out_shape=[jax.ShapeDtypeStruct((count, width), BF16)] * 3 + [jax.ShapeDtypeStruct((8, width), F32)] * 2,
        input_output_aliases=aliases,
        compiler_params=pltpu.CompilerParams(vmem_limit_bytes=56 * 2**20),
        cost_estimate=SHORT,
        name="attend_back",
    )(*operands)


def qkv_grad_kernel(block_rows, core_ref, dq_ref, dk_ref, dv_ref, n1_ref, keep_ref, give_ref, stage_s, sem):
    width = n1_ref.shape[1]
    cols = dq_ref.shape[1]
    step = pl.program_id(0)
    n1 = n1_ref[...]
    for j, ref in enumerate((dq_ref, dk_ref, dv_ref)):
        put_halves(stage_s.at[step, j], mm(ref[...], n1, FIRST))
        send_rows(core_ref[0], block_rows, stage_s.at[step, j], j * width + step * cols, 0, keep_ref, give_ref, sem)

    @pl.when(step == pl.num_programs(0) - 1)
    def _():
        pltpu.make_async_copy(stage_s, stage_s, sem).wait()


def qkv_grad(core, dq, dk, dv, n1, block_rows):
    count, width = n1.shape
    cols = width // 2
    tall = pl.BlockSpec((count, cols), lambda p: (0, p))
    hbm = pl.BlockSpec(memory_space=pl.ANY)
    return pl.pallas_call(
        functools.partial(qkv_grad_kernel, block_rows),
        grid=(2,),
        in_specs=[pl.BlockSpec(memory_space=pltpu.SMEM)] + [tall] * 3 + [pl.BlockSpec((count, width), lambda p: (0, 0))],
        out_specs=[hbm, hbm],
        out_shape=grad_shapes(block_rows, 3 * width, width),
        scratch_shapes=[pltpu.VMEM((2, 3, 2, cols, width // 2), BF16), pltpu.SemaphoreType.DMA],
        compiler_params=pltpu.CompilerParams(vmem_limit_bytes=56 * 2**20),
        cost_estimate=SHORT,
        name="qkv_grad",
    )(core, dq, dk, dv, n1)


def input_kernel(dq_ref, dk_ref, dv_ref, w_ref, x_ref, dm_ref, vec_ref, sums_ref, gb_ref, gf_ref, up_ref, ig_ref, out_ref):
    step = pl.program_id(0)
    d = jnp.concatenate([dq_ref[...], dk_ref[...], dv_ref[...]], axis=1)
    dn = mm(d, w_ref[...], PLAIN)
    unit, inverse = norm_parts(x_ref[...].astype(F32))
    ig_ref[...] = dm_ref[...] + norm_back(unit, inverse, dn, vec_ref[0:1, :])
    row = lambda a: jnp.sum(a, axis=0, keepdims=True)
    sums = jnp.concatenate([row(dn * unit), row(dn)], axis=0)

    @pl.when(step == 0)
    def _():
        width = dn.shape[1]
        half = width // 2
        out_ref[0:2] = sums
        out_ref[2:4] = sums_ref[0:2]
        out_ref[4:7] = gb_ref[0:3]
        out_ref[7:8] = sums_ref[2:3]
        for i in range(4):
            out_ref[8 + i:9 + i] = up_ref[:, i * width:(i + 1) * width]
        out_ref[12:13] = sums_ref[3:4]
        lane = lax.broadcasted_iota(jnp.int32, (width, half), 0)
        slot = lax.broadcasted_iota(jnp.int32, (width, half), 1)
        pick = jnp.where((lane // 64 == slot // 32) & (lane % 32 == slot % 32), 1.0, 0.0)
        both = lax.dot_general(gf_ref[...], pick, PLAIN, precision=lax.Precision.HIGHEST, preferred_element_type=F32)
        out_ref[13:14, :half] = both[0:1]
        out_ref[13:14, half:] = both[1:2]

    @pl.when(step > 0)
    def _():
        out_ref[0:2] += sums


def input_back(dq, dk, dv, weights, x, dm, vectors, sums, grad_bias, grad_freq, bias_up):
    count, width = x.shape
    tile = 256
    part = pl.BlockSpec((tile, width), lambda i: (i, 0))
    whole = lambda i: (0, 0)
    fixed = lambda a: pl.BlockSpec(a.shape, whole)
    return pl.pallas_call(
        input_kernel,
        grid=(count // tile,),
        in_specs=[part] * 3 + [pl.BlockSpec((3 * width, width), whole), part, part]
        + [fixed(a) for a in (vectors, sums, grad_bias, grad_freq, bias_up)],
        out_specs=[part, fixed(vectors)],
        out_shape=[jax.ShapeDtypeStruct((count, width), F32), jax.ShapeDtypeStruct(vectors.shape, F32)],
        compiler_params=pltpu.CompilerParams(vmem_limit_bytes=56 * 2**20),
        cost_estimate=SHORT,
        name="input_back",
    )(dq, dk, dv, weights, x, dm, vectors, sums, grad_bias, grad_freq, bias_up)


def fold_kernel(pos_ref, keep_ref, got_ref, send_ref, hold_ref):
    rows = keep_ref.shape[1] // 2
    deep = 4
    piece = rows // deep
    more, less = MORE, piece - MORE
    for m in range(keep_ref.shape[0] // 2):
        both = []
        for y in (0, 1):
            here = slice(y * rows, y * rows + rows)
            even, odd = (
                keep_ref[2 * m + e, here, :].astype(F32) + got_ref[2 * m + e, here, :].astype(F32) for e in (0, 1)
            )
            parts = []
            for z in range(deep):
                at = z * piece
                parts.append((
                    jnp.concatenate([even[at:at + more], odd[at:at + less]], axis=0),
                    jnp.concatenate([even[at + more:at + piece], odd[at + less:at + piece]], axis=0),
                ))
            both.append([jnp.concatenate([p[x] for p in parts], axis=0).astype(BF16) for x in (0, 1)])
        for y in (0, 1):
            for x in (0, 1):
                for way in range(4):
                    @pl.when((pos_ref[way, 0] == y) & (pos_ref[way, 1] == x))
                    def _(way=way, y=y, x=x):
                        (send_ref, hold_ref)[way // 2][way % 2, m] = both[y][x]


def fold(pos, keep, got):
    count, rows, cols = keep.shape
    some = 4 if count % 4 == 0 else 2
    whole = pl.BlockSpec((some, rows, cols), lambda i, pos: (i, 0, 0))
    out = pl.BlockSpec((2, some // 2, rows // 2, cols), lambda i, pos: (0, i, 0, 0))
    shape = jax.ShapeDtypeStruct((2, count // 2, rows // 2, cols), BF16)
    return pl.pallas_call(
        fold_kernel,
        grid_spec=pltpu.PrefetchScalarGridSpec(
            num_scalar_prefetch=1, grid=(count // some,), in_specs=[whole, whole], out_specs=[out, out]),
        compiler_params=pltpu.CompilerParams(vmem_limit_bytes=40 * 2**20),
        out_shape=[shape, shape],
        cost_estimate=SHORT,
        name="fold",
    )(pos, keep, got)


def pack_kernel(owner_ref, *refs):
    early, late, out_ref, total_s = refs[:4], refs[4:8], refs[8], refs[9]
    square = None
    start = 0
    rows = early[0].shape[1]
    for parts in (early, late):
        total = parts[0][...].astype(F32)
        for part in parts[1:]:
            total = total + part[...].astype(F32)
        total_s[start:start + total.shape[0], :rows] = total
        start += total.shape[0]
        more = jnp.sum(total * total).reshape(1, 1)
        square = more if square is None else square + more
    total_s[:, rows:] = jnp.zeros((start, total_s.shape[1] - rows, total_s.shape[2]), F32)
    lane = lax.broadcasted_iota(jnp.int32, (8, out_ref.shape[2]), 1)
    one, two, three = split3(square)
    extra = jnp.where(lane == 0, one, jnp.where(lane == 1, two, jnp.where(lane == 2, three, 0.0)))
    devices = out_ref.shape[0]
    skip = jnp.where(owner_ref[devices] == 0, MORE, rows - MORE)
    for p in range(devices):
        block = owner_ref[p]
        at = lax.rem(block, 2) * skip
        mine = total_s[lax.div(block, 2), pl.ds(pl.multiple_of(at, 8), MORE), :]
        out_ref[p] = jnp.concatenate([mine, extra], axis=0).astype(BF16)


def pack(owner, x, early, late):
    blocks = early[0].shape[0] + late[0].shape[0]
    rows, cols = early[0].shape[1:]
    vmem = pl.BlockSpec(memory_space=pltpu.VMEM)
    return pl.pallas_call(
        pack_kernel,
        in_specs=[pl.BlockSpec(memory_space=pltpu.SMEM)] + [vmem] * 8,
        out_specs=vmem,
        out_shape=jax.ShapeDtypeStruct((owner.shape[0], MORE + 8, cols), BF16),
        scratch_shapes=[pltpu.VMEM((blocks, rows + 8, cols), F32)],
        compiler_params=pltpu.CompilerParams(vmem_limit_bytes=32 * 2**20),
        cost_estimate=SHORT,
        name="pack",
    )(jnp.concatenate([owner, x.reshape(1).astype(owner.dtype)]), *early, *late)


def clip_of(square, vec):
    norm = jnp.sqrt(square + jnp.sum(vec * vec).reshape(1, 1))
    return norm, jnp.minimum(1.0, 1.0 / (norm + 1e-06))


def adam_kernel(own_ref, a_ref, b_ref, as_ref, bs_ref, vt_ref, vw_ref, vm_ref, vv_ref, w_ref, m_ref, v_ref,
                g_out, v_out, w_out, vg_out, vv_out, vw_out, norm_out):
    def squares(ref):
        block = ref[...].astype(F32)
        lane = lax.broadcasted_iota(jnp.int32, block.shape, 4)
        row = lax.broadcasted_iota(jnp.int32, block.shape, 3)
        return jnp.sum(jnp.where((lane < 3) & (row == 0), block, 0.0)).reshape(1, 1)

    norm, clip = clip_of(squares(as_ref) + squares(bs_ref), vt_ref[...])
    mine = pl.program_id(1) == own_ref[0]
    even = own_ref[1] == 0
    deep = a_ref.shape[0]
    piece = w_ref.shape[0] // deep
    runs = []
    for z in range(deep):
        left, right = (jnp.where(mine, a_ref[z, 0, x].astype(F32), b_ref[z, 0, x].astype(F32)) for x in (0, 1))
        runs.append(jnp.where(
            even,
            jnp.concatenate([left[:MORE], right[:piece - MORE]], axis=0),
            jnp.concatenate([left[:piece - MORE], right[:MORE]], axis=0),
        ))
    grad = jnp.concatenate(runs, axis=0) * clip
    second, weight = adam(w_ref[...], m_ref[...], v_ref[...], grad, 0.02, 0.05)
    g_out[...] = grad
    v_out[...] = second
    w_out[...] = weight

    @pl.when((pl.program_id(0) == 0) & (pl.program_id(1) == 0))
    def _():
        vec_grad = vt_ref[...] * clip
        second, weight = adam(vw_ref[...], vm_ref[...], vv_ref[...], vec_grad, 0.2, 0.0)
        vg_out[...] = vec_grad
        vv_out[...] = second
        vw_out[...] = weight
        norm_out[...] = norm


def adam_rows(own, mine, other, vec_total, vectors, vec_first, vec_second, weight, first, second):
    rows, width = weight.shape
    deep, tall, wide, piece, cols = mine.shape
    part = pl.BlockSpec((deep, 1, wide, piece, cols), lambda y, h: (0, y, 0, 0, 0))
    marks = pl.BlockSpec((deep, tall, wide, 8, 128), lambda y, x: (0, 0, 0, piece // 8 - 1, 0))
    flat = pl.BlockSpec((rows // tall, cols), lambda y, h: (y, h))
    vec = pl.BlockSpec(vectors.shape, lambda y, x: (0, 0))
    shape = jax.ShapeDtypeStruct((rows, width), F32)
    small = jax.ShapeDtypeStruct(vectors.shape, F32)
    return pl.pallas_call(
        adam_kernel,
        grid=(tall, width // cols),
        in_specs=[pl.BlockSpec(memory_space=pltpu.SMEM), part, part, marks, marks] + [vec] * 4 + [flat] * 3,
        out_specs=[flat] * 3 + [vec] * 3 + [pl.BlockSpec((1, 1), lambda y, x: (0, 0))],
        out_shape=[shape] * 3 + [small] * 3 + [jax.ShapeDtypeStruct((1, 1), F32)],
        compiler_params=pltpu.CompilerParams(vmem_limit_bytes=60 * 2**20),
        cost_estimate=SHORT,
        name="adam",
    )(own, mine, other, mine, other, vec_total, vectors, vec_first, vec_second, weight, first, second)


from jax.sharding import PartitionSpec as P

HEADS = 12
STEP = 7


def place_tokens(heights, widths, count):
    sizes = heights * widths
    ends = jnp.cumsum(sizes)
    starts = ends - sizes
    places = jnp.arange(count, dtype=jnp.int32)
    segment = jnp.sum((places[:, None] >= ends[None, :]).astype(jnp.int32), axis=1)
    slots = jnp.arange(heights.shape[0], dtype=jnp.int32)
    picks = (segment[:, None] == slots[None, :]).astype(jnp.int32)
    begin = jnp.sum(picks * starts[None, :], axis=1)
    across = jnp.maximum(jnp.sum(picks * widths[None, :], axis=1), 1)
    offset = places - begin
    live = places < ends[-1]
    return (segment, offset // across, offset % across, live)


def adam(weight, first, second, grad, rate, decay):
    first_new = 0.5 * first + 0.5 * grad
    second_new = 0.5 * second + 0.5 * grad * grad
    correct = 1.0 - 0.5**STEP
    direction = first_new / correct / (jnp.sqrt(second_new / correct) + 1e-08)
    return (second_new, weight - rate * (direction + decay * weight))


def pairwise(bits, total):
    return [(i, i ^ bits) for i in range(total)]


def sum_part(value, devices, step, stop):
    while step < stop:
        value = value + lax.ppermute(value, "dp", pairwise(step, devices))
        step *= 2
    return value


CORES = ("group", "dp")
SWAP = [(0, 1), (1, 0)]


def cross(value, bit0, bit1, devices):
    perm = [(i, i ^ (bit0 if i < devices else bit1)) for i in range(2 * devices)]
    return lax.ppermute(value, CORES, perm)


def along_z(values, devices):
    return [
        lax.ppermute(v, "dp", [(i, (i + 4 * (s + 1)) % devices) for i in range(devices)])
        for s, v in enumerate(values)
    ]


def along_line(value, devices, step, up):
    last = devices // 4
    perm = []
    for z in range(last):
        near = z - 1 if up else z + 1
        far = z - step if up else z + step
        if 0 <= far < last:
            perm += [(4 * near + i, 4 * z + i) for i in range(4)]
    return lax.ppermute(value, "dp", perm)


def gather_pieces(master, inverse, core, me, devices, freqs, make_angles, late, make_late, tables):
    tie = lax.optimization_barrier
    block_rows, width = master.shape
    half = block_rows // 2
    mine = lax.dynamic_slice_in_dim(master, core * half, half, 0).astype(BF16)
    large = mine[:LARGE]
    small = mine[LARGE:]
    z = me // 4
    deep = lax.rem(z - inverse // 4 + 4, 4)
    apart = me ^ inverse
    one = jnp.where(core == 0, apart & 1, (apart >> 1) & 1)
    two = jnp.where(core == 0, (apart >> 1) & 1, apart & 1)
    slots = jnp.stack([
        8 * two + 4 * one + deep,
        4 * deep + 2 * two + one,
        8 * one + 4 * two + deep,
        4 * deep + 2 * one + two,
    ]).astype(jnp.int32)
    up = along_z([large] * 3, devices)
    small = jnp.stack([small, cross(small, 1, 2, devices)])
    small, freqs = tie((small, freqs))
    small = jnp.concatenate([small, cross(small, 2, 1, devices)])
    large = jnp.stack([large] + up)
    large, small, tables, slots, angles = tie((large, small, tables, slots, make_angles(freqs)))
    first = cross(large, 1, 2, devices)
    ups = [along_line(small, devices, 1, True)]
    downs = [along_line(small, devices, 1, False)]
    first, ups[0], downs[0], late = tie((first, ups[0], downs[0], late))
    done = make_late(*late)
    first = jnp.concatenate([large, first])
    second = cross(first, 2, 1, devices)
    for step in (2, 3):
        ups.append(along_line(ups[-1], devices, step, True))
        downs.append(along_line(downs[-1], devices, step, False))
        if step == 2:
            ups[1], downs[1], done = tie((ups[1], downs[1], done))
    small = jnp.concatenate([small] + [jnp.where(z >= s, ups[s - 1], downs[3 - s]) for s in (1, 2, 3)])
    other = [lax.ppermute(a, "group", SWAP) for a in (first, second, small)]
    return (first, second, small, *other), slots, angles + done + tables


def quarters(core, me):
    x, y = me & 1, (me >> 1) & 1
    one = jnp.where(core == 0, x, y)
    two = jnp.where(core == 0, y, x)
    pairs = [(1 - one, 1 - two), (1 - one, two), (one, 1 - two), (one, two)]
    return jnp.stack([
        jnp.stack([jnp.where(core == 0, b, a), jnp.where(core == 0, a, b)]) for a, b in pairs
    ]).astype(jnp.int32)


def add_low(*terms):
    total = terms[0].astype(F32)
    for term in terms[1:]:
        total = total + term.astype(F32)
    return total.astype(BF16)


def sum_z(low, me, devices):
    count, rows, cols = low.shape
    z = me // 4
    low = low.reshape(count, 4, rows // 4, cols)
    pick = lambda at: lax.dynamic_index_in_dim(low, at, 1, keepdims=False)
    return (pick(z), *along_z([pick(lax.rem(z + s, 4)) for s in (1, 2, 3)], devices))


def reduce_plain(local_mat, owner_block, devices):
    rows, width = local_mat.shape
    block_rows = rows // devices
    term = local_mat.reshape(devices, block_rows, width)[owner_block].reshape(rows, width)
    share = lax.psum_scatter(term.astype(F32), "dp", scatter_dimension=0, tiled=True)
    return lax.psum(share.astype(BF16), "group").astype(F32)


def local(
    tokens,
    cotangent,
    grid_h,
    grid_w,
    owner_block,
    master,
    first_mom,
    second_mom,
    vectors,
    vec_first,
    vec_second,
):
    devices = lax.axis_size("dp")
    core = lax.axis_index("group")
    me = lax.axis_index("dp")
    count = tokens.shape[1]
    width = tokens.shape[2]
    heads = HEADS
    head_dim = width // heads
    half = head_dim // 2
    block_rows = master.shape[0]
    stack = devices * block_rows
    quick = devices == 16 and block_rows == 2 * (LARGE + SMALL) and width % 256 == 0
    inverse = jnp.argsort(owner_block)
    segment, rows_pos, cols_pos, live = place_tokens(grid_h[0], grid_w[0], count)
    x = tokens[0]

    def spread(part):
        return jnp.broadcast_to(part.reshape(heads, 1, half), (heads, 2, half)).reshape(1, width)

    freqs = (spread(vectors[13, : width // 2]), spread(vectors[13, width // 2 :]))

    def make_angles(freqs):
        down = rows_pos.astype(F32)[:, None]
        right = cols_pos.astype(F32)[:, None]
        angle = down * freqs[0] + right * freqs[1]
        lower = (jnp.arange(width) % head_dim < half)[None]
        cosine = jnp.cos(angle)
        sine = jnp.sin(angle)
        return (cosine, jnp.where(lower, -sine, sine))

    late = (x, cotangent[0])

    def make_late(x, cot):
        unit, _ = norm_parts(x.astype(F32))
        grad_two = jnp.where(live[:, None], cot, jnp.zeros((), BF16))
        return ((unit * vectors[0] + vectors[1]).astype(BF16), grad_two)

    def make_tables():
        ids = jnp.arange(128)[None]
        match = segment[:, None] == ids
        key_mask = jnp.where(match | ((ids >= 8) & (ids < 11)), 1.0, 0.0).astype(BF16)
        query_mask = jnp.where((ids < 8) & ~match, MASKED, 0.0).astype(BF16)
        places = jnp.stack([rows_pos, cols_pos], axis=1).astype(F32)
        return (key_mask, query_mask, places,
                vectors[4:7].reshape(1, 3 * width), vectors[8:12].reshape(1, 4 * width))

    if quick:
        weights, slots, tables = gather_pieces(master, inverse, core, me, devices, freqs, make_angles, late, make_late, make_tables())
    else:
        low = lax.all_gather(master.astype(BF16), "dp", axis=0, tiled=True)
        weights = low.reshape(devices, block_rows, width)[inverse].reshape(stack, width)
        slots = jnp.zeros((4, devices), jnp.int32)
        tables = make_angles(freqs) + make_late(*late) + make_tables()
    cosine, sine, first_in, grad_two, key_mask, query_mask, places, bias_qkv, bias_one = tables
    here = core.reshape(1).astype(jnp.int32)
    query, key, value, attn, stat, *placed = attend(
        here, slots, first_in, bias_qkv,
        cosine, sine, query_mask, key_mask, weights, stack,
    )
    if quick:
        weights = placed[0]
    whole_rows = block_rows if quick else 0
    block_out, grad_middle, grad_attn, sums, bias_up, keep_mlp, give_mlp = mlp(
        here, x, attn, grad_two, vectors, weights, bias_one, whole_rows
    )
    pairs = width // 128
    blocked = lambda a: a.reshape(-1, block_rows, width // 2)
    tie = lax.optimization_barrier
    if quick:
        pos = quarters(core, me)
        got = lax.ppermute(give_mlp, "group", SWAP)
    back = None
    cuts = (0, 1, pairs - 1, pairs)
    for start, stop in zip(cuts[:-1], cuts[1:]):
        back = attend_back(
            start, stop, back, query, key, value, grad_attn, attn, stat, cosine, sine, query_mask, key_mask, places
        )
        if quick and start == 0:
            (send, hold), back = tie((fold(pos, blocked(keep_mlp), blocked(got)), back))
            came = cross(send, 1, 2, devices)
        if quick and start == 1:
            send, back = tie((add_low(hold[0], came[0]), back))
            again = cross(send, 2, 1, devices)
    grad_q, grad_k, grad_v, grad_bias, grad_freq = back
    keep_qkv, give_qkv = qkv_grad(here, grad_q, grad_k, grad_v, first_in, whole_rows)
    if quick:
        again, give_qkv = tie((again, give_qkv))
        low, grad_v, give_qkv = tie((add_low(hold[1], came[1], again), grad_v, give_qkv))
        late = sum_z(low, me, devices)
    if quick:
        got_qkv = lax.ppermute(give_qkv, "group", SWAP)
        send, hold = fold(pos, blocked(keep_qkv), blocked(got_qkv))
        third = send.shape[2] // 3
        send = [send[:, :, third * i:third * (i + 1)] for i in range(3)]
        send, grad_v = tie((send, grad_v))
    input_grad, local_vec = input_back(
        grad_q, grad_k, grad_v, weights, x, grad_middle, vectors, sums, grad_bias, grad_freq, bias_up
    )
    if quick:
        send[2], local_vec = tie((send[2], local_vec))
        came = [cross(a, 1, 2, devices) for a in send]
        came, local_vec, late = tie((came, local_vec, late))
        came = jnp.concatenate(came, axis=2)
        again = cross(add_low(hold[0], came[0]), 2, 1, devices)
        vec_total = sum_part(local_vec, devices, 4, devices)
        again, vec_total = tie((again, vec_total))
        early = sum_z(add_low(hold[1], came[1], again), me, devices)
        early, vec_total = tie((early, sum_part(vec_total, devices, 1, 4)))
        load = pack(owner_block, me & 1, early, late)
        mine = lax.all_to_all(load, "dp", 0, 0, tiled=True)
        other = lax.ppermute(mine, "group", SWAP)
        vec_total = vec_total + lax.ppermute(lax.optimization_barrier((vec_total, mine))[0], "group", SWAP)
        shape = (devices // 4, 2, 2, *load.shape[1:])
        own = jnp.stack([core, owner_block[me] % 2]).astype(jnp.int32)
        mat_grad, mat_second, mat_weight, vec_grad, vec_second_new, vec_weight, norm = adam_rows(
            own, mine.reshape(shape), other.reshape(shape), vec_total, vectors, vec_first, vec_second,
            master, first_mom, second_mom,
        )
        grad_norm = norm.reshape(())
    else:
        vec_total = lax.psum(local_vec, CORES)
        share = reduce_plain(jnp.concatenate([keep_qkv, keep_mlp]), owner_block, devices)
        square = lax.psum(jnp.sum(share * share), "dp")
        grad_norm = jnp.sqrt(square + jnp.sum(vec_total * vec_total))
        clip = jnp.minimum(1.0, 1.0 / (grad_norm + 1e-06))
        mat_grad = share * clip
        mat_second, mat_weight = adam(master, first_mom, second_mom, mat_grad, 0.02, 0.05)
        vec_grad = vec_total * clip
        vec_second_new, vec_weight = adam(vectors, vec_first, vec_second, vec_grad, 0.2, 0.0)
    return (
        block_out[None],
        input_grad[None],
        mat_grad,
        mat_second,
        mat_weight,
        vec_grad,
        vec_second_new,
        vec_weight,
        grad_norm,
    )


def solution(mesh):
    return jax.shard_map(
        local,
        mesh=mesh,
        in_specs=(
            P("group", "dp", None),
            P("group", "dp", None),
            P("group", "dp"),
            P("group", "dp"),
            P(),
            P("dp", None),
            P("dp", None),
            P("dp", None),
            P(),
            P(),
            P(),
        ),
        out_specs=(
            P("group", "dp", None),
            P("group", "dp", None),
            P("dp", None),
            P("dp", None),
            P("dp", None),
            P(),
            P(),
            P(),
            P(),
        ),
        check_vma=False,
    )
```

```python
import functools
import jax
import jax.numpy as jnp
from jax import lax
from jax.experimental import pallas as pl
from jax.experimental.pallas import tpu as pltpu

F32 = jnp.float32
BF16 = jnp.bfloat16
LAST = (((1,), (1,)), ((), ()))
FIRST = (((0,), (0,)), ((), ()))
PLAIN = (((1,), (0,)), ((), ()))
MASKED = -1e9
MORE = 40
SHORT = pl.CostEstimate(flops=1000, bytes_accessed=1000, transcendentals=0)


def mm(left, right, dims):
    return lax.dot_general(left, right, dims, preferred_element_type=F32)


def norm_parts(value):
    centre = value - jnp.mean(value, axis=-1, keepdims=True)
    spread = jnp.mean(centre * centre, axis=-1, keepdims=True)
    inverse = lax.rsqrt(spread + 1e-6)
    return centre * inverse, inverse


def norm_back(unit, inverse, grad, gain):
    scaled = grad * gain
    first = jnp.mean(scaled, axis=-1, keepdims=True)
    second = jnp.mean(scaled * unit, axis=-1, keepdims=True)
    return inverse * (scaled - first - unit * second)


def swap_halves(value):
    lane = lax.broadcasted_iota(jnp.int32, value.shape, 1)
    return jnp.where(
        lane % 64 < 32, pltpu.roll(value, 96, 1), pltpu.roll(value, 32, 1)
    )


def split3(value):
    one = value.astype(BF16).astype(F32)
    rest = value - one
    two = rest.astype(BF16).astype(F32)
    return one, two, rest - two


LARGE = 208
SMALL = 80


def place_pieces(core, slot_ref, mine, other, block, side, dst, sem):
    for which, (first, second, small) in enumerate((mine, other)):
        @pl.when((core == side) if which == 0 else (core != side))
        def _():
            large_slot = slot_ref[2 * which, block]
            small_slot = slot_ref[2 * which + 1, block]

            @pl.when(large_slot < 8)
            def _():
                pltpu.make_async_copy(first.at[large_slot], dst(0, LARGE), sem).start()

            @pl.when(large_slot >= 8)
            def _():
                pltpu.make_async_copy(second.at[large_slot - 8], dst(0, LARGE), sem).start()

            pltpu.make_async_copy(small.at[small_slot], dst(LARGE, SMALL), sem).start()


def attend_kernel(blocks, core_ref, slot_ref, n1_ref, bq_ref, bk_ref, bv_ref,
                  cos_ref, sin_ref, qm_ref, km_ref, *rest):
    if blocks:
        mine, other = rest[0:3], rest[3:6]
        q_ref, k_ref, v_ref, attn_ref, stat_ref, w_ref, w_s, near, far, back = rest[6:]
    else:
        w_ref, q_ref, k_ref, v_ref, attn_ref, stat_ref, w_s, near = rest
    count, width = n1_ref.shape
    step = pl.program_id(0)

    @pl.when(step == 0)
    def _():
        if blocks:
            core = core_ref[0]
            rows = w_ref.shape[0] // blocks

            def start(block, sem):
                for side in (0, 1):
                    def dst(offset, size):
                        base = block * rows + side * (rows // 2) + offset
                        return w_s.at[pl.ds(pl.multiple_of(base, 16), size)]
                    place_pieces(core, slot_ref, mine, other, block, side, dst, sem)

            def near_block(block, carry):
                start(block, near)
                return carry

            def far_block(block, carry):
                start(block, far)
                return carry

            lax.fori_loop(0, 3 * width // rows, near_block, 0)
            lax.fori_loop(3 * width // rows, blocks, far_block, 0)
        else:
            pltpu.make_async_copy(w_ref.at[pl.ds(0, 3 * width)], w_s, near).start()
        head = w_s.at[pl.ds(0, 3 * width)]
        pltpu.make_async_copy(head, head, near).wait()

    if blocks:
        @pl.when(step == 1)
        def _():
            tail = w_s.at[pl.ds(3 * width, w_s.shape[0] - 3 * width)]
            pltpu.make_async_copy(tail, tail, far).wait()
            pltpu.make_async_copy(w_s, w_ref, back).start()

    def third(j):
        return w_s[pl.ds(pl.multiple_of(j * width + step * 128, 128), 128), :]

    w = jnp.concatenate([third(0), third(1), third(2)], axis=0)
    qkv = mm(n1_ref[...], w, LAST)
    q = qkv[:, :128] + bq_ref[...]
    k = qkv[:, 128:256] + bk_ref[...]
    v = (qkv[:, 256:] + bv_ref[...]).astype(BF16)
    c = cos_ref[...]
    s = sin_ref[...]
    qr = ((q * c + swap_halves(q) * s).astype(BF16).astype(F32) * 0.125).astype(BF16)
    kr = (k * c + swap_halves(k) * s).astype(BF16)
    q_ref[...] = qr
    k_ref[...] = kr
    v_ref[...] = v
    lane = lax.broadcasted_iota(jnp.int32, (1, 128), 1)
    k_aug = jnp.concatenate([kr, km_ref[...]], axis=1)
    v_aug = jnp.concatenate([v, jnp.ones((count, 128), BF16)], axis=1)
    zero = jnp.zeros((), BF16)
    tile = 256
    for i in range(count // tile):
        rows = pl.ds(i * tile, tile)
        out = None
        stats = []
        for h in (0, 1):
            mine_lanes = (lane // 64) == h
            qa = jnp.concatenate(
                [jnp.where(mine_lanes, qr[i * tile:(i + 1) * tile], zero), qm_ref[rows, :]], axis=1)
            scores = mm(qa, k_aug, LAST)
            top = jnp.max(scores, axis=-1, keepdims=True)
            e = jnp.exp(scores - top).astype(BF16)
            o = mm(e, v_aug, PLAIN)
            total = o[:, 128:]
            o = o[:, :128] / total
            out = o if out is None else jnp.where(lane < 64, out, o)
            stats.append(top + jnp.log(total[:, :1]))
        attn_ref[rows, :] = out.astype(BF16)
        stat_ref[rows, :] = jnp.where(lane < 64, stats[0], stats[1])

    if blocks:
        @pl.when(step == pl.num_programs(0) - 1)
        def _():
            pltpu.make_async_copy(w_s, w_ref, back).wait()


def attend(core, slots, n1, bqkv, cos, sin, qm, km, weights, stack):
    count, width = n1.shape
    pairs = width // 128
    pieces = isinstance(weights, tuple)
    blocks = slots.shape[1] if pieces else 0
    whole = lambda p: (0, 0)
    col = lambda p: (0, p)
    smem = pl.BlockSpec(memory_space=pltpu.SMEM)
    hbm = pl.BlockSpec(memory_space=pl.ANY)
    given = weights if pieces else (weights,)
    specs = [smem, smem] + [
        pl.BlockSpec((count, width), whole),
        pl.BlockSpec((1, 128), col),
        pl.BlockSpec((1, 128), lambda p: (0, p + pairs)),
        pl.BlockSpec((1, 128), lambda p: (0, p + 2 * pairs)),
        pl.BlockSpec((count, 128), col),
        pl.BlockSpec((count, 128), col),
        pl.BlockSpec((count, 128), whole),
        pl.BlockSpec((count, 128), whole),
    ] + [hbm] * len(given)
    outs = [pl.BlockSpec((count, 128), col)] * 5
    shape = lambda d: jax.ShapeDtypeStruct((count, width), d)
    shapes = [shape(BF16)] * 4 + [shape(F32)]
    scratch = [pltpu.VMEM((stack if pieces else 3 * width, width), BF16), pltpu.SemaphoreType.DMA]
    if pieces:
        outs.append(hbm)
        shapes.append(jax.ShapeDtypeStruct((stack, width), BF16))
        scratch += [pltpu.SemaphoreType.DMA] * 2
    return pl.pallas_call(
        functools.partial(attend_kernel, blocks),
        grid=(pairs,),
        in_specs=specs,
        out_specs=outs,
        out_shape=shapes,
        scratch_shapes=scratch,
        compiler_params=pltpu.CompilerParams(vmem_limit_bytes=56 * 2**20),
        cost_estimate=SHORT,
        name="attend",
    )(core, slots, n1, bqkv, bqkv, bqkv, cos, sin, qm, km, *given)


def gelu_both(x):
    cdf = 0.5 + 0.5 * lax.erf(x * 0.7071067811865476)
    return x * cdf, cdf + x * jnp.exp(x * x * -0.5) * 0.3989422804014327


def put_halves(stage, value):
    half = value.shape[1] // 2
    low = value.astype(BF16)
    stage[0] = low[:, :half]
    stage[1] = low[:, half:]


def send_rows(core, block_rows, stage, row, base, keep_ref, give_ref, sem):
    rows, half = stage.shape[1:]
    here = pl.ds(pl.multiple_of(row - base, 64), rows)
    if block_rows:
        pltpu.make_async_copy(stage.at[core], keep_ref.at[here], sem).start()
        pltpu.make_async_copy(stage.at[1 - core], give_ref.at[here], sem).start()
    else:
        for c in (0, 1):
            pltpu.make_async_copy(stage.at[c], keep_ref.at[here, pl.ds(c * half, half)], sem).start()


def mlp_kernel(block_rows, base, core_ref, x_ref, at_ref, dz_ref, vec_ref, wo_ref, w1_ref, w2_ref, b1_ref,
               out_ref, dm_ref, da_ref, sums_ref, gb_ref, keep_ref, give_ref,
               middle_s, n2_s, acc_s, stage_s, proj_s, sems):
    step = pl.program_id(0)
    last = pl.num_programs(0) - 1
    count, width = x_ref.shape
    core = core_ref[0]
    tile = w1_ref.shape[0]

    @pl.when(step == 0)
    def _():
        middle = x_ref[...].astype(F32) + mm(at_ref[...], wo_ref[...], LAST) + vec_ref[7:8, :]
        middle_s[...] = middle
        unit, _ = norm_parts(middle)
        n2_s[...] = (unit * vec_ref[2:3, :] + vec_ref[3:4, :]).astype(BF16)
        acc_s[...] = jnp.zeros_like(acc_s)
        dm_ref[...] = jnp.zeros_like(dm_ref)

    slot = lax.rem(step, 2)

    @pl.when(step >= 2)
    def _():
        pltpu.make_async_copy(stage_s.at[slot], stage_s.at[slot], sems.at[slot]).wait()

    n2 = n2_s[...]
    dz = dz_ref[...]
    w1 = w1_ref[...]
    w2 = w2_ref[...]
    pre = mm(w1, n2, LAST) + b1_ref[...].reshape(tile, 1)
    back = mm(w2, dz, LAST)
    act, slope = gelu_both(pre)
    hidden = act.astype(BF16)
    put_halves(stage_s.at[slot, 1], mm(hidden, dz, PLAIN))
    dpre = (back * slope).astype(BF16)
    gb_ref[...] = jnp.sum(dpre.astype(F32), axis=1, keepdims=True).reshape(1, tile)
    put_halves(stage_s.at[slot, 0], mm(dpre, n2, PLAIN))
    acc_s[...] += mm(hidden, w2, FIRST)
    dm_ref[...] += mm(dpre, w1, FIRST)
    for j in (0, 1):
        send_rows(core, block_rows, stage_s.at[slot, j], (4 + 4 * j) * width + step * tile,
                  base, keep_ref, give_ref, sems.at[slot])

    @pl.when(step == last)
    def _():
        middle = middle_s[...]
        out_ref[...] = (middle + acc_s[...] + vec_ref[12:13, :]).astype(BF16)
        unit, inverse = norm_parts(middle)
        dn = dm_ref[...]
        dy = dz_ref[...].astype(F32)
        dm = dy + norm_back(unit, inverse, dn, vec_ref[2:3, :])
        dm_ref[...] = dm
        low = dm.astype(BF16)
        row = lambda a: jnp.sum(a, axis=0, keepdims=True)
        sums_ref[...] = jnp.concatenate(
            [row(dn * unit), row(dn), row(low.astype(F32)), row(dy), jnp.zeros((4, width), F32)], axis=0)
        put_halves(proj_s, mm(low, at_ref[...], FIRST))
        send_rows(core, block_rows, proj_s, 3 * width, base, keep_ref, give_ref, sems.at[2])
        da_ref[...] = mm(low, wo_ref[...], PLAIN).astype(BF16)
        pltpu.make_async_copy(stage_s.at[slot], stage_s.at[slot], sems.at[slot]).wait()
        pltpu.make_async_copy(stage_s.at[1 - slot], stage_s.at[1 - slot], sems.at[1 - slot]).wait()
        pltpu.make_async_copy(proj_s, proj_s, sems.at[2]).wait()


def grad_shapes(block_rows, rows, width):
    if block_rows:
        half = jax.ShapeDtypeStruct((rows, width // 2), BF16)
        return [half, half]
    return [jax.ShapeDtypeStruct((rows, width), BF16), jax.ShapeDtypeStruct((16, width), BF16)]


def mlp(core, x, attn, dz, vectors, weights, b1, block_rows, tile=256):
    count, width = x.shape
    units = 4 * width
    stack = weights.shape[0]
    base = 3 * width
    whole = lambda t: (0, 0)
    big = pl.BlockSpec((count, width), whole)
    hbm = pl.BlockSpec(memory_space=pl.ANY)
    return pl.pallas_call(
        functools.partial(mlp_kernel, block_rows, base),
        grid=(units // tile,),
        in_specs=[pl.BlockSpec(memory_space=pltpu.SMEM), big, big, big, pl.BlockSpec(vectors.shape, whole),
                  pl.BlockSpec((width, width), lambda t: (3, 0)),
                  pl.BlockSpec((tile, width), lambda t: (4 * width // tile + t, 0)),
                  pl.BlockSpec((tile, width), lambda t: (8 * width // tile + t, 0)),
                  pl.BlockSpec((1, tile), lambda t: (0, t))],
        out_specs=[big, big, big, pl.BlockSpec((8, width), whole), pl.BlockSpec((1, tile), lambda t: (0, t)), hbm, hbm],
        out_shape=[
            jax.ShapeDtypeStruct((count, width), BF16),
            jax.ShapeDtypeStruct((count, width), F32),
            jax.ShapeDtypeStruct((count, width), BF16),
            jax.ShapeDtypeStruct((8, width), F32),
            jax.ShapeDtypeStruct((1, units), F32),
        ] + grad_shapes(block_rows, stack - 3 * width, width),
        scratch_shapes=[
            pltpu.VMEM((count, width), F32),
            pltpu.VMEM((count, width), BF16),
            pltpu.VMEM((count, width), F32),
            pltpu.VMEM((2, 2, 2, tile, width // 2), BF16),
            pltpu.VMEM((2, width, width // 2), BF16),
            pltpu.SemaphoreType.DMA((3,)),
        ],
        compiler_params=pltpu.CompilerParams(vmem_limit_bytes=60 * 2**20),
        cost_estimate=SHORT,
        name="mlp",
    )(core, x, attn, dz, vectors, weights, weights, weights, b1)


def back_kernel(first, q_ref, k_ref, v_ref, da_ref, at_ref, stat_ref, cos_ref, sin_ref,
                qm_ref, km_ref, pos_ref, *rest):
    dq_ref, dk_ref, dv_ref, gb_ref, gf_ref = rest if first else rest[5:]
    count = q_ref.shape[0]
    lane = lax.broadcasted_iota(jnp.int32, (1, 128), 1)
    zero = jnp.zeros((), BF16)
    q = q_ref[...]
    k = k_ref[...]
    v = v_ref[...]
    da = da_ref[...]
    prod = da.astype(F32) * at_ref[...].astype(F32)
    qm = qm_ref[...].astype(F32)
    k_aug = jnp.concatenate([k, km_ref[...]], axis=1)
    v_aug = jnp.concatenate([v, jnp.broadcast_to((lane < 2).astype(BF16), (count, 128))], axis=1)
    tile = 256
    dq = dk = dv = None
    for h in (0, 1):
        mine = (lane // 64) == h
        qh = jnp.where(mine, q, zero)
        kh = jnp.where(mine, k, zero)
        dah = jnp.where(mine, da, zero)
        delta = jnp.sum(jnp.where(mine, prod, 0.0), axis=-1, keepdims=True)
        d1, d2, _ = split3(delta)
        l1, l2, l3 = split3(stat_ref[:, 64 * h:64 * h + 1])
        extra = jnp.where(lane == 8, -l1, jnp.where(lane == 9, -l2, jnp.where(lane == 10, -l3, qm)))
        q_aug = jnp.concatenate([qh, extra.astype(BF16)], axis=1)
        da_aug = jnp.concatenate(
            [dah, jnp.where(lane == 0, -d1, jnp.where(lane == 1, -d2, 0.0)).astype(BF16)], axis=1)
        dks, dvs, dqh = [], [], None
        for i in range(count // tile):
            sl = slice(i * tile, (i + 1) * tile)
            p = jnp.exp(mm(k_aug[sl], q_aug, LAST))
            dp = mm(v_aug[sl], da_aug, LAST)
            ds = (p * dp).astype(BF16)
            dvs.append(mm(p.astype(BF16), dah, PLAIN))
            dks.append(mm(ds, qh, PLAIN))
            part = mm(ds, kh[sl], FIRST)
            dqh = part if dqh is None else dqh + part
        dkh = jnp.concatenate(dks, axis=0)
        dvh = jnp.concatenate(dvs, axis=0)
        dq = dqh if dq is None else dq + dqh
        dk = dkh if dk is None else dk + dkh
        dv = dvh if dv is None else dv + dvh
    dq = dq * 0.125
    c = cos_ref[...]
    s = sin_ref[...]
    turned = dq * swap_halves(q.astype(F32) * 8.0) + dk * swap_halves(k.astype(F32))
    turned = jnp.where(lane % 64 < 32, -turned, turned)
    row = lambda a: jnp.sum(a, axis=0, keepdims=True)
    gf_ref[...] = jnp.concatenate(
        [row(turned * pos_ref[:, 0:1]), row(turned * pos_ref[:, 1:2]), jnp.zeros((6, 128), F32)], axis=0)
    dqp = (dq * c - swap_halves(dq) * s).astype(BF16)
    dkp = (dk * c - swap_halves(dk) * s).astype(BF16)
    dvp = dv.astype(BF16)
    gb_ref[...] = jnp.concatenate(
        [row(dqp.astype(F32)), row(dkp.astype(F32)), row(dvp.astype(F32)), jnp.zeros((5, 128), F32)], axis=0)
    dq_ref[...] = dqp
    dk_ref[...] = dkp
    dv_ref[...] = dvp


def attend_back(start, stop, before, q, k, v, da, attn, stat, cos, sin, qm, km, pos):
    count, width = q.shape
    whole = lambda p: (0, 0)
    col = lambda p: (0, p + start)
    tall = pl.BlockSpec((count, 128), col)
    fixed = pl.BlockSpec((count, 128), whole)
    small = pl.BlockSpec((8, 128), col)
    in_specs = [tall] * 8 + [fixed] * 2 + [pl.BlockSpec((count, 2), whole)]
    operands = [q, k, v, da, attn, stat, cos, sin, qm, km, pos]
    aliases = {}
    if before is not None:
        aliases = {len(operands) + i: i for i in range(5)}
        in_specs += [pl.BlockSpec(memory_space=pl.ANY)] * 5
        operands += list(before)
    return pl.pallas_call(
        functools.partial(back_kernel, before is None),
        grid=(stop - start,),
        in_specs=in_specs,
        out_specs=[tall] * 3 + [small] * 2,
        out_shape=[jax.ShapeDtypeStruct((count, width), BF16)] * 3 + [jax.ShapeDtypeStruct((8, width), F32)] * 2,
        input_output_aliases=aliases,
        compiler_params=pltpu.CompilerParams(vmem_limit_bytes=56 * 2**20),
        cost_estimate=SHORT,
        name="attend_back",
    )(*operands)


def qkv_grad_kernel(block_rows, core_ref, dq_ref, dk_ref, dv_ref, n1_ref, keep_ref, give_ref, stage_s, sem):
    width = n1_ref.shape[1]
    cols = dq_ref.shape[1]
    step = pl.program_id(0)
    n1 = n1_ref[...]
    for j, ref in enumerate((dq_ref, dk_ref, dv_ref)):
        put_halves(stage_s.at[step, j], mm(ref[...], n1, FIRST))
        send_rows(core_ref[0], block_rows, stage_s.at[step, j], j * width + step * cols, 0, keep_ref, give_ref, sem)

    @pl.when(step == pl.num_programs(0) - 1)
    def _():
        pltpu.make_async_copy(stage_s, stage_s, sem).wait()


def qkv_grad(core, dq, dk, dv, n1, block_rows):
    count, width = n1.shape
    cols = width // 2
    tall = pl.BlockSpec((count, cols), lambda p: (0, p))
    hbm = pl.BlockSpec(memory_space=pl.ANY)
    return pl.pallas_call(
        functools.partial(qkv_grad_kernel, block_rows),
        grid=(2,),
        in_specs=[pl.BlockSpec(memory_space=pltpu.SMEM)] + [tall] * 3 + [pl.BlockSpec((count, width), lambda p: (0, 0))],
        out_specs=[hbm, hbm],
        out_shape=grad_shapes(block_rows, 3 * width, width),
        scratch_shapes=[pltpu.VMEM((2, 3, 2, cols, width // 2), BF16), pltpu.SemaphoreType.DMA],
        compiler_params=pltpu.CompilerParams(vmem_limit_bytes=56 * 2**20),
        cost_estimate=SHORT,
        name="qkv_grad",
    )(core, dq, dk, dv, n1)


def input_kernel(dq_ref, dk_ref, dv_ref, w_ref, x_ref, dm_ref, vec_ref, sums_ref, gb_ref, gf_ref, up_ref, ig_ref, out_ref):
    step = pl.program_id(0)
    d = jnp.concatenate([dq_ref[...], dk_ref[...], dv_ref[...]], axis=1)
    dn = mm(d, w_ref[...], PLAIN)
    unit, inverse = norm_parts(x_ref[...].astype(F32))
    ig_ref[...] = dm_ref[...] + norm_back(unit, inverse, dn, vec_ref[0:1, :])
    row = lambda a: jnp.sum(a, axis=0, keepdims=True)
    sums = jnp.concatenate([row(dn * unit), row(dn)], axis=0)

    @pl.when(step == 0)
    def _():
        width = dn.shape[1]
        half = width // 2
        out_ref[0:2] = sums
        out_ref[2:4] = sums_ref[0:2]
        out_ref[4:7] = gb_ref[0:3]
        out_ref[7:8] = sums_ref[2:3]
        for i in range(4):
            out_ref[8 + i:9 + i] = up_ref[:, i * width:(i + 1) * width]
        out_ref[12:13] = sums_ref[3:4]
        lane = lax.broadcasted_iota(jnp.int32, (width, half), 0)
        slot = lax.broadcasted_iota(jnp.int32, (width, half), 1)
        pick = jnp.where((lane // 64 == slot // 32) & (lane % 32 == slot % 32), 1.0, 0.0)
        both = lax.dot_general(gf_ref[...], pick, PLAIN, precision=lax.Precision.HIGHEST, preferred_element_type=F32)
        out_ref[13:14, :half] = both[0:1]
        out_ref[13:14, half:] = both[1:2]

    @pl.when(step > 0)
    def _():
        out_ref[0:2] += sums


def input_back(dq, dk, dv, weights, x, dm, vectors, sums, grad_bias, grad_freq, bias_up):
    count, width = x.shape
    tile = 256
    part = pl.BlockSpec((tile, width), lambda i: (i, 0))
    whole = lambda i: (0, 0)
    fixed = lambda a: pl.BlockSpec(a.shape, whole)
    return pl.pallas_call(
        input_kernel,
        grid=(count // tile,),
        in_specs=[part] * 3 + [pl.BlockSpec((3 * width, width), whole), part, part]
        + [fixed(a) for a in (vectors, sums, grad_bias, grad_freq, bias_up)],
        out_specs=[part, fixed(vectors)],
        out_shape=[jax.ShapeDtypeStruct((count, width), F32), jax.ShapeDtypeStruct(vectors.shape, F32)],
        compiler_params=pltpu.CompilerParams(vmem_limit_bytes=56 * 2**20),
        cost_estimate=SHORT,
        name="input_back",
    )(dq, dk, dv, weights, x, dm, vectors, sums, grad_bias, grad_freq, bias_up)


def fold_kernel(pos_ref, keep_ref, got_ref, send_ref, hold_ref):
    rows = keep_ref.shape[1] // 2
    deep = 4
    piece = rows // deep
    more, less = MORE, piece - MORE
    for m in range(keep_ref.shape[0] // 2):
        both = []
        for y in (0, 1):
            here = slice(y * rows, y * rows + rows)
            even, odd = (
                keep_ref[2 * m + e, here, :].astype(F32) + got_ref[2 * m + e, here, :].astype(F32) for e in (0, 1)
            )
            parts = []
            for z in range(deep):
                at = z * piece
                parts.append((
                    jnp.concatenate([even[at:at + more], odd[at:at + less]], axis=0),
                    jnp.concatenate([even[at + more:at + piece], odd[at + less:at + piece]], axis=0),
                ))
            both.append([jnp.concatenate([p[x] for p in parts], axis=0).astype(BF16) for x in (0, 1)])
        for y in (0, 1):
            for x in (0, 1):
                for way in range(4):
                    @pl.when((pos_ref[way, 0] == y) & (pos_ref[way, 1] == x))
                    def _(way=way, y=y, x=x):
                        (send_ref, hold_ref)[way // 2][way % 2, m] = both[y][x]


def fold(pos, keep, got):
    count, rows, cols = keep.shape
    some = next(s for s in (6, 4, 2) if count % s == 0)
    whole = pl.BlockSpec((some, rows, cols), lambda i, pos: (i, 0, 0))
    out = pl.BlockSpec((2, some // 2, rows // 2, cols), lambda i, pos: (0, i, 0, 0))
    shape = jax.ShapeDtypeStruct((2, count // 2, rows // 2, cols), BF16)
    return pl.pallas_call(
        fold_kernel,
        grid_spec=pltpu.PrefetchScalarGridSpec(
            num_scalar_prefetch=1, grid=(count // some,), in_specs=[whole, whole], out_specs=[out, out]),
        compiler_params=pltpu.CompilerParams(vmem_limit_bytes=40 * 2**20),
        out_shape=[shape, shape],
        cost_estimate=SHORT,
        name="fold",
    )(pos, keep, got)


def pack_kernel(owner_ref, *refs):
    early, late, out_ref, total_s = refs[:4], refs[4:8], refs[8], refs[9]
    square = None
    start = 0
    rows = early[0].shape[1]
    for parts in (early, late):
        total = parts[0][...].astype(F32)
        for part in parts[1:]:
            total = total + part[...].astype(F32)
        total_s[start:start + total.shape[0], :rows] = total
        start += total.shape[0]
        more = jnp.sum(total * total).reshape(1, 1)
        square = more if square is None else square + more
    total_s[:, rows:] = jnp.zeros((start, total_s.shape[1] - rows, total_s.shape[2]), F32)
    lane = lax.broadcasted_iota(jnp.int32, (8, out_ref.shape[2]), 1)
    one, two, three = split3(square)
    extra = jnp.where(lane == 0, one, jnp.where(lane == 1, two, jnp.where(lane == 2, three, 0.0)))
    devices = out_ref.shape[0]
    skip = jnp.where(owner_ref[devices] == 0, MORE, rows - MORE)
    for p in range(devices):
        block = owner_ref[p]
        at = lax.rem(block, 2) * skip
        mine = total_s[lax.div(block, 2), pl.ds(pl.multiple_of(at, 8), MORE), :]
        out_ref[p] = jnp.concatenate([mine, extra], axis=0).astype(BF16)


def pack(owner, x, early, late):
    blocks = early[0].shape[0] + late[0].shape[0]
    rows, cols = early[0].shape[1:]
    vmem = pl.BlockSpec(memory_space=pltpu.VMEM)
    return pl.pallas_call(
        pack_kernel,
        in_specs=[pl.BlockSpec(memory_space=pltpu.SMEM)] + [vmem] * 8,
        out_specs=vmem,
        out_shape=jax.ShapeDtypeStruct((owner.shape[0], MORE + 8, cols), BF16),
        scratch_shapes=[pltpu.VMEM((blocks, rows + 8, cols), F32)],
        compiler_params=pltpu.CompilerParams(vmem_limit_bytes=32 * 2**20),
        cost_estimate=SHORT,
        name="pack",
    )(jnp.concatenate([owner, x.reshape(1).astype(owner.dtype)]), *early, *late)


def clip_of(square, vec):
    norm = jnp.sqrt(square + jnp.sum(vec * vec).reshape(1, 1))
    return norm, jnp.minimum(1.0, 1.0 / (norm + 1e-06))


def adam_kernel(own_ref, a_ref, b_ref, as_ref, bs_ref, vt_ref, vw_ref, vm_ref, vv_ref, w_ref, m_ref, v_ref,
                g_out, v_out, w_out, vg_out, vv_out, vw_out, norm_out):
    def squares(ref):
        block = ref[...].astype(F32)
        lane = lax.broadcasted_iota(jnp.int32, block.shape, 4)
        row = lax.broadcasted_iota(jnp.int32, block.shape, 3)
        return jnp.sum(jnp.where((lane < 3) & (row == 0), block, 0.0)).reshape(1, 1)

    norm, clip = clip_of(squares(as_ref) + squares(bs_ref), vt_ref[...])
    mine = pl.program_id(1) == own_ref[0]
    even = own_ref[1] == 0
    deep = a_ref.shape[0]
    piece = w_ref.shape[0] // deep
    runs = []
    for z in range(deep):
        left, right = (jnp.where(mine, a_ref[z, 0, x].astype(F32), b_ref[z, 0, x].astype(F32)) for x in (0, 1))
        runs.append(jnp.where(
            even,
            jnp.concatenate([left[:MORE], right[:piece - MORE]], axis=0),
            jnp.concatenate([left[:piece - MORE], right[:MORE]], axis=0),
        ))
    grad = jnp.concatenate(runs, axis=0) * clip
    second, weight = adam(w_ref[...], m_ref[...], v_ref[...], grad, 0.02, 0.05)
    g_out[...] = grad
    v_out[...] = second
    w_out[...] = weight

    @pl.when((pl.program_id(0) == 0) & (pl.program_id(1) == 0))
    def _():
        vec_grad = vt_ref[...] * clip
        second, weight = adam(vw_ref[...], vm_ref[...], vv_ref[...], vec_grad, 0.2, 0.0)
        vg_out[...] = vec_grad
        vv_out[...] = second
        vw_out[...] = weight
        norm_out[...] = norm


def adam_rows(own, mine, other, vec_total, vectors, vec_first, vec_second, weight, first, second):
    rows, width = weight.shape
    deep, tall, wide, piece, cols = mine.shape
    part = pl.BlockSpec((deep, 1, wide, piece, cols), lambda y, h: (0, y, 0, 0, 0))
    marks = pl.BlockSpec((deep, tall, wide, 8, 128), lambda y, x: (0, 0, 0, piece // 8 - 1, 0))
    flat = pl.BlockSpec((rows // tall, cols), lambda y, h: (y, h))
    vec = pl.BlockSpec(vectors.shape, lambda y, x: (0, 0))
    shape = jax.ShapeDtypeStruct((rows, width), F32)
    small = jax.ShapeDtypeStruct(vectors.shape, F32)
    return pl.pallas_call(
        adam_kernel,
        grid=(tall, width // cols),
        in_specs=[pl.BlockSpec(memory_space=pltpu.SMEM), part, part, marks, marks] + [vec] * 4 + [flat] * 3,
        out_specs=[flat] * 3 + [vec] * 3 + [pl.BlockSpec((1, 1), lambda y, x: (0, 0))],
        out_shape=[shape] * 3 + [small] * 3 + [jax.ShapeDtypeStruct((1, 1), F32)],
        compiler_params=pltpu.CompilerParams(vmem_limit_bytes=60 * 2**20),
        cost_estimate=SHORT,
        name="adam",
    )(own, mine, other, mine, other, vec_total, vectors, vec_first, vec_second, weight, first, second)


from jax.sharding import PartitionSpec as P

HEADS = 12
STEP = 7


def place_tokens(heights, widths, count):
    sizes = heights * widths
    ends = jnp.cumsum(sizes)
    starts = ends - sizes
    places = jnp.arange(count, dtype=jnp.int32)
    segment = jnp.sum((places[:, None] >= ends[None, :]).astype(jnp.int32), axis=1)
    slots = jnp.arange(heights.shape[0], dtype=jnp.int32)
    picks = (segment[:, None] == slots[None, :]).astype(jnp.int32)
    begin = jnp.sum(picks * starts[None, :], axis=1)
    across = jnp.maximum(jnp.sum(picks * widths[None, :], axis=1), 1)
    offset = places - begin
    live = places < ends[-1]
    return (segment, offset // across, offset % across, live)


def adam(weight, first, second, grad, rate, decay):
    first_new = 0.5 * first + 0.5 * grad
    second_new = 0.5 * second + 0.5 * grad * grad
    correct = 1.0 - 0.5**STEP
    direction = first_new / correct / (jnp.sqrt(second_new / correct) + 1e-08)
    return (second_new, weight - rate * (direction + decay * weight))


def pairwise(bits, total):
    return [(i, i ^ bits) for i in range(total)]


def sum_part(value, devices, step, stop):
    while step < stop:
        value = value + lax.ppermute(value, "dp", pairwise(step, devices))
        step *= 2
    return value


CORES = ("group", "dp")
SWAP = [(0, 1), (1, 0)]


def cross(value, bit0, bit1, devices):
    perm = [(i, i ^ (bit0 if i < devices else bit1)) for i in range(2 * devices)]
    return lax.ppermute(value, CORES, perm)


def along_z(values, devices):
    return [
        lax.ppermute(v, "dp", [(i, (i + 4 * (s + 1)) % devices) for i in range(devices)])
        for s, v in enumerate(values)
    ]


def along_line(value, devices, step, up):
    last = devices // 4
    perm = []
    for z in range(last):
        near = z - 1 if up else z + 1
        far = z - step if up else z + step
        if 0 <= far < last:
            perm += [(4 * near + i, 4 * z + i) for i in range(4)]
    return lax.ppermute(value, "dp", perm)


def gather_pieces(master, inverse, core, me, devices, freqs, make_angles, late, make_late, tables):
    tie = lax.optimization_barrier
    block_rows, width = master.shape
    half = block_rows // 2
    mine = lax.dynamic_slice_in_dim(master, core * half, half, 0).astype(BF16)
    large = mine[:LARGE]
    small = mine[LARGE:]
    z = me // 4
    deep = lax.rem(z - inverse // 4 + 4, 4)
    apart = me ^ inverse
    one = jnp.where(core == 0, apart & 1, (apart >> 1) & 1)
    two = jnp.where(core == 0, (apart >> 1) & 1, apart & 1)
    slots = jnp.stack([
        8 * two + 4 * one + deep,
        4 * deep + 2 * two + one,
        8 * one + 4 * two + deep,
        4 * deep + 2 * one + two,
    ]).astype(jnp.int32)
    up = along_z([large] * 3, devices)
    small = jnp.stack([small, cross(small, 1, 2, devices)])
    small, freqs = tie((small, freqs))
    small = jnp.concatenate([small, cross(small, 2, 1, devices)])
    large = jnp.stack([large] + up)
    large, small, tables, slots, angles = tie((large, small, tables, slots, make_angles(freqs)))
    first = cross(large, 1, 2, devices)
    ups = [along_line(small, devices, 1, True)]
    downs = [along_line(small, devices, 1, False)]
    first, ups[0], downs[0], late = tie((first, ups[0], downs[0], late))
    done = make_late(*late)
    first = jnp.concatenate([large, first])
    second = cross(first, 2, 1, devices)
    for step in (2, 3):
        ups.append(along_line(ups[-1], devices, step, True))
        downs.append(along_line(downs[-1], devices, step, False))
        if step == 2:
            ups[1], downs[1], done = tie((ups[1], downs[1], done))
    small = jnp.concatenate([small] + [jnp.where(z >= s, ups[s - 1], downs[3 - s]) for s in (1, 2, 3)])
    other = [lax.ppermute(a, "group", SWAP) for a in (first, second, small)]
    return (first, second, small, *other), slots, angles + done + tables


def quarters(core, me):
    x, y = me & 1, (me >> 1) & 1
    one = jnp.where(core == 0, x, y)
    two = jnp.where(core == 0, y, x)
    pairs = [(1 - one, 1 - two), (1 - one, two), (one, 1 - two), (one, two)]
    return jnp.stack([
        jnp.stack([jnp.where(core == 0, b, a), jnp.where(core == 0, a, b)]) for a, b in pairs
    ]).astype(jnp.int32)


def add_low(*terms):
    total = terms[0].astype(F32)
    for term in terms[1:]:
        total = total + term.astype(F32)
    return total.astype(BF16)


def sum_z(low, me, devices):
    count, rows, cols = low.shape
    z = me // 4
    low = low.reshape(count, 4, rows // 4, cols)
    pick = lambda at: lax.dynamic_index_in_dim(low, at, 1, keepdims=False)
    return (pick(z), *along_z([pick(lax.rem(z + s, 4)) for s in (1, 2, 3)], devices))


def reduce_plain(local_mat, owner_block, devices):
    rows, width = local_mat.shape
    block_rows = rows // devices
    term = local_mat.reshape(devices, block_rows, width)[owner_block].reshape(rows, width)
    share = lax.psum_scatter(term.astype(F32), "dp", scatter_dimension=0, tiled=True)
    return lax.psum(share.astype(BF16), "group").astype(F32)


def local(
    tokens,
    cotangent,
    grid_h,
    grid_w,
    owner_block,
    master,
    first_mom,
    second_mom,
    vectors,
    vec_first,
    vec_second,
):
    devices = lax.axis_size("dp")
    core = lax.axis_index("group")
    me = lax.axis_index("dp")
    count = tokens.shape[1]
    width = tokens.shape[2]
    heads = HEADS
    head_dim = width // heads
    half = head_dim // 2
    block_rows = master.shape[0]
    stack = devices * block_rows
    quick = devices == 16 and block_rows == 2 * (LARGE + SMALL) and width % 256 == 0
    inverse = jnp.argsort(owner_block)
    segment, rows_pos, cols_pos, live = place_tokens(grid_h[0], grid_w[0], count)
    x = tokens[0]

    def spread(part):
        return jnp.broadcast_to(part.reshape(heads, 1, half), (heads, 2, half)).reshape(1, width)

    freqs = (spread(vectors[13, : width // 2]), spread(vectors[13, width // 2 :]))

    def make_angles(freqs):
        down = rows_pos.astype(F32)[:, None]
        right = cols_pos.astype(F32)[:, None]
        angle = down * freqs[0] + right * freqs[1]
        lower = (jnp.arange(width) % head_dim < half)[None]
        cosine = jnp.cos(angle)
        sine = jnp.sin(angle)
        return (cosine, jnp.where(lower, -sine, sine))

    late = (x, cotangent[0])

    def make_late(x, cot):
        unit, _ = norm_parts(x.astype(F32))
        grad_two = jnp.where(live[:, None], cot, jnp.zeros((), BF16))
        return ((unit * vectors[0] + vectors[1]).astype(BF16), grad_two)

    def make_tables():
        ids = jnp.arange(128)[None]
        match = segment[:, None] == ids
        key_mask = jnp.where(match | ((ids >= 8) & (ids < 11)), 1.0, 0.0).astype(BF16)
        query_mask = jnp.where((ids < 8) & ~match, MASKED, 0.0).astype(BF16)
        places = jnp.stack([rows_pos, cols_pos], axis=1).astype(F32)
        return (key_mask, query_mask, places,
                vectors[4:7].reshape(1, 3 * width), vectors[8:12].reshape(1, 4 * width))

    if quick:
        weights, slots, tables = gather_pieces(master, inverse, core, me, devices, freqs, make_angles, late, make_late, make_tables())
    else:
        low = lax.all_gather(master.astype(BF16), "dp", axis=0, tiled=True)
        weights = low.reshape(devices, block_rows, width)[inverse].reshape(stack, width)
        slots = jnp.zeros((4, devices), jnp.int32)
        tables = make_angles(freqs) + make_late(*late) + make_tables()
    cosine, sine, first_in, grad_two, key_mask, query_mask, places, bias_qkv, bias_one = tables
    here = core.reshape(1).astype(jnp.int32)
    query, key, value, attn, stat, *placed = attend(
        here, slots, first_in, bias_qkv,
        cosine, sine, query_mask, key_mask, weights, stack,
    )
    if quick:
        weights = placed[0]
    whole_rows = block_rows if quick else 0
    block_out, grad_middle, grad_attn, sums, bias_up, keep_mlp, give_mlp = mlp(
        here, x, attn, grad_two, vectors, weights, bias_one, whole_rows
    )
    pairs = width // 128
    blocked = lambda a: a.reshape(-1, block_rows, width // 2)
    tie = lax.optimization_barrier
    if quick:
        pos = quarters(core, me)
        got = lax.ppermute(give_mlp, "group", SWAP)
    back = None
    cuts = (0, 1, pairs - 1, pairs)
    for start, stop in zip(cuts[:-1], cuts[1:]):
        back = attend_back(
            start, stop, back, query, key, value, grad_attn, attn, stat, cosine, sine, query_mask, key_mask, places
        )
        if quick and start == 0:
            (send, hold), back = tie((fold(pos, blocked(keep_mlp), blocked(got)), back))
            came = cross(send, 1, 2, devices)
        if quick and start == 1:
            send, back = tie((add_low(hold[0], came[0]), back))
            again = cross(send, 2, 1, devices)
    grad_q, grad_k, grad_v, grad_bias, grad_freq = back
    keep_qkv, give_qkv = qkv_grad(here, grad_q, grad_k, grad_v, first_in, whole_rows)
    if quick:
        again, give_qkv = tie((again, give_qkv))
        low, grad_v, give_qkv = tie((add_low(hold[1], came[1], again), grad_v, give_qkv))
        late = sum_z(low, me, devices)
    if quick:
        got_qkv = lax.ppermute(give_qkv, "group", SWAP)
        send, hold = fold(pos, blocked(keep_qkv), blocked(got_qkv))
        third = send.shape[2] // 3
        send = [send[:, :, third * i:third * (i + 1)] for i in range(3)]
        send, grad_v = tie((send, grad_v))
    input_grad, local_vec = input_back(
        grad_q, grad_k, grad_v, weights, x, grad_middle, vectors, sums, grad_bias, grad_freq, bias_up
    )
    if quick:
        send[2], local_vec = tie((send[2], local_vec))
        came = [cross(a, 1, 2, devices) for a in send]
        came, local_vec, late = tie((came, local_vec, late))
        came = jnp.concatenate(came, axis=2)
        again = cross(add_low(hold[0], came[0]), 2, 1, devices)
        vec_total = sum_part(local_vec, devices, 4, devices)
        again, vec_total = tie((again, vec_total))
        early = sum_z(add_low(hold[1], came[1], again), me, devices)
        early, vec_total = tie((early, sum_part(vec_total, devices, 1, 4)))
        load = pack(owner_block, me & 1, early, late)
        mine = lax.all_to_all(load, "dp", 0, 0, tiled=True)
        other = lax.ppermute(mine, "group", SWAP)
        vec_total = vec_total + lax.ppermute(lax.optimization_barrier((vec_total, mine))[0], "group", SWAP)
        shape = (devices // 4, 2, 2, *load.shape[1:])
        own = jnp.stack([core, owner_block[me] % 2]).astype(jnp.int32)
        mat_grad, mat_second, mat_weight, vec_grad, vec_second_new, vec_weight, norm = adam_rows(
            own, mine.reshape(shape), other.reshape(shape), vec_total, vectors, vec_first, vec_second,
            master, first_mom, second_mom,
        )
        grad_norm = norm.reshape(())
    else:
        vec_total = lax.psum(local_vec, CORES)
        share = reduce_plain(jnp.concatenate([keep_qkv, keep_mlp]), owner_block, devices)
        square = lax.psum(jnp.sum(share * share), "dp")
        grad_norm = jnp.sqrt(square + jnp.sum(vec_total * vec_total))
        clip = jnp.minimum(1.0, 1.0 / (grad_norm + 1e-06))
        mat_grad = share * clip
        mat_second, mat_weight = adam(master, first_mom, second_mom, mat_grad, 0.02, 0.05)
        vec_grad = vec_total * clip
        vec_second_new, vec_weight = adam(vectors, vec_first, vec_second, vec_grad, 0.2, 0.0)
    return (
        block_out[None],
        input_grad[None],
        mat_grad,
        mat_second,
        mat_weight,
        vec_grad,
        vec_second_new,
        vec_weight,
        grad_norm,
    )


def solution(mesh):
    return jax.shard_map(
        local,
        mesh=mesh,
        in_specs=(
            P("group", "dp", None),
            P("group", "dp", None),
            P("group", "dp"),
            P("group", "dp"),
            P(),
            P("dp", None),
            P("dp", None),
            P("dp", None),
            P(),
            P(),
            P(),
        ),
        out_specs=(
            P("group", "dp", None),
            P("group", "dp", None),
            P("dp", None),
            P("dp", None),
            P("dp", None),
            P(),
            P(),
            P(),
            P(),
        ),
        check_vma=False,
    )
```
